32 devices in a mesh: dp: 4 (over z), mp: 4 (over y, x), grid: 2 (over core).
Axes of the slice: x: 2, y: 2, z: 4, core: 2. Of those that a mesh axis runs over, the one named last changes fastest.
Arguments:
- tokens: bfloat16 [12608, 1024], P(('dp', 'grid')), may hold values from -6 to 6
- cotangent: bfloat16 [12608, 1024], P(('dp', 'grid')), may hold values from -6 to 6
- w_qkv: bfloat16 [1024, 3, 1024], P('grid', None, 'mp'), may hold values from -0.1875 to 0.1875
- qv_bias: bfloat16 [2, 1024], P('grid', 'mp'), may hold values from -1.75 to 1.75
- w_proj: bfloat16 [1024, 1024], P('mp', 'grid'), may hold values from -0.75 to 0.75
- proj_bias: bfloat16 [1024], P('grid'), may hold values from -1.75 to 1.75
- norm_gains: bfloat16 [2, 1024], P(None, 'grid'), may hold values from 0.099609375 to 1.8984375
- norm_shifts: bfloat16 [2, 1024], P(None, 'grid'), may hold values from -1.75 to 1.75
- w_router: bfloat16 [1024, 16], P('grid'), may hold values from -0.125 to 0.125
- expert_shift: bfloat16 [16, 1024], P(None, 'grid'), may hold values from -12 to 12
- w_first: bfloat16 [16, 1024, 4096], P(('dp', 'mp'), 'grid'), may hold values from -0.1875 to 0.1875
- w_second: bfloat16 [16, 4096, 1024], P(('dp', 'mp'), None, 'grid'), may hold values from -1.5 to 1.5
- first_bias: bfloat16 [16, 4096], P(('dp', 'mp'), 'grid'), may hold values from -1.25 to 1.25
- routes: int32 [12608, 2], P(('dp', 'grid')), may hold values from 0 to 15, all different within a row; in each aligned block of 1576 rows (0 to 1575, 1576 to 3151, ...) at most 315 rows name the same one
- priority: int32 [12608, 2], P(('dp', 'grid')), may hold values from 0 to 3151, as said below
Outputs:
- block_out: bfloat16 [12608, 1024], P(('dp', 'grid'))
- grad_tokens: float32 [12608, 1024], P(('dp', 'grid'))
- grad_w_qkv: float32 [1024, 3, 1024], P('grid', None, 'mp')
- grad_qv_bias: float32 [2, 1024], P('grid', 'mp')
- grad_w_proj: float32 [1024, 1024], P('mp', 'grid')
- grad_proj_bias: float32 [1024], P('grid')
- grad_norm_gains: float32 [2, 1024], P(None, 'grid')
- grad_norm_shifts: float32 [2, 1024], P(None, 'grid')
- grad_router: float32 [1024, 16], P('grid')
- grad_expert_shift: float32 [16, 1024], P(None, 'grid')
- grad_first: float32 [16, 1024, 4096], P(('dp', 'mp'), 'grid')
- grad_second: float32 [16, 4096, 1024], P(('dp', 'mp'), None, 'grid')
- grad_first_bias: float32 [16, 4096], P(('dp', 'mp'), 'grid')
- keep_mask: int32 [12608, 2], P(('dp', 'grid'))
The draws below stay inside these ranges and needn't reach their ends.
Inputs may be any that keep to these rules, and one draw needn't show every extreme that they name: `routes`: each row names two different experts. Within each aligned block of 1576 rows (the rows of one device) no expert is named by more than 315 rows, a bound that some block reaches. `priority`: within each aligned block of 1576 rows the 3152 entries are a permutation of 0 to 3151.
All inputs are finite; a program needn't handle non-finite values.
Results may differ from the reference program's by a relative error of at most 0.02.
Values may be sent and summed in bfloat16 or wider, within the bound.
No kernel may reach another device: no remote copies, remote signals or barrier semaphores. Data moves between devices by JAX's collectives and lax.ppermute only.
A program may use at most 320 MiB of HBM per device.

```python
import math
import jax
import jax.numpy as jnp
import numpy as np
from jax import lax

D = 1024
HEAD = 64
F = 4096
IMG_LEN = 197
IMG_DEV = 8
E = 16
QUART = 1
TOK_DEV = 1576
TOKENS = 12608
SLOTS = 315
CAP = 887
N_DP = 4
N_GRID = 2


def draw_priority(key, part):
    key = jax.random.fold_in(key, 7)
    block_keys = jax.random.split(key, TOKENS // TOK_DEV)
    orders = jax.vmap(lambda block_key: jax.random.permutation(block_key, 2 * TOK_DEV))(block_keys)
    return orders.reshape(TOKENS, 2).astype(jnp.int32)


def levels(key, dims, cuts, smallest, high):
    level = 1.0
    for axis_at, parts in cuts:
        heights = jax.random.uniform(jax.random.fold_in(jax.random.fold_in(key, 6), axis_at), (parts,), jnp.float32, smallest / len(cuts), high / len(cuts))
        level = level * jnp.repeat(jnp.exp(heights), dims[axis_at] // parts).reshape((-1,) + (1,) * (len(dims) - 1 - axis_at))
    return level


def deal_out(key, own, number, rows, number_of, top, reach, slope):
    ranking = jax.random.permutation(key, number_of)
    heavy_load, ordinary = portions_of(number_of, rows * top, reach, slope, True), portions_of(number_of, rows * top, reach, slope, False)
    places = jnp.arange(number_of)

    def named(sizes, turn):
        used = int((sizes > 0).sum())
        fixed = max(1, used // 4)
        passed = fixed + (places - fixed + turn * (used - fixed)) % max(1, number_of - fixed)
        return jnp.zeros((number_of,), jnp.int32).at[ranking[jnp.where(places < fixed, places, passed)]].set(jnp.asarray(sizes, jnp.int32))

    sizes = jnp.where(number % 4 == 0, named(heavy_load, number // 4), named(ordinary, number - number // 4 - 1))
    mixed = jax.random.permutation(jax.random.fold_in(own, 3), number_of)
    giver, receiver = mixed[0:number_of // 2 * 2:2], mixed[1:number_of // 2 * 2:2]
    margin = jnp.minimum(sizes[giver] - 1, reach - sizes[receiver]) // 2
    margin = jnp.where((giver == ranking[0]) | (receiver == ranking[0]) | (sizes[receiver] == 0), 0, jnp.maximum(margin, 0))
    passed = jax.random.randint(jax.random.fold_in(own, 4), (number_of // 2,), 0, 1 << 20) % (margin + 1)
    sizes = sizes.at[giver].add(-passed).at[receiver].add(passed)
    labels = jnp.searchsorted(jnp.cumsum(sizes), jnp.arange(rows * top), side="right").astype(jnp.int32)
    grid = labels.reshape(top, rows).T
    grid = grid[jax.random.permutation(jax.random.fold_in(own, 1), rows)]
    turn = jax.random.randint(jax.random.fold_in(own, 2), (rows, 1), 0, top)
    return jnp.take_along_axis(grid, (jnp.arange(top)[None, :] + turn) % top, axis=1)


def portions_of(count, total, reach, skew, full):
    loads = [(1 << 20) // math.isqrt(rank ** skew) + 1 for rank in range(1, count + 1)]
    largest = reach if full else min(reach, max(-(-total // count), total * loads[0] // sum(loads)))
    least = 1 if total - largest >= count - 1 else 0
    holding, rest = [largest] + [least] * (count - 1), total - largest - least * (count - 1)
    while rest > 0:
        free = [i for i in range(1, count) if holding[i] < largest] or [i for i in range(1, count) if holding[i] < reach]
        pool, remaining = sum([loads[i] for i in free]), rest
        for i in free:
            extra = min(reach - holding[i], max(1, remaining * loads[i] // pool), rest)
            holding[i] = holding[i] + extra
            rest = rest - extra
    return np.array(holding)


def gaussian(own_key, extent, spread, most, shards=(), kind=jnp.bfloat16):
    drawn = jax.random.normal(own_key, extent, jnp.float32) * spread
    if len(shards) > 0:
        drawn = levels(own_key, extent, shards, -0.22, 0.18) * drawn
    return jnp.clip(drawn, min=-most, max=most).astype(kind)


def setup_inputs(seed: int = 0) -> dict:
    key_list = jax.random.split(jax.random.key(seed), 16)
    tokens = gaussian(key_list[0], (TOKENS, D), 1.0, 6.0, ((0, 8),))
    cotangent = gaussian(key_list[1], (TOKENS, D), 1.0, 6.0, ((0, 8),))
    w_qkv = gaussian(key_list[2], (D, 3, D), D ** -0.5, 0.1875, ((0, 2), (2, 4)))
    qv_bias = gaussian(key_list[3], (2, D), 0.3, 1.75, ((0, 2), (1, 4)))
    w_proj = gaussian(key_list[4], (D, D), (D // 16) ** -0.5, 0.75, ((0, 4), (1, 2)))
    proj_bias = gaussian(key_list[5], (D,), 0.3, 1.75, ((0, 2),))
    norm_gains = jnp.clip(1.0 + 0.18 * jax.random.normal(key_list[6], (2, D), jnp.float32), 0.099609375, 1.8984375).astype(jnp.bfloat16)
    norm_shifts = gaussian(key_list[7], (2, D), 0.3, 1.75, ((1, 2),))
    w_router = gaussian(key_list[8], (D, E), (2 * D) ** -0.5, 0.125, ((0, 2),))
    expert_shift = gaussian(key_list[9], (E, D), 2.0, 12.0, ((1, 2),))
    w_first = gaussian(key_list[10], (E * QUART, D, F // QUART), D ** -0.5, 0.1875, ((0, 16), (1, 2)))
    w_second = gaussian(key_list[11], (E * QUART, F // QUART, D), (max(F // (E * E), 1)) ** -0.5, 1.5, ((0, 16), (2, 2)))
    first_bias = gaussian(key_list[12], (E * QUART, F // QUART), 0.2, 1.25, ((0, 16), (1, 2)))
    routes_keys = jax.random.split(jax.random.fold_in(key_list[13], 1), TOKENS // TOK_DEV)
    routes_turns = jax.random.permutation(jax.random.fold_in(key_list[13], 3), TOKENS // TOK_DEV)
    routes = jax.vmap(lambda own, number: deal_out(jax.random.fold_in(key_list[13], 2), own, number, TOK_DEV, E, 2, SLOTS, 1))(routes_keys, routes_turns).reshape((TOKENS, 2))
    priority = draw_priority(jax.random.fold_in(key_list[15], 71), 0)
    return dict(tokens=tokens, cotangent=cotangent, w_qkv=w_qkv, qv_bias=qv_bias, w_proj=w_proj, proj_bias=proj_bias, norm_gains=norm_gains, norm_shifts=norm_shifts, w_router=w_router, expert_shift=expert_shift, w_first=w_first, w_second=w_second, first_bias=first_bias, routes=routes, priority=priority)


precise = lax.Precision.HIGHEST

@jax.custom_vjp
def low(v):
    return lax.optimization_barrier(v.astype(jnp.bfloat16)).astype(jnp.float32)

@jax.custom_vjp
def low_back(v):
    return v

def low_keep(v):
    return (low(v), None)

def low_pass(kept, grad):
    return (grad,)

def back_keep(v):
    return (v, None)

def back_low(kept, grad):
    return (low(grad),)
low.defvjp(low_keep, low_pass)
low_back.defvjp(back_keep, back_low)

def matmul(left, right):
    return jnp.dot(left, right, precision=precise, preferred_element_type=jnp.float32)

def softmax_last(values):
    row_top = lax.optimization_barrier(jnp.max(values, axis=-1, keepdims=True))
    exp_vals = jnp.exp(values - row_top)
    return exp_vals / lax.optimization_barrier(jnp.sum(exp_vals, axis=-1, keepdims=True))

def gelu_tanh(values):
    return 0.5 * values * (1.0 + jnp.tanh(0.7978845608028654 * (values + 0.044715 * values * values * values)))

def layer_norm(values, gain, shift):
    centred = values - lax.optimization_barrier(jnp.mean(values, axis=-1, keepdims=True))
    inv_std = lax.rsqrt(lax.optimization_barrier(jnp.mean(centred * centred, axis=-1, keepdims=True)) + 1e-06)
    return centred * inv_std * gain + shift

def attend(block_rows):
    split_heads = block_rows.reshape(IMG_DEV, IMG_LEN, 3, D // HEAD, HEAD)
    queries = split_heads[:, :, 0]
    keyset = split_heads[:, :, 1]
    valset = split_heads[:, :, 2]
    scores = low_back(jnp.einsum('iqhd,ikhd->ihqk', queries, keyset, precision=precise) * HEAD ** (-0.5))
    att_probs = low(softmax_last(scores))
    head_mix = jnp.einsum('ihqk,ikhd->iqhd', att_probs, valset, precision=precise)
    return head_mix.reshape(IMG_DEV * IMG_LEN, D)

def expert(packed):
    rows_all, first_weight, first_shift, second_weight = packed
    part_width = F // QUART
    running = jnp.zeros((rows_all.shape[0], D), jnp.float32)
    for block_index in range(QUART):
        low_col = block_index * part_width
        rows_in = low_back(rows_all)
        pre_act = low_back(matmul(rows_in, first_weight[:, low_col:low_col + part_width]) + first_shift[low_col:low_col + part_width])
        active = low(gelu_tanh(pre_act))
        running = running + low(low_back(matmul(active, second_weight[low_col:low_col + part_width])))
    return running

def local_places(packed_block):
    route_block, rank_block = packed_block
    expert_ids = jnp.arange(E, dtype=jnp.int32)
    pair_hot = (route_block[:, None] == expert_ids[None, :]).astype(jnp.float32)
    earlier = (rank_block[None, :] < rank_block[:, None]).astype(jnp.float32)
    before = jnp.dot(earlier, pair_hot, precision=precise)
    place_local = lax.optimization_barrier(jnp.sum(before * pair_hot, axis=1))
    return (place_local.astype(jnp.int32), lax.optimization_barrier(jnp.sum(pair_hot, axis=0)).astype(jnp.int32))

def reference(tokens, cotangent, w_qkv, qv_bias, w_proj, proj_bias, norm_gains, norm_shifts, w_router, expert_shift, w_first, w_second, first_bias, routes, priority):
    blocks_all = TOKENS // TOK_DEV
    route_blocks = routes.reshape(blocks_all, 2 * TOK_DEV)
    place_local, counts = lax.map(local_places, (route_blocks, priority.reshape(blocks_all, 2 * TOK_DEV)))
    grouped = counts.reshape(N_DP, N_GRID, E)
    offsets = (jnp.cumsum(grouped, axis=0) - grouped).reshape(blocks_all, E)
    place = place_local + jnp.take_along_axis(offsets, route_blocks, axis=1)
    keep_mask = (place < CAP).astype(jnp.int32).reshape(TOKENS, 2)
    keep_float = keep_mask.astype(jnp.float32)
    block_ids = jnp.arange(blocks_all, dtype=jnp.int32)[:, None]
    group_index = jnp.broadcast_to(block_ids % N_GRID, (blocks_all, 2 * TOK_DEV)).reshape(-1)
    row_index = (block_ids // N_GRID * SLOTS + place_local).reshape(-1).astype(jnp.int32)
    route_flat = routes.reshape(-1)

    def forward(inputs, qkv_weight, qv_shift, proj_weight, proj_shift, gain_rows, shift_rows, router_weight, expert_bias, first_blocks, second_blocks, fshift_blocks):
        first_weight = first_blocks.reshape(E, QUART, D, F // QUART).transpose(0, 2, 1, 3).reshape(E, D, F)
        second_weight = second_blocks.reshape(E, F, D)
        first_shift = fshift_blocks.reshape(E, F)
        hidden_one = low(layer_norm(inputs, gain_rows[0], shift_rows[0]))
        qkv_rows = matmul(hidden_one, qkv_weight.reshape(D, 3 * D)).reshape(TOKENS, 3, D)
        qkv_rows = low(low_back(qkv_rows + jnp.stack([qv_shift[0], jnp.zeros_like(qv_shift[0]), qv_shift[1]])[None]))
        head_mix = lax.map(jax.checkpoint(attend), qkv_rows.reshape(blocks_all, TOK_DEV, 3, D))
        head_mix = low(low_back(head_mix.reshape(TOKENS, D)))
        after_attn = inputs + low_back(matmul(head_mix, proj_weight) + proj_shift)
        hidden_two = low(layer_norm(after_attn, gain_rows[1], shift_rows[1]))
        router_probs = softmax_last(low_back(matmul(hidden_two, router_weight)))
        route_hot = (routes[:, :, None] == jnp.arange(E, dtype=jnp.int32)[None, None, :]).astype(jnp.float32)
        gates = lax.optimization_barrier(jnp.sum(route_hot * router_probs[:, None, :], axis=-1))
        pair_rows = jnp.broadcast_to(hidden_two[:, None, :], (TOKENS, 2, D)).reshape(2 * TOKENS, D) * keep_float.reshape(-1, 1)
        expert_in = jnp.zeros((E, N_GRID, N_DP * SLOTS, D), jnp.float32).at[route_flat, group_index, row_index].add(pair_rows)
        results = lax.map(jax.checkpoint(expert), (expert_in.reshape(E, N_GRID * N_DP * SLOTS, D), first_weight, first_shift, second_weight))
        pair_out = results.reshape(E, N_GRID, N_DP * SLOTS, D)[route_flat, group_index, row_index].reshape(TOKENS, 2, D)
        pair_out = pair_out + jnp.take(expert_bias, routes, axis=0)
        weight = gates * keep_float
        return after_attn + lax.optimization_barrier(jnp.sum(weight[:, :, None] * pair_out, axis=1))
    floats = tuple((argument.astype(jnp.float32) for argument in (tokens, w_qkv, qv_bias, w_proj, proj_bias, norm_gains, norm_shifts, w_router, expert_shift, w_first, w_second, first_bias)))
    block_out, pull_back = jax.vjp(forward, *floats)
    grads = pull_back(cotangent.astype(jnp.float32))
    return (block_out.astype(jnp.bfloat16), grads[0], grads[1], grads[2], grads[3], grads[4], grads[5], grads[6], grads[7], grads[8], grads[9], grads[10], grads[11], keep_mask)
```

```python
import functools
from typing import NamedTuple

import jax
import jax.numpy as jnp
from jax import lax
from jax.experimental import pallas as pl
from jax.experimental.pallas import tpu as pltpu
from jax.sharding import PartitionSpec as P

HEAD = 64
IMG_LEN = 197
EXP_DEV = 4
BF = jnp.bfloat16
F32 = jnp.float32
I32 = jnp.int32
VMEM_BYTES = 56 * 1024 * 1024
LOW = -1e30


class Sizes(NamedTuple):
    T: int
    D: int
    half: int
    n: int
    X: int
    E: int
    S: int
    SP: int
    CR: int
    R: int
    TP: int
    W: int
    images: int
    quarters: int
    F: int
    cap: int
    win: int
    fblk: int
    key: int


class Order:
    def __init__(self):
        self.last = None


def up(value, step):
    return -(-value // step) * step


def dot_nn(a, b):
    return jnp.dot(a, b, preferred_element_type=F32)


def dot_nt(a, b):
    return lax.dot_general(a, b, (((1,), (1,)), ((), ())), preferred_element_type=F32)


def dot_tn(a, b):
    return lax.dot_general(a, b, (((0,), (0,)), ((), ())), preferred_element_type=F32)


def split_low(values):
    high = values.astype(BF)
    return high, (values - high.astype(F32)).astype(BF)


def shape_of(dims, dtype):
    return jax.ShapeDtypeStruct(dims, dtype)


def whole(array, buffers=None):
    dims = tuple(array.shape)
    extra = {} if buffers is None else {"pipeline_mode": pl.Buffered(buffers)}
    return pl.BlockSpec(dims, lambda i, s: (0,) * len(dims), **extra)


def rows_of(dims):
    return pl.BlockSpec(dims, lambda i, s: (i,) + (0,) * (len(dims) - 1))


def cols_of(dims):
    return pl.BlockSpec(dims, lambda i, s: (0,) * (len(dims) - 1) + (i,))


def call(order, body, place, args, specs, outs, out_specs, grid, scratch=(), name=None):
    extra = [] if order.last is None else [order.last]
    count = len(args)

    def wrapped(place, *refs):
        body(place, *refs[:count], *refs[count + len(extra) :])

    result = pl.pallas_call(
        wrapped,
        grid_spec=pltpu.PrefetchScalarGridSpec(
            num_scalar_prefetch=1,
            grid=grid,
            in_specs=list(specs) + [pl.BlockSpec(memory_space=pl.ANY)] * len(extra),
            out_specs=list(out_specs),
            scratch_shapes=list(scratch),
        ),
        out_shape=list(outs),
        compiler_params=pltpu.CompilerParams(
            dimension_semantics=("arbitrary",) * len(grid), vmem_limit_bytes=VMEM_BYTES
        ),
        cost_estimate=pl.CostEstimate(flops=1000, bytes_accessed=1000, transcendentals=0),
        name=name,
    )(place, *args, *extra)
    order.last = min(result, key=lambda o: o.size)
    return result


def swap_mp(c, value, mask):
    return lax.ppermute(value, "mp", [(i, i ^ mask) for i in range(c.n)])


def swap_grid(value):
    return lax.ppermute(value, "grid", [(0, 1), (1, 0)])


def trade(value, axis):
    return lax.all_to_all(value, axis, split_axis=0, concat_axis=0, tiled=True)


def groups_a(c):
    return [[0, 2], [1, 3]] if c.n == 4 else [[k] for k in range(c.n)]


def groups_b(c):
    return [[0, 1], [2, 3]] if c.n == 4 else [[k] for k in range(c.n)]


def reduce_mp(c, arrays):
    a, b = arrays[: len(arrays) // 2], arrays[len(arrays) // 2 :]
    if c.n != 4:
        return [[x[0]] + [swap_mp(c, x[k], k) for k in range(1, c.n)] for x in (a, b)]
    ra = swap_mp(c, a[1], 1)
    rb = swap_mp(c, b[1], 2)
    ta = (a[0][1:].astype(F32) + ra[1:].astype(F32)).astype(BF)
    tb = (b[0][1:].astype(F32) + rb[1:].astype(F32)).astype(BF)
    return [[a[0], ra, swap_mp(c, ta, 2)], [b[0], rb, swap_mp(c, tb, 1)]]


def piece_outs(c, more_a=0, more_b=0):
    outs = [shape_of((len(g), c.R + more_a, c.half), BF) for g in groups_a(c)]
    return outs + [shape_of((len(g), c.R + more_b, c.half), BF) for g in groups_b(c)]


def first_block(array):
    dims = tuple(array.shape)
    return pl.BlockSpec((None,) + dims[1:], lambda i, s: (0, 0, 0))


def add_up(refs):
    total = refs[0][...].astype(F32)
    for ref in refs[1:]:
        total = total + ref[...].astype(F32)
    return total


def gather_mp(c, value):
    if c.n != 4 or value.shape[0] != 2:
        parts = [value] + [swap_mp(c, value, k) for k in range(1, c.n)]
        return [[(p, h) for h in range(value.shape[0])] for p in parts]
    one = swap_mp(c, value, 1)
    two = swap_mp(c, value, 2)
    far_a = swap_mp(c, one[0:1], 2)
    far_b = swap_mp(c, two[1:2], 1)
    near = [[(p, 0), (p, 1)] for p in (value, one, two)]
    return near + [[(far_a, 0), (far_b, 0)]]


def flat(pieces):
    return [pair for piece in pieces for pair in piece]


def fold(c, value, axes):
    for axis, size in axes:
        mask = 1
        while mask < size:
            value = value + lax.ppermute(value, axis, [(i, i ^ mask) for i in range(size)])
            mask *= 2
    return value


def finish_sums(c, one, parts, grid):
    def half_of(side):
        cols = lax.dynamic_slice_in_dim(one, side * c.half, c.half, 1)
        row = lax.dynamic_index_in_dim(parts, side, 0, True)
        return jnp.concatenate([cols, jnp.pad(row, ((0, 0), (0, c.half - c.W)))], axis=0)

    return fold(c, half_of(grid) + swap_grid(half_of(1 - grid)), (("dp", c.X),))


def sum_proj(c, value):
    if c.n != 4:
        return jnp.sum(trade(value, "mp").astype(F32), axis=0).astype(BF)
    pair = (value[:2].astype(F32) + swap_mp(c, value[2:], 1).astype(F32)).astype(BF)
    return (pair[0].astype(F32) + swap_mp(c, pair[1], 2).astype(F32)).astype(BF)


def sum_dp(c, value):
    parts = trade(value.reshape((c.X, value.shape[0] // c.X) + value.shape[1:]), "dp")
    total = jnp.sum(parts.astype(F32), axis=0).astype(BF)
    spread = jnp.broadcast_to(total[None], (c.X,) + total.shape)
    return trade(spread, "dp").reshape(value.shape).astype(F32)


def expert_of(c, place, j):
    return j * EXP_DEV + place[3]


def offset_at(place, j):
    return place[4 + j]


def window_out(c, place, j):
    return place[4 + c.X + j]


def window_in(c, place, j):
    return pl.multiple_of(place[4 + 2 * c.X + j], 16)


def windows_body(c, place, counts, out_ref, off_ref):
    def window(offset):
        return jnp.minimum((offset >> 4) << 4, c.CR - c.SP)

    def before(e, source):
        total = jnp.int32(0)
        for b in range(c.X):
            total = total + jnp.where(b < source, counts[b, e], 0)
        return total

    for i in range(4):
        out_ref[i] = place[i]
    for i in range(4 + 3 * c.X, 32):
        out_ref[i] = jnp.int32(0)
    here = place[0] * EXP_DEV + place[3]
    for j in range(c.X):
        offset = before(expert_of(c, place, j), place[0])
        out_ref[4 + j] = offset
        out_ref[4 + c.X + j] = window(offset)
        out_ref[4 + 2 * c.X + j] = window(before(here, j))
    for e in range(c.E):
        off_ref[e : e + 1, :] = jnp.full((1, 128), before(e, place[0]), I32)


def windows(c, order, place, counts):
    return call(
        order,
        functools.partial(windows_body, c),
        place,
        [counts],
        [pl.BlockSpec(memory_space=pltpu.SMEM)],
        [shape_of((32,), I32), shape_of((c.E, 128), I32)],
        [pl.BlockSpec(memory_space=pltpu.SMEM), whole(shape_of((c.E, 128), I32))],
        (1,),
        name="windows",
    )


def route_body(c, place, row_ref, col_ref, rt_ref, slot_ref, rtb_ref, all_ref):
    first = jnp.broadcast_to(row_ref[0:1, :], (8, c.TP))
    second = jnp.broadcast_to(row_ref[1:2, :], (8, c.TP))

    def one(i, state):
        a, b = state
        for q in range(8):
            keys = col_ref[pl.ds(pl.multiple_of(i * 64 + q * 8, 8), 8), :]
            for k in range(2):
                key = keys[:, k : k + 1]
                a = a + (key < first).astype(I32)
                b = b + (key < second).astype(I32)
        return a, b

    zero = jnp.zeros((8, c.TP), I32)
    a, b = lax.fori_loop(0, c.TP // 64, one, (zero, zero))
    a = jnp.sum(a, axis=0, keepdims=True)
    b = jnp.sum(b, axis=0, keepdims=True)
    rt = rt_ref[...]
    start = jnp.zeros((1, 1), I32)
    for e in range(c.E):
        in_first = rt[0:1, :] == e
        in_second = rt[1:2, :] == e
        number = jnp.sum(in_first.astype(I32) + in_second.astype(I32), axis=1, keepdims=True)
        all_ref[e : e + 1, :] = jnp.where(in_first, a - start, jnp.where(in_second, b - start, -1))
        start = start + number
    for r in range(c.n):
        slot_ref[r] = all_ref[:, r * c.R : (r + 1) * c.R]
        rtb_ref[r] = jnp.concatenate([rt[:, r * c.R : (r + 1) * c.R]] * 4, axis=0)


def route(c, order, place, routes, priority):
    key = routes * c.key + priority
    big = 1 << 30
    pad = c.TP - c.T
    row = jnp.pad(key.T, ((0, 0), (0, pad)), constant_values=big)
    col = jnp.pad(key, ((0, pad), (0, 0)), constant_values=big)
    rt = jnp.pad(routes.T, ((0, 0), (0, pad)), constant_values=-1)
    outs = [shape_of((c.n, c.E, c.R), I32), shape_of((c.n, 8, c.R), I32)]
    return call(
        order,
        functools.partial(route_body, c),
        place,
        [row, col, rt],
        [whole(row), whole(col), whole(rt)],
        outs,
        [whole(o) for o in outs],
        (1,),
        [pltpu.VMEM((c.E, c.TP), I32)],
        name="route",
    )


def last_rows(c, tile, high, low):
    row = lax.broadcasted_iota(I32, (16, 1), 0)
    return jnp.where(row == 14, high, jnp.where(row == 15, low, tile))


def dispatch_body(c, rows_all, weighted, place, *refs):
    refs = list(refs)
    slot_ref, src_ref = refs[:2]
    refs = refs[2:]
    if weighted:
        weight_ref = refs.pop(0)
    out_ref, hot_ref, *refs = refs

    @pl.when(pl.program_id(0) == 0)
    def _():
        for j in range(c.X):
            e = expert_of(c, place, j)
            offset = offset_at(place, j)
            total = jnp.zeros((8, c.half), F32)
            for r in range(c.n):
                slot = slot_ref[r, pl.ds(e, 1), :]
                kept = (slot >= 0) & (slot + offset < c.cap)
                row = jnp.where(kept, slot + (offset - window_out(c, place, j)), -1)
                hot = (lax.broadcasted_iota(I32, (c.half, c.R), 0) == row).astype(BF)
                hot_ref[j, r] = hot[: c.SP]
                if weighted:
                    high, low = split_low(weight_ref[r, pl.ds(e, 1), :])
                    both = jnp.concatenate(
                        [jnp.broadcast_to(high, (8, c.R)), jnp.broadcast_to(low, (8, c.R))], axis=0
                    )
                    got = dot_nt(both, hot)
                    total = total + jnp.where(
                        lax.broadcasted_iota(I32, (8, 1), 0) == 0, got[0:8], got[8:16]
                    )
            if weighted:
                refs[0][j] = total

    for j in range(c.X):
        acc = None
        for r in range(c.n):
            length = min(c.R, rows_all - r * c.R)
            if length <= 0:
                continue
            part = dot_nn(hot_ref[j, r, :, :length], src_ref[r * c.R : r * c.R + length, :])
            acc = part if acc is None else acc + part
        out_ref[j] = acc.astype(BF)
        if weighted:

            @pl.when(pl.program_id(0) == 0)
            def _():
                tile = last_rows(c, acc[c.SP - 16 :], refs[0][j, 0:1, :], refs[0][j, 1:2, :])
                out_ref[j, c.SP - 16 :, :] = tile.astype(BF)


def dispatch(c, order, place, slot, source, weight=None):
    rows_all = source.shape[0]
    args = [slot, source]
    specs = [whole(slot), pl.BlockSpec((rows_all, c.half), lambda i, s: (0, i ^ s[2]))]
    scratch = [pltpu.VMEM((c.X, c.n, c.SP, c.R), BF)]
    if weight is not None:
        args.append(weight)
        specs.append(whole(weight))
        scratch.append(pltpu.VMEM((c.X, 8, c.half), F32))
    return call(
        order,
        functools.partial(dispatch_body, c, rows_all, weight is not None),
        place,
        args,
        specs,
        [shape_of((c.X, c.SP, c.D), BF)],
        [cols_of((c.X, c.SP, c.half))],
        (2,),
        scratch,
        name="dispatch",
    )[0]


def norm_rows(values):
    centred = values - jnp.mean(values, axis=-1, keepdims=True)
    inv_std = lax.rsqrt(jnp.mean(centred * centred, axis=-1, keepdims=True) + 1e-06)
    return centred * inv_std, inv_std


def norm_back(grad_norm, gain, normed, inv_std):
    scaled = grad_norm * gain
    return inv_std * (
        scaled
        - jnp.mean(scaled, axis=-1, keepdims=True)
        - normed * jnp.mean(scaled * normed, axis=-1, keepdims=True)
    )


def small_row(c, small_ref, index, count=1):
    return small_ref[index : index + count, :].astype(F32)


def own_cols(c, place):
    return pl.ds(pl.multiple_of(place[2] * c.half, c.half), c.half)


def other_cols(c, place):
    return pl.ds(pl.multiple_of((1 - place[2]) * c.half, c.half), c.half)


def live_rows(c, first, count):
    return (first + lax.broadcasted_iota(I32, (count, 1), 0)) < c.T


def qkv_body(c, place, tok_ref, small_ref, own_ref, oth_ref, hid_ref, qkv_ref, normed_ref):
    live = live_rows(c, pl.program_id(0) * c.R, c.R)
    values = jnp.where(live, tok_ref[...].astype(F32), 0.0)
    normed, _ = norm_rows(values)
    hidden = normed * small_row(c, small_ref, 0) + small_row(c, small_ref, 2)
    normed_ref[...] = normed.astype(BF)
    hid_ref[...] = jnp.where(live, hidden, 0.0).astype(BF)
    own = hid_ref[:, own_cols(c, place)]
    oth = hid_ref[:, other_cols(c, place)]
    for part in range(3):
        acc = dot_nn(own, own_ref[part]) + dot_nn(oth, oth_ref[part])
        if part != 1:
            bias = small_row(c, small_ref, 5)
            at = 0 if part == 0 else c.half
            acc = acc + bias[:, at : at + c.W]
        qkv_ref[:, part * c.W : (part + 1) * c.W] = acc.astype(BF)


def image_window(c):
    start = pl.program_id(0) * IMG_LEN
    low = pl.multiple_of(start // 16 * 16, 16)
    return low, start - low


def groups_of(c):
    lanes = min(128, c.W)
    return [(at, lanes) for at in range(0, c.W, lanes)]


def head_mask(lanes, head):
    lane = lax.broadcasted_iota(I32, (1, lanes), 1)
    return (lane >= head * HEAD) & (lane < (head + 1) * HEAD)


def attend_body(c, place, qkv_ref, mix_ref):
    @pl.when(pl.program_id(0) == 0)
    def _():
        mix_ref[...] = jnp.zeros_like(mix_ref)

    low, off = image_window(c)
    row = lax.broadcasted_iota(I32, (c.win, 1), 0)
    col = lax.broadcasted_iota(I32, (1, c.win), 1)
    in_row = (row >= off) & (row < off + IMG_LEN)
    in_col = (col >= off) & (col < off + IMG_LEN)
    for group, (at, lanes) in enumerate(groups_of(c)):
        q = qkv_ref[pl.ds(low, c.win), at : at + lanes] * BF(HEAD**-0.5)
        k = qkv_ref[pl.ds(low, c.win), c.W + at : c.W + at + lanes]
        v = qkv_ref[pl.ds(low, c.win), 2 * c.W + at : 2 * c.W + at + lanes]
        total = jnp.zeros((c.win, lanes), F32)
        for head in range(lanes // HEAD):
            mask = head_mask(lanes, head)
            scores = dot_nt(jnp.where(mask, q, BF(0)), k)
            scores = jnp.where(in_col, scores, LOW)
            top = jnp.max(scores, axis=-1, keepdims=True)
            exps = jnp.exp(scores - top)
            probs = exps / jnp.sum(exps, axis=-1, keepdims=True)
            total = total + dot_nn(probs.astype(BF), jnp.where(mask, v, BF(0)))
        old = mix_ref[group, pl.ds(low, c.win), :]
        mix_ref[group, pl.ds(low, c.win), :] = jnp.where(in_row, total.astype(BF), old)


def attend_back_body(c, place, qkv_ref, *refs):
    pieces, (out_ref, sums_ref, grad_ref) = refs[: c.n], refs[c.n :]
    @pl.when(pl.program_id(0) == 0)
    def _():
        out_ref[...] = jnp.zeros_like(out_ref)
        sums_ref[...] = jnp.zeros_like(sums_ref)
        for k in range(c.n):
            at = pl.multiple_of((place[1] ^ k) * c.R, 16)
            grad_ref[pl.ds(at, c.R), :] = pieces[k][...]

    low, off = image_window(c)
    row = lax.broadcasted_iota(I32, (c.win, 1), 0)
    in_row = (row >= off) & (row < off + IMG_LEN)
    scale = HEAD**-0.5
    for at, lanes in groups_of(c):
        q = qkv_ref[pl.ds(low, c.win), at : at + lanes] * BF(scale)
        k = qkv_ref[pl.ds(low, c.win), c.W + at : c.W + at + lanes]
        v = qkv_ref[pl.ds(low, c.win), 2 * c.W + at : 2 * c.W + at + lanes]
        do = jnp.where(in_row, grad_ref[pl.ds(low, c.win), at : at + lanes], BF(0))
        dq = jnp.zeros((c.win, lanes), F32)
        dk = jnp.zeros((c.win, lanes), F32)
        dv = jnp.zeros((c.win, lanes), F32)
        for head in range(lanes // HEAD):
            mask = head_mask(lanes, head)
            qh = jnp.where(mask, q, BF(0))
            doh = jnp.where(mask, do, BF(0))
            kh = jnp.where(mask, k, BF(0))
            scores = jnp.where(in_row, dot_nt(k, qh), LOW)
            top = jnp.max(scores, axis=0, keepdims=True)
            exps = jnp.exp(scores - top)
            soft = exps / jnp.sum(exps, axis=0, keepdims=True)
            dp = dot_nt(v, doh)
            delta = jnp.sum(soft * dp, axis=0, keepdims=True)
            ds = (soft * (dp - delta)).astype(BF)
            dq = dq + dot_tn(ds, kh)
            dk = dk + dot_nn(ds, qh)
            dv = dv + dot_nn(soft.astype(BF), doh)
        for part, grad in enumerate((dq * scale, dk, dv)):
            lane = part * c.W + at
            low_grad = jnp.where(in_row, grad, 0.0).astype(BF)
            old = out_ref[pl.ds(low, c.win), lane : lane + lanes]
            out_ref[pl.ds(low, c.win), lane : lane + lanes] = jnp.where(in_row, low_grad, old)
            summed = jnp.sum(low_grad.astype(F32), axis=0, keepdims=True)
            sums_ref[0:1, lane : lane + lanes] += summed


def middle_body(c, place, *refs):
    refs = list(refs)
    groups = groups_of(c)
    count = c.n * len(groups)
    mixes, refs = refs[:count], refs[count:]
    w_ref, tok_ref, small_ref, off_ref, slot_ref, rt_ref = refs[:6]
    hid_ref, weight_ref, mine_ref, keep_ref = refs[6:10]
    after_ref, probs_ref, keep_lane_ref, weight_lane_ref, acc_ref = refs[10:]
    step = pl.program_id(0)
    for h in range(2):
        acc = None
        for k in range(c.n):
            for group, (at, lanes) in enumerate(groups):
                weights = w_ref[(place[1] ^ k) * 2 + h, at : at + lanes, :]
                part = dot_nn(mixes[k * len(groups) + group][...], weights)
                acc = part if acc is None else acc + part
        acc_ref[:, h * c.half : (h + 1) * c.half] = acc
    live = live_rows(c, step * c.R, c.R)
    tok = jnp.where(live, tok_ref[...].astype(F32), 0.0)
    after = tok + acc_ref[...] + small_row(c, small_ref, 4)
    normed, _ = norm_rows(after)
    hidden = (normed * small_row(c, small_ref, 1) + small_row(c, small_ref, 3)).astype(BF)
    hid_ref[...] = hidden
    router = small_ref[6 + c.E : 6 + 2 * c.E, :]
    logits = dot_nt(router, hidden)
    exps = jnp.exp(logits - jnp.max(logits, axis=0, keepdims=True))
    probs = exps / jnp.sum(exps, axis=0, keepdims=True)
    slot = slot_ref[0]
    kept = (slot >= 0) & (slot + off_ref[:, 0:1] < c.cap)
    weight = jnp.where(kept, probs, 0.0)
    weight_ref[0] = weight
    for j in range(c.X):
        e = expert_of(c, place, j)
        offset = offset_at(place, j)
        slot_j = slot_ref[0, pl.ds(e, 1), :]
        kept_j = (slot_j >= 0) & (slot_j + offset < c.cap)
        row = jnp.where(kept_j, slot_j + (offset - window_out(c, place, j)), -1)
        mine_ref[0, j : j + 1, :] = row
    for j in range(c.X, 8):
        mine_ref[0, j : j + 1, :] = jnp.full((1, c.R), -1, I32)
    expert = lax.broadcasted_iota(I32, (c.E, c.R), 0)
    rows = []
    for k in range(2):
        picked = jnp.where((rt_ref[0, k : k + 1, :] == expert) & kept, 1.0, 0.0)
        rows.append(jnp.sum(picked, axis=0, keepdims=True))
    keep_ref[0] = jnp.concatenate(rows * 4, axis=0)

    @pl.when(step == place[1])
    def _():
        after_ref[...] = after
        probs_ref[...] = probs
        keep_lane_ref[...] = jnp.where(kept, 1.0, 0.0)
        weight_lane_ref[...] = weight


def middle(c, order, place, mixes, proj, tokens, small, offsets, slot, rt):
    args = [pair[0] for pair in flat(mixes)] + [proj, tokens, small, offsets, slot, rt]
    specs = [
        pl.BlockSpec((None, c.R, a.shape[2]), lambda i, s, at=at: (at, i, 0))
        for a, at in flat(mixes)
    ]
    specs += [whole(proj), rows_of((c.R, c.D)), whole(small), whole(offsets)]
    specs += [rows_of((1, c.E, c.R)), rows_of((1, 8, c.R))]
    outs = [
        shape_of((c.TP, c.D), BF),
        shape_of((c.n, c.E, c.R), F32),
        shape_of((c.n, 8, c.R), I32),
        shape_of((c.n, 8, c.R), F32),
        shape_of((c.R, c.D), F32),
        shape_of((c.E, c.R), F32),
        shape_of((c.E, c.R), F32),
        shape_of((c.E, c.R), F32),
    ]
    out_specs = [
        rows_of((c.R, c.D)),
        rows_of((1, c.E, c.R)),
        rows_of((1, 8, c.R)),
        rows_of((1, 8, c.R)),
    ] + [whole(o) for o in outs[4:]]
    return call(
        order,
        functools.partial(middle_body, c),
        place,
        args,
        specs,
        outs,
        out_specs,
        (c.n,),
        [pltpu.VMEM((c.R, c.D), F32)],
        name="middle",
    )


def pack_rows(c, place, rows, out_ref):
    main = c.SP - 16
    used = lax.broadcasted_iota(I32, (16, 1), 0) < c.S + 15 - main
    out_ref[...] = jnp.zeros_like(out_ref)
    for j in range(c.X):
        at = window_in(c, place, j)
        out_ref[pl.ds(at, main), :] += rows[j, :main, :]
        tail = jnp.where(used, rows[j, main:, :], BF(0))
        out_ref[pl.ds(pl.multiple_of(at + main, 16), 16), :] += tail


def last_pair(c, tile, lanes):
    tile = tile[:, :lanes].astype(F32)
    return tile[14:15, :], tile[15:16, :]


def row_chunks(c, size):
    return [(at, min(size, c.CR - at)) for at in range(0, c.CR, size)]


def grad_active_body(c, place, *refs):
    rows, own_ref, oth_ref, out_ref, all_ref = refs

    @pl.when(pl.program_id(0) == 0)
    def _():
        pack_rows(c, place, rows, all_ref)

    weights = jnp.concatenate([own_ref[...], oth_ref[...]], axis=1)
    for at, size in row_chunks(c, 448):
        out_ref[at : at + size, :] = dot_nt(all_ref[at : at + size, :], weights).astype(BF)


def grad_active(c, order, place, rows, own_w, oth_w):
    outs = [shape_of((c.CR, c.F), BF), shape_of((c.CR, c.D), BF)]
    return call(
        order,
        functools.partial(grad_active_body, c),
        place,
        [rows, own_w, oth_w],
        [whole(rows, 1)] + [rows_of((c.fblk, c.half))] * 2,
        outs,
        [cols_of((c.CR, c.fblk)), whole(outs[1])],
        (c.F // c.fblk,),
        name="grad_active",
    )


def expert_body(c, place, *refs):
    rows, own_ref, oth_ref, bias_ref, ga_ref = refs[:5]
    act_ref, gp_ref, gb_ref, all_ref, col_ref, back_ref = refs[5:11]
    acc_ref, dot_ref, row_ref = refs[11:]
    step = pl.program_id(0)

    @pl.when(step == 0)
    def _():
        acc_ref[...] = jnp.zeros_like(acc_ref)
        dot_ref[...] = jnp.zeros_like(dot_ref)
        pack_rows(c, place, rows, all_ref)
        col_ref[...] = jnp.zeros_like(col_ref)
        eye = lax.broadcasted_iota(I32, (c.SP, c.SP), 0) == lax.broadcasted_iota(I32, (c.SP, c.SP), 1)
        for j in range(c.X):
            high, low = last_pair(c, rows[j, c.SP - 16 :, :], c.SP)
            col = jnp.sum(jnp.where(eye, high + low, 0.0), axis=1, keepdims=True)
            col_ref[pl.ds(window_in(c, place, j), c.SP), :] += jnp.broadcast_to(col, (c.SP, 128))

    bias = bias_ref[...]
    weights = jnp.concatenate([own_ref[...], oth_ref[...]], axis=0)
    summed = jnp.zeros((1, c.fblk), F32)
    lead = 0.7978845608028654
    cube = lead * 0.044715
    for at, size in row_chunks(c, 224):
        rows_at = slice(at, at + size)
        pre = dot_nn(all_ref[rows_at, :], weights) + bias
        square = pre * pre
        turn = jnp.tanh(pre * (cube * square + lead))
        above = 1.0 + turn
        active = (0.5 * pre) * above
        slope = above * (1.0 + (1.0 - turn) * (pre * (3 * cube * square + lead)))
        ga = ga_ref[rows_at, :].astype(F32)
        product = active * ga
        part = product[:, 0:128]
        for lane in range(128, c.fblk, 128):
            part = part + product[:, lane : lane + 128]
        dot_ref[rows_at, :] += part
        grad = ga * slope * (0.5 * col_ref[rows_at, 0:1])
        act_ref[rows_at, :] = active.astype(BF)
        grad_low = grad.astype(BF)
        gp_ref[rows_at, :] = grad_low
        summed = summed + jnp.sum(grad, axis=0, keepdims=True)
        acc_ref[rows_at, :] += dot_nt(grad_low, weights)
    gb_ref[...] = jnp.broadcast_to(summed, (8, c.fblk))

    @pl.when(step == pl.num_programs(0) - 1)
    def _():
        ones = jnp.ones((8, 128), BF)
        row_ref[...] = jnp.zeros_like(row_ref)
        for j in range(c.X):
            at = window_in(c, place, j)
            back_ref[j] = acc_ref[pl.ds(at, c.SP), :].astype(BF)
            a, rest = split_low(dot_ref[pl.ds(at, c.SP), :])
            total = dot_nt(ones, a) + dot_nt(ones, rest)
            high = total.astype(BF).astype(F32)
            row_ref[0:8, : c.SP] = high
            row_ref[8:16, : c.SP] = total - high
            tile = back_ref[j, c.SP - 16 :, : c.half].astype(F32)
            tile = last_rows(c, tile, row_ref[0:1, :], row_ref[8:9, :])
            back_ref[j, c.SP - 16 :, : c.half] = tile.astype(BF)


def expert(c, order, place, rows, own_w, oth_w, bias, ga):
    args = [rows, own_w, oth_w, bias, ga]
    specs = [whole(rows, 1)]
    specs += [cols_of((c.half, c.fblk))] * 2
    specs += [cols_of((1, c.fblk)), cols_of((c.CR, c.fblk))]
    outs = [
        shape_of((c.CR, c.F), BF),
        shape_of((c.CR, c.F), BF),
        shape_of((8, c.F), F32),
    ]
    out_specs = [cols_of((c.CR, c.fblk))] * 2 + [cols_of((8, c.fblk))]
    late = [shape_of((c.CR, c.D), BF), shape_of((c.CR, 128), F32)]
    late.append(shape_of((c.X, c.SP, c.D), BF))
    return call(
        order,
        functools.partial(expert_body, c),
        place,
        args,
        specs,
        outs + late,
        out_specs + [whole(o, 1) for o in late],
        (c.F // c.fblk,),
        [
            pltpu.VMEM((c.CR, c.D), F32),
            pltpu.VMEM((c.CR, 128), F32),
            pltpu.VMEM((16, c.half), F32),
        ],
        name="expert",
    )


def produce_body(c, place, *refs):
    col_ref, act_ref, own_ref, oth_ref, out_ref, acc_ref = refs
    step = pl.program_id(0)

    @pl.when(step == 0)
    def _():
        acc_ref[...] = jnp.zeros_like(acc_ref)

    weights = jnp.concatenate([own_ref[...], oth_ref[...]], axis=1)
    for at, size in row_chunks(c, 448):
        acc_ref[at : at + size, :] += dot_nn(act_ref[at : at + size, :], weights)

    @pl.when(step == pl.num_programs(0) - 1)
    def _():
        for j in range(c.X):
            rows_at = pl.ds(window_in(c, place, j), c.SP)
            col = col_ref[rows_at, 0:1]
            out_ref[j] = (acc_ref[rows_at, :] * col).astype(BF)


def produce(c, order, place, col, act, own_w, oth_w):
    out = shape_of((c.X, c.SP, c.D), BF)
    return call(
        order,
        functools.partial(produce_body, c),
        place,
        [col, act, own_w, oth_w],
        [
            whole(col),
            cols_of((c.CR, c.fblk)),
            rows_of((c.fblk, c.half)),
            rows_of((c.fblk, c.half)),
        ],
        [out],
        [whole(out, 1)],
        (c.F // c.fblk,),
        [pltpu.VMEM((c.CR, c.D), F32)],
        name="produce",
    )[0]


def grad_second_body(c, own, place, *refs):
    refs = list(refs)
    all_ref, col_ref, act_ref = refs[:3]
    out_ref, row_ref = refs[-2:]

    @pl.when(pl.program_id(0) == 0)
    def _():
        row_ref[...] = (all_ref[...].astype(F32) * col_ref[:, 0:1]).astype(BF)

    acc = dot_tn(act_ref[...], row_ref[...])
    if own:
        acc = acc + refs[3][...].astype(F32)
    out_ref[...] = acc.astype(out_ref.dtype)


def grad_second(c, order, place, rows, col, act, add=None):
    own = add is not None
    args = [rows, col, act]
    specs = [
        pl.BlockSpec((c.CR, c.half), lambda i, s: (0, 0 if own else 1)),
        whole(col),
        cols_of((c.CR, c.fblk)),
    ]
    if own:
        args.append(add)
        specs.append(rows_of((c.fblk, c.half)))
    out = shape_of((c.F, c.half), F32 if own else BF)
    return call(
        order,
        functools.partial(grad_second_body, c, own),
        place,
        args,
        specs,
        [out],
        [rows_of((c.fblk, c.half))],
        (c.F // c.fblk,),
        [pltpu.VMEM((c.CR, c.half), BF)],
        name="grad_second",
    )[0]


def grad_first_body(c, own, place, *refs):
    acc = dot_tn(refs[0][...], refs[1][...])
    if own:
        acc = acc + refs[2][...].astype(F32)
    refs[-1][...] = acc.astype(refs[-1].dtype)


def grad_first(c, order, place, rows, gp, add=None):
    own = add is not None
    args = [rows, gp]
    specs = [
        pl.BlockSpec((c.CR, c.half), lambda i, s: (0, 0 if own else 1)),
        cols_of((c.CR, c.fblk)),
    ]
    if own:
        args.append(add)
        specs.append(cols_of((c.half, c.fblk)))
    out = shape_of((c.half, c.F), F32 if own else BF)
    return call(
        order,
        functools.partial(grad_first_body, c, own),
        place,
        args,
        specs,
        [out],
        [cols_of((c.half, c.fblk))],
        (c.F // c.fblk,),
        name="grad_first",
    )[0]


def combine_body(c, with_dots, place, *refs):
    refs = list(refs)
    rows_ref = refs.pop(0)
    tail_ref = refs.pop(0) if with_dots else None
    mine_ref = refs.pop(0)
    groups = [(0, g) for g in groups_a(c)] + [(1, g) for g in groups_b(c)]
    outs, (hot_ref, row_ref) = refs[: len(groups)], refs[len(groups) :]
    pad = hot_ref.shape[2] // c.X

    @pl.when(pl.program_id(0) == 0)
    def _():
        row_ref[...] = jnp.zeros_like(row_ref)
        slots = lax.broadcasted_iota(I32, (c.R, pad), 1)
        expert = lax.broadcasted_iota(I32, (c.E, 1), 0)
        for k in range(c.n):
            at = pl.multiple_of((place[1] ^ k) * c.R, 16)
            pulls = jnp.zeros((c.E, c.R), F32)
            for j in range(c.X):
                hot = (mine_ref[pl.ds(at, c.R), j : j + 1] == slots).astype(BF)
                hot_ref[k, :, j * pad : (j + 1) * pad] = hot
                if with_dots:
                    high, low = last_pair(c, tail_ref[j], pad)
                    both = jnp.concatenate(
                        [jnp.broadcast_to(high, (8, pad)), jnp.broadcast_to(low, (8, pad))], axis=0
                    )
                    got = dot_nt(both.astype(BF), hot)
                    got = got[0:1, :] + got[8:9, :]
                    pulls = jnp.where(expert == expert_of(c, place, j), got, pulls)
            if with_dots:
                for (side, group), out_ref in zip(groups, outs):
                    if side == 0 and k in group:
                        at = group.index(k)
                        out_ref[at, c.R :, :] = jnp.zeros((c.E, c.half), BF)
                        out_ref[at, c.R :, : c.R] = pulls.astype(BF)

    for j in range(c.X):
        row_ref[j * pad : j * pad + c.SP, :] = rows_ref[j]
    for half in range(2):

        @pl.when(pl.program_id(0) == half)
        def _():
            for (side, group), out_ref in zip(groups, outs):
                if side == half:
                    for at, k in enumerate(group):
                        out_ref[at, : c.R, :] = dot_nn(hot_ref[k], row_ref[...]).astype(BF)


def combine(c, order, place, rows, mine, with_dots=False):
    pad = up(c.SP, 128)
    args = [rows]
    specs = [pl.BlockSpec((c.X, c.SP, c.half), lambda i, s: (0, 0, i ^ s[2]))]
    if with_dots:
        args.append(rows)
        specs.append(pl.BlockSpec((c.X, 16, c.half), lambda i, s: (0, c.SP // 16 - 1, 0)))
    args.append(mine)
    specs.append(whole(mine))
    outs = piece_outs(c, c.E if with_dots else 0)
    result = call(
        order,
        functools.partial(combine_body, c, with_dots),
        place,
        args,
        specs,
        outs,
        [whole(o, 1) for o in outs],
        (2,),
        [pltpu.VMEM((c.n, c.R, c.X * pad), BF), pltpu.VMEM((c.X * pad, c.half), BF)],
        name="combine",
    )
    return list(result)


def back_two_body(c, place, *refs):
    refs = list(refs)
    count = (len(refs) - 11 - c.n) // 2
    a, b, refs = refs[:count], refs[count : 2 * count], refs[2 * count :]
    w_ref, after_ref, probs_ref, keep_ref, weight_ref, cot_ref, hid_ref, small_ref = refs[:8]
    ga_ref, gb_ref, sums_ref = refs[8:11]
    mixes = refs[11:]
    sum_a = add_up(a)
    live = live_rows(c, place[1] * c.R, c.R)
    cot = jnp.where(live, cot_ref[...], BF(0))
    eshift = small_ref[6 : 6 + c.E, :]
    router = small_ref[6 + c.E : 6 + 2 * c.E, :]
    kept = keep_ref[...] > 0
    pulls = jnp.where(kept, sum_a[c.R :, : c.R] + dot_nt(eshift, cot), 0.0)
    probs = probs_ref[...]
    glog = (probs * (pulls - jnp.sum(probs * pulls, axis=0, keepdims=True))).astype(BF)
    two = jnp.concatenate([sum_a[: c.R], add_up(b)], axis=1) + dot_tn(glog, router)
    normed, inv_std = norm_rows(after_ref[...])
    grad_after = cot.astype(F32) + norm_back(two, small_row(c, small_ref, 1), normed, inv_std)
    ga_ref[...] = grad_after
    low = grad_after.astype(BF)
    gb_ref[...] = low
    high, rest = split_low(weight_ref[...])
    hid = jnp.where(live, hid_ref[...], BF(0))
    sums_ref[0:1, :] = jnp.sum(two * normed, axis=0, keepdims=True)
    sums_ref[1:2, :] = jnp.sum(two, axis=0, keepdims=True)
    sums_ref[2:3, :] = jnp.sum(low.astype(F32), axis=0, keepdims=True)
    sums_ref[3:8, :] = jnp.zeros((5, c.D), F32)
    sums_ref[8 : 8 + c.E, :] = dot_nn(high, cot) + dot_nn(rest, cot)
    sums_ref[8 + c.E : 8 + 2 * c.E, :] = dot_nn(glog, hid)
    for k in range(c.n):
        lane = place[1] ^ k
        mix = dot_nt(gb_ref[:, : c.half], w_ref[2 * lane])
        mix = mix + dot_nt(gb_ref[:, c.half :], w_ref[2 * lane + 1])
        mixes[k][...] = mix.astype(BF)


def back_two(c, order, place, sums, proj, lanes, cotangent, hidden, small):
    args = [*sums[0], *sums[1], proj, *lanes, cotangent, hidden, small]
    lane_rows = pl.BlockSpec((c.R, c.D), lambda i, s: (s[1], 0))
    specs = [first_block(a) for a in [*sums[0], *sums[1]]]
    specs += [whole(a) for a in [proj, *lanes]] + [lane_rows, lane_rows, whole(small)]
    outs = [
        shape_of((c.R, c.D), F32),
        shape_of((c.R, c.D), BF),
        shape_of((8 + 2 * c.E, c.D), F32),
    ] + [shape_of((c.R, c.W), BF) for _ in range(c.n)]
    result = call(
        order,
        functools.partial(back_two_body, c),
        place,
        args,
        specs,
        outs,
        [whole(o) for o in outs],
        (1,),
        name="back_two",
    )
    return (*result[:3], list(result[3:]))


def block_out_body(c, place, *refs):
    refs = list(refs)
    count = (len(refs) - 4) // 2
    a, b, refs = refs[:count], refs[count : 2 * count], refs[2 * count :]
    after_ref, weight_ref, small_ref, out_ref = refs
    high, low = split_low(weight_ref[...])
    eshift = small_ref[6 : 6 + c.E, :]
    shift = dot_tn(high, eshift) + dot_tn(low, eshift)
    for h, pieces in enumerate((a, b)):
        cols = slice(h * c.half, (h + 1) * c.half)
        out_ref[h] = (after_ref[:, cols] + add_up(pieces) + shift[:, cols]).astype(BF)


def block_out(c, order, place, sums, after, weight, small):
    args = [*sums[0], *sums[1], after, weight, small]
    out = shape_of((2, c.R, c.half), BF)
    return call(
        order,
        functools.partial(block_out_body, c),
        place,
        args,
        [first_block(a) for a in args[:-3]] + [whole(a) for a in args[-3:]],
        [out],
        [whole(out)],
        (1,),
        name="block_out",
    )[0]


def grad_proj_body(c, place, *refs):
    groups = groups_of(c)
    count = c.n * len(groups)
    mixes, (gb_ref, sums_ref, own_ref, oth_ref) = refs[:count], refs[count:]
    height = sums_ref.shape[0]
    slot = [0, 2, 1, 3] if c.n == 4 else [place[1] ^ k for k in range(c.n)]
    for cols, out_ref in ((own_cols(c, place), own_ref), (other_cols(c, place), oth_ref)):
        out_ref[...] = jnp.zeros_like(out_ref)
        sums = sums_ref[:, cols].astype(BF)
        for k in range(c.n):
            for group, (at, lanes) in enumerate(groups):
                part = dot_tn(mixes[k * len(groups) + group][...], gb_ref[:, cols])
                out_ref[slot[k], at : at + lanes, :] = part.astype(BF)
            out_ref[slot[k], c.W : c.W + height, :] = sums


def grad_proj(c, order, place, mixes, grad_branch, sums):
    rows = up(c.W + sums.shape[0], 16 * c.X)
    specs = [
        pl.BlockSpec((None, c.R, a.shape[2]), lambda i, s, at=at: (at, s[1], 0))
        for a, at in flat(mixes)
    ]
    outs = [shape_of((c.n, rows, c.half), BF)] * 2
    return call(
        order,
        functools.partial(grad_proj_body, c),
        place,
        [pair[0] for pair in flat(mixes)] + [grad_branch, sums],
        specs + [whole(grad_branch), whole(sums)],
        outs,
        [whole(o) for o in outs],
        (1,),
        name="grad_proj",
    )


def grad_one_body(c, place, dqkv_ref, normed_ref, own_ref, oth_ref, *outs):
    sums_ref = outs[-1]
    groups = [(0, g) for g in groups_a(c)] + [(1, g) for g in groups_b(c)]
    for side in range(2):
        cols = slice(side * c.half, (side + 1) * c.half)
        weights = [jnp.where(place[2] == side, own_ref[p], oth_ref[p]) for p in range(3)]
        gain = jnp.zeros((1, c.half), F32)
        shift = jnp.zeros((1, c.half), F32)
        for (where, group), out_ref in zip(groups, outs):
            if where != side:
                continue
            for row, k in enumerate(group):
                rows_at = pl.ds(pl.multiple_of((place[1] ^ k) * c.R, 16), c.R)
                acc = None
                for part in range(3):
                    rows = dqkv_ref[rows_at, part * c.W : (part + 1) * c.W]
                    term = dot_nt(rows, weights[part])
                    acc = term if acc is None else acc + term
                out_ref[row, : c.R, :] = acc.astype(BF)
                normed = normed_ref[rows_at, cols].astype(F32)
                gain = gain + jnp.sum(acc * normed, axis=0, keepdims=True)
                shift = shift + jnp.sum(acc, axis=0, keepdims=True)
        sums_ref[0:1, cols] = gain
        sums_ref[1:2, cols] = shift
        row = lax.broadcasted_iota(I32, (16, 1), 0)
        tile = jnp.where(row == 0, gain, jnp.where(row == 1, shift, 0.0)).astype(BF)
        for (where, group), out_ref in zip(groups, outs):
            if where == side:
                for at in range(len(group)):
                    out_ref[at, c.R :, :] = tile


def grad_one(c, order, place, dqkv, normed, own_w, oth_w):
    outs = piece_outs(c, 16, 16) + [shape_of((2, c.D), F32)]
    result = call(
        order,
        functools.partial(grad_one_body, c),
        place,
        [dqkv, normed, own_w, oth_w],
        [whole(dqkv), whole(normed), whole(own_w), whole(oth_w)],
        outs,
        [whole(o) for o in outs],
        (1,),
        name="grad_one",
    )
    return list(result[:-1]), result[-1]


def grad_qkv_body(c, own, place, *refs):
    hid_ref, dqkv_ref = refs[:2]
    add_ref = refs[2] if own else None
    out_ref = refs[-1]
    acc = dot_tn(hid_ref[...], dqkv_ref[...])
    if own:
        acc = acc + add_ref[0].astype(F32)
    out_ref[0] = acc.astype(BF)


def grad_qkv(c, order, place, hidden, dqkv, add=None):
    own = add is not None
    args = [hidden, dqkv]
    specs = [
        pl.BlockSpec((c.TP, c.half), lambda i, s: (0, s[2] if own else 1 - s[2])),
        cols_of((c.TP, c.W)),
    ]
    if c.W % 128:
        dqkv = dqkv.reshape(c.TP, 3, c.W).transpose(1, 0, 2)
        args[1] = dqkv
        specs[1] = pl.BlockSpec((None, c.TP, c.W), lambda i, s: (i, 0, 0))
    if own:
        args.append(add)
        specs.append(rows_of((1, c.half, c.W)))
    out = shape_of((3, c.half, c.W), BF)
    return call(
        order,
        functools.partial(grad_qkv_body, c, own),
        place,
        args,
        specs,
        [out],
        [rows_of((1, c.half, c.W))],
        (3,),
        name="grad_qkv",
    )[0]


def back_one_body(c, place, *refs):
    refs = list(refs)
    count = (len(refs) - 5) // 2
    a, b, refs = refs[:count], refs[count : 2 * count], refs[2 * count :]
    tok_ref, after_ref, small_ref, out_ref, sums_ref = refs
    live = live_rows(c, place[1] * c.R, c.R)
    normed, inv_std = norm_rows(jnp.where(live, tok_ref[...].astype(F32), 0.0))
    one = jnp.concatenate([add_up(a)[: c.R], add_up(b)[: c.R]], axis=1)
    grad = after_ref[...] + norm_back(one, small_row(c, small_ref, 0), normed, inv_std)
    for h in range(2):
        out_ref[h] = grad[:, h * c.half : (h + 1) * c.half].astype(BF)
    for h, refs in enumerate((a, b)):
        tiles = [ref[c.R :, :].astype(F32) for ref in refs]
        pair = (tiles[0] + tiles[1]).astype(BF).astype(F32)
        for tile in tiles[2:]:
            pair = pair + tile
        sums_ref[:, h * c.half : (h + 1) * c.half] = pair[0:2]


def back_one(c, order, place, sums, tokens, after, small):
    args = [*sums[0], *sums[1], tokens, after, small]
    lane_rows = pl.BlockSpec((c.R, c.D), lambda i, s: (s[1], 0))
    specs = [first_block(a) for a in args[:-3]] + [lane_rows, whole(after), whole(small)]
    outs = [shape_of((2, c.R, c.half), BF), shape_of((2, c.D), F32)]
    return call(
        order,
        functools.partial(back_one_body, c),
        place,
        args,
        specs,
        outs,
        [whole(o) for o in outs],
        (1,),
        name="back_one",
    )


def assemble_body(c, place, *refs):
    pieces, out_ref = refs[:-1], refs[-1]
    for k in range(c.n):

        @pl.when((place[1] ^ k) == pl.program_id(0))
        def _():
            for h in range(2):
                values = pieces[2 * k + h][...].astype(out_ref.dtype)
                out_ref[:, h * c.half : (h + 1) * c.half] = values


def assemble(c, order, place, pieces, dtype):
    out = shape_of((c.T, c.D), dtype)
    return call(
        order,
        functools.partial(assemble_body, c),
        place,
        [pair[0] for pair in flat(pieces)],
        [
            pl.BlockSpec((None, c.R, c.half), lambda i, s, at=at: (at, 0, 0))
            for _, at in flat(pieces)
        ],
        [out],
        [rows_of((c.R, c.D))],
        (-(-c.T // c.R),),
        name="assemble",
    )[0]


def local(
    tokens,
    cotangent,
    w_qkv,
    qv_bias,
    w_proj,
    proj_bias,
    norm_gains,
    norm_shifts,
    w_router,
    expert_shift,
    w_first,
    w_second,
    first_bias,
    routes,
    priority,
):
    T, D = tokens.shape
    n = lax.axis_size("mp")
    E = w_router.shape[1]
    S = 16 * T // (5 * E)
    R = up(-(-T // n), 16)
    F = w_first.shape[2]
    W = w_proj.shape[0]
    win = up(IMG_LEN + 15, 16)
    SP = up(S + 17, 16)
    cap = (9 * T + 4 * EXP_DEV - 1) // (4 * EXP_DEV)
    c = Sizes(
        T=T,
        D=D,
        half=D // 2,
        n=n,
        X=E // EXP_DEV,
        E=E,
        S=S,
        SP=SP,
        CR=up(cap, 128),
        R=R,
        TP=n * R,
        W=W,
        images=T // IMG_LEN,
        quarters=n // EXP_DEV,
        F=F,
        cap=cap,
        win=win,
        fblk=min(1024, F),
        key=4 * T,
    )
    order = Order()
    dp, mp, grid = lax.axis_index("dp"), lax.axis_index("mp"), lax.axis_index("grid")
    here = jnp.stack([dp, mp, grid, mp // c.quarters]).astype(I32)

    experts = jnp.arange(E, dtype=I32)[:, None, None]
    count = jnp.sum((routes.T[None] == experts).astype(I32), axis=(1, 2))[None]
    counts = trade(jnp.broadcast_to(count, (c.X, E)), "dp")
    slot, rt = route(c, order, here, routes, priority)
    place, offsets = windows(c, order, here, counts)
    grad_out = dispatch(c, order, place, slot, cotangent)
    grad_in = trade(grad_out, "dp")

    bias_rows = F // 2 // c.half
    packed = jnp.concatenate(
        [
            norm_gains,
            norm_shifts,
            proj_bias[None],
            jnp.pad(qv_bias, ((0, 0), (0, c.half - W))),
            expert_shift,
            w_router.T,
            first_bias.reshape(bias_rows, c.half),
        ],
        axis=0,
    )
    packed = jnp.pad(packed, ((0, up(packed.shape[0], 16) - packed.shape[0]), (0, 0)))
    packed_oth = swap_grid(packed)
    small = jnp.where(
        grid == 0,
        jnp.concatenate([packed, packed_oth], axis=1),
        jnp.concatenate([packed_oth, packed], axis=1),
    )
    bias = small[6 + 2 * E : 6 + 2 * E + bias_rows].reshape(bias_rows, 2, c.half)
    bias = bias.transpose(1, 0, 2).reshape(1, F).astype(F32)
    qkv_own = w_qkv.transpose(1, 0, 2)
    qkv_oth = swap_grid(qkv_own)
    first_own = w_first[0]
    second_own = w_second[0]
    proj_tied, second_tied, first_tied, _ = lax.optimization_barrier(
        (w_proj, second_own, first_own, grad_out)
    )
    proj = lax.all_gather(proj_tied, ("mp", "grid"))
    second_oth = swap_grid(second_tied)
    first_oth = swap_grid(first_tied)

    outs = [shape_of((c.TP, D), BF), shape_of((c.TP, 3 * W), BF), shape_of((c.TP, D), BF)]
    hidden_one, qkv, normed_one = call(
        order,
        functools.partial(qkv_body, c),
        place,
        [tokens, small, qkv_own, qkv_oth],
        [rows_of((c.R, D)), whole(small), whole(qkv_own), whole(qkv_oth)],
        outs,
        [rows_of((c.R, D)), rows_of((c.R, 3 * W)), rows_of((c.R, D))],
        (n,),
        name="qkv",
    )
    groups = groups_of(c)
    out = shape_of((len(groups), c.TP, groups[0][1]), BF)
    mix = call(
        order,
        functools.partial(attend_body, c),
        place,
        [qkv],
        [whole(qkv)],
        [out],
        [whole(out)],
        (c.images,),
        name="attend",
    )[0]
    mixes = gather_mp(c, mix)
    hidden_two, weight, mine, keep, after, probs, keep_lane, weight_lane = middle(
        c, order, place, mixes, proj, tokens, small, offsets, slot, rt
    )
    keep_mask = keep[:, :2, :].transpose(0, 2, 1).reshape(c.TP, 2)[:T].astype(I32)
    mine = mine.transpose(0, 2, 1).reshape(c.TP, 8)

    rows_in = trade(dispatch(c, order, place, slot, hidden_two, weight), "dp")
    ga, grad_all = grad_active(c, order, place, grad_in, second_own, second_oth)
    act, gp, gb, row_all, col, back = expert(
        c, order, place, rows_in, first_own, first_oth, bias, ga
    )
    back = trade(back, "dp")
    second_part = swap_grid(grad_second(c, order, place, grad_all, col, act))
    first_part = swap_grid(grad_first(c, order, place, row_all, gp))
    gb = gb[0:1].reshape(2, F // 2)
    gb_own = lax.dynamic_index_in_dim(gb, grid, 0, True)
    gb_oth = lax.dynamic_index_in_dim(gb, 1 - grid, 0, True)
    grad_fbias = gb_own + swap_grid(gb_oth)
    prod = produce(c, order, place, col, act, second_own, second_oth)

    two_sums = reduce_mp(c, combine(c, order, place, back, mine, True))
    prod = trade(prod, "dp")
    grad_second_out = grad_second(c, order, place, grad_all, col, act, second_part)
    grad_first_out = grad_first(c, order, place, row_all, gp, first_part)
    grad_after, grad_branch, sums_two, grad_mix = back_two(
        c,
        order,
        place,
        two_sums,
        proj,
        [after, probs, keep_lane, weight_lane],
        cotangent,
        hidden_two,
        small,
    )
    grad_mix = [grad_mix[0]] + [swap_mp(c, grad_mix[k], k) for k in range(1, n)]
    proj_a, proj_b = grad_proj(c, order, place, mixes, grad_branch, sums_two)

    outs = [shape_of((c.TP, 3 * W), BF), shape_of((8, 3 * W), F32)]
    dqkv, dqkv_sums = call(
        order,
        functools.partial(attend_back_body, c),
        place,
        [qkv, *grad_mix],
        [whole(qkv)] + [whole(p) for p in grad_mix],
        outs,
        [whole(o) for o in outs],
        (c.images,),
        [pltpu.VMEM((c.TP, W), BF)],
        name="attend_back",
    )
    one_pieces, one_parts = grad_one(c, order, place, dqkv, normed_one, qkv_own, qkv_oth)
    one_sums = reduce_mp(c, one_pieces)
    qkv_part = swap_grid(grad_qkv(c, order, place, hidden_one, dqkv))
    grad_w_qkv = grad_qkv(c, order, place, hidden_one, dqkv, qkv_part)
    grad_w_qkv = sum_dp(c, grad_w_qkv.reshape(3 * c.half, W)).reshape(3, c.half, W)
    prod_pieces = combine(c, order, place, prod, mine)
    grad_low, sums_one = back_one(c, order, place, one_sums, tokens, grad_after, small)
    grad_low = gather_mp(c, grad_low)
    out_sums = reduce_mp(c, prod_pieces)
    out_lane = block_out(c, order, place, out_sums, after, weight_lane, small)
    out_lane = gather_mp(c, out_lane)

    proj_low = (proj_a.astype(F32) + swap_grid(proj_b).astype(F32)).astype(BF)
    proj_sum = sum_dp(c, sum_proj(c, proj_low))
    rest = proj_sum[W : W + 8 + 2 * E]
    qv_rows = jnp.concatenate([dqkv_sums[0:1, :W], dqkv_sums[0:1, 2 * W :]], axis=0)
    if n != 4:
        sums_one = fold(c, one_parts, (("mp", n),))
    sums_one = finish_sums(c, sums_one, qv_rows, grid)
    grad_tokens = assemble(c, order, place, grad_low, F32)
    block = assemble(c, order, place, out_lane, BF)
    return (
        block,
        grad_tokens,
        grad_w_qkv.transpose(1, 0, 2),
        sums_one[2:3, :W],
        proj_sum[:W],
        rest[2],
        jnp.stack([sums_one[0], rest[0]]),
        jnp.stack([sums_one[1], rest[1]]),
        rest[8 + E : 8 + 2 * E].T,
        rest[8 : 8 + E],
        grad_first_out[None],
        grad_second_out[None],
        grad_fbias,
        keep_mask,
    )


def solution(mesh):
    return jax.shard_map(
        local,
        mesh=mesh,
        in_specs=(
            P(("dp", "grid"), None),
            P(("dp", "grid"), None),
            P("grid", None, "mp"),
            P("grid", "mp"),
            P("mp", "grid"),
            P("grid"),
            P(None, "grid"),
            P(None, "grid"),
            P("grid", None),
            P(None, "grid"),
            P(("dp", "mp"), "grid", None),
            P(("dp", "mp"), None, "grid"),
            P(("dp", "mp"), "grid"),
            P(("dp", "grid"), None),
            P(("dp", "grid"), None),
        ),
        out_specs=(
            P(("dp", "grid"), None),
            P(("dp", "grid"), None),
            P("grid", None, "mp"),
            P("grid", "mp"),
            P("mp", "grid"),
            P("grid"),
            P(None, "grid"),
            P(None, "grid"),
            P("grid", None),
            P(None, "grid"),
            P(("dp", "mp"), "grid", None),
            P(("dp", "mp"), None, "grid"),
            P(("dp", "mp"), "grid"),
            P(("dp", "grid"), None),
        ),
        check_vma=False,
    )
```

```python
import functools
from typing import NamedTuple

import jax
import jax.numpy as jnp
from jax import lax
from jax.experimental import pallas as pl
from jax.experimental.pallas import tpu as pltpu
from jax.sharding import PartitionSpec as P

HEAD = 64
IMG_LEN = 197
EXP_DEV = 4
BF = jnp.bfloat16
F32 = jnp.float32
I32 = jnp.int32
VMEM_BYTES = 56 * 1024 * 1024
LOW = -1e30


class Sizes(NamedTuple):
    T: int
    D: int
    half: int
    n: int
    X: int
    E: int
    S: int
    Q: int
    SP: int
    CR: tuple
    R: int
    TP: int
    W: int
    images: int
    quarters: int
    F: int
    cap: int
    win: int
    fblk: int
    key: int


class Order:
    def __init__(self):
        self.after = []

    def tie(self, value):
        self.after.append(value)

    def hold(self, *values):
        return lax.optimization_barrier((*values, *self.after))[: len(values)]


def up(value, step):
    return -(-value // step) * step


def dot_nn(a, b):
    return jnp.dot(a, b, preferred_element_type=F32)


def dot_nt(a, b):
    return lax.dot_general(a, b, (((1,), (1,)), ((), ())), preferred_element_type=F32)


def dot_tn(a, b):
    return lax.dot_general(a, b, (((0,), (0,)), ((), ())), preferred_element_type=F32)


def split_low(values):
    high = values.astype(BF)
    return high, (values - high.astype(F32)).astype(BF)


def shape_of(dims, dtype):
    return jax.ShapeDtypeStruct(dims, dtype)


def whole(array, buffers=None):
    dims = tuple(array.shape)
    extra = {} if buffers is None else {"pipeline_mode": pl.Buffered(buffers)}
    return pl.BlockSpec(dims, lambda i, s: (0,) * len(dims), **extra)


def rows_of(dims):
    return pl.BlockSpec(dims, lambda i, s: (i,) + (0,) * (len(dims) - 1))


def cols_of(dims):
    return pl.BlockSpec(dims, lambda i, s: (0,) * (len(dims) - 1) + (i,))


def call(order, body, place, args, specs, outs, out_specs, grid, scratch=(), name=None, cost=0):
    extra = order.after
    count = len(args)

    def wrapped(place, *refs):
        body(place, *refs[:count], *refs[count + len(extra) :])

    result = pl.pallas_call(
        wrapped,
        grid_spec=pltpu.PrefetchScalarGridSpec(
            num_scalar_prefetch=1,
            grid=grid,
            in_specs=list(specs) + [pl.BlockSpec(memory_space=pl.ANY)] * len(extra),
            out_specs=list(out_specs),
            scratch_shapes=list(scratch),
        ),
        out_shape=list(outs),
        compiler_params=pltpu.CompilerParams(
            dimension_semantics=("arbitrary",) * len(grid), vmem_limit_bytes=VMEM_BYTES
        ),
        cost_estimate=pl.CostEstimate(
            flops=1000 + int(1.1e9 * cost), bytes_accessed=1000, transcendentals=0
        ),
        name=name,
    )(place, *args, *extra)
    order.after = [min(result, key=lambda o: o.size)]
    return result


def swap_mp(c, value, mask):
    return lax.ppermute(value, "mp", [(i, i ^ mask) for i in range(c.n)])


def swap_grid(value):
    return lax.ppermute(value, "grid", [(0, 1), (1, 0)])


def held(value, *others):
    return lax.optimization_barrier((value, *others))[0]


def trade(value, axis):
    return lax.all_to_all(value, axis, split_axis=0, concat_axis=0, tiled=True)


def groups_a(c):
    return [[0, 2], [1, 3]] if c.n == 4 else [[k] for k in range(c.n)]


def groups_b(c):
    return [[0, 1], [2, 3]] if c.n == 4 else [[k] for k in range(c.n)]


def reduce_start(c, arrays):
    a, b = arrays[: len(arrays) // 2], arrays[len(arrays) // 2 :]
    if c.n != 4:
        return [[x[0]] + [swap_mp(c, x[k], k) for k in range(1, c.n)] for x in (a, b)]
    return [[a[0], swap_mp(c, a[1], 1)], [b[0], swap_mp(c, b[1], 2)]]


def reduce_end(c, order, state):
    if c.n != 4:
        return state
    (a, ra), (b, rb) = state
    ra, rb = order.hold(ra, rb)
    ta = (a[1:].astype(F32) + ra[1:].astype(F32)).astype(BF)
    tb = (b[1:].astype(F32) + rb[1:].astype(F32)).astype(BF)
    order.tie(ta)
    order.tie(tb)
    return [[a, ra, swap_mp(c, ta, 2)], [b, rb, swap_mp(c, tb, 1)]]


def piece_outs(c, more_a=0, more_b=0):
    outs = [shape_of((len(g), c.R + more_a, c.half), BF) for g in groups_a(c)]
    return outs + [shape_of((len(g), c.R + more_b, c.half), BF) for g in groups_b(c)]


def first_block(array):
    dims = tuple(array.shape)
    return pl.BlockSpec((None,) + dims[1:], lambda i, s: (0, 0, 0))


def add_up(refs):
    total = refs[0][...].astype(F32)
    for ref in refs[1:]:
        total = total + ref[...].astype(F32)
    return total


def gather_mp(c, value):
    if c.n != 4 or value.shape[0] != 2:
        parts = [value] + [swap_mp(c, value, k) for k in range(1, c.n)]
        return [[(p, h) for h in range(value.shape[0])] for p in parts]
    one = swap_mp(c, value, 1)
    two = swap_mp(c, value, 2)
    far_a = swap_mp(c, one[0:1], 2)
    far_b = swap_mp(c, two[1:2], 1)
    near = [[(p, 0), (p, 1)] for p in (value, one, two)]
    return near + [[(far_a, 0), (far_b, 0)]]


def flat(pieces):
    return [pair for piece in pieces for pair in piece]


def fold(c, value, axes):
    for axis, size in axes:
        mask = 1
        while mask < size:
            value = value + lax.ppermute(value, axis, [(i, i ^ mask) for i in range(size)])
            mask *= 2
    return value


def finish_sums(c, one, parts, grid):
    def half_of(side):
        cols = lax.dynamic_slice_in_dim(one, side * c.half, c.half, 1)
        row = lax.dynamic_index_in_dim(parts, side, 0, True)
        return jnp.concatenate([cols, jnp.pad(row, ((0, 0), (0, c.half - c.W)))], axis=0)

    return fold(c, half_of(grid) + swap_grid(half_of(1 - grid)), (("dp", c.X),))


def sum_proj(c, value):
    if c.n != 4:
        return jnp.sum(trade(value, "mp").astype(F32), axis=0).astype(BF)
    pair = (value[:2].astype(F32) + swap_mp(c, value[2:], 1).astype(F32)).astype(BF)
    return (pair[0].astype(F32) + swap_mp(c, pair[1], 2).astype(F32)).astype(BF)


def expert_of(c, place, j):
    return j * EXP_DEV + place[3]


def offset_at(place, j):
    return place[4 + j]


def window_slot(c, place, j, slot):
    return slot + jnp.where(slot < c.Q, place[4 + c.X + j], place[4 + 2 * c.X + j])


def window_in(c, place, half, j):
    return pl.multiple_of(place[4 + (3 + half) * c.X + j], 16)


def windows_body(c, place, counts, out_ref, off_ref):
    def window(offset, half):
        return jnp.minimum((offset >> 4) << 4, c.CR[half] - c.SP)

    def before(e, source):
        state = (jnp.int32(0),) * 3
        result = state
        for b in range(c.X):
            result = [jnp.where(source == b, new, old) for new, old in zip(state, result)]
            number = counts[b, e]
            kept = jnp.clip(c.cap - state[0], 0, number)
            first = jnp.minimum(kept, c.Q)
            state = (state[0] + number, state[1] + first, state[2] + kept - first)
        return result

    for i in range(4):
        out_ref[i] = place[i]
    for i in range(4 + 5 * c.X, 64):
        out_ref[i] = jnp.int32(0)
    here = place[0] * EXP_DEV + place[3]
    for j in range(c.X):
        offset, first, second = before(expert_of(c, place, j), place[0])
        out_ref[4 + j] = offset
        out_ref[4 + c.X + j] = first - window(first, 0)
        out_ref[4 + 2 * c.X + j] = c.SP + second - c.Q - window(second, 1)
        _, first, second = before(here, j)
        out_ref[4 + 3 * c.X + j] = window(first, 0)
        out_ref[4 + 4 * c.X + j] = window(second, 1)
    for e in range(c.E):
        off_ref[e : e + 1, :] = jnp.full((1, 128), before(e, place[0])[0], I32)


def windows(c, order, place, counts):
    return call(
        order,
        functools.partial(windows_body, c),
        place,
        [counts],
        [pl.BlockSpec(memory_space=pltpu.SMEM)],
        [shape_of((64,), I32), shape_of((c.E, 128), I32)],
        [pl.BlockSpec(memory_space=pltpu.SMEM), whole(shape_of((c.E, 128), I32))],
        (1,),
        name="windows",
    )


def route_body(c, place, row_ref, col_ref, rt_ref, slot_ref, blocks_ref, rtb_ref):
    pad = jnp.full((1, c.TP - c.T), 1 << 30, I32)
    first = jnp.broadcast_to(jnp.concatenate([row_ref[0:1, :], pad], axis=1), (8, c.TP))
    second = jnp.broadcast_to(jnp.concatenate([row_ref[1:2, :], pad], axis=1), (8, c.TP))

    def count(at, state):
        a, b = state
        keys = col_ref[pl.ds(at, 8), :]
        for k in range(2):
            key = keys[:, k : k + 1]
            a = a + (key < first).astype(I32)
            b = b + (key < second).astype(I32)
        return a, b

    def one(i, state):
        for q in range(8):
            state = count(pl.multiple_of(i * 64 + q * 8, 8), state)
        return state

    zero = jnp.zeros((8, c.TP), I32)
    state = lax.fori_loop(0, c.T // 64, one, (zero, zero))
    for at in range(c.T // 64 * 64, c.T, 8):
        state = count(at, state)
    a = jnp.sum(state[0], axis=0, keepdims=True)
    b = jnp.sum(state[1], axis=0, keepdims=True)
    pad = jnp.full((2, c.TP - c.T), -1, I32)
    rt = jnp.concatenate([rt_ref[...], pad], axis=1)
    start = jnp.zeros((1, 1), I32)
    for e in range(c.E):
        in_first = rt[0:1, :] == e
        in_second = rt[1:2, :] == e
        number = jnp.sum(in_first.astype(I32) + in_second.astype(I32), axis=1, keepdims=True)
        slot_ref[e : e + 1, :] = jnp.where(in_first, a - start, jnp.where(in_second, b - start, -1))
        start = start + number
    for r in range(c.n):
        blocks_ref[r] = slot_ref[:, r * c.R : (r + 1) * c.R]
        rtb_ref[r] = jnp.concatenate([rt[:, r * c.R : (r + 1) * c.R]] * 4, axis=0)


def route(c, order, place, routes, priority):
    key = routes * c.key + priority
    row = routes.T * c.key + priority.T
    rt = routes.T
    outs = [
        shape_of((c.E, c.TP), I32),
        shape_of((c.n, c.E, c.R), I32),
        shape_of((c.n, 8, c.R), I32),
    ]
    return call(
        order,
        functools.partial(route_body, c),
        place,
        [row, key, rt],
        [whole(row), whole(key), whole(rt)],
        outs,
        [whole(o) for o in outs],
        (1,),
        name="route",
    )


def last_rows(c, tile, high, low):
    row = lax.broadcasted_iota(I32, (16, 1), 0)
    return jnp.where(row == 14, high, jnp.where(row == 15, low, tile))


def dispatch_body(c, rows_all, halves, weighted, place, *refs):
    refs = list(refs)
    slot_ref, src_ref = refs[:2]
    refs = refs[2:]
    if weighted:
        weight_ref = refs.pop(0)
    out_ref, hot_ref = refs

    @pl.when(pl.program_id(0) == 0)
    def _():
        for j in range(c.X):
            slot = slot_ref[pl.ds(expert_of(c, place, j), 1), :]
            kept = (slot >= 0) & (slot + offset_at(place, j) < c.cap)
            row = jnp.where(kept, window_slot(c, place, j, slot), -1)
            for index, half in enumerate(halves):
                slots = lax.broadcasted_iota(I32, (c.SP, c.TP), 0) + half * c.SP
                hot_ref[index, j * c.SP : (j + 1) * c.SP, :] = (slots == row).astype(BF)

    for index in range(len(halves)):
        acc = dot_nn(hot_ref[index, :, :rows_all], src_ref[...])
        for j in range(c.X):
            at = (len(halves) * j + index) * c.SP
            out_ref[at : at + c.SP, :] = acc[j * c.SP : (j + 1) * c.SP].astype(BF)
        if weighted:

            @pl.when(pl.program_id(0) == 0)
            def _():
                gates = dot_nn(hot_ref[index], weight_ref[...])
                lane = lax.broadcasted_iota(I32, (1, 128), 1)
                wide = (c.SP, c.half)
                eye = lax.broadcasted_iota(I32, wide, 0) == lax.broadcasted_iota(I32, wide, 1)
                for j in range(c.X):
                    e = expert_of(c, place, j)
                    mine = gates[j * c.SP : (j + 1) * c.SP]
                    rows = []
                    for at in (e, e + 64):
                        col = jnp.sum(jnp.where(lane == at, mine, 0.0), axis=1, keepdims=True)
                        rows.append(jnp.sum(jnp.where(eye, col, 0.0), axis=0, keepdims=True))
                    end = (j + 1) * c.SP
                    tile = last_rows(c, acc[end - 16 : end], rows[0], rows[1])
                    out_ref[end - 16 : end, :] = tile.astype(BF)


def dispatch(c, order, place, slot, source, halves, weight=None):
    rows_all = source.shape[0]
    args = [slot, source]
    specs = [whole(slot), pl.BlockSpec((rows_all, c.half), lambda i, s: (0, i ^ s[2]))]
    if weight is not None:
        args.append(weight)
        specs.append(whole(weight))
    size = len(halves) * c.SP
    return call(
        order,
        functools.partial(dispatch_body, c, rows_all, halves, weight is not None),
        place,
        args,
        specs,
        [shape_of((c.X * size, c.D), BF)],
        [cols_of((c.X * size, c.half))],
        (2,),
        [pltpu.VMEM((len(halves), c.X * c.SP, c.TP), BF)],
        name="dispatch",
    )[0].reshape(c.X, size, c.D)


def norm_rows(values):
    centred = values - jnp.mean(values, axis=-1, keepdims=True)
    inv_std = lax.rsqrt(jnp.mean(centred * centred, axis=-1, keepdims=True) + 1e-06)
    return centred * inv_std, inv_std


def norm_back(grad_norm, gain, normed, inv_std):
    scaled = grad_norm * gain
    return inv_std * (
        scaled
        - jnp.mean(scaled, axis=-1, keepdims=True)
        - normed * jnp.mean(scaled * normed, axis=-1, keepdims=True)
    )


def small_row(c, small_ref, index, count=1):
    return small_ref[index : index + count, :].astype(F32)


def own_cols(c, place):
    return pl.ds(pl.multiple_of(place[2] * c.half, c.half), c.half)


def other_cols(c, place):
    return pl.ds(pl.multiple_of((1 - place[2]) * c.half, c.half), c.half)


def live_rows(c, first, count):
    return (first + lax.broadcasted_iota(I32, (count, 1), 0)) < c.T


def qkv_body(c, place, tok_ref, small_ref, own_ref, oth_ref, hid_ref, qkv_ref, normed_ref, w_ref):
    @pl.when(pl.program_id(0) == 0)
    def _():
        for part in range(3):
            lanes = slice(part * c.W, (part + 1) * c.W)
            w_ref[own_cols(c, place), lanes] = own_ref[part]
            w_ref[other_cols(c, place), lanes] = oth_ref[part]

    live = live_rows(c, pl.program_id(0) * c.R, c.R)
    values = jnp.where(live, tok_ref[...].astype(F32), 0.0)
    normed, _ = norm_rows(values)
    hidden = normed * small_row(c, small_ref, 0) + small_row(c, small_ref, 2)
    normed_ref[...] = normed.astype(BF)
    hidden = jnp.where(live, hidden, 0.0).astype(BF)
    hid_ref[...] = hidden
    acc = dot_nn(hidden, w_ref[...])
    bias = small_row(c, small_ref, 5)
    zero = jnp.zeros((1, c.W), F32)
    shift = jnp.concatenate([bias[:, : c.W], zero, bias[:, c.half : c.half + c.W]], axis=1)
    qkv_ref[...] = (acc + shift).astype(BF)


def image_window(c):
    start = pl.program_id(0) * IMG_LEN
    low = pl.multiple_of(start // 16 * 16, 16)
    return low, start - low


def groups_of(c):
    lanes = min(128, c.W)
    return [(at, lanes) for at in range(0, c.W, lanes)]


def head_mask(lanes, head):
    lane = lax.broadcasted_iota(I32, (1, lanes), 1)
    return (lane >= head * HEAD) & (lane < (head + 1) * HEAD)


def stack_heads(c, values):
    heads = range(c.W // HEAD)
    return jnp.concatenate([jnp.where(head_mask(c.W, h), values, BF(0)) for h in heads], axis=0)


def pick_heads(c, values):
    total = None
    for h in range(c.W // HEAD):
        part = jnp.where(head_mask(c.W, h), values[h * c.win : (h + 1) * c.win], 0.0)
        total = part if total is None else total + part
    return total


def attend_body(c, place, qkv_ref, mix_ref):
    @pl.when(pl.program_id(0) == 0)
    def _():
        mix_ref[...] = jnp.zeros_like(mix_ref)

    low, off = image_window(c)
    row = lax.broadcasted_iota(I32, (c.win, 1), 0)
    col = lax.broadcasted_iota(I32, (1, c.win), 1)
    in_row = (row >= off) & (row < off + IMG_LEN)
    in_col = (col >= off) & (col < off + IMG_LEN)
    q = stack_heads(c, qkv_ref[pl.ds(low, c.win), : c.W] * BF(HEAD**-0.5))
    k = qkv_ref[pl.ds(low, c.win), c.W : 2 * c.W]
    v = qkv_ref[pl.ds(low, c.win), 2 * c.W :]
    scores = jnp.where(in_col, dot_nt(q, k), LOW)
    exps = jnp.exp(scores - jnp.max(scores, axis=-1, keepdims=True))
    probs = exps * (1.0 / jnp.sum(exps, axis=-1, keepdims=True))
    total = pick_heads(c, dot_nn(probs.astype(BF), v)).astype(BF)
    for group, (at, lanes) in enumerate(groups_of(c)):
        old = mix_ref[group, pl.ds(low, c.win), :]
        mix_ref[group, pl.ds(low, c.win), :] = jnp.where(in_row, total[:, at : at + lanes], old)


def attend_back_body(c, place, qkv_ref, *refs):
    pieces, (out_ref, sums_ref, grad_ref) = refs[: c.n], refs[c.n :]

    @pl.when(pl.program_id(0) == 0)
    def _():
        out_ref[...] = jnp.zeros_like(out_ref)
        sums_ref[...] = jnp.zeros_like(sums_ref)
        for k in range(c.n):
            at = pl.multiple_of((place[1] ^ k) * c.R, 16)
            grad_ref[pl.ds(at, c.R), :] = pieces[k][...]

    low, off = image_window(c)
    row = lax.broadcasted_iota(I32, (c.win, 1), 0)
    in_row = (row >= off) & (row < off + IMG_LEN)
    scale = HEAD**-0.5
    q = stack_heads(c, qkv_ref[pl.ds(low, c.win), : c.W] * BF(scale))
    k = qkv_ref[pl.ds(low, c.win), c.W : 2 * c.W]
    v = qkv_ref[pl.ds(low, c.win), 2 * c.W :]
    do = stack_heads(c, jnp.where(in_row, grad_ref[pl.ds(low, c.win), :], BF(0)))
    scores = jnp.where(in_row, dot_nt(k, q), LOW)
    exps = jnp.exp(scores - jnp.max(scores, axis=0, keepdims=True))
    soft = exps * (1.0 / jnp.sum(exps, axis=0, keepdims=True))
    dp = dot_nt(v, do)
    delta = jnp.sum(soft * dp, axis=0, keepdims=True)
    ds = (soft * (dp - delta)).astype(BF)
    dq = pick_heads(c, dot_tn(ds, k)) * scale
    dk = dot_nn(ds, q)
    dv = dot_nn(soft.astype(BF), do)
    for part, grad in enumerate((dq, dk, dv)):
        lanes = slice(part * c.W, (part + 1) * c.W)
        low_grad = jnp.where(in_row, grad, 0.0).astype(BF)
        old = out_ref[pl.ds(low, c.win), lanes]
        out_ref[pl.ds(low, c.win), lanes] = jnp.where(in_row, low_grad, old)
        sums_ref[0:1, lanes] += jnp.sum(low_grad.astype(F32), axis=0, keepdims=True)


def middle_body(c, place, *refs):
    refs = list(refs)
    groups = groups_of(c)
    count = c.n * len(groups)
    mixes, refs = refs[:count], refs[count:]
    w_ref, tok_ref, small_ref, off_ref, slot_ref, rt_ref = refs[:6]
    hid_ref, weight_ref, mine_ref, keep_ref = refs[6:10]
    after_ref, probs_ref, keep_lane_ref, weight_lane_ref, proj_ref = refs[10:]
    step = pl.program_id(0)

    @pl.when(step == 0)
    def _():
        for k in range(c.n):
            for h in range(2):
                cols = slice(h * c.half, (h + 1) * c.half)
                proj_ref[k * c.W : (k + 1) * c.W, cols] = w_ref[(place[1] ^ k) * 2 + h]

    branch = dot_nn(jnp.concatenate([mix[...] for mix in mixes], axis=1), proj_ref[...])
    live = live_rows(c, step * c.R, c.R)
    tok = jnp.where(live, tok_ref[...].astype(F32), 0.0)
    after = tok + branch + small_row(c, small_ref, 4)
    normed, _ = norm_rows(after)
    hidden = (normed * small_row(c, small_ref, 1) + small_row(c, small_ref, 3)).astype(BF)
    hid_ref[...] = hidden
    router = small_ref[6 + c.E : 6 + 2 * c.E, :]
    logits = dot_nt(router, hidden)
    exps = jnp.exp(logits - jnp.max(logits, axis=0, keepdims=True))
    probs = exps / jnp.sum(exps, axis=0, keepdims=True)
    slot = slot_ref[0]
    kept = (slot >= 0) & (slot + off_ref[:, 0:1] < c.cap)
    weight = jnp.where(kept, probs, 0.0)
    high, rest = split_low(weight)
    lane = lax.broadcasted_iota(I32, (c.E, 128), 1)
    index = lax.broadcasted_iota(I32, (c.E, 128), 0)
    both = dot_tn(high, (lane == index).astype(BF)) + dot_tn(rest, (lane == index + 64).astype(BF))
    weight_ref[...] = both.astype(BF)
    for j in range(c.X):
        e = expert_of(c, place, j)
        slot_j = slot_ref[0, pl.ds(e, 1), :]
        kept_j = (slot_j >= 0) & (slot_j + offset_at(place, j) < c.cap)
        row = jnp.where(kept_j, window_slot(c, place, j, slot_j), -1)
        mine_ref[0, j : j + 1, :] = row
    for j in range(c.X, 8):
        mine_ref[0, j : j + 1, :] = jnp.full((1, c.R), -1, I32)
    expert = lax.broadcasted_iota(I32, (c.E, c.R), 0)
    rows = []
    for k in range(2):
        picked = jnp.where((rt_ref[0, k : k + 1, :] == expert) & kept, 1.0, 0.0)
        rows.append(jnp.sum(picked, axis=0, keepdims=True))
    keep_ref[0] = jnp.concatenate(rows * 4, axis=0)

    @pl.when(step == place[1])
    def _():
        after_ref[...] = after
        probs_ref[...] = probs
        keep_lane_ref[...] = jnp.where(kept, 1.0, 0.0)
        weight_lane_ref[...] = weight


def middle(c, order, place, mixes, proj, tokens, small, offsets, slot, rt):
    args = [pair[0] for pair in flat(mixes)] + [proj, tokens, small, offsets, slot, rt]
    specs = [
        pl.BlockSpec((None, c.R, a.shape[2]), lambda i, s, at=at: (at, i, 0))
        for a, at in flat(mixes)
    ]
    specs += [whole(proj), rows_of((c.R, c.D)), whole(small), whole(offsets)]
    specs += [rows_of((1, c.E, c.R)), rows_of((1, 8, c.R))]
    outs = [
        shape_of((c.TP, c.D), BF),
        shape_of((c.TP, 128), BF),
        shape_of((c.n, 8, c.R), I32),
        shape_of((c.n, 8, c.R), F32),
        shape_of((c.R, c.D), F32),
        shape_of((c.E, c.R), F32),
        shape_of((c.E, c.R), F32),
        shape_of((c.E, c.R), F32),
    ]
    out_specs = [
        rows_of((c.R, c.D)),
        rows_of((c.R, 128)),
        rows_of((1, 8, c.R)),
        rows_of((1, 8, c.R)),
    ] + [whole(o) for o in outs[4:]]
    return call(
        order,
        functools.partial(middle_body, c),
        place,
        args,
        specs,
        outs,
        out_specs,
        (c.n,),
        [pltpu.VMEM((c.D, c.D), BF)],
        name="middle",
    )


def pack_rows(c, place, half, rows, out_ref, base=0, start=0):
    main = c.SP - 16
    used = lax.broadcasted_iota(I32, (16, 1), 0) < 14
    out_ref[base : base + c.CR[half], :] = jnp.zeros((c.CR[half], c.D), BF)
    for j in range(c.X):
        at = pl.multiple_of(window_in(c, place, half, j) + base, 16)
        out_ref[pl.ds(at, main), :] += rows[j, start : start + main, :]
        tail = jnp.where(used, rows[j, start + main : start + c.SP, :], BF(0))
        out_ref[pl.ds(pl.multiple_of(at + main, 16), 16), :] += tail


def last_pair(c, tile, lanes):
    tile = tile[:, :lanes].astype(F32)
    return tile[14:15, :], tile[15:16, :]


def row_chunks(rows, size):
    return [slice(at, min(at + size, rows)) for at in range(0, rows, size)]


def grad_active_body(c, place, *refs):
    rows, own_ref, oth_ref, *outs, all_ref = refs

    @pl.when(pl.program_id(0) == 0)
    def _():
        pack_rows(c, place, 0, rows, all_ref)
        pack_rows(c, place, 1, rows, all_ref, c.CR[0], c.SP)

    weights = jnp.concatenate([own_ref[...], oth_ref[...]], axis=1)
    for half, base in enumerate((0, c.CR[0])):
        for at in row_chunks(c.CR[half], 320):
            values = all_ref[base + at.start : base + at.stop, :]
            outs[half][at, :] = dot_nt(values, weights).astype(BF)


def grad_active(c, order, place, rows, own_w, oth_w):
    outs = [shape_of((rows, c.F), BF) for rows in c.CR] + [shape_of((sum(c.CR), c.D), BF)]
    return call(
        order,
        functools.partial(grad_active_body, c),
        place,
        [rows, own_w, oth_w],
        [whole(rows, 1)] + [rows_of((c.fblk, c.half))] * 2,
        outs,
        [cols_of((rows, c.fblk)) for rows in c.CR] + [whole(outs[2])],
        (c.F // c.fblk,),
        name="grad_active",
    )


def expert_body(c, half, place, *refs):
    rows, own_ref, oth_ref, bias_ref, ga_ref = refs[:5]
    act_ref, gp_ref, gb_ref, all_ref, col_ref, back_ref = refs[5:11]
    acc_ref, dot_ref, row_ref = refs[11:]
    step = pl.program_id(0)

    @pl.when(step == 0)
    def _():
        acc_ref[...] = jnp.zeros_like(acc_ref)
        dot_ref[...] = jnp.zeros_like(dot_ref)
        pack_rows(c, place, half, rows, all_ref)
        col_ref[...] = jnp.zeros_like(col_ref)
        eye = lax.broadcasted_iota(I32, (c.SP, c.SP), 0) == lax.broadcasted_iota(I32, (c.SP, c.SP), 1)
        for j in range(c.X):
            high, low = last_pair(c, rows[j, c.SP - 16 :, :], c.SP)
            col = jnp.sum(jnp.where(eye, high + low, 0.0), axis=1, keepdims=True)
            col_ref[pl.ds(window_in(c, place, half, j), c.SP), :] += jnp.broadcast_to(col, (c.SP, 128))

    bias = bias_ref[...]
    weights = jnp.concatenate([own_ref[...], oth_ref[...]], axis=0)
    summed = jnp.zeros((1, c.fblk), F32)
    lead = 0.7978845608028654
    cube = lead * 0.044715
    chunks = row_chunks(c.CR[half], 224)
    ahead = dot_nn(all_ref[chunks[0], :], weights)
    for i, rows_at in enumerate(chunks):
        pre = ahead + bias
        if i + 1 < len(chunks):
            ahead = dot_nn(all_ref[chunks[i + 1], :], weights)
        square = pre * pre
        turn = jnp.tanh(pre * (cube * square + lead))
        above = 1.0 + turn
        active = (0.5 * pre) * above
        slope = above * (1.0 + (1.0 - turn) * (pre * (3 * cube * square + lead)))
        ga = ga_ref[rows_at, :].astype(F32)
        product = active * ga
        part = product[:, 0:128]
        for lane in range(128, c.fblk, 128):
            part = part + product[:, lane : lane + 128]
        dot_ref[rows_at, :] += part
        grad = ga * slope * (0.5 * col_ref[rows_at, 0:1])
        act_ref[rows_at, :] = active.astype(BF)
        grad_low = grad.astype(BF)
        gp_ref[rows_at, :] = grad_low
        summed = summed + jnp.sum(grad, axis=0, keepdims=True)
        acc_ref[rows_at, :] += dot_nt(grad_low, weights)
    gb_ref[...] = jnp.broadcast_to(summed, (8, c.fblk))

    @pl.when(step == pl.num_programs(0) - 1)
    def _():
        ones = jnp.ones((8, 128), BF)
        row_ref[...] = jnp.zeros_like(row_ref)
        for j in range(c.X):
            at = window_in(c, place, half, j)
            back_ref[j] = acc_ref[pl.ds(at, c.SP), :].astype(BF)
            a, rest = split_low(dot_ref[pl.ds(at, c.SP), :])
            total = dot_nt(ones, a) + dot_nt(ones, rest)
            high = total.astype(BF).astype(F32)
            row_ref[0:8, : c.SP] = high
            row_ref[8:16, : c.SP] = total - high
            tile = back_ref[j, c.SP - 16 :, : c.half].astype(F32)
            tile = last_rows(c, tile, row_ref[0:1, :], row_ref[8:9, :])
            back_ref[j, c.SP - 16 :, : c.half] = tile.astype(BF)


def expert(c, order, place, half, rows, own_w, oth_w, bias, ga):
    args = [rows, own_w, oth_w, bias, ga]
    count = c.CR[half]
    specs = [whole(rows, 1)]
    specs += [cols_of((c.half, c.fblk))] * 2
    specs += [cols_of((1, c.fblk)), cols_of((count, c.fblk))]
    outs = [
        shape_of((count, c.F), BF),
        shape_of((count, c.F), BF),
        shape_of((8, c.F), F32),
    ]
    out_specs = [cols_of((count, c.fblk))] * 2 + [cols_of((8, c.fblk))]
    late = [shape_of((count, c.D), BF), shape_of((count, 128), F32)]
    late.append(shape_of((c.X, c.SP, c.D), BF))
    return call(
        order,
        functools.partial(expert_body, c, half),
        place,
        args,
        specs,
        outs + late,
        out_specs + [whole(o, 1) for o in late],
        (c.F // c.fblk,),
        [
            pltpu.VMEM((count, c.D), F32),
            pltpu.VMEM((count, 128), F32),
            pltpu.VMEM((16, c.half), F32),
        ],
        name="expert",
    )


def produce_body(c, place, *refs):
    cols, acts, own_ref, oth_ref, out_ref, accs = refs[:2], refs[2:4], refs[4], refs[5], refs[6], refs[7:]
    step = pl.program_id(0)

    @pl.when(step == 0)
    def _():
        for acc_ref in accs:
            acc_ref[...] = jnp.zeros_like(acc_ref)

    weights = jnp.concatenate([own_ref[...], oth_ref[...]], axis=1)
    for half in range(2):
        for at in row_chunks(c.CR[half], 320):
            accs[half][at, :] += dot_nn(acts[half][at, :], weights)

    @pl.when(step == pl.num_programs(0) - 1)
    def _():
        for half in range(2):
            for j in range(c.X):
                rows_at = pl.ds(window_in(c, place, half, j), c.SP)
                col = cols[half][rows_at, 0:1]
                out_ref[j, half * c.SP : (half + 1) * c.SP, :] = (accs[half][rows_at, :] * col).astype(BF)


def produce(c, order, place, cols, acts, own_w, oth_w):
    out = shape_of((c.X, 2 * c.SP, c.D), BF)
    return call(
        order,
        functools.partial(produce_body, c),
        place,
        [*cols, *acts, own_w, oth_w],
        [whole(col) for col in cols]
        + [cols_of((rows, c.fblk)) for rows in c.CR]
        + [rows_of((c.fblk, c.half))] * 2,
        [out],
        [whole(out, 1)],
        (c.F // c.fblk,),
        [pltpu.VMEM((rows, c.D), F32) for rows in c.CR],
        name="produce",
    )[0]


def grad_second_body(c, own, place, *refs):
    all_ref, cols, acts = refs[0], refs[1:3], refs[3:5]
    out_ref, row_ref = refs[-2:]

    @pl.when(pl.program_id(0) == 0)
    def _():
        for half, base in enumerate((0, c.CR[0])):
            rows_at = slice(base, base + c.CR[half])
            row_ref[rows_at, :] = (all_ref[rows_at, :].astype(F32) * cols[half][:, 0:1]).astype(BF)

    acc = dot_tn(acts[0][...], row_ref[: c.CR[0], :])
    acc = acc + dot_tn(acts[1][...], row_ref[c.CR[0] :, :])
    if own:
        acc = acc + refs[5][...].astype(F32)
    out_ref[...] = acc.astype(out_ref.dtype)


def grad_second(c, order, place, rows, cols, acts, add=None):
    own = add is not None
    args = [rows, *cols, *acts]
    total = sum(c.CR)
    specs = [pl.BlockSpec((total, c.half), lambda i, s: (0, 0 if own else 1))]
    specs += [whole(col) for col in cols] + [cols_of((count, c.fblk)) for count in c.CR]
    if own:
        args.append(add)
        specs.append(rows_of((c.fblk, c.half)))
    out = shape_of((c.F, c.half), F32 if own else BF)
    return call(
        order,
        functools.partial(grad_second_body, c, own),
        place,
        args,
        specs,
        [out],
        [rows_of((c.fblk, c.half))],
        (c.F // c.fblk,),
        [pltpu.VMEM((total, c.half), BF)],
        name="grad_second",
    )[0]


def grad_first_body(c, own, place, *refs):
    acc = dot_tn(refs[0][...], refs[2][...]) + dot_tn(refs[1][...], refs[3][...])
    if own:
        acc = acc + refs[4][...].astype(F32)
    refs[-1][...] = acc.astype(refs[-1].dtype)


def grad_first(c, order, place, rows, gps, add=None):
    own = add is not None
    args = [*rows, *gps]
    specs = [pl.BlockSpec((count, c.half), lambda i, s: (0, 0 if own else 1)) for count in c.CR]
    specs += [cols_of((count, c.fblk)) for count in c.CR]
    if own:
        args.append(add)
        specs.append(cols_of((c.half, c.fblk)))
    out = shape_of((c.half, c.F), F32 if own else BF)
    return call(
        order,
        functools.partial(grad_first_body, c, own),
        place,
        args,
        specs,
        [out],
        [cols_of((c.half, c.fblk))],
        (c.F // c.fblk,),
        name="grad_first",
    )[0]


def combine_body(c, with_dots, place, *refs):
    refs = list(refs)
    halves = 2 if with_dots else 1
    rows, refs = refs[:halves], refs[halves:]
    tails = []
    if with_dots:
        tails, refs = refs[:2], refs[2:]
    mine_ref = refs.pop(0)
    groups = [(0, g) for g in groups_a(c)] + [(1, g) for g in groups_b(c)]
    outs, (hot_ref, row_ref) = refs[: len(groups)], refs[len(groups) :]
    pad = hot_ref.shape[1] // c.X

    @pl.when(pl.program_id(0) == 0)
    def _():
        row_ref[...] = jnp.zeros_like(row_ref)
        slots = lax.broadcasted_iota(I32, (c.R, pad), 1)
        for k in range(c.n):
            at = pl.multiple_of((place[1] ^ k) * c.R, 16)
            for j in range(c.X):
                hot = (mine_ref[pl.ds(at, c.R), j : j + 1] == slots).astype(BF)
                hot_ref[k * c.R : (k + 1) * c.R, j * pad : (j + 1) * pad] = hot
        if with_dots:
            wide = (c.SP, c.half)
            eye = lax.broadcasted_iota(I32, wide, 0) == lax.broadcasted_iota(I32, wide, 1)
            lane = lax.broadcasted_iota(I32, (1, 128), 1)
            for half in range(2):
                for j in range(c.X):
                    high, low = last_pair(c, tails[half][j], c.half)
                    high = jnp.sum(jnp.where(eye, high, 0.0), axis=1, keepdims=True)
                    low = jnp.sum(jnp.where(eye, low, 0.0), axis=1, keepdims=True)
                    e = expert_of(c, place, j)
                    cols = jnp.where(lane == e, high, jnp.where(lane == e + 64, low, 0.0))
                    at = j * pad + half * c.SP
                    row_ref[at : at + c.SP, :128] = cols.astype(BF)
            pulls = dot_nn(hot_ref[...], row_ref[:, :128]).astype(BF)
            expert = lax.broadcasted_iota(I32, (c.E, 128), 0)
            lane = lax.broadcasted_iota(I32, (c.E, 128), 1)
            pick = ((lane == expert) | (lane == expert + 64)).astype(BF)
            for (side, group), out_ref in zip(groups, outs):
                for at, k in enumerate(group):
                    if side == 0:
                        got = dot_nt(pick, pulls[k * c.R : (k + 1) * c.R])
                        out_ref[at, c.R :, :] = jnp.zeros((c.E, c.half), BF)
                        out_ref[at, c.R :, : c.R] = got.astype(BF)

    for half, rows_ref in enumerate(rows):
        size = rows_ref.shape[1]
        for j in range(c.X):
            at = j * pad + half * size
            row_ref[at : at + size, :] = rows_ref[j]
    result = dot_nn(hot_ref[...], row_ref[...]).astype(BF)
    for half in range(2):

        @pl.when(pl.program_id(0) == half)
        def _():
            for (side, group), out_ref in zip(groups, outs):
                if side == half:
                    for at, k in enumerate(group):
                        out_ref[at, : c.R, :] = result[k * c.R : (k + 1) * c.R]


def combine(c, order, place, rows, mine, with_dots=False, cost=0):
    pad = up(2 * c.SP, 128)
    args = list(rows)
    specs = [pl.BlockSpec((c.X, r.shape[1], c.half), lambda i, s: (0, 0, i ^ s[2])) for r in rows]
    if with_dots:
        args += list(rows)
        specs += [pl.BlockSpec((c.X, 16, c.half), lambda i, s: (0, c.SP // 16 - 1, 0))] * 2
    args.append(mine)
    specs.append(whole(mine))
    outs = piece_outs(c, c.E if with_dots else 0)
    result = call(
        order,
        functools.partial(combine_body, c, with_dots),
        place,
        args,
        specs,
        outs,
        [whole(o, 1) for o in outs],
        (2,),
        [pltpu.VMEM((c.n * c.R, c.X * pad), BF), pltpu.VMEM((c.X * pad, c.half), BF)],
        name="combine",
        cost=cost,
    )
    return list(result)


def back_two_body(c, place, *refs):
    refs = list(refs)
    count = (len(refs) - 11 - c.n) // 2
    a, b, refs = refs[:count], refs[count : 2 * count], refs[2 * count :]
    w_ref, after_ref, probs_ref, keep_ref, weight_ref, cot_ref, hid_ref, small_ref = refs[:8]
    ga_ref, gb_ref, sums_ref = refs[8:11]
    mixes = refs[11:]
    sum_a = add_up(a)
    live = live_rows(c, place[1] * c.R, c.R)
    cot = jnp.where(live, cot_ref[...], BF(0))
    eshift = small_ref[6 : 6 + c.E, :]
    router = small_ref[6 + c.E : 6 + 2 * c.E, :]
    kept = keep_ref[...] > 0
    pulls = jnp.where(kept, sum_a[c.R :, : c.R] + dot_nt(eshift, cot), 0.0)
    probs = probs_ref[...]
    glog = (probs * (pulls - jnp.sum(probs * pulls, axis=0, keepdims=True))).astype(BF)
    two = jnp.concatenate([sum_a[: c.R], add_up(b)], axis=1) + dot_tn(glog, router)
    normed, inv_std = norm_rows(after_ref[...])
    grad_after = cot.astype(F32) + norm_back(two, small_row(c, small_ref, 1), normed, inv_std)
    ga_ref[...] = grad_after
    low = grad_after.astype(BF)
    gb_ref[...] = low
    high, rest = split_low(weight_ref[...])
    hid = jnp.where(live, hid_ref[...], BF(0))
    sums_ref[0:1, :] = jnp.sum(two * normed, axis=0, keepdims=True)
    sums_ref[1:2, :] = jnp.sum(two, axis=0, keepdims=True)
    sums_ref[2:3, :] = jnp.sum(low.astype(F32), axis=0, keepdims=True)
    sums_ref[3:8, :] = jnp.zeros((5, c.D), F32)
    sums_ref[8 : 8 + c.E, :] = dot_nn(high, cot) + dot_nn(rest, cot)
    sums_ref[8 + c.E : 8 + 2 * c.E, :] = dot_nn(glog, hid)
    for k in range(c.n):
        lane = place[1] ^ k
        mix = dot_nt(gb_ref[:, : c.half], w_ref[2 * lane])
        mix = mix + dot_nt(gb_ref[:, c.half :], w_ref[2 * lane + 1])
        mixes[k][...] = mix.astype(BF)


def back_two(c, order, place, sums, proj, lanes, cotangent, hidden, small):
    args = [*sums[0], *sums[1], proj, *lanes, cotangent, hidden, small]
    lane_rows = pl.BlockSpec((c.R, c.D), lambda i, s: (s[1], 0))
    specs = [first_block(a) for a in [*sums[0], *sums[1]]]
    specs += [whole(a) for a in [proj, *lanes]] + [lane_rows, lane_rows, whole(small)]
    outs = [
        shape_of((c.R, c.D), F32),
        shape_of((c.R, c.D), BF),
        shape_of((8 + 2 * c.E, c.D), F32),
    ] + [shape_of((c.R, c.W), BF) for _ in range(c.n)]
    result = call(
        order,
        functools.partial(back_two_body, c),
        place,
        args,
        specs,
        outs,
        [whole(o) for o in outs],
        (1,),
        name="back_two",
    )
    return (*result[:3], list(result[3:]))


def block_out_body(c, place, *refs):
    refs = list(refs)
    count = (len(refs) - 4) // 2
    a, b, refs = refs[:count], refs[count : 2 * count], refs[2 * count :]
    after_ref, weight_ref, small_ref, out_ref = refs
    high, low = split_low(weight_ref[...])
    eshift = small_ref[6 : 6 + c.E, :]
    shift = dot_tn(high, eshift) + dot_tn(low, eshift)
    for h, pieces in enumerate((a, b)):
        cols = slice(h * c.half, (h + 1) * c.half)
        out_ref[h] = (after_ref[:, cols] + add_up(pieces) + shift[:, cols]).astype(BF)


def block_out(c, order, place, sums, after, weight, small):
    args = [*sums[0], *sums[1], after, weight, small]
    out = shape_of((2, c.R, c.half), BF)
    return call(
        order,
        functools.partial(block_out_body, c),
        place,
        args,
        [first_block(a) for a in args[:-3]] + [whole(a) for a in args[-3:]],
        [out],
        [whole(out)],
        (1,),
        name="block_out",
    )[0]


def grad_proj_body(c, place, *refs):
    groups = groups_of(c)
    count = c.n * len(groups)
    mixes, (gb_ref, sums_ref, own_ref, oth_ref) = refs[:count], refs[count:]
    height = sums_ref.shape[0]
    slot = [0, 2, 1, 3] if c.n == 4 else [place[1] ^ k for k in range(c.n)]
    for cols, out_ref in ((own_cols(c, place), own_ref), (other_cols(c, place), oth_ref)):
        out_ref[...] = jnp.zeros_like(out_ref)
        sums = sums_ref[:, cols].astype(BF)
        for k in range(c.n):
            for group, (at, lanes) in enumerate(groups):
                part = dot_tn(mixes[k * len(groups) + group][...], gb_ref[:, cols])
                out_ref[slot[k], at : at + lanes, :] = part.astype(BF)
            out_ref[slot[k], c.W : c.W + height, :] = sums


def grad_proj(c, order, place, mixes, grad_branch, sums):
    rows = up(c.W + sums.shape[0], 16 * c.X)
    specs = [
        pl.BlockSpec((None, c.R, a.shape[2]), lambda i, s, at=at: (at, s[1], 0))
        for a, at in flat(mixes)
    ]
    outs = [shape_of((c.n, rows, c.half), BF)] * 2
    return call(
        order,
        functools.partial(grad_proj_body, c),
        place,
        [pair[0] for pair in flat(mixes)] + [grad_branch, sums],
        specs + [whole(grad_branch), whole(sums)],
        outs,
        [whole(o) for o in outs],
        (1,),
        name="grad_proj",
    )


def grad_one_body(c, place, dqkv_ref, normed_ref, own_ref, oth_ref, *outs):
    sums_ref = outs[-1]
    groups = [(0, g) for g in groups_a(c)] + [(1, g) for g in groups_b(c)]
    for side in range(2):
        cols = slice(side * c.half, (side + 1) * c.half)
        weights = [jnp.where(place[2] == side, own_ref[p], oth_ref[p]) for p in range(3)]
        gain = jnp.zeros((1, c.half), F32)
        shift = jnp.zeros((1, c.half), F32)
        for (where, group), out_ref in zip(groups, outs):
            if where != side:
                continue
            for row, k in enumerate(group):
                rows_at = pl.ds(pl.multiple_of((place[1] ^ k) * c.R, 16), c.R)
                acc = None
                for part in range(3):
                    rows = dqkv_ref[rows_at, part * c.W : (part + 1) * c.W]
                    term = dot_nt(rows, weights[part])
                    acc = term if acc is None else acc + term
                out_ref[row, : c.R, :] = acc.astype(BF)
                normed = normed_ref[rows_at, cols].astype(F32)
                gain = gain + jnp.sum(acc * normed, axis=0, keepdims=True)
                shift = shift + jnp.sum(acc, axis=0, keepdims=True)
        sums_ref[0:1, cols] = gain
        sums_ref[1:2, cols] = shift
        row = lax.broadcasted_iota(I32, (16, 1), 0)
        tile = jnp.where(row == 0, gain, jnp.where(row == 1, shift, 0.0)).astype(BF)
        for (where, group), out_ref in zip(groups, outs):
            if where == side:
                for at in range(len(group)):
                    out_ref[at, c.R :, :] = tile


def grad_one(c, order, place, dqkv, normed, own_w, oth_w):
    outs = piece_outs(c, 16, 16) + [shape_of((2, c.D), F32)]
    result = call(
        order,
        functools.partial(grad_one_body, c),
        place,
        [dqkv, normed, own_w, oth_w],
        [whole(dqkv), whole(normed), whole(own_w), whole(oth_w)],
        outs,
        [whole(o) for o in outs],
        (1,),
        name="grad_one",
    )
    return list(result[:-1]), result[-1]


def grad_qkv_body(c, place, hid_ref, dqkv_ref, own_ref, oth_ref):
    own_ref[0] = dot_tn(hid_ref[:, own_cols(c, place)], dqkv_ref[...]).astype(BF)
    oth_ref[0] = dot_tn(hid_ref[:, other_cols(c, place)], dqkv_ref[...]).astype(BF)


def grad_qkv(c, order, place, hidden, dqkv):
    specs = [whole(hidden, 1), cols_of((c.TP, c.W))]
    if c.W % 128:
        dqkv = dqkv.reshape(c.TP, 3, c.W).transpose(1, 0, 2)
        specs[1] = pl.BlockSpec((None, c.TP, c.W), lambda i, s: (i, 0, 0))
    return call(
        order,
        functools.partial(grad_qkv_body, c),
        place,
        [hidden, dqkv],
        specs,
        [shape_of((3, c.half, c.W), BF)] * 2,
        [rows_of((1, c.half, c.W))] * 2,
        (3,),
        name="grad_qkv",
    )


def back_one_body(c, place, *refs):
    refs = list(refs)
    count = (len(refs) - 5) // 2
    a, b, refs = refs[:count], refs[count : 2 * count], refs[2 * count :]
    tok_ref, after_ref, small_ref, out_ref, sums_ref = refs
    live = live_rows(c, place[1] * c.R, c.R)
    normed, inv_std = norm_rows(jnp.where(live, tok_ref[...].astype(F32), 0.0))
    one = jnp.concatenate([add_up(a)[: c.R], add_up(b)[: c.R]], axis=1)
    grad = after_ref[...] + norm_back(one, small_row(c, small_ref, 0), normed, inv_std)
    for h in range(2):
        out_ref[h] = grad[:, h * c.half : (h + 1) * c.half].astype(BF)
    for h, refs in enumerate((a, b)):
        tiles = [ref[c.R :, :].astype(F32) for ref in refs]
        pair = (tiles[0] + tiles[1]).astype(BF).astype(F32)
        for tile in tiles[2:]:
            pair = pair + tile
        sums_ref[:, h * c.half : (h + 1) * c.half] = pair[0:2]


def back_one(c, order, place, sums, tokens, after, small):
    args = [*sums[0], *sums[1], tokens, after, small]
    lane_rows = pl.BlockSpec((c.R, c.D), lambda i, s: (s[1], 0))
    specs = [first_block(a) for a in args[:-3]] + [lane_rows, whole(after), whole(small)]
    outs = [shape_of((2, c.R, c.half), BF), shape_of((2, c.D), F32)]
    return call(
        order,
        functools.partial(back_one_body, c),
        place,
        args,
        specs,
        outs,
        [whole(o) for o in outs],
        (1,),
        name="back_one",
    )


def assemble_body(c, place, *refs):
    pieces, out_ref = refs[:-1], refs[-1]
    for k in range(c.n):

        @pl.when((place[1] ^ k) == pl.program_id(0))
        def _():
            for h in range(2):
                values = pieces[2 * k + h][...].astype(out_ref.dtype)
                out_ref[:, h * c.half : (h + 1) * c.half] = values


def assemble(c, order, place, pieces, dtype):
    out = shape_of((c.T, c.D), dtype)
    return call(
        order,
        functools.partial(assemble_body, c),
        place,
        [pair[0] for pair in flat(pieces)],
        [
            pl.BlockSpec((None, c.R, c.half), lambda i, s, at=at: (at, 0, 0))
            for _, at in flat(pieces)
        ],
        [out],
        [rows_of((c.R, c.D))],
        (-(-c.T // c.R),),
        name="assemble",
    )[0]


def local(
    tokens,
    cotangent,
    w_qkv,
    qv_bias,
    w_proj,
    proj_bias,
    norm_gains,
    norm_shifts,
    w_router,
    expert_shift,
    w_first,
    w_second,
    first_bias,
    routes,
    priority,
):
    T, D = tokens.shape
    n = lax.axis_size("mp")
    E = w_router.shape[1]
    S = 16 * T // (5 * E)
    R = up(-(-T // n), 16)
    F = w_first.shape[2]
    W = w_proj.shape[0]
    win = up(IMG_LEN + 15, 16)
    Q = (S + 1) // 2
    cap = (9 * T + 4 * EXP_DEV - 1) // (4 * EXP_DEV)
    X = E // EXP_DEV
    full = min(cap // S, X)
    c = Sizes(
        T=T,
        D=D,
        half=D // 2,
        n=n,
        X=X,
        E=E,
        S=S,
        Q=Q,
        SP=up(Q + 17, 16),
        CR=(up(min(cap, X * Q), 16), up(full * (S - Q) + max(0, cap - full * S - Q), 16)),
        R=R,
        TP=n * R,
        W=W,
        images=T // IMG_LEN,
        quarters=n // EXP_DEV,
        F=F,
        cap=cap,
        win=win,
        fblk=min(1024, F),
        key=4 * T,
    )
    order = Order()
    dp, mp, grid = lax.axis_index("dp"), lax.axis_index("mp"), lax.axis_index("grid")
    here = jnp.stack([dp, mp, grid, mp // c.quarters]).astype(I32)

    experts = jnp.arange(E, dtype=I32)[:, None, None]
    count = jnp.sum((routes.T[None] == experts).astype(I32), axis=(1, 2))[None]
    counts = trade(jnp.broadcast_to(count, (c.X, E)), "dp")
    slot, blocks, rt = route(c, order, here, routes, priority)
    place, offsets = windows(c, order, here, counts)
    grad_out = dispatch(c, order, place, slot, cotangent, (0, 1))
    grad_in = trade(grad_out, "dp")

    bias_rows = F // 2 // c.half
    packed = jnp.concatenate(
        [
            norm_gains,
            norm_shifts,
            proj_bias[None],
            jnp.pad(qv_bias, ((0, 0), (0, c.half - W))),
            expert_shift,
            w_router.T,
            first_bias.reshape(bias_rows, c.half),
        ],
        axis=0,
    )
    packed = jnp.pad(packed, ((0, up(packed.shape[0], 16) - packed.shape[0]), (0, 0)))
    packed_oth = swap_grid(packed)
    small = jnp.where(
        grid == 0,
        jnp.concatenate([packed, packed_oth], axis=1),
        jnp.concatenate([packed_oth, packed], axis=1),
    )
    bias = small[6 + 2 * E : 6 + 2 * E + bias_rows].reshape(bias_rows, 2, c.half)
    bias = bias.transpose(1, 0, 2).reshape(1, F).astype(F32)
    qkv_own = w_qkv.transpose(1, 0, 2)
    qkv_oth = swap_grid(qkv_own)
    first_own = w_first[0]
    second_own = w_second[0]
    proj_tied, second_tied, first_tied, _ = lax.optimization_barrier(
        (w_proj, second_own, first_own, grad_out)
    )
    proj = lax.all_gather(proj_tied, ("mp", "grid"))
    second_oth = swap_grid(second_tied)
    first_oth = swap_grid(first_tied)

    outs = [shape_of((c.TP, D), BF), shape_of((c.TP, 3 * W), BF), shape_of((c.TP, D), BF)]
    hidden_one, qkv, normed_one = call(
        order,
        functools.partial(qkv_body, c),
        place,
        [tokens, small, qkv_own, qkv_oth],
        [rows_of((c.R, D)), whole(small), whole(qkv_own), whole(qkv_oth)],
        outs,
        [rows_of((c.R, D)), rows_of((c.R, 3 * W)), rows_of((c.R, D))],
        (n,),
        [pltpu.VMEM((D, 3 * W), BF)],
        name="qkv",
    )
    groups = groups_of(c)
    out = shape_of((len(groups), c.TP, groups[0][1]), BF)
    mix = call(
        order,
        functools.partial(attend_body, c),
        place,
        [qkv],
        [whole(qkv)],
        [out],
        [whole(out)],
        (c.images,),
        name="attend",
    )[0]
    mixes = gather_mp(c, mix)
    hidden_two, weight, mine, keep, after, probs, keep_lane, weight_lane = middle(
        c, order, place, mixes, proj, tokens, small, offsets, blocks, rt
    )
    keep_mask = keep[:, :2, :].transpose(0, 2, 1).reshape(c.TP, 2)[:T].astype(I32)
    mine = mine.transpose(0, 2, 1).reshape(c.TP, 8)

    rows_a = trade(dispatch(c, order, place, slot, hidden_two, (0,), weight), "dp")
    rows_b = dispatch(c, order, place, slot, hidden_two, (1,), weight)
    ga_a, ga_b, grad_all = grad_active(c, order, place, grad_in, second_own, second_oth)
    rows_b = trade(held(rows_b, rows_a, grad_all), "dp")
    act_a, gp_a, gb_a, all_a, col_a, back_a = expert(
        c, order, place, 0, rows_a, first_own, first_oth, bias, ga_a
    )
    back_a = trade(held(back_a, rows_b), "dp")
    act_b, gp_b, gb_b, all_b, col_b, back_b = expert(
        c, order, place, 1, rows_b, first_own, first_oth, bias, ga_b
    )
    back_b = trade(held(back_b, back_a), "dp")
    order.tie(back_a)
    cols, acts, gps, alls = [col_a, col_b], [act_a, act_b], [gp_a, gp_b], [all_a, all_b]
    second_part = swap_grid(grad_second(c, order, place, grad_all, cols, acts))
    first_part = swap_grid(grad_first(c, order, place, alls, gps))
    prod = produce(c, order, place, cols, acts, second_own, second_oth)
    gb = (gb_a + gb_b)[0:1].reshape(2, F // 2)
    gb_own = lax.dynamic_index_in_dim(gb, grid, 0, True)
    gb_oth = lax.dynamic_index_in_dim(gb, 1 - grid, 0, True)
    grad_fbias = gb_own + swap_grid(gb_oth)

    pieces = combine(c, order, place, [back_a, back_b], mine, True)
    prod = trade(held(prod, back_b), "dp")
    two_sums = reduce_start(c, pieces)
    grad_second_out = grad_second(c, order, place, grad_all, cols, acts, second_part)
    two_sums = reduce_end(c, order, two_sums)
    grad_first_out = grad_first(c, order, place, alls, gps, first_part)
    grad_after, grad_branch, sums_two, grad_mix = back_two(
        c,
        order,
        place,
        two_sums,
        proj,
        [after, probs, keep_lane, weight_lane],
        cotangent,
        hidden_two,
        small,
    )
    grad_mix = [grad_mix[0]] + [swap_mp(c, grad_mix[k], k) for k in range(1, n)]
    pieces = combine(c, order, place, [prod], mine, cost=10)
    out_sums = reduce_start(c, [held(p, *grad_mix) for p in pieces])
    proj_a, proj_b = grad_proj(c, order, place, mixes, grad_branch, sums_two)
    proj_b = swap_grid(held(proj_b, *grad_mix))

    outs = [shape_of((c.TP, 3 * W), BF), shape_of((8, 3 * W), F32)]
    dqkv, dqkv_sums = call(
        order,
        functools.partial(attend_back_body, c),
        place,
        [qkv, *grad_mix],
        [whole(qkv)] + [whole(p) for p in grad_mix],
        outs,
        [whole(o) for o in outs],
        (c.images,),
        [pltpu.VMEM((c.TP, W), BF)],
        name="attend_back",
    )
    out_sums = reduce_end(c, order, out_sums)
    one_pieces, one_parts = grad_one(c, order, place, dqkv, normed_one, qkv_own, qkv_oth)
    one_sums = reduce_start(c, [held(p, out_sums[0][-1], out_sums[1][-1]) for p in one_pieces])
    qkv_a, qkv_b = grad_qkv(c, order, place, hidden_one, dqkv)
    out_lane = block_out(c, order, place, out_sums, after, weight_lane, small)
    one_sums = reduce_end(c, order, one_sums)
    grad_low, sums_one = back_one(c, order, place, one_sums, tokens, grad_after, small)
    out_lane = gather_mp(c, held(out_lane, one_sums[0][-1], one_sums[1][-1]))
    grad_low = gather_mp(c, grad_low)

    qkv_b = swap_grid(qkv_b)
    qkv_low = (qkv_a.astype(F32) + qkv_b.astype(F32)).astype(BF)
    proj_low = (proj_a.astype(F32) + proj_b.astype(F32)).astype(BF)
    proj_low = sum_proj(c, proj_low)
    shared = jnp.concatenate([qkv_low.reshape(-1, c.half), proj_low], axis=0)
    shared = lax.psum(shared, "dp").astype(F32)
    grad_w_qkv = shared[: 3 * W].reshape(3, c.half, W)
    proj_sum = shared[3 * W :]
    rest = proj_sum[W : W + 8 + 2 * E]
    qv_rows = jnp.concatenate([dqkv_sums[0:1, :W], dqkv_sums[0:1, 2 * W :]], axis=0)
    if n != 4:
        sums_one = fold(c, one_parts, (("mp", n),))
    sums_one = finish_sums(c, sums_one, qv_rows, grid)
    block = assemble(c, order, place, out_lane, BF)
    grad_tokens = assemble(c, order, place, grad_low, F32)
    return (
        block,
        grad_tokens,
        grad_w_qkv.transpose(1, 0, 2),
        sums_one[2:3, :W],
        proj_sum[:W],
        rest[2],
        jnp.stack([sums_one[0], rest[0]]),
        jnp.stack([sums_one[1], rest[1]]),
        rest[8 + E : 8 + 2 * E].T,
        rest[8 : 8 + E],
        grad_first_out[None],
        grad_second_out[None],
        grad_fbias,
        keep_mask,
    )


def solution(mesh):
    return jax.shard_map(
        local,
        mesh=mesh,
        in_specs=(
            P(("dp", "grid"), None),
            P(("dp", "grid"), None),
            P("grid", None, "mp"),
            P("grid", "mp"),
            P("mp", "grid"),
            P("grid"),
            P(None, "grid"),
            P(None, "grid"),
            P("grid", None),
            P(None, "grid"),
            P(("dp", "mp"), "grid", None),
            P(("dp", "mp"), None, "grid"),
            P(("dp", "mp"), "grid"),
            P(("dp", "grid"), None),
            P(("dp", "grid"), None),
        ),
        out_specs=(
            P(("dp", "grid"), None),
            P(("dp", "grid"), None),
            P("grid", None, "mp"),
            P("grid", "mp"),
            P("mp", "grid"),
            P("grid"),
            P(None, "grid"),
            P(None, "grid"),
            P("grid", None),
            P(None, "grid"),
            P(("dp", "mp"), "grid", None),
            P(("dp", "mp"), None, "grid"),
            P(("dp", "mp"), "grid"),
            P(("dp", "grid"), None),
        ),
        check_vma=False,
    )
```

```python
import functools
from typing import NamedTuple

import jax
import jax.numpy as jnp
from jax import lax
from jax.experimental import pallas as pl
from jax.experimental.pallas import tpu as pltpu
from jax.sharding import PartitionSpec as P

HEAD = 64
IMG_LEN = 197
EXP_DEV = 4
BF = jnp.bfloat16
F32 = jnp.float32
I32 = jnp.int32
VMEM_BYTES = 56 * 1024 * 1024
LOW = -1e30


class Sizes(NamedTuple):
    T: int
    D: int
    half: int
    n: int
    X: int
    E: int
    S: int
    Q: int
    SP: int
    CR: tuple
    R: int
    TP: int
    W: int
    images: int
    quarters: int
    F: int
    cap: int
    win: int
    fblk: int
    key: int


class Order:
    def __init__(self):
        self.after = []

    def tie(self, value):
        self.after.append(value)

    def hold(self, *values):
        return lax.optimization_barrier((*values, *self.after))[: len(values)]


def up(value, step):
    return -(-value // step) * step


def dot_nn(a, b):
    return jnp.dot(a, b, preferred_element_type=F32)


def dot_nt(a, b):
    return lax.dot_general(a, b, (((1,), (1,)), ((), ())), preferred_element_type=F32)


def dot_tn(a, b):
    return lax.dot_general(a, b, (((0,), (0,)), ((), ())), preferred_element_type=F32)


def split_low(values):
    high = values.astype(BF)
    return high, (values - high.astype(F32)).astype(BF)


def shape_of(dims, dtype):
    return jax.ShapeDtypeStruct(dims, dtype)


def whole(array, buffers=None):
    dims = tuple(array.shape)
    extra = {} if buffers is None else {"pipeline_mode": pl.Buffered(buffers)}
    return pl.BlockSpec(dims, lambda i, s: (0,) * len(dims), **extra)


def rows_of(dims):
    return pl.BlockSpec(dims, lambda i, s: (i,) + (0,) * (len(dims) - 1))


def cols_of(dims):
    return pl.BlockSpec(dims, lambda i, s: (0,) * (len(dims) - 1) + (i,))


def call(order, body, place, args, specs, outs, out_specs, grid, scratch=(), name=None, cost=0):
    extra = order.after
    count = len(args)

    def wrapped(place, *refs):
        body(place, *refs[:count], *refs[count + len(extra) :])

    result = pl.pallas_call(
        wrapped,
        grid_spec=pltpu.PrefetchScalarGridSpec(
            num_scalar_prefetch=1,
            grid=grid,
            in_specs=list(specs) + [pl.BlockSpec(memory_space=pl.ANY)] * len(extra),
            out_specs=list(out_specs),
            scratch_shapes=list(scratch),
        ),
        out_shape=list(outs),
        compiler_params=pltpu.CompilerParams(
            dimension_semantics=("arbitrary",) * len(grid), vmem_limit_bytes=VMEM_BYTES
        ),
        cost_estimate=pl.CostEstimate(
            flops=1000 + int(1.1e9 * cost), bytes_accessed=1000, transcendentals=0
        ),
        name=name,
    )(place, *args, *extra)
    order.after = [min(result, key=lambda o: o.size)]
    return result


def swap_mp(c, value, mask):
    return lax.ppermute(value, "mp", [(i, i ^ mask) for i in range(c.n)])


def swap_grid(value):
    return lax.ppermute(value, "grid", [(0, 1), (1, 0)])


def held(value, *others):
    return lax.optimization_barrier((value, *others))[0]


def trade(value, axis):
    return lax.all_to_all(value, axis, split_axis=0, concat_axis=0, tiled=True)


def groups_a(c):
    return [[0, 2], [1, 3]] if c.n == 4 else [[k] for k in range(c.n)]


def groups_b(c):
    return [[0, 1], [2, 3]] if c.n == 4 else [[k] for k in range(c.n)]


def reduce_start(c, arrays):
    a, b = arrays[: len(arrays) // 2], arrays[len(arrays) // 2 :]
    if c.n != 4:
        return [[x[0]] + [swap_mp(c, x[k], k) for k in range(1, c.n)] for x in (a, b)]
    return [[a[0], swap_mp(c, a[1], 1)], [b[0], swap_mp(c, b[1], 2)]]


def reduce_end(c, order, state):
    if c.n != 4:
        return state
    (a, ra), (b, rb) = state
    ra, rb = order.hold(ra, rb)
    ta = (a[1:].astype(F32) + ra[1:].astype(F32)).astype(BF)
    tb = (b[1:].astype(F32) + rb[1:].astype(F32)).astype(BF)
    order.tie(ta)
    order.tie(tb)
    return [[a, ra, swap_mp(c, ta, 2)], [b, rb, swap_mp(c, tb, 1)]]


def piece_outs(c, more_a=0, more_b=0):
    outs = [shape_of((len(g), c.R + more_a, c.half), BF) for g in groups_a(c)]
    return outs + [shape_of((len(g), c.R + more_b, c.half), BF) for g in groups_b(c)]


def first_block(array):
    dims = tuple(array.shape)
    return pl.BlockSpec((None,) + dims[1:], lambda i, s: (0, 0, 0))


def same_sum(c, refs, rows):
    parts = [ref[rows, :].astype(F32) for ref in refs]
    if c.n == 4:
        return (parts[0] + parts[1]).astype(BF).astype(F32) + parts[2]
    while len(parts) > 1:
        parts = [parts[i] + parts[i + 1] for i in range(0, len(parts), 2)]
    return parts[0]


def add_up(refs):
    total = refs[0][...].astype(F32)
    for ref in refs[1:]:
        total = total + ref[...].astype(F32)
    return total


def sum_dp_start(c, value):
    parts = trade(value.reshape((c.X, value.shape[0] // c.X) + value.shape[1:]), "dp")
    total = jnp.sum(parts.astype(F32), axis=0).astype(BF)
    return jnp.broadcast_to(total[None], (c.X,) + total.shape)


def sum_dp_end(c, spread):
    return trade(spread, "dp").reshape((-1,) + spread.shape[2:]).astype(F32)


def gather_mp(c, value, until=None):
    if c.n != 4 or value.shape[0] != 2:
        parts = [value] + [swap_mp(c, value, k) for k in range(1, c.n)]
        return [[(p, h) for h in range(value.shape[0])] for p in parts], parts[1:]
    one = swap_mp(c, value, 1)
    two = swap_mp(c, value, 2)
    ends = one[0:1], two[1:2]
    if until is not None:
        ends = held(ends[0], until), held(ends[1], until)
    far_a = swap_mp(c, ends[0], 2)
    far_b = swap_mp(c, ends[1], 1)
    near = [[(p, 0), (p, 1)] for p in (value, one, two)]
    return near + [[(far_a, 0), (far_b, 0)]], [one, two]


def flat(pieces):
    return [pair for piece in pieces for pair in piece]


def fold(c, value, axes):
    for axis, size in axes:
        mask = 1
        while mask < size:
            value = value + lax.ppermute(value, axis, [(i, i ^ mask) for i in range(size)])
            mask *= 2
    return value


def finish_sums(c, one, parts, grid):
    def half_of(side):
        cols = lax.dynamic_slice_in_dim(one, side * c.half, c.half, 1)
        row = lax.dynamic_index_in_dim(parts, side, 0, True)
        return jnp.concatenate([cols, jnp.pad(row, ((0, 0), (0, c.half - c.W)))], axis=0)

    return fold(c, half_of(grid) + swap_grid(half_of(1 - grid)), (("dp", c.X),))


def expert_of(c, place, j):
    return j * EXP_DEV + place[3]


def offset_at(place, j):
    return place[4 + j]


def window_slot(c, place, j, slot):
    return slot + jnp.where(slot < c.Q, place[4 + c.X + j], place[4 + 2 * c.X + j])


def window_in(c, place, half, j):
    return pl.multiple_of(place[4 + (3 + half) * c.X + j], 16)


def windows_body(c, place, counts, out_ref, off_ref):
    def window(offset, half):
        return jnp.minimum((offset >> 4) << 4, c.CR[half] - c.SP)

    def before(e, source):
        state = (jnp.int32(0),) * 3
        result = state
        for b in range(c.X):
            result = [jnp.where(source == b, new, old) for new, old in zip(state, result)]
            number = counts[b, e]
            kept = jnp.clip(c.cap - state[0], 0, number)
            first = jnp.minimum(kept, c.Q)
            state = (state[0] + number, state[1] + first, state[2] + kept - first)
        return result

    for i in range(4):
        out_ref[i] = place[i]
    for i in range(4 + 5 * c.X, 64):
        out_ref[i] = jnp.int32(0)
    here = place[0] * EXP_DEV + place[3]
    for j in range(c.X):
        offset, first, second = before(expert_of(c, place, j), place[0])
        out_ref[4 + j] = offset
        out_ref[4 + c.X + j] = first - window(first, 0)
        out_ref[4 + 2 * c.X + j] = c.SP + second - c.Q - window(second, 1)
        _, first, second = before(here, j)
        out_ref[4 + 3 * c.X + j] = window(first, 0)
        out_ref[4 + 4 * c.X + j] = window(second, 1)
    for e in range(c.E):
        off_ref[e : e + 1, :] = jnp.full((1, 128), before(e, place[0])[0], I32)


def windows(c, order, place, counts):
    return call(
        order,
        functools.partial(windows_body, c),
        place,
        [counts],
        [pl.BlockSpec(memory_space=pltpu.SMEM)],
        [shape_of((64,), I32), shape_of((c.E, 128), I32)],
        [pl.BlockSpec(memory_space=pltpu.SMEM), whole(shape_of((c.E, 128), I32))],
        (1,),
        name="windows",
    )


def route_body(c, place, row_ref, col_ref, rt_ref, slot_ref, blocks_ref, rtb_ref):
    pad = jnp.full((1, c.TP - c.T), 1 << 30, I32)
    first = jnp.broadcast_to(jnp.concatenate([row_ref[0:1, :], pad], axis=1), (8, c.TP))
    second = jnp.broadcast_to(jnp.concatenate([row_ref[1:2, :], pad], axis=1), (8, c.TP))

    def count(at, state):
        a, b = state
        keys = col_ref[pl.ds(at, 8), :]
        for k in range(2):
            key = keys[:, k : k + 1]
            a = a + (key < first).astype(I32)
            b = b + (key < second).astype(I32)
        return a, b

    def one(i, state):
        for q in range(8):
            state = count(pl.multiple_of(i * 64 + q * 8, 8), state)
        return state

    zero = jnp.zeros((8, c.TP), I32)
    state = lax.fori_loop(0, c.T // 64, one, (zero, zero))
    for at in range(c.T // 64 * 64, c.T, 8):
        state = count(at, state)
    a = jnp.sum(state[0], axis=0, keepdims=True)
    b = jnp.sum(state[1], axis=0, keepdims=True)
    pad = jnp.full((2, c.TP - c.T), -1, I32)
    rt = jnp.concatenate([rt_ref[...], pad], axis=1)
    start = jnp.zeros((1, 1), I32)
    for e in range(c.E):
        in_first = rt[0:1, :] == e
        in_second = rt[1:2, :] == e
        number = jnp.sum(in_first.astype(I32) + in_second.astype(I32), axis=1, keepdims=True)
        slot_ref[e : e + 1, :] = jnp.where(in_first, a - start, jnp.where(in_second, b - start, -1))
        start = start + number
    for r in range(c.n):
        blocks_ref[r] = slot_ref[:, r * c.R : (r + 1) * c.R]
        rtb_ref[r] = jnp.concatenate([rt[:, r * c.R : (r + 1) * c.R]] * 4, axis=0)


def route(c, order, place, routes, priority):
    key = routes * c.key + priority
    row = routes.T * c.key + priority.T
    rt = routes.T
    outs = [
        shape_of((c.E, c.TP), I32),
        shape_of((c.n, c.E, c.R), I32),
        shape_of((c.n, 8, c.R), I32),
    ]
    return call(
        order,
        functools.partial(route_body, c),
        place,
        [row, key, rt],
        [whole(row), whole(key), whole(rt)],
        outs,
        [whole(o) for o in outs],
        (1,),
        name="route",
    )


def last_rows(c, tile, high, low):
    row = lax.broadcasted_iota(I32, (16, 1), 0)
    return jnp.where(row == 14, high, jnp.where(row == 15, low, tile))


def dispatch_body(c, rows_all, halves, weighted, place, *refs):
    refs = list(refs)
    slot_ref, src_ref = refs[:2]
    refs = refs[2:]
    if weighted:
        weight_ref = refs.pop(0)
    out_ref, hot_ref = refs

    @pl.when(pl.program_id(0) == 0)
    def _():
        for j in range(c.X):
            slot = slot_ref[pl.ds(expert_of(c, place, j), 1), :]
            kept = (slot >= 0) & (slot + offset_at(place, j) < c.cap)
            row = jnp.where(kept, window_slot(c, place, j, slot), -1)
            for index, half in enumerate(halves):
                slots = lax.broadcasted_iota(I32, (c.SP, c.TP), 0) + half * c.SP
                hot_ref[index, j * c.SP : (j + 1) * c.SP, :] = (slots == row).astype(BF)

    for index in range(len(halves)):
        acc = dot_nn(hot_ref[index, :, :rows_all], src_ref[...])
        for j in range(c.X):
            at = (len(halves) * j + index) * c.SP
            out_ref[at : at + c.SP, :] = acc[j * c.SP : (j + 1) * c.SP].astype(BF)
        if weighted:

            @pl.when(pl.program_id(0) == 0)
            def _():
                gates = dot_nn(hot_ref[index], weight_ref[...])
                lane = lax.broadcasted_iota(I32, (1, 128), 1)
                wide = (c.SP, c.half)
                eye = lax.broadcasted_iota(I32, wide, 0) == lax.broadcasted_iota(I32, wide, 1)
                for j in range(c.X):
                    e = expert_of(c, place, j)
                    mine = gates[j * c.SP : (j + 1) * c.SP]
                    rows = []
                    for at in (e, e + 64):
                        col = jnp.sum(jnp.where(lane == at, mine, 0.0), axis=1, keepdims=True)
                        rows.append(jnp.sum(jnp.where(eye, col, 0.0), axis=0, keepdims=True))
                    end = (j + 1) * c.SP
                    tile = last_rows(c, acc[end - 16 : end], rows[0], rows[1])
                    out_ref[end - 16 : end, :] = tile.astype(BF)


def dispatch(c, order, place, slot, source, halves, weight=None):
    rows_all = source.shape[0]
    args = [slot, source]
    specs = [whole(slot), pl.BlockSpec((rows_all, c.half), lambda i, s: (0, i ^ s[2]))]
    if weight is not None:
        args.append(weight)
        specs.append(whole(weight))
    size = len(halves) * c.SP
    return call(
        order,
        functools.partial(dispatch_body, c, rows_all, halves, weight is not None),
        place,
        args,
        specs,
        [shape_of((c.X * size, c.D), BF)],
        [cols_of((c.X * size, c.half))],
        (2,),
        [pltpu.VMEM((len(halves), c.X * c.SP, c.TP), BF)],
        name="dispatch",
    )[0].reshape(c.X, size, c.D)


def norm_rows(values):
    centred = values - jnp.mean(values, axis=-1, keepdims=True)
    inv_std = lax.rsqrt(jnp.mean(centred * centred, axis=-1, keepdims=True) + 1e-06)
    return centred * inv_std, inv_std


def norm_back(grad_norm, gain, normed, inv_std):
    scaled = grad_norm * gain
    return inv_std * (
        scaled
        - jnp.mean(scaled, axis=-1, keepdims=True)
        - normed * jnp.mean(scaled * normed, axis=-1, keepdims=True)
    )


def small_row(c, small_ref, index, count=1):
    return small_ref[index : index + count, :].astype(F32)


def own_cols(c, place):
    return pl.ds(pl.multiple_of(place[2] * c.half, c.half), c.half)


def other_cols(c, place):
    return pl.ds(pl.multiple_of((1 - place[2]) * c.half, c.half), c.half)


def live_rows(c, first, count):
    return (first + lax.broadcasted_iota(I32, (count, 1), 0)) < c.T


def qkv_body(c, place, tok_ref, small_ref, own_ref, oth_ref, hid_ref, qkv_ref, normed_ref, w_ref):
    @pl.when(pl.program_id(0) == 0)
    def _():
        for part in range(3):
            lanes = slice(part * c.W, (part + 1) * c.W)
            w_ref[own_cols(c, place), lanes] = own_ref[part]
            w_ref[other_cols(c, place), lanes] = oth_ref[part]

    live = live_rows(c, pl.program_id(0) * c.R, c.R)
    values = jnp.where(live, tok_ref[...].astype(F32), 0.0)
    normed, _ = norm_rows(values)
    hidden = normed * small_row(c, small_ref, 0) + small_row(c, small_ref, 2)
    normed_ref[...] = normed.astype(BF)
    hidden = jnp.where(live, hidden, 0.0).astype(BF)
    hid_ref[...] = hidden
    acc = dot_nn(hidden, w_ref[...])
    bias = small_row(c, small_ref, 5)
    zero = jnp.zeros((1, c.W), F32)
    shift = jnp.concatenate([bias[:, : c.W], zero, bias[:, c.half : c.half + c.W]], axis=1)
    qkv_ref[...] = (acc + shift).astype(BF)


def image_window(c):
    start = pl.program_id(0) * IMG_LEN
    low = pl.multiple_of(start // 16 * 16, 16)
    return low, start - low


def groups_of(c):
    lanes = min(128, c.W)
    return [(at, lanes) for at in range(0, c.W, lanes)]


def head_mask(lanes, head):
    lane = lax.broadcasted_iota(I32, (1, lanes), 1)
    return (lane >= head * HEAD) & (lane < (head + 1) * HEAD)


def stack_heads(c, values):
    heads = range(c.W // HEAD)
    return jnp.concatenate([jnp.where(head_mask(c.W, h), values, BF(0)) for h in heads], axis=0)


def pick_heads(c, values):
    total = None
    for h in range(c.W // HEAD):
        part = jnp.where(head_mask(c.W, h), values[h * c.win : (h + 1) * c.win], 0.0)
        total = part if total is None else total + part
    return total


def attend_body(c, place, qkv_ref, mix_ref):
    @pl.when(pl.program_id(0) == 0)
    def _():
        mix_ref[...] = jnp.zeros_like(mix_ref)

    low, off = image_window(c)
    row = lax.broadcasted_iota(I32, (c.win, 1), 0)
    col = lax.broadcasted_iota(I32, (1, c.win), 1)
    in_row = (row >= off) & (row < off + IMG_LEN)
    in_col = (col >= off) & (col < off + IMG_LEN)
    q = stack_heads(c, qkv_ref[pl.ds(low, c.win), : c.W] * BF(HEAD**-0.5))
    k = qkv_ref[pl.ds(low, c.win), c.W : 2 * c.W]
    v = qkv_ref[pl.ds(low, c.win), 2 * c.W :]
    scores = jnp.where(in_col, dot_nt(q, k), LOW)
    exps = jnp.exp(scores - jnp.max(scores, axis=-1, keepdims=True))
    probs = exps * (1.0 / jnp.sum(exps, axis=-1, keepdims=True))
    total = pick_heads(c, dot_nn(probs.astype(BF), v)).astype(BF)
    for group, (at, lanes) in enumerate(groups_of(c)):
        old = mix_ref[group, pl.ds(low, c.win), :]
        mix_ref[group, pl.ds(low, c.win), :] = jnp.where(in_row, total[:, at : at + lanes], old)


def attend_back_body(c, place, qkv_ref, *refs):
    pieces, (out_ref, sums_ref, grad_ref) = refs[: c.n], refs[c.n :]

    @pl.when(pl.program_id(0) == 0)
    def _():
        out_ref[...] = jnp.zeros_like(out_ref)
        sums_ref[...] = jnp.zeros_like(sums_ref)
        for k in range(c.n):
            at = pl.multiple_of((place[1] ^ k) * c.R, 16)
            grad_ref[pl.ds(at, c.R), :] = pieces[k][...]

    low, off = image_window(c)
    row = lax.broadcasted_iota(I32, (c.win, 1), 0)
    in_row = (row >= off) & (row < off + IMG_LEN)
    scale = HEAD**-0.5
    q = stack_heads(c, qkv_ref[pl.ds(low, c.win), : c.W] * BF(scale))
    k = qkv_ref[pl.ds(low, c.win), c.W : 2 * c.W]
    v = qkv_ref[pl.ds(low, c.win), 2 * c.W :]
    do = stack_heads(c, jnp.where(in_row, grad_ref[pl.ds(low, c.win), :], BF(0)))
    scores = jnp.where(in_row, dot_nt(k, q), LOW)
    exps = jnp.exp(scores - jnp.max(scores, axis=0, keepdims=True))
    soft = exps * (1.0 / jnp.sum(exps, axis=0, keepdims=True))
    dp = dot_nt(v, do)
    delta = jnp.sum(soft * dp, axis=0, keepdims=True)
    ds = (soft * (dp - delta)).astype(BF)
    dq = pick_heads(c, dot_tn(ds, k)) * scale
    dk = dot_nn(ds, q)
    dv = dot_nn(soft.astype(BF), do)
    for part, grad in enumerate((dq, dk, dv)):
        lanes = slice(part * c.W, (part + 1) * c.W)
        low_grad = jnp.where(in_row, grad, 0.0).astype(BF)
        old = out_ref[pl.ds(low, c.win), lanes]
        out_ref[pl.ds(low, c.win), lanes] = jnp.where(in_row, low_grad, old)
        sums_ref[0:1, lanes] += jnp.sum(low_grad.astype(F32), axis=0, keepdims=True)


def middle_body(c, place, *refs):
    refs = list(refs)
    groups = groups_of(c)
    count = c.n * len(groups)
    mixes, refs = refs[:count], refs[count:]
    own_ref, oth_ref, tok_ref, small_ref, off_ref, slot_ref, rt_ref = refs[:7]
    hid_ref, weight_ref, mine_ref, keep_ref = refs[7:11]
    after_ref, probs_ref, keep_lane_ref, weight_lane_ref, proj_ref = refs[11:]
    step = pl.program_id(0)

    @pl.when(step == 0)
    def _():
        for k in range(c.n):
            proj_ref[k * c.W : (k + 1) * c.W, own_cols(c, place)] = own_ref[k]
            proj_ref[k * c.W : (k + 1) * c.W, other_cols(c, place)] = oth_ref[k]

    branch = dot_nn(jnp.concatenate([mix[...] for mix in mixes], axis=1), proj_ref[...])
    live = live_rows(c, step * c.R, c.R)
    tok = jnp.where(live, tok_ref[...].astype(F32), 0.0)
    after = tok + branch + small_row(c, small_ref, 4)
    normed, _ = norm_rows(after)
    hidden = (normed * small_row(c, small_ref, 1) + small_row(c, small_ref, 3)).astype(BF)
    hid_ref[...] = hidden
    router = small_ref[6 + c.E : 6 + 2 * c.E, :]
    logits = dot_nt(router, hidden)
    exps = jnp.exp(logits - jnp.max(logits, axis=0, keepdims=True))
    probs = exps / jnp.sum(exps, axis=0, keepdims=True)
    slot = slot_ref[0]
    kept = (slot >= 0) & (slot + off_ref[:, 0:1] < c.cap)
    weight = jnp.where(kept, probs, 0.0)
    high, rest = split_low(weight)
    lane = lax.broadcasted_iota(I32, (c.E, 128), 1)
    index = lax.broadcasted_iota(I32, (c.E, 128), 0)
    both = dot_tn(high, (lane == index).astype(BF)) + dot_tn(rest, (lane == index + 64).astype(BF))
    weight_ref[...] = both.astype(BF)
    for j in range(c.X):
        e = expert_of(c, place, j)
        slot_j = slot_ref[0, pl.ds(e, 1), :]
        kept_j = (slot_j >= 0) & (slot_j + offset_at(place, j) < c.cap)
        row = jnp.where(kept_j, window_slot(c, place, j, slot_j), -1)
        mine_ref[0, j : j + 1, :] = row
    for j in range(c.X, 8):
        mine_ref[0, j : j + 1, :] = jnp.full((1, c.R), -1, I32)
    expert = lax.broadcasted_iota(I32, (c.E, c.R), 0)
    rows = []
    for k in range(2):
        picked = jnp.where((rt_ref[0, k : k + 1, :] == expert) & kept, 1.0, 0.0)
        rows.append(jnp.sum(picked, axis=0, keepdims=True))
    keep_ref[0] = jnp.concatenate(rows * 4, axis=0)

    @pl.when(step == place[1])
    def _():
        after_ref[...] = after
        probs_ref[...] = probs
        keep_lane_ref[...] = jnp.where(kept, 1.0, 0.0)
        weight_lane_ref[...] = weight


def middle(c, order, place, mixes, own_w, oth_w, tokens, small, offsets, slot, rt):
    args = [pair[0] for pair in flat(mixes)] + [own_w, oth_w, tokens, small, offsets, slot, rt]
    specs = [
        pl.BlockSpec((None, c.R, a.shape[2]), lambda i, s, at=at: (at, i, 0))
        for a, at in flat(mixes)
    ]
    specs += [whole(own_w), whole(oth_w), rows_of((c.R, c.D)), whole(small), whole(offsets)]
    specs += [rows_of((1, c.E, c.R)), rows_of((1, 8, c.R))]
    outs = [
        shape_of((c.TP, c.D), BF),
        shape_of((c.TP, 128), BF),
        shape_of((c.n, 8, c.R), I32),
        shape_of((c.n, 8, c.R), F32),
        shape_of((c.R, c.D), F32),
        shape_of((c.E, c.R), F32),
        shape_of((c.E, c.R), F32),
        shape_of((c.E, c.R), F32),
    ]
    out_specs = [
        rows_of((c.R, c.D)),
        rows_of((c.R, 128)),
        rows_of((1, 8, c.R)),
        rows_of((1, 8, c.R)),
    ] + [whole(o) for o in outs[4:]]
    return call(
        order,
        functools.partial(middle_body, c),
        place,
        args,
        specs,
        outs,
        out_specs,
        (c.n,),
        [pltpu.VMEM((c.D, c.D), BF)],
        name="middle",
    )


def pack_rows(c, place, half, rows, out_ref, base=0, start=0):
    main = c.SP - 16
    used = lax.broadcasted_iota(I32, (16, 1), 0) < 14
    out_ref[base : base + c.CR[half], :] = jnp.zeros((c.CR[half], c.D), BF)
    for j in range(c.X):
        at = pl.multiple_of(window_in(c, place, half, j) + base, 16)
        out_ref[pl.ds(at, main), :] += rows[j, start : start + main, :]
        tail = jnp.where(used, rows[j, start + main : start + c.SP, :], BF(0))
        out_ref[pl.ds(pl.multiple_of(at + main, 16), 16), :] += tail


def last_pair(c, tile, lanes):
    tile = tile[:, :lanes].astype(F32)
    return tile[14:15, :], tile[15:16, :]


def row_chunks(rows, size):
    return [slice(at, min(at + size, rows)) for at in range(0, rows, size)]


def grad_active_body(c, place, *refs):
    rows, own_ref, oth_ref, *outs, all_ref = refs

    @pl.when(pl.program_id(0) == 0)
    def _():
        pack_rows(c, place, 0, rows, all_ref)
        pack_rows(c, place, 1, rows, all_ref, c.CR[0], c.SP)

    weights = jnp.concatenate([own_ref[...], oth_ref[...]], axis=1)
    for half, base in enumerate((0, c.CR[0])):
        for at in row_chunks(c.CR[half], 320):
            values = all_ref[base + at.start : base + at.stop, :]
            outs[half][at, :] = dot_nt(values, weights).astype(BF)


def grad_active(c, order, place, rows, own_w, oth_w):
    outs = [shape_of((rows, c.F), BF) for rows in c.CR] + [shape_of((sum(c.CR), c.D), BF)]
    return call(
        order,
        functools.partial(grad_active_body, c),
        place,
        [rows, own_w, oth_w],
        [whole(rows, 1)] + [rows_of((c.fblk, c.half))] * 2,
        outs,
        [cols_of((rows, c.fblk)) for rows in c.CR] + [whole(outs[2])],
        (c.F // c.fblk,),
        name="grad_active",
    )


def expert_body(c, half, place, *refs):
    rows, own_ref, oth_ref, bias_ref, ga_ref = refs[:5]
    act_ref, gp_ref, gb_ref, all_ref, col_ref, back_ref = refs[5:11]
    acc_ref, dot_ref, row_ref = refs[11:]
    step = pl.program_id(0)

    @pl.when(step == 0)
    def _():
        acc_ref[...] = jnp.zeros_like(acc_ref)
        dot_ref[...] = jnp.zeros_like(dot_ref)
        pack_rows(c, place, half, rows, all_ref)
        col_ref[...] = jnp.zeros_like(col_ref)
        eye = lax.broadcasted_iota(I32, (c.SP, c.SP), 0) == lax.broadcasted_iota(I32, (c.SP, c.SP), 1)
        for j in range(c.X):
            high, low = last_pair(c, rows[j, c.SP - 16 :, :], c.SP)
            col = jnp.sum(jnp.where(eye, high + low, 0.0), axis=1, keepdims=True)
            col_ref[pl.ds(window_in(c, place, half, j), c.SP), :] += jnp.broadcast_to(col, (c.SP, 128))

    bias = bias_ref[...]
    weights = jnp.concatenate([own_ref[...], oth_ref[...]], axis=0)
    summed = jnp.zeros((1, c.fblk), F32)
    lead = 0.7978845608028654
    cube = lead * 0.044715
    chunks = row_chunks(c.CR[half], 224)
    ahead = dot_nn(all_ref[chunks[0], :], weights)
    for i, rows_at in enumerate(chunks):
        pre = ahead + bias
        if i + 1 < len(chunks):
            ahead = dot_nn(all_ref[chunks[i + 1], :], weights)
        square = pre * pre
        turn = jnp.tanh(pre * (cube * square + lead))
        above = 1.0 + turn
        active = (0.5 * pre) * above
        slope = above * (1.0 + (1.0 - turn) * (pre * (3 * cube * square + lead)))
        ga = ga_ref[rows_at, :].astype(F32)
        product = active * ga
        part = product[:, 0:128]
        for lane in range(128, c.fblk, 128):
            part = part + product[:, lane : lane + 128]
        dot_ref[rows_at, :] += part
        grad = ga * slope * (0.5 * col_ref[rows_at, 0:1])
        act_ref[rows_at, :] = active.astype(BF)
        grad_low = grad.astype(BF)
        gp_ref[rows_at, :] = grad_low
        summed = summed + jnp.sum(grad, axis=0, keepdims=True)
        acc_ref[rows_at, :] += dot_nt(grad_low, weights)
    gb_ref[...] = jnp.broadcast_to(summed, (8, c.fblk))

    @pl.when(step == pl.num_programs(0) - 1)
    def _():
        ones = jnp.ones((8, 128), BF)
        row_ref[...] = jnp.zeros_like(row_ref)
        for j in range(c.X):
            at = window_in(c, place, half, j)
            back_ref[j] = acc_ref[pl.ds(at, c.SP), :].astype(BF)
            a, rest = split_low(dot_ref[pl.ds(at, c.SP), :])
            total = dot_nt(ones, a) + dot_nt(ones, rest)
            high = total.astype(BF).astype(F32)
            row_ref[0:8, : c.SP] = high
            row_ref[8:16, : c.SP] = total - high
            tile = back_ref[j, c.SP - 16 :, : c.half].astype(F32)
            tile = last_rows(c, tile, row_ref[0:1, :], row_ref[8:9, :])
            back_ref[j, c.SP - 16 :, : c.half] = tile.astype(BF)


def expert(c, order, place, half, rows, own_w, oth_w, bias, ga):
    args = [rows, own_w, oth_w, bias, ga]
    count = c.CR[half]
    specs = [whole(rows, 1)]
    specs += [cols_of((c.half, c.fblk))] * 2
    specs += [cols_of((1, c.fblk)), cols_of((count, c.fblk))]
    outs = [
        shape_of((count, c.F), BF),
        shape_of((count, c.F), BF),
        shape_of((8, c.F), F32),
    ]
    out_specs = [cols_of((count, c.fblk))] * 2 + [cols_of((8, c.fblk))]
    late = [shape_of((count, c.D), BF), shape_of((count, 128), F32)]
    late.append(shape_of((c.X, c.SP, c.D), BF))
    return call(
        order,
        functools.partial(expert_body, c, half),
        place,
        args,
        specs,
        outs + late,
        out_specs + [whole(o, 1) for o in late],
        (c.F // c.fblk,),
        [
            pltpu.VMEM((count, c.D), F32),
            pltpu.VMEM((count, 128), F32),
            pltpu.VMEM((16, c.half), F32),
        ],
        name="expert",
    )


def produce_body(c, place, *refs):
    cols, acts, own_ref, oth_ref, out_ref, accs = refs[:2], refs[2:4], refs[4], refs[5], refs[6], refs[7:]
    step = pl.program_id(0)

    @pl.when(step == 0)
    def _():
        for acc_ref in accs:
            acc_ref[...] = jnp.zeros_like(acc_ref)

    weights = jnp.concatenate([own_ref[...], oth_ref[...]], axis=1)
    for half in range(2):
        for at in row_chunks(c.CR[half], 320):
            accs[half][at, :] += dot_nn(acts[half][at, :], weights)

    @pl.when(step == pl.num_programs(0) - 1)
    def _():
        for half in range(2):
            for j in range(c.X):
                rows_at = pl.ds(window_in(c, place, half, j), c.SP)
                col = cols[half][rows_at, 0:1]
                out_ref[j, half * c.SP : (half + 1) * c.SP, :] = (accs[half][rows_at, :] * col).astype(BF)


def produce(c, order, place, cols, acts, own_w, oth_w):
    out = shape_of((c.X, 2 * c.SP, c.D), BF)
    return call(
        order,
        functools.partial(produce_body, c),
        place,
        [*cols, *acts, own_w, oth_w],
        [whole(col) for col in cols]
        + [cols_of((rows, c.fblk)) for rows in c.CR]
        + [rows_of((c.fblk, c.half))] * 2,
        [out],
        [whole(out, 1)],
        (c.F // c.fblk,),
        [pltpu.VMEM((rows, c.D), F32) for rows in c.CR],
        name="produce",
    )[0]


def grad_second_body(c, own, place, *refs):
    all_ref, cols, acts = refs[0], refs[1:3], refs[3:5]
    out_ref, row_ref = refs[-2:]

    @pl.when(pl.program_id(0) == 0)
    def _():
        for half, base in enumerate((0, c.CR[0])):
            rows_at = slice(base, base + c.CR[half])
            row_ref[rows_at, :] = (all_ref[rows_at, :].astype(F32) * cols[half][:, 0:1]).astype(BF)

    acc = dot_tn(acts[0][...], row_ref[: c.CR[0], :])
    acc = acc + dot_tn(acts[1][...], row_ref[c.CR[0] :, :])
    if own:
        acc = acc + refs[5][...].astype(F32)
    out_ref[...] = acc.astype(out_ref.dtype)


def grad_second(c, order, place, rows, cols, acts, add=None):
    own = add is not None
    args = [rows, *cols, *acts]
    total = sum(c.CR)
    specs = [pl.BlockSpec((total, c.half), lambda i, s: (0, 0 if own else 1))]
    specs += [whole(col) for col in cols] + [cols_of((count, c.fblk)) for count in c.CR]
    if own:
        args.append(add)
        specs.append(rows_of((c.fblk, c.half)))
    out = shape_of((c.F, c.half), F32 if own else BF)
    return call(
        order,
        functools.partial(grad_second_body, c, own),
        place,
        args,
        specs,
        [out],
        [rows_of((c.fblk, c.half))],
        (c.F // c.fblk,),
        [pltpu.VMEM((total, c.half), BF)],
        name="grad_second",
    )[0]


def grad_first_body(c, own, place, *refs):
    acc = dot_tn(refs[0][...], refs[2][...]) + dot_tn(refs[1][...], refs[3][...])
    if own:
        acc = acc + refs[4][...].astype(F32)
    refs[-1][...] = acc.astype(refs[-1].dtype)


def grad_first(c, order, place, rows, gps, add=None):
    own = add is not None
    args = [*rows, *gps]
    specs = [pl.BlockSpec((count, c.half), lambda i, s: (0, 0 if own else 1)) for count in c.CR]
    specs += [cols_of((count, c.fblk)) for count in c.CR]
    if own:
        args.append(add)
        specs.append(cols_of((c.half, c.fblk)))
    out = shape_of((c.half, c.F), F32 if own else BF)
    return call(
        order,
        functools.partial(grad_first_body, c, own),
        place,
        args,
        specs,
        [out],
        [cols_of((c.half, c.fblk))],
        (c.F // c.fblk,),
        name="grad_first",
    )[0]


def combine_body(c, with_dots, place, *refs):
    refs = list(refs)
    extra_ref = None if with_dots else refs.pop(0)
    halves = 2 if with_dots else 1
    rows, refs = refs[:halves], refs[halves:]
    tails = []
    if with_dots:
        tails, refs = refs[:2], refs[2:]
    mine_ref = refs.pop(0)
    groups = [(0, g) for g in groups_a(c)] + [(1, g) for g in groups_b(c)]
    outs, (hot_ref, row_ref) = refs[: len(groups)], refs[len(groups) :]
    pad = hot_ref.shape[1] // c.X

    @pl.when(pl.program_id(0) == 0)
    def _():
        row_ref[...] = jnp.zeros_like(row_ref)
        slots = lax.broadcasted_iota(I32, (c.R, pad), 1)
        for k in range(c.n):
            at = pl.multiple_of((place[1] ^ k) * c.R, 16)
            for j in range(c.X):
                hot = (mine_ref[pl.ds(at, c.R), j : j + 1] == slots).astype(BF)
                hot_ref[k * c.R : (k + 1) * c.R, j * pad : (j + 1) * pad] = hot
        if with_dots:
            wide = (c.SP, c.half)
            eye = lax.broadcasted_iota(I32, wide, 0) == lax.broadcasted_iota(I32, wide, 1)
            lane = lax.broadcasted_iota(I32, (1, 128), 1)
            for half in range(2):
                for j in range(c.X):
                    high, low = last_pair(c, tails[half][j], c.half)
                    high = jnp.sum(jnp.where(eye, high, 0.0), axis=1, keepdims=True)
                    low = jnp.sum(jnp.where(eye, low, 0.0), axis=1, keepdims=True)
                    e = expert_of(c, place, j)
                    cols = jnp.where(lane == e, high, jnp.where(lane == e + 64, low, 0.0))
                    at = j * pad + half * c.SP
                    row_ref[at : at + c.SP, :128] = cols.astype(BF)
            pulls = dot_nn(hot_ref[...], row_ref[:, :128]).astype(BF)
            expert = lax.broadcasted_iota(I32, (c.E, 128), 0)
            lane = lax.broadcasted_iota(I32, (c.E, 128), 1)
            pick = ((lane == expert) | (lane == expert + 64)).astype(BF)
            for (side, group), out_ref in zip(groups, outs):
                for at, k in enumerate(group):
                    if side == 0:
                        got = dot_nt(pick, pulls[k * c.R : (k + 1) * c.R])
                        out_ref[at, c.R :, :] = jnp.zeros((c.E, c.half), BF)
                        out_ref[at, c.R :, : c.R] = got.astype(BF)

    for half, rows_ref in enumerate(rows):
        size = rows_ref.shape[1]
        for j in range(c.X):
            at = j * pad + half * size
            row_ref[at : at + size, :] = rows_ref[j]
    result = dot_nn(hot_ref[...], row_ref[...]).astype(BF)
    for half in range(2):

        @pl.when(pl.program_id(0) == half)
        def _():
            for (side, group), out_ref in zip(groups, outs):
                if side == half:
                    for at, k in enumerate(group):
                        out_ref[at, : c.R, :] = result[k * c.R : (k + 1) * c.R]
                        if extra_ref is not None:
                            more = extra_ref.shape[1] // 2
                            out_ref[at, c.R :, :] = extra_ref[k, half * more : (half + 1) * more, :]


def combine(c, order, place, rows, mine, extra=None, cost=0):
    pad = up(2 * c.SP, 128)
    args = list(rows)
    specs = [pl.BlockSpec((c.X, r.shape[1], c.half), lambda i, s: (0, 0, i ^ s[2])) for r in rows]
    if extra is None:
        args += list(rows)
        specs += [pl.BlockSpec((c.X, 16, c.half), lambda i, s: (0, c.SP // 16 - 1, 0))] * 2
        outs = piece_outs(c, c.E)
    else:
        args.insert(0, extra)
        specs.insert(0, whole(extra))
        outs = piece_outs(c, extra.shape[1] // 2, extra.shape[1] // 2)
    args.append(mine)
    specs.append(whole(mine))
    result = call(
        order,
        functools.partial(combine_body, c, extra is None),
        place,
        args,
        specs,
        outs,
        [whole(o, 1) for o in outs],
        (2,),
        [pltpu.VMEM((c.n * c.R, c.X * pad), BF), pltpu.VMEM((c.X * pad, c.half), BF)],
        name="combine",
        cost=cost,
    )
    return list(result)


def back_two_body(c, place, *refs):
    refs = list(refs)
    groups = groups_of(c)
    heads, refs = refs[: c.n * len(groups)], refs[c.n * len(groups) :]
    count = (len(refs) - 14 - c.n) // 2
    a, b, refs = refs[:count], refs[count : 2 * count], refs[2 * count :]
    own_ref, oth_ref, after_ref, probs_ref, keep_ref, weight_ref, cot_ref, hid_ref, small_ref = refs[:9]
    ga_ref, proj_own_ref, proj_oth_ref = refs[9:12]
    mixes, (gb_ref, sums_ref) = refs[12:-2], refs[-2:]
    sum_a = add_up(a)
    live = live_rows(c, place[1] * c.R, c.R)
    cot = jnp.where(live, cot_ref[...], BF(0))
    eshift = small_ref[6 : 6 + c.E, :]
    router = small_ref[6 + c.E : 6 + 2 * c.E, :]
    kept = keep_ref[...] > 0
    pulls = jnp.where(kept, sum_a[c.R :, : c.R] + dot_nt(eshift, cot), 0.0)
    probs = probs_ref[...]
    glog = (probs * (pulls - jnp.sum(probs * pulls, axis=0, keepdims=True))).astype(BF)
    two = jnp.concatenate([sum_a[: c.R], add_up(b)], axis=1) + dot_tn(glog, router)
    normed, inv_std = norm_rows(after_ref[...])
    grad_after = cot.astype(F32) + norm_back(two, small_row(c, small_ref, 1), normed, inv_std)
    ga_ref[...] = grad_after
    low = grad_after.astype(BF)
    gb_ref[...] = low
    high, rest = split_low(weight_ref[...])
    hid = jnp.where(live, hid_ref[...], BF(0))
    sums_ref[0:1, :] = jnp.sum(two * normed, axis=0, keepdims=True)
    sums_ref[1:2, :] = jnp.sum(two, axis=0, keepdims=True)
    sums_ref[2:3, :] = jnp.sum(low.astype(F32), axis=0, keepdims=True)
    sums_ref[3:8, :] = jnp.zeros((5, c.D), F32)
    sums_ref[8 : 8 + c.E, :] = dot_nn(high, cot) + dot_nn(rest, cot)
    sums_ref[8 + c.E : 8 + 2 * c.E, :] = dot_nn(glog, hid)
    for k in range(c.n):
        mix = dot_nt(gb_ref[:, own_cols(c, place)], own_ref[k])
        mix = mix + dot_nt(gb_ref[:, other_cols(c, place)], oth_ref[k])
        mixes[k][...] = mix.astype(BF)
    height = sums_ref.shape[0]
    for cols, out_ref in ((own_cols(c, place), proj_own_ref), (other_cols(c, place), proj_oth_ref)):
        sums = sums_ref[:, cols].astype(BF)
        for k in range(c.n):
            for group, (at, lanes) in enumerate(groups):
                part = dot_tn(heads[k * len(groups) + group][...], gb_ref[:, cols])
                out_ref[k, at : at + lanes, :] = part.astype(BF)
            out_ref[k, c.W : c.W + height, :] = sums
            rest = out_ref.shape[1] - c.W - height
            out_ref[k, c.W + height :, :] = jnp.zeros((rest, c.half), BF)


def back_two(c, order, place, heads, sums, own_w, oth_w, lanes, cotangent, hidden, small):
    height = 8 + 2 * c.E
    rows = up(c.W + height, 32)
    args = [pair[0] for pair in flat(heads)]
    specs = [
        pl.BlockSpec((None, c.R, a.shape[2]), lambda i, s, at=at: (at, s[1], 0))
        for a, at in flat(heads)
    ]
    args += [*sums[0], *sums[1], own_w, oth_w, *lanes, cotangent, hidden, small]
    lane_rows = pl.BlockSpec((c.R, c.D), lambda i, s: (s[1], 0))
    specs += [first_block(a) for a in [*sums[0], *sums[1]]]
    specs += [whole(a) for a in [own_w, oth_w, *lanes]] + [lane_rows, lane_rows, whole(small)]
    outs = [shape_of((c.R, c.D), F32)] + [shape_of((c.n, rows, c.half), BF)] * 2
    outs += [shape_of((c.R, c.W), BF) for _ in range(c.n)]
    result = call(
        order,
        functools.partial(back_two_body, c),
        place,
        args,
        specs,
        outs,
        [whole(o) for o in outs],
        (1,),
        [pltpu.VMEM((c.R, c.D), BF), pltpu.VMEM((height, c.D), F32)],
        name="back_two",
    )
    return (*result[:3], list(result[3:]))


def block_out_body(c, place, *refs):
    refs = list(refs)
    count = (len(refs) - 5) // 2
    a, b, refs = refs[:count], refs[count : 2 * count], refs[2 * count :]
    after_ref, weight_ref, small_ref, out_ref, proj_ref = refs
    high, low = split_low(weight_ref[...])
    eshift = small_ref[6 : 6 + c.E, :]
    shift = dot_tn(high, eshift) + dot_tn(low, eshift)
    more = proj_ref.shape[0] // 2
    for h, pieces in enumerate((a, b)):
        cols = slice(h * c.half, (h + 1) * c.half)
        total = add_up([ref.at[: c.R, :] for ref in pieces])
        out_ref[h] = (after_ref[:, cols] + total + shift[:, cols]).astype(BF)
        proj_ref[h * more : (h + 1) * more, :] = same_sum(c, pieces, slice(c.R, c.R + more)).astype(BF)


def block_out(c, order, place, sums, after, weight, small):
    args = [*sums[0], *sums[1], after, weight, small]
    more = 2 * (sums[0][0].shape[1] - c.R)
    outs = [shape_of((2, c.R, c.half), BF), shape_of((more, c.half), BF)]
    return call(
        order,
        functools.partial(block_out_body, c),
        place,
        args,
        [first_block(a) for a in args[:-3]] + [whole(a) for a in args[-3:]],
        outs,
        [whole(o) for o in outs],
        (1,),
        name="block_out",
    )


def grad_one_body(c, place, dqkv_ref, normed_ref, own_ref, oth_ref, *outs):
    sums_ref = outs[-1]
    groups = [(0, g) for g in groups_a(c)] + [(1, g) for g in groups_b(c)]
    for side in range(2):
        cols = slice(side * c.half, (side + 1) * c.half)
        weights = [jnp.where(place[2] == side, own_ref[p], oth_ref[p]) for p in range(3)]
        gain = jnp.zeros((1, c.half), F32)
        shift = jnp.zeros((1, c.half), F32)
        for (where, group), out_ref in zip(groups, outs):
            if where != side:
                continue
            for row, k in enumerate(group):
                rows_at = pl.ds(pl.multiple_of((place[1] ^ k) * c.R, 16), c.R)
                acc = None
                for part in range(3):
                    rows = dqkv_ref[rows_at, part * c.W : (part + 1) * c.W]
                    term = dot_nt(rows, weights[part])
                    acc = term if acc is None else acc + term
                out_ref[row, : c.R, :] = acc.astype(BF)
                normed = normed_ref[rows_at, cols].astype(F32)
                gain = gain + jnp.sum(acc * normed, axis=0, keepdims=True)
                shift = shift + jnp.sum(acc, axis=0, keepdims=True)
        sums_ref[0:1, cols] = gain
        sums_ref[1:2, cols] = shift
        row = lax.broadcasted_iota(I32, (16, 1), 0)
        tile = jnp.where(row == 0, gain, jnp.where(row == 1, shift, 0.0)).astype(BF)
        for (where, group), out_ref in zip(groups, outs):
            if where == side:
                for at in range(len(group)):
                    out_ref[at, c.R :, :] = tile


def grad_one(c, order, place, dqkv, normed, own_w, oth_w):
    outs = piece_outs(c, 16, 16) + [shape_of((2, c.D), F32)]
    result = call(
        order,
        functools.partial(grad_one_body, c),
        place,
        [dqkv, normed, own_w, oth_w],
        [whole(dqkv), whole(normed), whole(own_w), whole(oth_w)],
        outs,
        [whole(o) for o in outs],
        (1,),
        name="grad_one",
    )
    return list(result[:-1]), result[-1]


def grad_qkv_body(c, place, hid_ref, dqkv_ref, own_ref, oth_ref):
    own_ref[0] = dot_tn(hid_ref[:, own_cols(c, place)], dqkv_ref[...]).astype(BF)
    oth_ref[0] = dot_tn(hid_ref[:, other_cols(c, place)], dqkv_ref[...]).astype(BF)


def grad_qkv(c, order, place, hidden, dqkv):
    specs = [whole(hidden, 1), cols_of((c.TP, c.W))]
    if c.W % 128:
        dqkv = dqkv.reshape(c.TP, 3, c.W).transpose(1, 0, 2)
        specs[1] = pl.BlockSpec((None, c.TP, c.W), lambda i, s: (i, 0, 0))
    return call(
        order,
        functools.partial(grad_qkv_body, c),
        place,
        [hidden, dqkv],
        specs,
        [shape_of((3, c.half, c.W), BF)] * 2,
        [rows_of((1, c.half, c.W))] * 2,
        (3,),
        name="grad_qkv",
    )


def back_one_body(c, place, *refs):
    refs = list(refs)
    count = (len(refs) - 5) // 2
    a, b, refs = refs[:count], refs[count : 2 * count], refs[2 * count :]
    tok_ref, after_ref, small_ref, out_ref, sums_ref = refs
    live = live_rows(c, place[1] * c.R, c.R)
    normed, inv_std = norm_rows(jnp.where(live, tok_ref[...].astype(F32), 0.0))
    one = jnp.concatenate([add_up(a)[: c.R], add_up(b)[: c.R]], axis=1)
    grad = after_ref[...] + norm_back(one, small_row(c, small_ref, 0), normed, inv_std)
    for h in range(2):
        out_ref[h] = grad[:, h * c.half : (h + 1) * c.half].astype(BF)
    for h, refs in enumerate((a, b)):
        tiles = [ref[c.R :, :].astype(F32) for ref in refs]
        pair = (tiles[0] + tiles[1]).astype(BF).astype(F32)
        for tile in tiles[2:]:
            pair = pair + tile
        sums_ref[:, h * c.half : (h + 1) * c.half] = pair[0:2]


def back_one(c, order, place, sums, tokens, after, small):
    args = [*sums[0], *sums[1], tokens, after, small]
    lane_rows = pl.BlockSpec((c.R, c.D), lambda i, s: (s[1], 0))
    specs = [first_block(a) for a in args[:-3]] + [lane_rows, whole(after), whole(small)]
    outs = [shape_of((2, c.R, c.half), BF), shape_of((2, c.D), F32)]
    return call(
        order,
        functools.partial(back_one_body, c),
        place,
        args,
        specs,
        outs,
        [whole(o) for o in outs],
        (1,),
        name="back_one",
    )


def assemble_body(c, place, *refs):
    pieces, out_ref = refs[:-1], refs[-1]
    for k in range(c.n):

        @pl.when((place[1] ^ k) == pl.program_id(0))
        def _():
            for h in range(2):
                values = pieces[2 * k + h][...].astype(out_ref.dtype)
                out_ref[:, h * c.half : (h + 1) * c.half] = values


def assemble(c, order, place, pieces, dtype):
    out = shape_of((c.T, c.D), dtype)
    return call(
        order,
        functools.partial(assemble_body, c),
        place,
        [pair[0] for pair in flat(pieces)],
        [
            pl.BlockSpec((None, c.R, c.half), lambda i, s, at=at: (at, 0, 0))
            for _, at in flat(pieces)
        ],
        [out],
        [rows_of((c.R, c.D))],
        (-(-c.T // c.R),),
        name="assemble",
    )[0]


def local(
    tokens,
    cotangent,
    w_qkv,
    qv_bias,
    w_proj,
    proj_bias,
    norm_gains,
    norm_shifts,
    w_router,
    expert_shift,
    w_first,
    w_second,
    first_bias,
    routes,
    priority,
):
    T, D = tokens.shape
    n = lax.axis_size("mp")
    E = w_router.shape[1]
    S = 16 * T // (5 * E)
    R = up(-(-T // n), 16)
    F = w_first.shape[2]
    W = w_proj.shape[0]
    win = up(IMG_LEN + 15, 16)
    Q = (S + 1) // 2
    cap = (9 * T + 4 * EXP_DEV - 1) // (4 * EXP_DEV)
    X = E // EXP_DEV
    full = min(cap // S, X)
    c = Sizes(
        T=T,
        D=D,
        half=D // 2,
        n=n,
        X=X,
        E=E,
        S=S,
        Q=Q,
        SP=up(Q + 17, 16),
        CR=(up(min(cap, X * Q), 16), up(full * (S - Q) + max(0, cap - full * S - Q), 16)),
        R=R,
        TP=n * R,
        W=W,
        images=T // IMG_LEN,
        quarters=n // EXP_DEV,
        F=F,
        cap=cap,
        win=win,
        fblk=min(1024, F),
        key=4 * T,
    )
    order = Order()
    dp, mp, grid = lax.axis_index("dp"), lax.axis_index("mp"), lax.axis_index("grid")
    here = jnp.stack([dp, mp, grid, mp // c.quarters]).astype(I32)

    experts = jnp.arange(E, dtype=I32)[:, None, None]
    count = jnp.sum((routes.T[None] == experts).astype(I32), axis=(1, 2))[None]
    counts = trade(jnp.broadcast_to(count, (c.X, E)), "dp")
    bias_rows = F // 2 // c.half
    packed = jnp.concatenate(
        [
            norm_gains,
            norm_shifts,
            proj_bias[None],
            jnp.pad(qv_bias, ((0, 0), (0, c.half - W))),
            expert_shift,
            w_router.T,
            first_bias.reshape(bias_rows, c.half),
        ],
        axis=0,
    )
    packed = jnp.pad(packed, ((0, up(packed.shape[0], 16) - packed.shape[0]), (0, 0)))
    packed_oth = swap_grid(packed)
    small = jnp.where(
        grid == 0,
        jnp.concatenate([packed, packed_oth], axis=1),
        jnp.concatenate([packed_oth, packed], axis=1),
    )
    bias = small[6 + 2 * E : 6 + 2 * E + bias_rows].reshape(bias_rows, 2, c.half)
    bias = bias.transpose(1, 0, 2).reshape(1, F).astype(F32)
    qkv_own = w_qkv.transpose(1, 0, 2)
    qkv_oth = swap_grid(qkv_own)
    slot, blocks, rt = route(c, order, here, routes, priority)
    order.tie(packed_oth)
    order.tie(qkv_oth)
    proj_own = jnp.stack([w_proj] + [swap_mp(c, w_proj, k) for k in range(1, n)])
    order.tie(proj_own)
    place, offsets = windows(c, order, here, counts)
    grad_out = dispatch(c, order, place, slot, cotangent, (0, 1))
    grad_in = trade(grad_out, "dp")

    first_own = w_first[0]
    second_own = w_second[0]
    second_tied, first_tied, _ = lax.optimization_barrier((second_own, first_own, grad_out))
    second_oth = swap_grid(second_tied)
    first_oth = swap_grid(first_tied)

    proj_oth = swap_grid(proj_own)

    outs = [shape_of((c.TP, D), BF), shape_of((c.TP, 3 * W), BF), shape_of((c.TP, D), BF)]
    hidden_one, qkv, normed_one = call(
        order,
        functools.partial(qkv_body, c),
        place,
        [tokens, small, qkv_own, qkv_oth],
        [rows_of((c.R, D)), whole(small), whole(qkv_own), whole(qkv_oth)],
        outs,
        [rows_of((c.R, D)), rows_of((c.R, 3 * W)), rows_of((c.R, D))],
        (n,),
        [pltpu.VMEM((D, 3 * W), BF)],
        name="qkv",
    )
    groups = groups_of(c)
    out = shape_of((len(groups), c.TP, groups[0][1]), BF)
    mix = call(
        order,
        functools.partial(attend_body, c),
        place,
        [qkv],
        [whole(qkv)],
        [out],
        [whole(out)],
        (c.images,),
        name="attend",
    )[0]
    mixes, _ = gather_mp(c, mix)
    hidden_two, weight, mine, keep, after, probs, keep_lane, weight_lane = middle(
        c, order, place, mixes, proj_own, proj_oth, tokens, small, offsets, blocks, rt
    )
    keep_mask = keep[:, :2, :].transpose(0, 2, 1).reshape(c.TP, 2)[:T].astype(I32)
    mine = mine.transpose(0, 2, 1).reshape(c.TP, 8)

    rows_a = trade(dispatch(c, order, place, slot, hidden_two, (0,), weight), "dp")
    rows_b = dispatch(c, order, place, slot, hidden_two, (1,), weight)
    ga_a, ga_b, grad_all = grad_active(c, order, place, grad_in, second_own, second_oth)
    rows_b = trade(held(rows_b, rows_a, grad_all), "dp")
    act_a, gp_a, gb_a, all_a, col_a, back_a = expert(
        c, order, place, 0, rows_a, first_own, first_oth, bias, ga_a
    )
    back_a = trade(held(back_a, rows_b), "dp")
    act_b, gp_b, gb_b, all_b, col_b, back_b = expert(
        c, order, place, 1, rows_b, first_own, first_oth, bias, ga_b
    )
    back_b = trade(held(back_b, back_a), "dp")
    cols, acts, gps, alls = [col_a, col_b], [act_a, act_b], [gp_a, gp_b], [all_a, all_b]
    second_part = swap_grid(grad_second(c, order, place, grad_all, cols, acts))
    order.tie(back_a)
    first_part = swap_grid(grad_first(c, order, place, alls, gps))
    prod = produce(c, order, place, cols, acts, second_own, second_oth)
    gb = (gb_a + gb_b)[0:1].reshape(2, F // 2)
    gb_own = lax.dynamic_index_in_dim(gb, grid, 0, True)
    gb_oth = lax.dynamic_index_in_dim(gb, 1 - grid, 0, True)
    grad_fbias = gb_own + swap_grid(gb_oth)

    pieces = combine(c, order, place, [back_a, back_b], mine)
    prod = trade(held(prod, back_b), "dp")
    two_sums = reduce_start(c, pieces)
    grad_second_out = grad_second(c, order, place, grad_all, cols, acts, second_part)
    two_sums = reduce_end(c, order, two_sums)
    grad_first_out = grad_first(c, order, place, alls, gps, first_part)
    grad_after, proj_a, proj_b, grad_mix = back_two(
        c,
        order,
        place,
        mixes,
        two_sums,
        proj_own,
        proj_oth,
        [after, probs, keep_lane, weight_lane],
        cotangent,
        hidden_two,
        small,
    )
    grad_mix = [grad_mix[0]] + [swap_mp(c, grad_mix[k], k) for k in range(1, n)]
    proj_low = (proj_a.astype(F32) + swap_grid(proj_b).astype(F32)).astype(BF)
    pieces = combine(c, order, place, [prod], mine, proj_low, cost=10)
    out_sums = reduce_start(c, [held(p, *grad_mix) for p in pieces])

    outs = [shape_of((c.TP, 3 * W), BF), shape_of((8, 3 * W), F32)]
    dqkv, dqkv_sums = call(
        order,
        functools.partial(attend_back_body, c),
        place,
        [qkv, *grad_mix],
        [whole(qkv)] + [whole(p) for p in grad_mix],
        outs,
        [whole(o) for o in outs],
        (c.images,),
        [pltpu.VMEM((c.TP, W), BF)],
        name="attend_back",
    )
    one_pieces, one_parts = grad_one(c, order, place, dqkv, normed_one, qkv_own, qkv_oth)
    one_sums = reduce_start(c, one_pieces)
    out_sums = reduce_end(c, order, out_sums)
    qkv_a, qkv_b = grad_qkv(c, order, place, hidden_one, dqkv)
    out_lane, proj_sum = block_out(c, order, place, out_sums, after, weight_lane, small)
    one_sums = reduce_end(c, order, one_sums)
    qkv_b = swap_grid(qkv_b)
    qkv_low = (qkv_a.astype(F32) + qkv_b.astype(F32)).astype(BF)
    proj_rows = proj_sum.shape[0]
    shared = jnp.concatenate([qkv_low.reshape(-1, c.half), proj_sum], axis=0)
    shared = sum_dp_start(c, shared)
    grad_low, sums_one = back_one(c, order, place, one_sums, tokens, grad_after, small)
    grad_low, first_low = gather_mp(c, grad_low, shared)
    out_lane, _ = gather_mp(c, held(out_lane, *first_low))
    sums_one = held(sums_one, *[pair[0] for pair in grad_low[-1]])

    shared = sum_dp_end(c, shared)
    grad_w_qkv = shared[: 3 * W].reshape(3, c.half, W)
    proj_sum = shared[3 * W :]
    rest = proj_sum[W : W + 8 + 2 * E]
    qv_rows = jnp.concatenate([dqkv_sums[0:1, :W], dqkv_sums[0:1, 2 * W :]], axis=0)
    if n != 4:
        sums_one = fold(c, one_parts, (("mp", n),))
    sums_one = finish_sums(c, sums_one, qv_rows, grid)
    grad_tokens = assemble(c, order, place, grad_low, F32)
    block = assemble(c, order, place, out_lane, BF)
    return (
        block,
        grad_tokens,
        grad_w_qkv.transpose(1, 0, 2),
        sums_one[2:3, :W],
        proj_sum[:W],
        rest[2],
        jnp.stack([sums_one[0], rest[0]]),
        jnp.stack([sums_one[1], rest[1]]),
        rest[8 + E : 8 + 2 * E].T,
        rest[8 : 8 + E],
        grad_first_out[None],
        grad_second_out[None],
        grad_fbias,
        keep_mask,
    )


def solution(mesh):
    return jax.shard_map(
        local,
        mesh=mesh,
        in_specs=(
            P(("dp", "grid"), None),
            P(("dp", "grid"), None),
            P("grid", None, "mp"),
            P("grid", "mp"),
            P("mp", "grid"),
            P("grid"),
            P(None, "grid"),
            P(None, "grid"),
            P("grid", None),
            P(None, "grid"),
            P(("dp", "mp"), "grid", None),
            P(("dp", "mp"), None, "grid"),
            P(("dp", "mp"), "grid"),
            P(("dp", "grid"), None),
            P(("dp", "grid"), None),
        ),
        out_specs=(
            P(("dp", "grid"), None),
            P(("dp", "grid"), None),
            P("grid", None, "mp"),
            P("grid", "mp"),
            P("mp", "grid"),
            P("grid"),
            P(None, "grid"),
            P(None, "grid"),
            P("grid", None),
            P(None, "grid"),
            P(("dp", "mp"), "grid", None),
            P(("dp", "mp"), None, "grid"),
            P(("dp", "mp"), "grid"),
            P(("dp", "grid"), None),
        ),
        check_vma=False,
    )
```

```python
import functools
from typing import NamedTuple

import jax
import jax.numpy as jnp
from jax import lax
from jax.experimental import pallas as pl
from jax.experimental.pallas import tpu as pltpu
from jax.sharding import PartitionSpec as P

HEAD = 64
IMG_LEN = 197
EXP_DEV = 4
BF = jnp.bfloat16
F32 = jnp.float32
I32 = jnp.int32
VMEM_BYTES = 56 * 1024 * 1024
LOW = -1e30


class Sizes(NamedTuple):
    T: int
    D: int
    half: int
    n: int
    X: int
    E: int
    S: int
    Q: int
    SP: int
    CR: tuple
    R: int
    TP: int
    W: int
    images: int
    quarters: int
    F: int
    cap: int
    win: int
    fblk: int
    key: int


class Order:
    def __init__(self):
        self.after = []

    def tie(self, value):
        self.after.append(value)

    def hold(self, *values):
        return lax.optimization_barrier((*values, *self.after))[: len(values)]


def up(value, step):
    return -(-value // step) * step


def dot_nn(a, b):
    return jnp.dot(a, b, preferred_element_type=F32)


def dot_nt(a, b):
    return lax.dot_general(a, b, (((1,), (1,)), ((), ())), preferred_element_type=F32)


def dot_tn(a, b):
    return lax.dot_general(a, b, (((0,), (0,)), ((), ())), preferred_element_type=F32)


def split_low(values):
    high = values.astype(BF)
    return high, (values - high.astype(F32)).astype(BF)


def shape_of(dims, dtype):
    return jax.ShapeDtypeStruct(dims, dtype)


def whole(array, buffers=None):
    dims = tuple(array.shape)
    extra = {} if buffers is None else {"pipeline_mode": pl.Buffered(buffers)}
    return pl.BlockSpec(dims, lambda i, s: (0,) * len(dims), **extra)


def rows_of(dims):
    return pl.BlockSpec(dims, lambda i, s: (i,) + (0,) * (len(dims) - 1))


def cols_of(dims):
    return pl.BlockSpec(dims, lambda i, s: (0,) * (len(dims) - 1) + (i,))


def call(order, body, place, args, specs, outs, out_specs, grid, scratch=(), name=None, cost=0):
    extra = order.after
    count = len(args)

    def wrapped(place, *refs):
        body(place, *refs[:count], *refs[count + len(extra) :])

    result = pl.pallas_call(
        wrapped,
        grid_spec=pltpu.PrefetchScalarGridSpec(
            num_scalar_prefetch=1,
            grid=grid,
            in_specs=list(specs) + [pl.BlockSpec(memory_space=pl.ANY)] * len(extra),
            out_specs=list(out_specs),
            scratch_shapes=list(scratch),
        ),
        out_shape=list(outs),
        compiler_params=pltpu.CompilerParams(
            dimension_semantics=("arbitrary",) * len(grid), vmem_limit_bytes=VMEM_BYTES
        ),
        cost_estimate=pl.CostEstimate(
            flops=1000 + int(1.1e9 * cost), bytes_accessed=1000, transcendentals=0
        ),
        name=name,
    )(place, *args, *extra)
    order.after = [min(result, key=lambda o: o.size)]
    return result


def swap_mp(c, value, mask):
    return lax.ppermute(value, "mp", [(i, i ^ mask) for i in range(c.n)])


def swap_grid(value):
    return lax.ppermute(value, "grid", [(0, 1), (1, 0)])


def held(value, *others):
    return lax.optimization_barrier((value, *others))[0]


def trade(value, axis):
    return lax.all_to_all(value, axis, split_axis=0, concat_axis=0, tiled=True)


def groups_a(c):
    return [[0, 2], [1, 3]] if c.n == 4 else [[k] for k in range(c.n)]


def groups_b(c):
    return [[0, 1], [2, 3]] if c.n == 4 else [[k] for k in range(c.n)]


def reduce_start(c, arrays):
    a, b = arrays[: len(arrays) // 2], arrays[len(arrays) // 2 :]
    if c.n != 4:
        return [[x[0]] + [swap_mp(c, x[k], k) for k in range(1, c.n)] for x in (a, b)]
    return [[a[0], swap_mp(c, a[1], 1)], [b[0], swap_mp(c, b[1], 2)]]


def reduce_end(c, order, state):
    if c.n != 4:
        return state
    (a, ra), (b, rb) = state
    ra, rb = order.hold(ra, rb)
    ta = (a[1:].astype(F32) + ra[1:].astype(F32)).astype(BF)
    tb = (b[1:].astype(F32) + rb[1:].astype(F32)).astype(BF)
    order.tie(ta)
    order.tie(tb)
    return [[a, ra, swap_mp(c, ta, 2)], [b, rb, swap_mp(c, tb, 1)]]


def piece_outs(c, more_a=0, more_b=0):
    outs = [shape_of((len(g), c.R + more_a, c.half), BF) for g in groups_a(c)]
    return outs + [shape_of((len(g), c.R + more_b, c.half), BF) for g in groups_b(c)]


def first_block(array):
    dims = tuple(array.shape)
    return pl.BlockSpec((None,) + dims[1:], lambda i, s: (0, 0, 0))


def same_sum(c, refs, rows):
    parts = [ref[rows, :].astype(F32) for ref in refs]
    if c.n == 4:
        return (parts[0] + parts[1]).astype(BF).astype(F32) + parts[2]
    while len(parts) > 1:
        parts = [parts[i] + parts[i + 1] for i in range(0, len(parts), 2)]
    return parts[0]


def add_up(refs):
    total = refs[0][...].astype(F32)
    for ref in refs[1:]:
        total = total + ref[...].astype(F32)
    return total


def sum_dp_start(c, value):
    return trade(value.reshape((c.X, value.shape[0] // c.X) + value.shape[1:]), "dp")


def sum_dp_turn(c, parts):
    total = jnp.sum(parts.astype(F32), axis=0).astype(BF)
    return jnp.broadcast_to(total[None], (c.X,) + total.shape)


def sum_dp_end(c, spread):
    return trade(spread, "dp").reshape((-1,) + spread.shape[2:]).astype(F32)


def gather_mp(c, value, until=None):
    if c.n != 4 or value.shape[0] != 2:
        parts = [value] + [swap_mp(c, value, k) for k in range(1, c.n)]
        return [[(p, h) for h in range(value.shape[0])] for p in parts], parts[1:]
    one = swap_mp(c, value, 1)
    two = swap_mp(c, value, 2)
    ends = one[0:1], two[1:2]
    if until is not None:
        ends = held(ends[0], *until), held(ends[1], *until)
    far_a = swap_mp(c, ends[0], 2)
    far_b = swap_mp(c, ends[1], 1)
    near = [[(p, 0), (p, 1)] for p in (value, one, two)]
    return near + [[(far_a, 0), (far_b, 0)]], [one, two]


def gather_both(c, first, second, until):
    if c.n != 4:
        return gather_mp(c, first)[0], gather_mp(c, second)[0], first
    one, two = swap_mp(c, first, 1), swap_mp(c, first, 2)
    near = jnp.concatenate([one[0:1], second]), jnp.concatenate([two[1:2], second])
    by_two, by_one = [swap_mp(c, held(x, *until), mask) for x, mask in zip(near, (2, 1))]
    far_a, far_b = swap_mp(c, by_one[1:2], 2), swap_mp(c, by_two[2:3], 1)
    pieces = [[(p, 0), (p, 1)] for p in (first, one, two)] + [[(by_two, 0), (by_one, 0)]]
    others = [[(second, 0), (second, 1)], [(by_one, 1), (by_one, 2)], [(by_two, 1), (by_two, 2)]]
    return pieces, others + [[(far_a, 0), (far_b, 0)]], one


def flat(pieces):
    return [pair for piece in pieces for pair in piece]


def fold(c, value, axes):
    for axis, size in axes:
        mask = 1
        while mask < size:
            value = value + lax.ppermute(value, axis, [(i, i ^ mask) for i in range(size)])
            mask *= 2
    return value


def first_sums(c, sums, one_parts):
    if c.n != 4:
        return fold(c, one_parts, (("mp", c.n),))
    halves = []
    for a, b, far in sums:
        pair = (a[0, c.R : c.R + 2].astype(F32) + b[0, c.R : c.R + 2].astype(F32)).astype(BF)
        halves.append(pair.astype(F32) + far[0, c.R : c.R + 2].astype(F32))
    return jnp.concatenate(halves, axis=1)


def chip_sums(c, one, parts, grid):
    def half_of(side):
        cols = lax.dynamic_slice_in_dim(one, side * c.half, c.half, 1)
        row = lax.dynamic_index_in_dim(parts, side, 0, True)
        return jnp.concatenate([cols, jnp.pad(row, ((0, 0), (0, c.half - c.W)))], axis=0)

    return half_of(grid) + swap_grid(half_of(1 - grid))


def expert_of(c, place, j):
    return j * EXP_DEV + place[3]


def window_slot(c, slot):
    return jnp.where(slot < c.Q, slot, slot + (c.SP - c.Q))


def count_places(c, row_ref, col_ref, rt_ref, slot_ref, blocks_ref, rtb_ref):
    pad = jnp.full((1, c.TP - c.T), 1 << 30, I32)
    first = jnp.broadcast_to(jnp.concatenate([row_ref[0:1, :], pad], axis=1), (8, c.TP))
    second = jnp.broadcast_to(jnp.concatenate([row_ref[1:2, :], pad], axis=1), (8, c.TP))

    def count(at, state):
        a, b = state
        keys = col_ref[pl.ds(at, 8), :]
        for k in range(2):
            key = keys[:, k : k + 1]
            a = a + (key < first).astype(I32)
            b = b + (key < second).astype(I32)
        return a, b

    def one(i, state):
        for q in range(8):
            state = count(pl.multiple_of(i * 64 + q * 8, 8), state)
        return state

    zero = jnp.zeros((8, c.TP), I32)
    state = lax.fori_loop(0, c.T // 64, one, (zero, zero))
    for at in range(c.T // 64 * 64, c.T, 8):
        state = count(at, state)
    a = jnp.sum(state[0], axis=0, keepdims=True)
    b = jnp.sum(state[1], axis=0, keepdims=True)
    pad = jnp.full((2, c.TP - c.T), -1, I32)
    rt = jnp.concatenate([rt_ref[...], pad], axis=1)
    start = jnp.zeros((1, 1), I32)
    lane = lax.broadcasted_iota(I32, (1, c.half), 1)
    numbers = jnp.zeros((1, c.half), I32)
    for e in range(c.E):
        in_first = rt[0:1, :] == e
        in_second = rt[1:2, :] == e
        number = jnp.sum(in_first.astype(I32) + in_second.astype(I32), axis=1, keepdims=True)
        slot_ref[e : e + 1, :] = jnp.where(in_first, a - start, jnp.where(in_second, b - start, -1))
        start = start + number
        numbers = numbers + jnp.where(lane == e, number, 0)
    for r in range(c.n):
        blocks_ref[r] = slot_ref[:, r * c.R : (r + 1) * c.R]
        rtb_ref[r] = jnp.concatenate([rt[:, r * c.R : (r + 1) * c.R]] * 4, axis=0)
    return numbers


def fill_hot(c, place, slot_ref, hot_ref, halves):
    for j in range(c.X):
        row = window_slot(c, slot_ref[pl.ds(expert_of(c, place, j), 1), :])
        for index, half in enumerate(halves):
            slots = lax.broadcasted_iota(I32, (c.SP, c.TP), 0) + half * c.SP
            hot_ref[index, j * c.SP : (j + 1) * c.SP, :] = (slots == row).astype(BF)


def route_body(c, place, *refs):
    row_ref, col_ref, rt_ref, src_ref, slot_ref, blocks_ref, rtb_ref, out_ref, hot_ref, sum_ref = refs

    @pl.when(pl.program_id(0) == 0)
    def _():
        numbers = count_places(c, row_ref, col_ref, rt_ref, slot_ref, blocks_ref, rtb_ref)
        sum_ref[0:1, :] = (numbers >> 4).astype(F32)
        sum_ref[1:2, :] = (numbers & 15).astype(F32)
        fill_hot(c, place, slot_ref, hot_ref, (0, 1))

    for half in range(2):
        acc = dot_nn(hot_ref[half, :, : c.T], src_ref[...])
        for j in range(c.X):
            at = (2 * j + half) * c.SP
            out_ref[at : at + c.SP, :] = acc[j * c.SP : (j + 1) * c.SP].astype(BF)
            if half == 0:

                @pl.when(pl.program_id(0) == 0)
                def _():
                    tile = acc[(j + 1) * c.SP - 16 : (j + 1) * c.SP]
                    tile = last_rows(c, tile, sum_ref[0:1, :], sum_ref[1:2, :])
                    out_ref[at + c.SP - 16 : at + c.SP, :] = tile.astype(BF)


def route(c, order, place, routes, priority, source):
    key = routes * c.key + priority
    row = routes.T * c.key + priority.T
    rt = routes.T
    outs = [
        shape_of((c.E, c.TP), I32),
        shape_of((c.n, c.E, c.R), I32),
        shape_of((c.n, 8, c.R), I32),
        shape_of((2 * c.X * c.SP, c.D), BF),
    ]
    result = call(
        order,
        functools.partial(route_body, c),
        place,
        [row, key, rt, source],
        [whole(row), whole(key), whole(rt)]
        + [pl.BlockSpec((c.T, c.half), lambda i, s: (0, i ^ s[2]))],
        outs,
        [whole(o) for o in outs[:3]] + [cols_of((2 * c.X * c.SP, c.half))],
        (2,),
        [pltpu.VMEM((2, c.X * c.SP, c.TP), BF), pltpu.VMEM((8, c.half), F32)],
        name="route",
    )
    return (*result[:3], result[3].reshape(c.X, 2 * c.SP, c.D))


def keep_body(c, place, tail_ref, slot_ref, rt_ref, mine_ref, keep_ref, lane_ref):
    earlier = jnp.zeros((1, 128), F32)
    for b in range(c.X):
        high, low = last_pair(c, tail_ref[b], 128)
        earlier = earlier + jnp.where(b < place[0], high * 16.0 + low, 0.0)
    wide = (c.E, 128)
    eye = lax.broadcasted_iota(I32, wide, 0) == lax.broadcasted_iota(I32, wide, 1)
    offset = jnp.sum(jnp.where(eye, earlier, 0.0), axis=1, keepdims=True).astype(I32)
    slot = slot_ref[0]
    kept = (slot >= 0) & (slot + offset < c.cap)
    slots = jnp.where(kept, window_slot(c, slot), -1)
    expert = lax.broadcasted_iota(I32, (c.E, 1), 0)
    for j in range(8):
        if j < c.X:
            here = jnp.where(expert == expert_of(c, place, j), slots, -1)
            mine_ref[0, j : j + 1, :] = jnp.max(here, axis=0, keepdims=True)
        else:
            mine_ref[0, j : j + 1, :] = jnp.full((1, c.R), -1, I32)
    rows = []
    for k in range(2):
        picked = jnp.where((rt_ref[0, k : k + 1, :] == expert) & kept, 1.0, 0.0)
        rows.append(jnp.sum(picked, axis=0, keepdims=True))
    keep_ref[0] = jnp.concatenate(rows * 4, axis=0)

    @pl.when(pl.program_id(0) == place[1])
    def _():
        lane_ref[...] = jnp.where(kept, 1.0, 0.0)


def keep_of(c, order, place, rows, blocks, rt):
    outs = [
        shape_of((c.n, 8, c.R), I32),
        shape_of((c.n, 8, c.R), F32),
        shape_of((c.E, c.R), F32),
    ]
    tail = pl.BlockSpec((c.X, 16, c.half), lambda i, s: (0, c.SP // 16 - 1, 0))
    return call(
        order,
        functools.partial(keep_body, c),
        place,
        [rows, blocks, rt],
        [tail, rows_of((1, c.E, c.R)), rows_of((1, 8, c.R))],
        outs,
        [rows_of((1, 8, c.R)), rows_of((1, 8, c.R)), whole(outs[2])],
        (c.n,),
        name="keep",
    )


def last_rows(c, tile, high, low):
    row = lax.broadcasted_iota(I32, (16, 1), 0)
    return jnp.where(row == 14, high, jnp.where(row == 15, low, tile))


def dispatch_body(c, half, place, slot_ref, src_ref, weight_ref, out_ref, hot_ref):
    @pl.when(pl.program_id(0) == 0)
    def _():
        fill_hot(c, place, slot_ref, hot_ref, (half,))

    acc = dot_nn(hot_ref[0], src_ref[...])
    out_ref[...] = acc.astype(BF)

    @pl.when(pl.program_id(0) == 0)
    def _():
        gates = dot_nn(hot_ref[0], weight_ref[...])
        lane = lax.broadcasted_iota(I32, (1, 128), 1)
        wide = (c.SP, c.half)
        eye = lax.broadcasted_iota(I32, wide, 0) == lax.broadcasted_iota(I32, wide, 1)
        for j in range(c.X):
            e = expert_of(c, place, j)
            mine = gates[j * c.SP : (j + 1) * c.SP]
            rows = []
            for at in (e, e + 64):
                col = jnp.sum(jnp.where(lane == at, mine, 0.0), axis=1, keepdims=True)
                rows.append(jnp.sum(jnp.where(eye, col, 0.0), axis=0, keepdims=True))
            end = (j + 1) * c.SP
            tile = last_rows(c, acc[end - 16 : end], rows[0], rows[1])
            out_ref[end - 16 : end, :] = tile.astype(BF)


def dispatch(c, order, place, slot, source, weight, half):
    return call(
        order,
        functools.partial(dispatch_body, c, half),
        place,
        [slot, source, weight],
        [whole(slot), pl.BlockSpec((c.TP, c.half), lambda i, s: (0, i ^ s[2])), whole(weight)],
        [shape_of((c.X * c.SP, c.D), BF)],
        [cols_of((c.X * c.SP, c.half))],
        (2,),
        [pltpu.VMEM((1, c.X * c.SP, c.TP), BF)],
        name="dispatch",
    )[0].reshape(c.X, c.SP, c.D)


def norm_rows(values):
    centred = values - jnp.mean(values, axis=-1, keepdims=True)
    inv_std = lax.rsqrt(jnp.mean(centred * centred, axis=-1, keepdims=True) + 1e-06)
    return centred * inv_std, inv_std


def norm_back(grad_norm, gain, normed, inv_std):
    scaled = grad_norm * gain
    return inv_std * (
        scaled
        - jnp.mean(scaled, axis=-1, keepdims=True)
        - normed * jnp.mean(scaled * normed, axis=-1, keepdims=True)
    )


def small_row(c, small_ref, index, count=1):
    return small_ref[index : index + count, :].astype(F32)


def own_cols(c, place):
    return pl.ds(pl.multiple_of(place[2] * c.half, c.half), c.half)


def other_cols(c, place):
    return pl.ds(pl.multiple_of((1 - place[2]) * c.half, c.half), c.half)


def live_rows(c, first, count):
    return (first + lax.broadcasted_iota(I32, (count, 1), 0)) < c.T


def qkv_body(c, place, tok_ref, small_ref, own_ref, oth_ref, hid_ref, qkv_ref, normed_ref, w_ref):
    @pl.when(pl.program_id(0) == 0)
    def _():
        for part in range(3):
            lanes = slice(part * c.W, (part + 1) * c.W)
            w_ref[own_cols(c, place), lanes] = own_ref[part]
            w_ref[other_cols(c, place), lanes] = oth_ref[part]

    live = live_rows(c, pl.program_id(0) * c.R, c.R)
    values = jnp.where(live, tok_ref[...].astype(F32), 0.0)
    normed, _ = norm_rows(values)
    hidden = normed * small_row(c, small_ref, 0) + small_row(c, small_ref, 2)
    normed_ref[...] = normed.astype(BF)
    hidden = jnp.where(live, hidden, 0.0).astype(BF)
    hid_ref[...] = hidden
    acc = dot_nn(hidden, w_ref[...])
    bias = small_row(c, small_ref, 5)
    zero = jnp.zeros((1, c.W), F32)
    shift = jnp.concatenate([bias[:, : c.W], zero, bias[:, c.half : c.half + c.W]], axis=1)
    qkv_ref[...] = (acc + shift).astype(BF)


def image_window(c):
    start = pl.program_id(0) * IMG_LEN
    low = pl.multiple_of(start // 16 * 16, 16)
    return low, start - low


def groups_of(c):
    lanes = min(128, c.W)
    return [(at, lanes) for at in range(0, c.W, lanes)]


def head_mask(lanes, head):
    lane = lax.broadcasted_iota(I32, (1, lanes), 1)
    return (lane >= head * HEAD) & (lane < (head + 1) * HEAD)


def stack_heads(c, values):
    heads = range(c.W // HEAD)
    return jnp.concatenate([jnp.where(head_mask(c.W, h), values, BF(0)) for h in heads], axis=0)


def pick_heads(c, values):
    total = None
    for h in range(c.W // HEAD):
        part = jnp.where(head_mask(c.W, h), values[h * c.win : (h + 1) * c.win], 0.0)
        total = part if total is None else total + part
    return total


def attend_body(c, place, qkv_ref, mix_ref):
    @pl.when(pl.program_id(0) == 0)
    def _():
        mix_ref[...] = jnp.zeros_like(mix_ref)

    low, off = image_window(c)
    row = lax.broadcasted_iota(I32, (c.win, 1), 0)
    col = lax.broadcasted_iota(I32, (1, c.win), 1)
    in_row = (row >= off) & (row < off + IMG_LEN)
    in_col = (col >= off) & (col < off + IMG_LEN)
    q = stack_heads(c, qkv_ref[pl.ds(low, c.win), : c.W] * BF(HEAD**-0.5))
    k = qkv_ref[pl.ds(low, c.win), c.W : 2 * c.W]
    v = qkv_ref[pl.ds(low, c.win), 2 * c.W :]
    scores = jnp.where(in_col, dot_nt(q, k), LOW)
    exps = jnp.exp(scores - jnp.max(scores, axis=-1, keepdims=True))
    probs = exps * (1.0 / jnp.sum(exps, axis=-1, keepdims=True))
    total = pick_heads(c, dot_nn(probs.astype(BF), v)).astype(BF)
    for group, (at, lanes) in enumerate(groups_of(c)):
        old = mix_ref[group, pl.ds(low, c.win), :]
        mix_ref[group, pl.ds(low, c.win), :] = jnp.where(in_row, total[:, at : at + lanes], old)


def attend_back_body(c, place, qkv_ref, *refs):
    pieces, (out_ref, sums_ref, grad_ref) = refs[: c.n], refs[c.n :]

    @pl.when(pl.program_id(0) == 0)
    def _():
        out_ref[...] = jnp.zeros_like(out_ref)
        sums_ref[...] = jnp.zeros_like(sums_ref)
        for k in range(c.n):
            at = pl.multiple_of((place[1] ^ k) * c.R, 16)
            grad_ref[pl.ds(at, c.R), :] = pieces[k][...]

    low, off = image_window(c)
    row = lax.broadcasted_iota(I32, (c.win, 1), 0)
    in_row = (row >= off) & (row < off + IMG_LEN)
    scale = HEAD**-0.5
    q = stack_heads(c, qkv_ref[pl.ds(low, c.win), : c.W] * BF(scale))
    k = qkv_ref[pl.ds(low, c.win), c.W : 2 * c.W]
    v = qkv_ref[pl.ds(low, c.win), 2 * c.W :]
    do = stack_heads(c, jnp.where(in_row, grad_ref[pl.ds(low, c.win), :], BF(0)))
    scores = jnp.where(in_row, dot_nt(k, q), LOW)
    exps = jnp.exp(scores - jnp.max(scores, axis=0, keepdims=True))
    soft = exps * (1.0 / jnp.sum(exps, axis=0, keepdims=True))
    dp = dot_nt(v, do)
    delta = jnp.sum(soft * dp, axis=0, keepdims=True)
    ds = (soft * (dp - delta)).astype(BF)
    dq = pick_heads(c, dot_tn(ds, k)) * scale
    dk = dot_nn(ds, q)
    dv = dot_nn(soft.astype(BF), do)
    for part, grad in enumerate((dq, dk, dv)):
        lanes = slice(part * c.W, (part + 1) * c.W)
        low_grad = jnp.where(in_row, grad, 0.0).astype(BF)
        old = out_ref[pl.ds(low, c.win), lanes]
        out_ref[pl.ds(low, c.win), lanes] = jnp.where(in_row, low_grad, old)
        sums_ref[0:1, lanes] += jnp.sum(low_grad.astype(F32), axis=0, keepdims=True)


def middle_body(c, place, *refs):
    refs = list(refs)
    groups = groups_of(c)
    count = c.n * len(groups)
    mixes, refs = refs[:count], refs[count:]
    w_ref, tok_ref, small_ref, table_ref, slot_ref = refs[:5]
    hid_ref, weight_ref, after_ref, probs_ref, proj_ref = refs[5:]
    step = pl.program_id(0)

    @pl.when(step == 0)
    def _():
        for k in range(c.n):
            for h in range(2):
                cols = slice(h * c.half, (h + 1) * c.half)
                proj_ref[k * c.W : (k + 1) * c.W, cols] = w_ref[(place[1] ^ k) * 2 + h]

    branch = dot_nn(jnp.concatenate([mix[...] for mix in mixes], axis=1), proj_ref[...])
    live = live_rows(c, step * c.R, c.R)
    tok = jnp.where(live, tok_ref[...].astype(F32), 0.0)
    after = tok + branch + small_row(c, small_ref, 4)
    normed, _ = norm_rows(after)
    hidden = (normed * small_row(c, small_ref, 1) + small_row(c, small_ref, 3)).astype(BF)
    hid_ref[...] = hidden
    router = table_ref[c.E : 2 * c.E, :]
    logits = dot_nt(router, hidden)
    exps = jnp.exp(logits - jnp.max(logits, axis=0, keepdims=True))
    probs = exps / jnp.sum(exps, axis=0, keepdims=True)
    weight = jnp.where(slot_ref[0] >= 0, probs, 0.0)
    high, rest = split_low(weight)
    lane = lax.broadcasted_iota(I32, (c.E, 128), 1)
    index = lax.broadcasted_iota(I32, (c.E, 128), 0)
    both = dot_tn(high, (lane == index).astype(BF)) + dot_tn(rest, (lane == index + 64).astype(BF))
    weight_ref[...] = both.astype(BF)
    @pl.when(step == place[1])
    def _():
        after_ref[...] = after
        probs_ref[...] = probs


def middle(c, order, place, mixes, proj, tokens, small, table, blocks):
    args = [pair[0] for pair in flat(mixes)] + [proj, tokens, small, table, blocks]
    specs = [
        pl.BlockSpec((None, c.R, a.shape[2]), lambda i, s, at=at: (at, i, 0))
        for a, at in flat(mixes)
    ]
    specs += [whole(proj), rows_of((c.R, c.D)), whole(small), whole(table)]
    specs += [rows_of((1, c.E, c.R))]
    outs = [
        shape_of((c.TP, c.D), BF),
        shape_of((c.TP, 128), BF),
        shape_of((c.R, c.D), F32),
        shape_of((c.E, c.R), F32),
    ]
    return call(
        order,
        functools.partial(middle_body, c),
        place,
        args,
        specs,
        outs,
        [rows_of((c.R, c.D)), rows_of((c.R, 128)), whole(outs[2]), whole(outs[3])],
        (c.n,),
        [pltpu.VMEM((c.D, c.D), BF)],
        name="middle",
    )


def fill_packs(c, place, tails, packs):
    lane = lax.broadcasted_iota(I32, (1, 128), 1)
    here = place[0] * EXP_DEV + place[3]
    state = [jnp.zeros((1, 1), F32)] * 3
    for j in range(c.X):
        high, low = last_pair(c, tails[j], 128)
        number = jnp.sum(jnp.where(lane == here, high * 16.0 + low, 0.0), axis=1, keepdims=True)
        kept = jnp.clip(c.cap - state[0], 0.0, number)
        first = jnp.minimum(kept, float(c.Q))
        sizes = first, kept - first
        for half in range(2):
            wide = (c.CR[half], c.SP)
            slot = lax.broadcasted_iota(I32, wide, 1)
            at = lax.broadcasted_iota(I32, wide, 0) - state[1 + half].astype(I32)
            hot = (at == slot) & (slot < sizes[half].astype(I32))
            packs[half][:, j * c.SP : (j + 1) * c.SP] = hot.astype(BF)
        state = [state[0] + number, state[1] + sizes[0], state[2] + sizes[1]]


def last_pair(c, tile, lanes):
    tile = tile[:, :lanes].astype(F32)
    return tile[14:15, :], tile[15:16, :]


def row_chunks(rows, size):
    return [slice(at, min(at + size, rows)) for at in range(0, rows, size)]


def grad_active_body(c, place, rows_ref, own_ref, oth_ref, *outs):
    gas, all_ref, packs = outs[:2], outs[2], outs[3:]

    @pl.when(pl.program_id(0) == 0)
    def _():
        tails = [rows_ref[j, c.SP - 16 : c.SP, :] for j in range(c.X)]
        fill_packs(c, place, tails, packs)
        for half, base in enumerate((0, c.CR[0])):
            rows = [rows_ref[j, half * c.SP : (half + 1) * c.SP, :] for j in range(c.X)]
            got = dot_nn(packs[half][...], jnp.concatenate(rows, axis=0))
            all_ref[base : base + c.CR[half], :] = got.astype(BF)

    weights = jnp.concatenate([own_ref[...], oth_ref[...]], axis=1)
    for half, base in enumerate((0, c.CR[0])):
        for at in row_chunks(c.CR[half], 320):
            values = all_ref[base + at.start : base + at.stop, :]
            gas[half][at, :] = dot_nt(values, weights).astype(BF)


def grad_active(c, order, place, rows, own_w, oth_w):
    outs = [shape_of((count, c.F), BF) for count in c.CR] + [shape_of((sum(c.CR), c.D), BF)]
    outs += [shape_of((count, c.X * c.SP), BF) for count in c.CR]
    return call(
        order,
        functools.partial(grad_active_body, c),
        place,
        [rows, own_w, oth_w],
        [whole(rows, 1)] + [rows_of((c.fblk, c.half))] * 2,
        outs,
        [cols_of((count, c.fblk)) for count in c.CR] + [whole(o) for o in outs[2:]],
        (c.F // c.fblk,),
        name="grad_active",
    )


def expert_body(c, half, place, *refs):
    rows_ref, pack_ref, own_ref, oth_ref, bias_ref, ga_ref = refs[:6]
    act_ref, gp_ref, gb_ref, all_ref, col_ref, back_ref = refs[6:12]
    acc_ref, dot_ref, row_ref, wide_ref = refs[12:]
    step = pl.program_id(0)

    @pl.when(step == 0)
    def _():
        acc_ref[...] = jnp.zeros_like(acc_ref)
        dot_ref[...] = jnp.zeros_like(dot_ref)
        all_ref[...] = dot_nn(pack_ref[...], rows_ref[...]).astype(BF)
        eye = lax.broadcasted_iota(I32, (c.SP, c.SP), 0) == lax.broadcasted_iota(I32, (c.SP, c.SP), 1)
        lane = lax.broadcasted_iota(I32, (1, 128), 1)
        for j in range(c.X):
            end = (j + 1) * c.SP
            high, low = last_pair(c, rows_ref[end - 16 : end, :], c.SP)
            high = jnp.sum(jnp.where(eye, high, 0.0), axis=1, keepdims=True)
            low = jnp.sum(jnp.where(eye, low, 0.0), axis=1, keepdims=True)
            both = jnp.where(lane == 0, high, jnp.where(lane == 1, low, 0.0))
            wide_ref[j * c.SP : end, :] = both.astype(BF)
        both = dot_nn(pack_ref[...], wide_ref[...])
        col_ref[...] = jnp.broadcast_to(both[:, 0:1] + both[:, 1:2], (c.CR[half], 128))

    bias = bias_ref[...]
    weights = jnp.concatenate([own_ref[...], oth_ref[...]], axis=0)
    summed = jnp.zeros((1, c.fblk), F32)
    lead = 0.7978845608028654
    cube = lead * 0.044715
    chunks = row_chunks(c.CR[half], 224)
    ahead = dot_nn(all_ref[chunks[0], :], weights)
    for i, rows_at in enumerate(chunks):
        pre = ahead + bias
        if i + 1 < len(chunks):
            ahead = dot_nn(all_ref[chunks[i + 1], :], weights)
        square = pre * pre
        turn = jnp.tanh(pre * (cube * square + lead))
        above = 1.0 + turn
        active = (0.5 * pre) * above
        slope = above * (1.0 + (1.0 - turn) * (pre * (3 * cube * square + lead)))
        ga = ga_ref[rows_at, :].astype(F32)
        product = active * ga
        part = product[:, 0:128]
        for lane in range(128, c.fblk, 128):
            part = part + product[:, lane : lane + 128]
        dot_ref[rows_at, :] += part
        grad = ga * slope * (0.5 * col_ref[rows_at, 0:1])
        act_ref[rows_at, :] = active.astype(BF)
        grad_low = grad.astype(BF)
        gp_ref[rows_at, :] = grad_low
        summed = summed + jnp.sum(grad, axis=0, keepdims=True)
        acc_ref[rows_at, :] += dot_nt(grad_low, weights)
    gb_ref[...] = jnp.broadcast_to(summed, (8, c.fblk))

    @pl.when(step == pl.num_programs(0) - 1)
    def _():
        ones = jnp.ones((8, 128), BF)
        row_ref[...] = jnp.zeros_like(row_ref)
        back_ref[...] = dot_tn(pack_ref[...], acc_ref[...].astype(BF)).astype(BF)
        a, rest = split_low(dot_ref[...])
        total = dot_nt(ones, a) + dot_nt(ones, rest)
        high, low = split_low(total)
        high = dot_nn(high, pack_ref[...])
        low = dot_nn(low, pack_ref[...])
        for j in range(c.X):
            end = (j + 1) * c.SP
            row_ref[0:8, : c.SP] = high[:, j * c.SP : end]
            row_ref[8:16, : c.SP] = low[:, j * c.SP : end]
            tile = back_ref[end - 16 : end, : c.half].astype(F32)
            tile = last_rows(c, tile, row_ref[0:1, :], row_ref[8:9, :])
            back_ref[end - 16 : end, : c.half] = tile.astype(BF)


def expert(c, order, place, half, rows, pack, own_w, oth_w, bias, ga):
    rows = rows.reshape(c.X * c.SP, c.D)
    args = [rows, pack, own_w, oth_w, bias, ga]
    count = c.CR[half]
    specs = [whole(rows, 1), whole(pack, 1)]
    specs += [cols_of((c.half, c.fblk))] * 2
    specs += [cols_of((1, c.fblk)), cols_of((count, c.fblk))]
    outs = [
        shape_of((count, c.F), BF),
        shape_of((count, c.F), BF),
        shape_of((8, c.F), F32),
    ]
    out_specs = [cols_of((count, c.fblk))] * 2 + [cols_of((8, c.fblk))]
    late = [shape_of((count, c.D), BF), shape_of((count, 128), F32)]
    late.append(shape_of((c.X * c.SP, c.D), BF))
    result = call(
        order,
        functools.partial(expert_body, c, half),
        place,
        args,
        specs,
        outs + late,
        out_specs + [whole(o, 1) for o in late],
        (c.F // c.fblk,),
        [
            pltpu.VMEM((count, c.D), F32),
            pltpu.VMEM((count, 128), F32),
            pltpu.VMEM((16, c.half), F32),
            pltpu.VMEM((c.X * c.SP, 128), BF),
        ],
        name="expert",
    )
    return (*result[:5], result[5].reshape(c.X, c.SP, c.D))


def produce_body(c, place, *refs):
    cols, acts, packs, own_ref, oth_ref, out_ref = refs[:2], refs[2:4], refs[4:6], *refs[6:9]
    accs = refs[9:]
    step = pl.program_id(0)

    @pl.when(step == 0)
    def _():
        for acc_ref in accs:
            acc_ref[...] = jnp.zeros_like(acc_ref)

    weights = jnp.concatenate([own_ref[...], oth_ref[...]], axis=1)
    for half in range(2):
        for at in row_chunks(c.CR[half], 320):
            accs[half][at, :] += dot_nn(acts[half][at, :], weights)

    @pl.when(step == pl.num_programs(0) - 1)
    def _():
        for half in range(2):
            values = (accs[half][...] * cols[half][:, 0:1]).astype(BF)
            values = dot_tn(packs[half][...], values).astype(BF)
            for j in range(c.X):
                rows = values[j * c.SP : (j + 1) * c.SP]
                out_ref[j, half * c.SP : (half + 1) * c.SP, :] = rows


def produce(c, order, place, cols, acts, packs, own_w, oth_w):
    out = shape_of((c.X, 2 * c.SP, c.D), BF)
    return call(
        order,
        functools.partial(produce_body, c),
        place,
        [*cols, *acts, *packs, own_w, oth_w],
        [whole(col) for col in cols]
        + [cols_of((rows, c.fblk)) for rows in c.CR]
        + [whole(pack) for pack in packs]
        + [rows_of((c.fblk, c.half))] * 2,
        [out],
        [whole(out, 1)],
        (c.F // c.fblk,),
        [pltpu.VMEM((rows, c.D), F32) for rows in c.CR],
        name="produce",
    )[0]


def grad_second_body(c, own, place, *refs):
    all_ref, cols, acts = refs[0], refs[1:3], refs[3:5]
    out_ref, row_ref = refs[-2:]

    @pl.when(pl.program_id(0) == 0)
    def _():
        for half, base in enumerate((0, c.CR[0])):
            rows_at = slice(base, base + c.CR[half])
            row_ref[rows_at, :] = (all_ref[rows_at, :].astype(F32) * cols[half][:, 0:1]).astype(BF)

    acc = dot_tn(acts[0][...], row_ref[: c.CR[0], :])
    acc = acc + dot_tn(acts[1][...], row_ref[c.CR[0] :, :])
    if own:
        acc = acc + refs[5][...].astype(F32)
    out_ref[...] = acc.astype(out_ref.dtype)


def grad_second(c, order, place, rows, cols, acts, add=None):
    own = add is not None
    args = [rows, *cols, *acts]
    total = sum(c.CR)
    specs = [pl.BlockSpec((total, c.half), lambda i, s: (0, 0 if own else 1))]
    specs += [whole(col) for col in cols] + [cols_of((count, c.fblk)) for count in c.CR]
    if own:
        args.append(add)
        specs.append(rows_of((c.fblk, c.half)))
    out = shape_of((c.F, c.half), F32 if own else BF)
    return call(
        order,
        functools.partial(grad_second_body, c, own),
        place,
        args,
        specs,
        [out],
        [rows_of((c.fblk, c.half))],
        (c.F // c.fblk,),
        [pltpu.VMEM((total, c.half), BF)],
        name="grad_second",
    )[0]


def grad_first_body(c, own, place, *refs):
    acc = dot_tn(refs[0][...], refs[2][...]) + dot_tn(refs[1][...], refs[3][...])
    if own:
        acc = acc + refs[4][...].astype(F32)
    refs[-1][...] = acc.astype(refs[-1].dtype)


def grad_first(c, order, place, rows, gps, add=None):
    own = add is not None
    args = [*rows, *gps]
    specs = [pl.BlockSpec((count, c.half), lambda i, s: (0, 0 if own else 1)) for count in c.CR]
    specs += [cols_of((count, c.fblk)) for count in c.CR]
    if own:
        args.append(add)
        specs.append(cols_of((c.half, c.fblk)))
    out = shape_of((c.half, c.F), F32 if own else BF)
    return call(
        order,
        functools.partial(grad_first_body, c, own),
        place,
        args,
        specs,
        [out],
        [cols_of((c.half, c.fblk))],
        (c.F // c.fblk,),
        name="grad_first",
    )[0]


def combine_body(c, with_dots, place, *refs):
    refs = list(refs)
    extra_ref = None if with_dots else refs.pop(0)
    halves = 2 if with_dots else 1
    rows, refs = refs[:halves], refs[halves:]
    tails = []
    if with_dots:
        tails, refs = refs[:2], refs[2:]
    mine_ref = refs.pop(0)
    groups = [(0, g) for g in groups_a(c)] + [(1, g) for g in groups_b(c)]
    outs, (hot_ref, row_ref) = refs[: len(groups)], refs[len(groups) :]
    pad = hot_ref.shape[1] // c.X

    @pl.when(pl.program_id(0) == 0)
    def _():
        row_ref[...] = jnp.zeros_like(row_ref)
        slots = lax.broadcasted_iota(I32, (c.R, pad), 1)
        for k in range(c.n):
            at = pl.multiple_of((place[1] ^ k) * c.R, 16)
            for j in range(c.X):
                hot = (mine_ref[pl.ds(at, c.R), j : j + 1] == slots).astype(BF)
                hot_ref[k * c.R : (k + 1) * c.R, j * pad : (j + 1) * pad] = hot
        if with_dots:
            wide = (c.SP, c.half)
            eye = lax.broadcasted_iota(I32, wide, 0) == lax.broadcasted_iota(I32, wide, 1)
            lane = lax.broadcasted_iota(I32, (1, 128), 1)
            for half in range(2):
                for j in range(c.X):
                    high, low = last_pair(c, tails[half][j], c.half)
                    high = jnp.sum(jnp.where(eye, high, 0.0), axis=1, keepdims=True)
                    low = jnp.sum(jnp.where(eye, low, 0.0), axis=1, keepdims=True)
                    e = expert_of(c, place, j)
                    cols = jnp.where(lane == e, high, jnp.where(lane == e + 64, low, 0.0))
                    at = j * pad + half * c.SP
                    row_ref[at : at + c.SP, :128] = cols.astype(BF)
            pulls = dot_nn(hot_ref[...], row_ref[:, :128]).astype(BF)
            expert = lax.broadcasted_iota(I32, (c.E, 128), 0)
            lane = lax.broadcasted_iota(I32, (c.E, 128), 1)
            pick = ((lane == expert) | (lane == expert + 64)).astype(BF)
            for (side, group), out_ref in zip(groups, outs):
                for at, k in enumerate(group):
                    if side == 0:
                        got = dot_nt(pick, pulls[k * c.R : (k + 1) * c.R])
                        out_ref[at, c.R :, :] = jnp.zeros((c.E, c.half), BF)
                        out_ref[at, c.R :, : c.R] = got.astype(BF)

    for half, rows_ref in enumerate(rows):
        size = rows_ref.shape[1]
        for j in range(c.X):
            at = j * pad + half * size
            row_ref[at : at + size, :] = rows_ref[j]
    result = dot_nn(hot_ref[...], row_ref[...]).astype(BF)
    for half in range(2):

        @pl.when(pl.program_id(0) == half)
        def _():
            for (side, group), out_ref in zip(groups, outs):
                if side == half:
                    for at, k in enumerate(group):
                        out_ref[at, : c.R, :] = result[k * c.R : (k + 1) * c.R]
                        if extra_ref is not None:
                            more = extra_ref.shape[1] // 2
                            out_ref[at, c.R :, :] = extra_ref[k, half * more : (half + 1) * more, :]


def combine(c, order, place, rows, mine, extra=None, cost=0):
    pad = up(2 * c.SP, 128)
    args = list(rows)
    specs = [pl.BlockSpec((c.X, r.shape[1], c.half), lambda i, s: (0, 0, i ^ s[2])) for r in rows]
    if extra is None:
        args += list(rows)
        specs += [pl.BlockSpec((c.X, 16, c.half), lambda i, s: (0, c.SP // 16 - 1, 0))] * 2
        outs = piece_outs(c, c.E)
    else:
        args.insert(0, extra)
        specs.insert(0, whole(extra))
        outs = piece_outs(c, extra.shape[1] // 2, extra.shape[1] // 2)
    args.append(mine)
    specs.append(whole(mine))
    result = call(
        order,
        functools.partial(combine_body, c, extra is None),
        place,
        args,
        specs,
        outs,
        [whole(o, 1) for o in outs],
        (2,),
        [pltpu.VMEM((c.n * c.R, c.X * pad), BF), pltpu.VMEM((c.X * pad, c.half), BF)],
        name="combine",
        cost=cost,
    )
    return list(result)


def back_two_body(c, place, *refs):
    refs = list(refs)
    groups = groups_of(c)
    heads, refs = refs[: c.n * len(groups)], refs[c.n * len(groups) :]
    count = (len(refs) - 13 - c.n) // 2
    a, b, refs = refs[:count], refs[count : 2 * count], refs[2 * count :]
    w_ref, after_ref, probs_ref, keep_ref = refs[:4]
    cot_ref, hid_ref, small_ref, table_ref, ga_ref, proj_own_ref, proj_oth_ref = refs[4:11]
    mixes, (gb_ref, sums_ref) = refs[11:-2], refs[-2:]
    sum_a = add_up(a)
    live = live_rows(c, place[1] * c.R, c.R)
    cot = jnp.where(live, cot_ref[...], BF(0))
    eshift = table_ref[: c.E, :]
    router = table_ref[c.E : 2 * c.E, :]
    kept = keep_ref[...] > 0
    pulls = jnp.where(kept, sum_a[c.R :, : c.R] + dot_nt(eshift, cot), 0.0)
    probs = probs_ref[...]
    glog = (probs * (pulls - jnp.sum(probs * pulls, axis=0, keepdims=True))).astype(BF)
    two = jnp.concatenate([sum_a[: c.R], add_up(b)], axis=1) + dot_tn(glog, router)
    normed, inv_std = norm_rows(after_ref[...])
    grad_after = cot.astype(F32) + norm_back(two, small_row(c, small_ref, 1), normed, inv_std)
    ga_ref[...] = grad_after
    low = grad_after.astype(BF)
    gb_ref[...] = low
    high, rest = split_low(probs * keep_ref[...])
    hid = jnp.where(live, hid_ref[...], BF(0))
    sums_ref[0:1, :] = jnp.sum(two * normed, axis=0, keepdims=True)
    sums_ref[1:2, :] = jnp.sum(two, axis=0, keepdims=True)
    sums_ref[2:3, :] = jnp.sum(low.astype(F32), axis=0, keepdims=True)
    sums_ref[3:8, :] = jnp.zeros((5, c.D), F32)
    sums_ref[8 : 8 + c.E, :] = dot_nn(high, cot) + dot_nn(rest, cot)
    sums_ref[8 + c.E : 8 + 2 * c.E, :] = dot_nn(glog, hid)
    for k in range(c.n):
        lane = place[1] ^ k
        mix = dot_nt(gb_ref[:, : c.half], w_ref[2 * lane])
        mix = mix + dot_nt(gb_ref[:, c.half :], w_ref[2 * lane + 1])
        mixes[k][...] = mix.astype(BF)
    height = sums_ref.shape[0]
    for cols, out_ref in ((own_cols(c, place), proj_own_ref), (other_cols(c, place), proj_oth_ref)):
        sums = sums_ref[:, cols].astype(BF)
        for k in range(c.n):
            for group, (at, lanes) in enumerate(groups):
                part = dot_tn(heads[k * len(groups) + group][...], gb_ref[:, cols])
                out_ref[k, at : at + lanes, :] = part.astype(BF)
            out_ref[k, c.W : c.W + height, :] = sums
            rest = out_ref.shape[1] - c.W - height
            out_ref[k, c.W + height :, :] = jnp.zeros((rest, c.half), BF)


def back_two(c, order, place, heads, sums, proj, lanes, cotangent, hidden, small, table):
    height = 8 + 2 * c.E
    rows = up(c.W + height, 32)
    args = [pair[0] for pair in flat(heads)]
    specs = [
        pl.BlockSpec((None, c.R, a.shape[2]), lambda i, s, at=at: (at, s[1], 0))
        for a, at in flat(heads)
    ]
    args += [*sums[0], *sums[1], proj, *lanes, cotangent, hidden, small, table]
    lane_rows = pl.BlockSpec((c.R, c.D), lambda i, s: (s[1], 0))
    specs += [first_block(a) for a in [*sums[0], *sums[1]]]
    specs += [whole(a) for a in [proj, *lanes]] + [lane_rows, lane_rows]
    specs += [whole(small), whole(table)]
    outs = [shape_of((c.R, c.D), F32)] + [shape_of((c.n, rows, c.half), BF)] * 2
    outs += [shape_of((c.R, c.W), BF) for _ in range(c.n)]
    result = call(
        order,
        functools.partial(back_two_body, c),
        place,
        args,
        specs,
        outs,
        [whole(o) for o in outs],
        (1,),
        [pltpu.VMEM((c.R, c.D), BF), pltpu.VMEM((height, c.D), F32)],
        name="back_two",
    )
    return (*result[:3], list(result[3:]))


def block_out_body(c, place, *refs):
    refs = list(refs)
    count = (len(refs) - 6) // 2
    a, b, refs = refs[:count], refs[count : 2 * count], refs[2 * count :]
    after_ref, probs_ref, keep_ref, table_ref, out_ref, proj_ref = refs
    high, low = split_low(probs_ref[...] * keep_ref[...])
    eshift = table_ref[: c.E, :]
    shift = dot_tn(high, eshift) + dot_tn(low, eshift)
    more = proj_ref.shape[0] // 2
    for h, pieces in enumerate((a, b)):
        cols = slice(h * c.half, (h + 1) * c.half)
        total = add_up([ref.at[: c.R, :] for ref in pieces])
        out_ref[h] = (after_ref[:, cols] + total + shift[:, cols]).astype(BF)
        proj_ref[h * more : (h + 1) * more, :] = same_sum(c, pieces, slice(c.R, c.R + more)).astype(BF)


def block_out(c, order, place, sums, after, probs, keep, table):
    args = [*sums[0], *sums[1], after, probs, keep, table]
    more = 2 * (sums[0][0].shape[1] - c.R)
    outs = [shape_of((2, c.R, c.half), BF), shape_of((more, c.half), BF)]
    return call(
        order,
        functools.partial(block_out_body, c),
        place,
        args,
        [first_block(a) for a in args[:-4]] + [whole(a) for a in args[-4:]],
        outs,
        [whole(o) for o in outs],
        (1,),
        name="block_out",
    )


def grad_one_body(c, place, dqkv_ref, normed_ref, own_ref, oth_ref, *outs):
    sums_ref = outs[-1]
    groups = [(0, g) for g in groups_a(c)] + [(1, g) for g in groups_b(c)]
    for side in range(2):
        cols = slice(side * c.half, (side + 1) * c.half)
        weights = [jnp.where(place[2] == side, own_ref[p], oth_ref[p]) for p in range(3)]
        gain = jnp.zeros((1, c.half), F32)
        shift = jnp.zeros((1, c.half), F32)
        for (where, group), out_ref in zip(groups, outs):
            if where != side:
                continue
            for row, k in enumerate(group):
                rows_at = pl.ds(pl.multiple_of((place[1] ^ k) * c.R, 16), c.R)
                acc = None
                for part in range(3):
                    rows = dqkv_ref[rows_at, part * c.W : (part + 1) * c.W]
                    term = dot_nt(rows, weights[part])
                    acc = term if acc is None else acc + term
                out_ref[row, : c.R, :] = acc.astype(BF)
                normed = normed_ref[rows_at, cols].astype(F32)
                gain = gain + jnp.sum(acc * normed, axis=0, keepdims=True)
                shift = shift + jnp.sum(acc, axis=0, keepdims=True)
        sums_ref[0:1, cols] = gain
        sums_ref[1:2, cols] = shift
        row = lax.broadcasted_iota(I32, (16, 1), 0)
        tile = jnp.where(row == 0, gain, jnp.where(row == 1, shift, 0.0)).astype(BF)
        for (where, group), out_ref in zip(groups, outs):
            if where == side:
                for at in range(len(group)):
                    out_ref[at, c.R :, :] = tile


def grad_one(c, order, place, dqkv, normed, own_w, oth_w):
    outs = piece_outs(c, 16, 16) + [shape_of((2, c.D), F32)]
    result = call(
        order,
        functools.partial(grad_one_body, c),
        place,
        [dqkv, normed, own_w, oth_w],
        [whole(dqkv), whole(normed), whole(own_w), whole(oth_w)],
        outs,
        [whole(o) for o in outs],
        (1,),
        name="grad_one",
    )
    return list(result[:-1]), result[-1]


def grad_qkv_body(c, place, hid_ref, dqkv_ref, own_ref, oth_ref):
    own_ref[0] = dot_tn(hid_ref[:, own_cols(c, place)], dqkv_ref[...]).astype(BF)
    oth_ref[0] = dot_tn(hid_ref[:, other_cols(c, place)], dqkv_ref[...]).astype(BF)


def grad_qkv(c, order, place, hidden, dqkv):
    specs = [whole(hidden, 1), cols_of((c.TP, c.W))]
    if c.W % 128:
        dqkv = dqkv.reshape(c.TP, 3, c.W).transpose(1, 0, 2)
        specs[1] = pl.BlockSpec((None, c.TP, c.W), lambda i, s: (i, 0, 0))
    return call(
        order,
        functools.partial(grad_qkv_body, c),
        place,
        [hidden, dqkv],
        specs,
        [shape_of((3, c.half, c.W), BF)] * 2,
        [rows_of((1, c.half, c.W))] * 2,
        (3,),
        name="grad_qkv",
    )


def back_one_body(c, place, *refs):
    refs = list(refs)
    count = (len(refs) - 4) // 2
    a, b, refs = refs[:count], refs[count : 2 * count], refs[2 * count :]
    tok_ref, after_ref, small_ref, out_ref = refs
    live = live_rows(c, place[1] * c.R, c.R)
    normed, inv_std = norm_rows(jnp.where(live, tok_ref[...].astype(F32), 0.0))
    one = jnp.concatenate([add_up(a)[: c.R], add_up(b)[: c.R]], axis=1)
    grad = after_ref[...] + norm_back(one, small_row(c, small_ref, 0), normed, inv_std)
    for h in range(2):
        out_ref[h] = grad[:, h * c.half : (h + 1) * c.half].astype(BF)


def back_one(c, order, place, sums, tokens, after, small):
    args = [*sums[0], *sums[1], tokens, after, small]
    lane_rows = pl.BlockSpec((c.R, c.D), lambda i, s: (s[1], 0))
    specs = [first_block(a) for a in args[:-3]] + [lane_rows, whole(after), whole(small)]
    out = shape_of((2, c.R, c.half), BF)
    return call(
        order,
        functools.partial(back_one_body, c),
        place,
        args,
        specs,
        [out],
        [whole(out)],
        (1,),
        name="back_one",
    )[0]


def assemble_body(c, place, *refs):
    pieces, out_ref = refs[:-1], refs[-1]
    for k in range(c.n):

        @pl.when((place[1] ^ k) == pl.program_id(0))
        def _():
            for h in range(2):
                values = pieces[2 * k + h][...].astype(out_ref.dtype)
                out_ref[:, h * c.half : (h + 1) * c.half] = values


def assemble(c, order, place, pieces, dtype):
    out = shape_of((c.T, c.D), dtype)
    return call(
        order,
        functools.partial(assemble_body, c),
        place,
        [pair[0] for pair in flat(pieces)],
        [
            pl.BlockSpec((None, c.R, c.half), lambda i, s, at=at: (at, 0, 0))
            for _, at in flat(pieces)
        ],
        [out],
        [rows_of((c.R, c.D))],
        (-(-c.T // c.R),),
        name="assemble",
    )[0]


def local(
    tokens,
    cotangent,
    w_qkv,
    qv_bias,
    w_proj,
    proj_bias,
    norm_gains,
    norm_shifts,
    w_router,
    expert_shift,
    w_first,
    w_second,
    first_bias,
    routes,
    priority,
):
    T, D = tokens.shape
    n = lax.axis_size("mp")
    E = w_router.shape[1]
    S = 16 * T // (5 * E)
    R = up(-(-T // n), 16)
    F = w_first.shape[2]
    W = w_proj.shape[0]
    win = up(IMG_LEN + 15, 16)
    Q = (S + 1) // 2
    cap = (9 * T + 4 * EXP_DEV - 1) // (4 * EXP_DEV)
    X = E // EXP_DEV
    full = min(cap // S, X)
    c = Sizes(
        T=T,
        D=D,
        half=D // 2,
        n=n,
        X=X,
        E=E,
        S=S,
        Q=Q,
        SP=up(Q + 2, 16),
        CR=(up(min(cap, X * Q), 16), up(full * (S - Q) + max(0, cap - full * S - Q), 16)),
        R=R,
        TP=n * R,
        W=W,
        images=T // IMG_LEN,
        quarters=n // EXP_DEV,
        F=F,
        cap=cap,
        win=win,
        fblk=min(1024, F),
        key=4 * T,
    )
    order = Order()
    dp, mp, grid = lax.axis_index("dp"), lax.axis_index("mp"), lax.axis_index("grid")
    place = jnp.stack([dp, mp, grid, mp // c.quarters]).astype(I32)

    slot, blocks, rt, grad_out = route(c, order, place, routes, priority, cotangent)
    grad_in = trade(grad_out, "dp")

    def both_halves(rows):
        rows = jnp.pad(rows, ((0, up(rows.shape[0], 16) - rows.shape[0]), (0, 0)))
        other = swap_grid(rows)
        return jnp.where(
            grid == 0,
            jnp.concatenate([rows, other], axis=1),
            jnp.concatenate([other, rows], axis=1),
        )

    wide_bias = jnp.pad(qv_bias, ((0, 0), (0, c.half - W)))
    small = both_halves(
        jnp.concatenate([norm_gains, norm_shifts, proj_bias[None], wide_bias], axis=0)
    )
    qkv_own = w_qkv.transpose(1, 0, 2)
    qkv_oth = swap_grid(qkv_own)

    first_own = w_first[0]
    second_own = w_second[0]
    proj = lax.all_gather(w_proj, ("mp", "grid"))

    outs = [shape_of((c.TP, D), BF), shape_of((c.TP, 3 * W), BF), shape_of((c.TP, D), BF)]
    hidden_one, qkv, normed_one = call(
        order,
        functools.partial(qkv_body, c),
        place,
        [tokens, small, qkv_own, qkv_oth],
        [rows_of((c.R, D)), whole(small), whole(qkv_own), whole(qkv_oth)],
        outs,
        [rows_of((c.R, D)), rows_of((c.R, 3 * W)), rows_of((c.R, D))],
        (n,),
        [pltpu.VMEM((D, 3 * W), BF)],
        name="qkv",
    )
    bias_rows = F // 2 // c.half
    tied = held(jnp.concatenate([expert_shift, w_router.T]), qkv)
    table = both_halves(tied)
    bias = both_halves(held(first_bias.reshape(bias_rows, c.half), qkv))[:bias_rows]
    bias = bias.reshape(bias_rows, 2, c.half).transpose(1, 0, 2).reshape(1, F).astype(F32)
    order.tie(proj)
    second_oth = swap_grid(held(second_own, qkv))
    first_oth = swap_grid(held(first_own, qkv))
    groups = groups_of(c)
    out = shape_of((len(groups), c.TP, groups[0][1]), BF)
    mix = call(
        order,
        functools.partial(attend_body, c),
        place,
        [qkv],
        [whole(qkv)],
        [out],
        [whole(out)],
        (c.images,),
        name="attend",
    )[0]
    mixes, _ = gather_mp(c, mix)
    hidden_two, weight, after, probs = middle(
        c, order, place, mixes, proj, tokens, small, table, blocks
    )

    rows_a = trade(dispatch(c, order, place, slot, hidden_two, weight, 0), "dp")
    rows_b = dispatch(c, order, place, slot, hidden_two, weight, 1)
    ga_a, ga_b, grad_all, pack_a, pack_b = grad_active(
        c, order, place, grad_in, second_own, second_oth
    )
    mine, keep, keep_lane = keep_of(c, order, place, grad_in, blocks, rt)
    keep_mask = keep[:, :2, :].transpose(0, 2, 1).reshape(c.TP, 2)[:T].astype(I32)
    mine = mine.transpose(0, 2, 1).reshape(c.TP, 8)
    rows_b = trade(held(rows_b, rows_a, grad_all), "dp")
    act_a, gp_a, gb_a, all_a, col_a, back_a = expert(
        c, order, place, 0, rows_a, pack_a, first_own, first_oth, bias, ga_a
    )
    back_a = trade(held(back_a, rows_b), "dp")
    act_b, gp_b, gb_b, all_b, col_b, back_b = expert(
        c, order, place, 1, rows_b, pack_b, first_own, first_oth, bias, ga_b
    )
    back_b = trade(held(back_b, back_a), "dp")
    cols, acts, gps, alls = [col_a, col_b], [act_a, act_b], [gp_a, gp_b], [all_a, all_b]
    second_part = swap_grid(grad_second(c, order, place, grad_all, cols, acts))
    order.tie(back_a)
    first_part = swap_grid(grad_first(c, order, place, alls, gps))
    packs = [pack_a, pack_b]
    prod = produce(c, order, place, cols, acts, packs, second_own, second_oth)
    gb = (gb_a + gb_b)[0:1].reshape(2, F // 2)
    gb_own = lax.dynamic_index_in_dim(gb, grid, 0, True)
    gb_oth = lax.dynamic_index_in_dim(gb, 1 - grid, 0, True)
    grad_fbias = gb_own + swap_grid(gb_oth)

    pieces = combine(c, order, place, [back_a, back_b], mine)
    prod = trade(held(prod, back_b), "dp")
    two_sums = reduce_start(c, pieces)
    grad_second_out = grad_second(c, order, place, grad_all, cols, acts, second_part)
    two_sums = reduce_end(c, order, two_sums)
    grad_first_out = grad_first(c, order, place, alls, gps, first_part)
    grad_after, proj_a, proj_b, grad_mix = back_two(
        c,
        order,
        place,
        mixes,
        two_sums,
        proj,
        [after, probs, keep_lane],
        cotangent,
        hidden_two,
        small,
        table,
    )
    grad_mix = [grad_mix[0]] + [swap_mp(c, grad_mix[k], k) for k in range(1, n)]
    proj_low = (proj_a.astype(F32) + swap_grid(proj_b).astype(F32)).astype(BF)
    pieces = combine(c, order, place, [prod], mine, proj_low, cost=10)
    out_sums = reduce_start(c, [held(p, *grad_mix) for p in pieces])

    outs = [shape_of((c.TP, 3 * W), BF), shape_of((8, 3 * W), F32)]
    dqkv, dqkv_sums = call(
        order,
        functools.partial(attend_back_body, c),
        place,
        [qkv, *grad_mix],
        [whole(qkv)] + [whole(p) for p in grad_mix],
        outs,
        [whole(o) for o in outs],
        (c.images,),
        [pltpu.VMEM((c.TP, W), BF)],
        name="attend_back",
    )
    one_pieces, one_parts = grad_one(c, order, place, dqkv, normed_one, qkv_own, qkv_oth)
    one_sums = reduce_start(c, one_pieces)
    out_sums = reduce_end(c, order, out_sums)
    qkv_a, qkv_b = grad_qkv(c, order, place, hidden_one, dqkv)
    one_sums = reduce_end(c, order, one_sums)
    out_lane, proj_sum = block_out(c, order, place, out_sums, after, probs, keep_lane, table)

    qkv_b = swap_grid(qkv_b)
    qkv_low = (qkv_a.astype(F32) + qkv_b.astype(F32)).astype(BF)
    proj_end = 3 * W + proj_sum.shape[0]
    shared = jnp.concatenate([qkv_low.reshape(-1, c.half), proj_sum], axis=0)
    shared = jnp.pad(shared, ((0, up(shared.shape[0], 16 * c.X) - shared.shape[0]), (0, 0)))
    shared = sum_dp_start(c, shared)
    grad_low = back_one(c, order, place, one_sums, tokens, grad_after, small)
    qv_rows = jnp.concatenate([dqkv_sums[0:1, :W], dqkv_sums[0:1, 2 * W :]], axis=0)
    sums_one = held(first_sums(c, one_sums, one_parts), grad_low)
    sums_one = chip_sums(c, sums_one, qv_rows, grid)
    sums_one = fold(c, sums_one, (("dp", c.X),))
    grad_low, out_lane, one = gather_both(c, grad_low, out_lane, (sums_one,))
    shared = sum_dp_end(c, sum_dp_turn(c, held(shared, one)))
    grad_w_qkv = shared[: 3 * W].reshape(3, c.half, W)
    rest = shared[4 * W : 4 * W + 8 + 2 * E]
    grad_tokens = assemble(c, order, place, grad_low, F32)
    block = assemble(c, order, place, out_lane, BF)
    return (
        block,
        grad_tokens,
        grad_w_qkv.transpose(1, 0, 2),
        sums_one[2:3, :W],
        shared[3 * W : 4 * W],
        rest[2],
        jnp.stack([sums_one[0], rest[0]]),
        jnp.stack([sums_one[1], rest[1]]),
        rest[8 + E : 8 + 2 * E].T,
        rest[8 : 8 + E],
        grad_first_out[None],
        grad_second_out[None],
        grad_fbias,
        keep_mask,
    )


def solution(mesh):
    return jax.shard_map(
        local,
        mesh=mesh,
        in_specs=(
            P(("dp", "grid"), None),
            P(("dp", "grid"), None),
            P("grid", None, "mp"),
            P("grid", "mp"),
            P("mp", "grid"),
            P("grid"),
            P(None, "grid"),
            P(None, "grid"),
            P("grid", None),
            P(None, "grid"),
            P(("dp", "mp"), "grid", None),
            P(("dp", "mp"), None, "grid"),
            P(("dp", "mp"), "grid"),
            P(("dp", "grid"), None),
            P(("dp", "grid"), None),
        ),
        out_specs=(
            P(("dp", "grid"), None),
            P(("dp", "grid"), None),
            P("grid", None, "mp"),
            P("grid", "mp"),
            P("mp", "grid"),
            P("grid"),
            P(None, "grid"),
            P(None, "grid"),
            P("grid", None),
            P(None, "grid"),
            P(("dp", "mp"), "grid", None),
            P(("dp", "mp"), None, "grid"),
            P(("dp", "mp"), "grid"),
            P(("dp", "grid"), None),
        ),
        check_vma=False,
    )
```

```python
import functools
from typing import NamedTuple

import jax
import jax.numpy as jnp
from jax import lax
from jax.experimental import pallas as pl
from jax.experimental.pallas import tpu as pltpu
from jax.sharding import PartitionSpec as P

HEAD = 64
IMG_LEN = 197
EXP_DEV = 4
BF = jnp.bfloat16
F32 = jnp.float32
I32 = jnp.int32
VMEM_BYTES = 56 * 1024 * 1024
LOW = -1e30


class Sizes(NamedTuple):
    T: int
    D: int
    half: int
    n: int
    X: int
    E: int
    S: int
    Q: int
    SP: int
    CR: tuple
    R: int
    TP: int
    W: int
    images: int
    quarters: int
    F: int
    cap: int
    win: int
    fblk: int


class Order:
    def __init__(self):
        self.after = []

    def tie(self, value):
        self.after.append(value)

    def hold(self, *values):
        return lax.optimization_barrier((*values, *self.after))[: len(values)]


def up(value, step):
    return -(-value // step) * step


def dot_nn(a, b):
    return jnp.dot(a, b, preferred_element_type=F32)


def dot_nt(a, b):
    return lax.dot_general(a, b, (((1,), (1,)), ((), ())), preferred_element_type=F32)


def dot_tn(a, b):
    return lax.dot_general(a, b, (((0,), (0,)), ((), ())), preferred_element_type=F32)


def split_low(values):
    high = values.astype(BF)
    return high, (values - high.astype(F32)).astype(BF)


def shape_of(dims, dtype):
    return jax.ShapeDtypeStruct(dims, dtype)


def whole(array, buffers=None):
    dims = tuple(array.shape)
    extra = {} if buffers is None else {"pipeline_mode": pl.Buffered(buffers)}
    return pl.BlockSpec(dims, lambda i, s: (0,) * len(dims), **extra)


def rows_of(dims):
    return pl.BlockSpec(dims, lambda i, s: (i,) + (0,) * (len(dims) - 1))


def cols_of(dims):
    return pl.BlockSpec(dims, lambda i, s: (0,) * (len(dims) - 1) + (i,))


def call(order, body, place, args, specs, outs, out_specs, grid, scratch=(), name=None, cost=0):
    extra = order.after
    count = len(args)

    def wrapped(place, *refs):
        body(place, *refs[:count], *refs[count + len(extra) :])

    result = pl.pallas_call(
        wrapped,
        grid_spec=pltpu.PrefetchScalarGridSpec(
            num_scalar_prefetch=1,
            grid=grid,
            in_specs=list(specs) + [pl.BlockSpec(memory_space=pl.ANY)] * len(extra),
            out_specs=list(out_specs),
            scratch_shapes=list(scratch),
        ),
        out_shape=list(outs),
        compiler_params=pltpu.CompilerParams(
            dimension_semantics=("arbitrary",) * len(grid), vmem_limit_bytes=VMEM_BYTES
        ),
        cost_estimate=pl.CostEstimate(
            flops=1000 + int(1.1e9 * cost), bytes_accessed=1000, transcendentals=0
        ),
        name=name,
    )(place, *args, *extra)
    order.after = [min(result, key=lambda o: o.size)]
    return result


def swap_mp(c, value, mask):
    return lax.ppermute(value, "mp", [(i, i ^ mask) for i in range(c.n)])


def swap_grid(value):
    return lax.ppermute(value, "grid", [(0, 1), (1, 0)])


def held(value, *others):
    return lax.optimization_barrier((value, *others))[0]


def trade(value, axis):
    return lax.all_to_all(value, axis, split_axis=0, concat_axis=0, tiled=True)


def groups_a(c):
    return [[0, 2], [1, 3]] if c.n == 4 else [[k] for k in range(c.n)]


def groups_b(c):
    return [[0, 1], [2, 3]] if c.n == 4 else [[k] for k in range(c.n)]


def reduce_start(c, arrays):
    a, b = arrays[: len(arrays) // 2], arrays[len(arrays) // 2 :]
    if c.n != 4:
        return [[x[0]] + [swap_mp(c, x[k], k) for k in range(1, c.n)] for x in (a, b)]
    return [[a[0], swap_mp(c, a[1], 1)], [b[0], swap_mp(c, b[1], 2)]]


def reduce_end(c, order, state):
    if c.n != 4:
        return state
    (a, ra), (b, rb) = state
    ra, rb = order.hold(ra, rb)
    ta = (a[1:].astype(F32) + ra[1:].astype(F32)).astype(BF)
    tb = (b[1:].astype(F32) + rb[1:].astype(F32)).astype(BF)
    order.tie(ta)
    order.tie(tb)
    return [[a, ra, swap_mp(c, ta, 2)], [b, rb, swap_mp(c, tb, 1)]]


def piece_outs(c, more_a=0, more_b=0):
    outs = [shape_of((len(g), c.R + more_a, c.half), BF) for g in groups_a(c)]
    return outs + [shape_of((len(g), c.R + more_b, c.half), BF) for g in groups_b(c)]


def first_block(array):
    dims = tuple(array.shape)
    return pl.BlockSpec((None,) + dims[1:], lambda i, s: (0, 0, 0))


def same_sum(c, refs, rows):
    parts = [ref[rows, :].astype(F32) for ref in refs]
    if c.n == 4:
        return (parts[0] + parts[1]).astype(BF).astype(F32) + parts[2]
    while len(parts) > 1:
        parts = [parts[i] + parts[i + 1] for i in range(0, len(parts), 2)]
    return parts[0]


def add_up(refs):
    total = refs[0][...].astype(F32)
    for ref in refs[1:]:
        total = total + ref[...].astype(F32)
    return total


def sum_dp_start(c, value):
    return trade(value.reshape((c.X, value.shape[0] // c.X) + value.shape[1:]), "dp")


def sum_dp_turn(c, parts):
    total = jnp.sum(parts.astype(F32), axis=0).astype(BF)
    return jnp.broadcast_to(total[None], (c.X,) + total.shape)


def sum_dp_end(c, spread):
    return trade(spread, "dp").reshape((-1,) + spread.shape[2:]).astype(F32)


def gather_mp(c, value, until=None):
    if c.n != 4 or value.shape[0] != 2:
        parts = [value] + [swap_mp(c, value, k) for k in range(1, c.n)]
        return [[(p, h) for h in range(value.shape[0])] for p in parts], parts[1:]
    one = swap_mp(c, value, 1)
    two = swap_mp(c, value, 2)
    ends = one[0:1], two[1:2]
    if until is not None:
        ends = held(ends[0], *until), held(ends[1], *until)
    far_a = swap_mp(c, ends[0], 2)
    far_b = swap_mp(c, ends[1], 1)
    near = [[(p, 0), (p, 1)] for p in (value, one, two)]
    return near + [[(far_a, 0), (far_b, 0)]], [one, two]


def gather_both(c, first, second, filler):
    if c.n != 4:
        filled, _ = filler([first])
        return gather_mp(c, first)[0], gather_mp(c, second)[0], (first,), filled
    one, two = swap_mp(c, first, 1), swap_mp(c, first, 2)
    near = jnp.concatenate([one[0:1], second]), jnp.concatenate([two[1:2], second])
    by_two, by_one = [swap_mp(c, x, mask) for x, mask in zip(near, (2, 1))]
    filled, hold = filler(near)
    by_two, by_one = hold(by_two, by_one)
    far_a, far_b = swap_mp(c, by_one[1:2], 2), swap_mp(c, by_two[2:3], 1)
    pieces = [[(p, 0), (p, 1)] for p in (first, one, two)] + [[(by_two, 0), (by_one, 0)]]
    others = [[(second, 0), (second, 1)], [(by_one, 1), (by_one, 2)], [(by_two, 1), (by_two, 2)]]
    return pieces, others + [[(far_a, 0), (far_b, 0)]], (by_one, by_two), filled


def flat(pieces):
    return [pair for piece in pieces for pair in piece]


def fold(c, value, axes):
    for axis, size in axes:
        mask = 1
        while mask < size:
            value = value + lax.ppermute(value, axis, [(i, i ^ mask) for i in range(size)])
            mask *= 2
    return value


def first_sums(c, sums, one_parts):
    if c.n != 4:
        return fold(c, one_parts, (("mp", c.n),))
    halves = []
    for a, b, far in sums:
        pair = (a[0, c.R : c.R + 2].astype(F32) + b[0, c.R : c.R + 2].astype(F32)).astype(BF)
        halves.append(pair.astype(F32) + far[0, c.R : c.R + 2].astype(F32))
    return jnp.concatenate(halves, axis=1)


def chip_sums(c, one, parts, grid):
    def half_of(side):
        cols = lax.dynamic_slice_in_dim(one, side * c.half, c.half, 1)
        row = lax.dynamic_index_in_dim(parts, side, 0, True)
        return jnp.concatenate([cols, jnp.pad(row, ((0, 0), (0, c.half - c.W)))], axis=0)

    return half_of(grid) + swap_grid(half_of(1 - grid))


def expert_of(c, place, j):
    return j * EXP_DEV + place[3]


def window_slot(c, slot):
    return jnp.where(slot < c.Q, slot, slot + (c.SP - c.Q))


def count_places(c, rank_ref, rt_ref, slot_ref, blocks_ref, rtb_ref):
    pad = jnp.full((2, c.TP - c.T), -1, I32)
    rank = jnp.concatenate([rank_ref[...], pad], axis=1)
    rt = jnp.concatenate([rt_ref[...], pad], axis=1)
    side = 64
    index = lax.broadcasted_iota(I32, (side, c.TP), 0)
    rows = [(index == (rank[k : k + 1] >> 6)).astype(BF) for k in range(2)]
    cols = [index == (rank[k : k + 1] & 63) for k in range(2)]
    table = jnp.zeros((side, side), F32)
    for k in range(2):
        named = (rt[k : k + 1] + 1).astype(F32)
        table = table + dot_nt(rows[k], jnp.where(cols[k], named, 0.0).astype(BF))
    up_to = lax.broadcasted_iota(I32, (side, side), 0) < lax.broadcasted_iota(I32, (side, side), 1)
    above = lax.broadcasted_iota(I32, (side, side), 0) > lax.broadcasted_iota(I32, (side, side), 1)
    lane = lax.broadcasted_iota(I32, (1, 128), 1)
    named = [(table == e + 1.0).astype(F32) for e in range(c.E)]
    along = dot_nn(jnp.concatenate(named, axis=0).astype(BF), up_to.astype(BF))
    numbers = jnp.zeros((side, 128), F32)
    for e in range(c.E):
        numbers = numbers + jnp.where(lane == e, jnp.sum(named[e], axis=1, keepdims=True), 0.0)
    down = dot_nn(above.astype(BF), numbers.astype(BF))
    place_of = jnp.zeros((side, side), F32)
    for e in range(c.E):
        here = along[e * side : (e + 1) * side] + down[:, e : e + 1]
        place_of = place_of + named[e] * here
    place_of = place_of.astype(I32)
    high = (place_of >> 4).astype(F32).astype(BF)
    low = (place_of & 15).astype(F32).astype(BF)
    places = []
    for k in range(2):
        values = dot_tn(high, rows[k]) * 16.0 + dot_tn(low, rows[k])
        places.append(jnp.sum(jnp.where(cols[k], values, 0.0), axis=0, keepdims=True).astype(I32))
    for e in range(c.E):
        second = jnp.where(rt[1:2, :] == e, places[1], -1)
        slot_ref[e : e + 1, :] = jnp.where(rt[0:1, :] == e, places[0], second)
    for r in range(c.n):
        blocks_ref[r] = slot_ref[:, r * c.R : (r + 1) * c.R]
        rtb_ref[r] = jnp.concatenate([rt[:, r * c.R : (r + 1) * c.R]] * 4, axis=0)
    numbers = jnp.sum(numbers, axis=0, keepdims=True)
    return jnp.concatenate([numbers, jnp.zeros((1, c.half - 128), F32)], axis=1).astype(I32)


def fill_hot(c, place, slot_ref, hot_ref, halves):
    for j in range(c.X):
        row = window_slot(c, slot_ref[pl.ds(expert_of(c, place, j), 1), :])
        for index, half in enumerate(halves):
            slots = lax.broadcasted_iota(I32, (c.SP, c.TP), 0) + half * c.SP
            hot_ref[index, j * c.SP : (j + 1) * c.SP, :] = (slots == row).astype(BF)


def route_body(c, place, *refs):
    rank_ref, rt_ref, src_ref, slot_ref, blocks_ref, rtb_ref, out_ref, hot_ref, sum_ref = refs

    @pl.when(pl.program_id(0) == 0)
    def _():
        numbers = count_places(c, rank_ref, rt_ref, slot_ref, blocks_ref, rtb_ref)
        sum_ref[0:1, :] = (numbers >> 4).astype(F32)
        sum_ref[1:2, :] = (numbers & 15).astype(F32)
        fill_hot(c, place, slot_ref, hot_ref, (0, 1))

    for half in range(2):
        acc = dot_nn(hot_ref[half, :, : c.T], src_ref[...])
        for j in range(c.X):
            at = (2 * j + half) * c.SP
            out_ref[at : at + c.SP, :] = acc[j * c.SP : (j + 1) * c.SP].astype(BF)
            if half == 0:

                @pl.when(pl.program_id(0) == 0)
                def _():
                    tile = acc[(j + 1) * c.SP - 16 : (j + 1) * c.SP]
                    tile = last_rows(c, tile, sum_ref[0:1, :], sum_ref[1:2, :])
                    out_ref[at + c.SP - 16 : at + c.SP, :] = tile.astype(BF)


def route(c, order, place, routes, priority, source):
    rank = priority.T
    rt = routes.T
    outs = [
        shape_of((c.E, c.TP), I32),
        shape_of((c.n, c.E, c.R), I32),
        shape_of((c.n, 8, c.R), I32),
        shape_of((2 * c.X * c.SP, c.D), BF),
    ]
    result = call(
        order,
        functools.partial(route_body, c),
        place,
        [rank, rt, source],
        [whole(rank), whole(rt)]
        + [pl.BlockSpec((c.T, c.half), lambda i, s: (0, i ^ s[2]))],
        outs,
        [whole(o) for o in outs[:3]] + [cols_of((2 * c.X * c.SP, c.half))],
        (2,),
        [pltpu.VMEM((2, c.X * c.SP, c.TP), BF), pltpu.VMEM((8, c.half), F32)],
        name="route",
    )
    return (*result[:3], result[3].reshape(c.X, 2 * c.SP, c.D))


def keep_body(c, place, tail_ref, slot_ref, rt_ref, mine_ref, keep_ref, lane_ref):
    earlier = jnp.zeros((1, 128), F32)
    for b in range(c.X):
        high, low = last_pair(c, tail_ref[b], 128)
        earlier = earlier + jnp.where(b < place[0], high * 16.0 + low, 0.0)
    wide = (c.E, 128)
    eye = lax.broadcasted_iota(I32, wide, 0) == lax.broadcasted_iota(I32, wide, 1)
    offset = jnp.sum(jnp.where(eye, earlier, 0.0), axis=1, keepdims=True).astype(I32)
    slot = slot_ref[0]
    kept = (slot >= 0) & (slot + offset < c.cap)
    slots = jnp.where(kept, window_slot(c, slot), -1)
    expert = lax.broadcasted_iota(I32, (c.E, 1), 0)
    for j in range(8):
        if j < c.X:
            here = jnp.where(expert == expert_of(c, place, j), slots, -1)
            mine_ref[0, j : j + 1, :] = jnp.max(here, axis=0, keepdims=True)
        else:
            mine_ref[0, j : j + 1, :] = jnp.full((1, c.R), -1, I32)
    rows = []
    for k in range(2):
        picked = jnp.where((rt_ref[0, k : k + 1, :] == expert) & kept, 1.0, 0.0)
        rows.append(jnp.sum(picked, axis=0, keepdims=True))
    keep_ref[0] = jnp.concatenate(rows * 4, axis=0)

    @pl.when(pl.program_id(0) == place[1])
    def _():
        lane_ref[...] = jnp.where(kept, 1.0, 0.0)


def keep_of(c, order, place, rows, blocks, rt):
    outs = [
        shape_of((c.n, 8, c.R), I32),
        shape_of((c.n, 8, c.R), F32),
        shape_of((c.E, c.R), F32),
    ]
    tail = pl.BlockSpec((c.X, 16, c.half), lambda i, s: (0, c.SP // 16 - 1, 0))
    return call(
        order,
        functools.partial(keep_body, c),
        place,
        [rows, blocks, rt],
        [tail, rows_of((1, c.E, c.R)), rows_of((1, 8, c.R))],
        outs,
        [rows_of((1, 8, c.R)), rows_of((1, 8, c.R)), whole(outs[2])],
        (c.n,),
        name="keep",
    )


def last_rows(c, tile, high, low):
    row = lax.broadcasted_iota(I32, (16, 1), 0)
    return jnp.where(row == 14, high, jnp.where(row == 15, low, tile))


def dispatch_body(c, half, place, slot_ref, src_ref, weight_ref, out_ref, hot_ref):
    @pl.when(pl.program_id(0) == 0)
    def _():
        fill_hot(c, place, slot_ref, hot_ref, (half,))

    acc = dot_nn(hot_ref[0], src_ref[...])
    out_ref[...] = acc.astype(BF)

    @pl.when(pl.program_id(0) == 0)
    def _():
        gates = dot_nn(hot_ref[0], weight_ref[...])
        lane = lax.broadcasted_iota(I32, (1, 128), 1)
        wide = (c.SP, c.half)
        eye = lax.broadcasted_iota(I32, wide, 0) == lax.broadcasted_iota(I32, wide, 1)
        for j in range(c.X):
            e = expert_of(c, place, j)
            mine = gates[j * c.SP : (j + 1) * c.SP]
            rows = []
            for at in (e, e + 64):
                col = jnp.sum(jnp.where(lane == at, mine, 0.0), axis=1, keepdims=True)
                rows.append(jnp.sum(jnp.where(eye, col, 0.0), axis=0, keepdims=True))
            end = (j + 1) * c.SP
            tile = last_rows(c, acc[end - 16 : end], rows[0], rows[1])
            out_ref[end - 16 : end, :] = tile.astype(BF)


def dispatch(c, order, place, slot, source, weight, half):
    return call(
        order,
        functools.partial(dispatch_body, c, half),
        place,
        [slot, source, weight],
        [whole(slot), pl.BlockSpec((c.TP, c.half), lambda i, s: (0, i ^ s[2])), whole(weight)],
        [shape_of((c.X * c.SP, c.D), BF)],
        [cols_of((c.X * c.SP, c.half))],
        (2,),
        [pltpu.VMEM((1, c.X * c.SP, c.TP), BF)],
        name="dispatch",
    )[0].reshape(c.X, c.SP, c.D)


def norm_rows(values):
    centred = values - jnp.mean(values, axis=-1, keepdims=True)
    inv_std = lax.rsqrt(jnp.mean(centred * centred, axis=-1, keepdims=True) + 1e-06)
    return centred * inv_std, inv_std


def norm_back(grad_norm, gain, normed, inv_std):
    scaled = grad_norm * gain
    return inv_std * (
        scaled
        - jnp.mean(scaled, axis=-1, keepdims=True)
        - normed * jnp.mean(scaled * normed, axis=-1, keepdims=True)
    )


def small_row(c, small_ref, index, count=1):
    return small_ref[index : index + count, :].astype(F32)


def own_cols(c, place):
    return pl.ds(pl.multiple_of(place[2] * c.half, c.half), c.half)


def other_cols(c, place):
    return pl.ds(pl.multiple_of((1 - place[2]) * c.half, c.half), c.half)


def live_rows(c, first, count):
    return (first + lax.broadcasted_iota(I32, (count, 1), 0)) < c.T


def qkv_body(c, place, tok_ref, small_ref, own_ref, oth_ref, hid_ref, qkv_ref, normed_ref, w_ref):
    @pl.when(pl.program_id(0) == 0)
    def _():
        for part in range(3):
            lanes = slice(part * c.W, (part + 1) * c.W)
            w_ref[own_cols(c, place), lanes] = own_ref[part]
            w_ref[other_cols(c, place), lanes] = oth_ref[part]

    live = live_rows(c, pl.program_id(0) * c.R, c.R)
    values = jnp.where(live, tok_ref[...].astype(F32), 0.0)
    normed, _ = norm_rows(values)
    hidden = normed * small_row(c, small_ref, 0) + small_row(c, small_ref, 2)
    normed_ref[...] = normed.astype(BF)
    hidden = jnp.where(live, hidden, 0.0).astype(BF)
    hid_ref[...] = hidden
    acc = dot_nn(hidden, w_ref[...])
    bias = small_row(c, small_ref, 5)
    zero = jnp.zeros((1, c.W), F32)
    shift = jnp.concatenate([bias[:, : c.W], zero, bias[:, c.half : c.half + c.W]], axis=1)
    qkv_ref[...] = (acc + shift).astype(BF)


def image_window(c):
    start = pl.program_id(0) * IMG_LEN
    low = pl.multiple_of(start // 16 * 16, 16)
    return low, start - low


def groups_of(c):
    lanes = min(128, c.W)
    return [(at, lanes) for at in range(0, c.W, lanes)]


def head_mask(lanes, head):
    lane = lax.broadcasted_iota(I32, (1, lanes), 1)
    return (lane >= head * HEAD) & (lane < (head + 1) * HEAD)


def stack_heads(c, values):
    heads = range(c.W // HEAD)
    return jnp.concatenate([jnp.where(head_mask(c.W, h), values, BF(0)) for h in heads], axis=0)


def pick_heads(c, values):
    total = None
    for h in range(c.W // HEAD):
        part = jnp.where(head_mask(c.W, h), values[h * c.win : (h + 1) * c.win], 0.0)
        total = part if total is None else total + part
    return total


def attend_body(c, place, qkv_ref, mix_ref):
    @pl.when(pl.program_id(0) == 0)
    def _():
        mix_ref[...] = jnp.zeros_like(mix_ref)

    low, off = image_window(c)
    row = lax.broadcasted_iota(I32, (c.win, 1), 0)
    col = lax.broadcasted_iota(I32, (1, c.win), 1)
    in_row = (row >= off) & (row < off + IMG_LEN)
    in_col = (col >= off) & (col < off + IMG_LEN)
    q = stack_heads(c, qkv_ref[pl.ds(low, c.win), : c.W] * BF(HEAD**-0.5))
    k = qkv_ref[pl.ds(low, c.win), c.W : 2 * c.W]
    v = qkv_ref[pl.ds(low, c.win), 2 * c.W :]
    scores = jnp.where(in_col, dot_nt(q, k), LOW)
    exps = jnp.exp(scores - jnp.max(scores, axis=-1, keepdims=True))
    probs = exps * (1.0 / jnp.sum(exps, axis=-1, keepdims=True))
    total = pick_heads(c, dot_nn(probs.astype(BF), v)).astype(BF)
    for group, (at, lanes) in enumerate(groups_of(c)):
        old = mix_ref[group, pl.ds(low, c.win), :]
        mix_ref[group, pl.ds(low, c.win), :] = jnp.where(in_row, total[:, at : at + lanes], old)


def attend_back_body(c, place, qkv_ref, *refs):
    pieces, (out_ref, sums_ref, grad_ref) = refs[: c.n], refs[c.n :]

    @pl.when(pl.program_id(0) == 0)
    def _():
        out_ref[...] = jnp.zeros_like(out_ref)
        sums_ref[...] = jnp.zeros_like(sums_ref)
        for k in range(c.n):
            at = pl.multiple_of((place[1] ^ k) * c.R, 16)
            grad_ref[pl.ds(at, c.R), :] = pieces[k][...]

    low, off = image_window(c)
    row = lax.broadcasted_iota(I32, (c.win, 1), 0)
    in_row = (row >= off) & (row < off + IMG_LEN)
    scale = HEAD**-0.5
    q = stack_heads(c, qkv_ref[pl.ds(low, c.win), : c.W] * BF(scale))
    k = qkv_ref[pl.ds(low, c.win), c.W : 2 * c.W]
    v = qkv_ref[pl.ds(low, c.win), 2 * c.W :]
    do = stack_heads(c, jnp.where(in_row, grad_ref[pl.ds(low, c.win), :], BF(0)))
    scores = jnp.where(in_row, dot_nt(k, q), LOW)
    exps = jnp.exp(scores - jnp.max(scores, axis=0, keepdims=True))
    soft = exps * (1.0 / jnp.sum(exps, axis=0, keepdims=True))
    dp = dot_nt(v, do)
    delta = jnp.sum(soft * dp, axis=0, keepdims=True)
    ds = (soft * (dp - delta)).astype(BF)
    dq = pick_heads(c, dot_tn(ds, k)) * scale
    dk = dot_nn(ds, q)
    dv = dot_nn(soft.astype(BF), do)
    for part, grad in enumerate((dq, dk, dv)):
        lanes = slice(part * c.W, (part + 1) * c.W)
        low_grad = jnp.where(in_row, grad, 0.0).astype(BF)
        old = out_ref[pl.ds(low, c.win), lanes]
        out_ref[pl.ds(low, c.win), lanes] = jnp.where(in_row, low_grad, old)
        sums_ref[0:1, lanes] += jnp.sum(low_grad.astype(F32), axis=0, keepdims=True)


def middle_body(c, place, *refs):
    refs = list(refs)
    groups = groups_of(c)
    count = c.n * len(groups)
    mixes, refs = refs[:count], refs[count:]
    w_ref, tok_ref, small_ref, table_ref, slot_ref = refs[:5]
    hid_ref, weight_ref, after_ref, probs_ref, proj_ref = refs[5:]
    step = pl.program_id(0)

    @pl.when(step == 0)
    def _():
        for k in range(c.n):
            for h in range(2):
                cols = slice(h * c.half, (h + 1) * c.half)
                proj_ref[k * c.W : (k + 1) * c.W, cols] = w_ref[(place[1] ^ k) * 2 + h]

    branch = dot_nn(jnp.concatenate([mix[...] for mix in mixes], axis=1), proj_ref[...])
    live = live_rows(c, step * c.R, c.R)
    tok = jnp.where(live, tok_ref[...].astype(F32), 0.0)
    after = tok + branch + small_row(c, small_ref, 4)
    normed, _ = norm_rows(after)
    hidden = (normed * small_row(c, small_ref, 1) + small_row(c, small_ref, 3)).astype(BF)
    hid_ref[...] = hidden
    router = table_ref[c.E : 2 * c.E, :]
    logits = dot_nt(router, hidden)
    exps = jnp.exp(logits - jnp.max(logits, axis=0, keepdims=True))
    probs = exps / jnp.sum(exps, axis=0, keepdims=True)
    weight = jnp.where(slot_ref[0] >= 0, probs, 0.0)
    high, rest = split_low(weight)
    lane = lax.broadcasted_iota(I32, (c.E, 128), 1)
    index = lax.broadcasted_iota(I32, (c.E, 128), 0)
    both = dot_tn(high, (lane == index).astype(BF)) + dot_tn(rest, (lane == index + 64).astype(BF))
    weight_ref[...] = both.astype(BF)
    @pl.when(step == place[1])
    def _():
        after_ref[...] = after
        probs_ref[...] = probs


def middle(c, order, place, mixes, proj, tokens, small, table, blocks):
    args = [pair[0] for pair in flat(mixes)] + [proj, tokens, small, table, blocks]
    specs = [
        pl.BlockSpec((None, c.R, a.shape[2]), lambda i, s, at=at: (at, i, 0))
        for a, at in flat(mixes)
    ]
    specs += [whole(proj), rows_of((c.R, c.D)), whole(small), whole(table)]
    specs += [rows_of((1, c.E, c.R))]
    outs = [
        shape_of((c.TP, c.D), BF),
        shape_of((c.TP, 128), BF),
        shape_of((c.R, c.D), F32),
        shape_of((c.E, c.R), F32),
    ]
    return call(
        order,
        functools.partial(middle_body, c),
        place,
        args,
        specs,
        outs,
        [rows_of((c.R, c.D)), rows_of((c.R, 128)), whole(outs[2]), whole(outs[3])],
        (c.n,),
        [pltpu.VMEM((c.D, c.D), BF)],
        name="middle",
    )


def fill_packs(c, place, tails, packs):
    lane = lax.broadcasted_iota(I32, (1, 128), 1)
    here = place[0] * EXP_DEV + place[3]
    state = [jnp.zeros((1, 1), F32)] * 3
    for j in range(c.X):
        high, low = last_pair(c, tails[j], 128)
        number = jnp.sum(jnp.where(lane == here, high * 16.0 + low, 0.0), axis=1, keepdims=True)
        kept = jnp.clip(c.cap - state[0], 0.0, number)
        first = jnp.minimum(kept, float(c.Q))
        sizes = first, kept - first
        for half in range(2):
            wide = (c.CR[half], c.SP)
            slot = lax.broadcasted_iota(I32, wide, 1)
            at = lax.broadcasted_iota(I32, wide, 0) - state[1 + half].astype(I32)
            hot = (at == slot) & (slot < sizes[half].astype(I32))
            packs[half][:, j * c.SP : (j + 1) * c.SP] = hot.astype(BF)
        state = [state[0] + number, state[1] + sizes[0], state[2] + sizes[1]]


def last_pair(c, tile, lanes):
    tile = tile[:, :lanes].astype(F32)
    return tile[14:15, :], tile[15:16, :]


def row_chunks(rows, size):
    return [slice(at, min(at + size, rows)) for at in range(0, rows, size)]


def grad_active_body(c, place, rows_ref, own_ref, oth_ref, *outs):
    gas, all_ref, packs = outs[:2], outs[2], outs[3:]

    @pl.when(pl.program_id(0) == 0)
    def _():
        tails = [rows_ref[j, c.SP - 16 : c.SP, :] for j in range(c.X)]
        fill_packs(c, place, tails, packs)
        for half, base in enumerate((0, c.CR[0])):
            rows = [rows_ref[j, half * c.SP : (half + 1) * c.SP, :] for j in range(c.X)]
            got = dot_nn(packs[half][...], jnp.concatenate(rows, axis=0))
            all_ref[base : base + c.CR[half], :] = got.astype(BF)

    weights = jnp.concatenate([own_ref[...], oth_ref[...]], axis=1)
    for half, base in enumerate((0, c.CR[0])):
        for at in row_chunks(c.CR[half], 320):
            values = all_ref[base + at.start : base + at.stop, :]
            gas[half][at, :] = dot_nt(values, weights).astype(BF)


def grad_active(c, order, place, rows, own_w, oth_w):
    outs = [shape_of((count, c.F), BF) for count in c.CR] + [shape_of((sum(c.CR), c.D), BF)]
    outs += [shape_of((count, c.X * c.SP), BF) for count in c.CR]
    return call(
        order,
        functools.partial(grad_active_body, c),
        place,
        [rows, own_w, oth_w],
        [whole(rows, 1)] + [rows_of((c.fblk, c.half))] * 2,
        outs,
        [cols_of((count, c.fblk)) for count in c.CR] + [whole(o) for o in outs[2:]],
        (c.F // c.fblk,),
        name="grad_active",
    )


def expert_body(c, half, place, *refs):
    rows_ref, pack_ref, own_ref, oth_ref, bias_ref, ga_ref = refs[:6]
    act_ref, gp_ref, gb_ref, all_ref, col_ref, back_ref = refs[6:12]
    acc_ref, dot_ref, row_ref, wide_ref = refs[12:]
    step = pl.program_id(0)

    @pl.when(step == 0)
    def _():
        acc_ref[...] = jnp.zeros_like(acc_ref)
        dot_ref[...] = jnp.zeros_like(dot_ref)
        all_ref[...] = dot_nn(pack_ref[...], rows_ref[...]).astype(BF)
        eye = lax.broadcasted_iota(I32, (c.SP, c.SP), 0) == lax.broadcasted_iota(I32, (c.SP, c.SP), 1)
        lane = lax.broadcasted_iota(I32, (1, 128), 1)
        for j in range(c.X):
            end = (j + 1) * c.SP
            high, low = last_pair(c, rows_ref[end - 16 : end, :], c.SP)
            high = jnp.sum(jnp.where(eye, high, 0.0), axis=1, keepdims=True)
            low = jnp.sum(jnp.where(eye, low, 0.0), axis=1, keepdims=True)
            both = jnp.where(lane == 0, high, jnp.where(lane == 1, low, 0.0))
            wide_ref[j * c.SP : end, :] = both.astype(BF)
        both = dot_nn(pack_ref[...], wide_ref[...])
        col_ref[...] = jnp.broadcast_to(both[:, 0:1] + both[:, 1:2], (c.CR[half], 128))

    bias = bias_ref[...]
    weights = jnp.concatenate([own_ref[...], oth_ref[...]], axis=0)
    summed = jnp.zeros((1, c.fblk), F32)
    lead = 0.7978845608028654
    cube = lead * 0.044715
    chunks = row_chunks(c.CR[half], 224)
    ahead = dot_nn(all_ref[chunks[0], :], weights)
    for i, rows_at in enumerate(chunks):
        pre = ahead + bias
        if i + 1 < len(chunks):
            ahead = dot_nn(all_ref[chunks[i + 1], :], weights)
        square = pre * pre
        turn = jnp.tanh(pre * (cube * square + lead))
        above = 1.0 + turn
        active = (0.5 * pre) * above
        slope = above * (1.0 + (1.0 - turn) * (pre * (3 * cube * square + lead)))
        ga = ga_ref[rows_at, :].astype(F32)
        product = active * ga
        part = product[:, 0:128]
        for lane in range(128, c.fblk, 128):
            part = part + product[:, lane : lane + 128]
        dot_ref[rows_at, :] += part
        grad = ga * slope * (0.5 * col_ref[rows_at, 0:1])
        act_ref[rows_at, :] = active.astype(BF)
        grad_low = grad.astype(BF)
        gp_ref[rows_at, :] = grad_low
        summed = summed + jnp.sum(grad, axis=0, keepdims=True)
        acc_ref[rows_at, :] += dot_nt(grad_low, weights)
    gb_ref[...] = jnp.broadcast_to(summed, (8, c.fblk))

    @pl.when(step == pl.num_programs(0) - 1)
    def _():
        ones = jnp.ones((8, 128), BF)
        row_ref[...] = jnp.zeros_like(row_ref)
        back_ref[...] = dot_tn(pack_ref[...], acc_ref[...].astype(BF)).astype(BF)
        a, rest = split_low(dot_ref[...])
        total = dot_nt(ones, a) + dot_nt(ones, rest)
        high, low = split_low(total)
        high = dot_nn(high, pack_ref[...])
        low = dot_nn(low, pack_ref[...])
        for j in range(c.X):
            end = (j + 1) * c.SP
            row_ref[0:8, : c.SP] = high[:, j * c.SP : end]
            row_ref[8:16, : c.SP] = low[:, j * c.SP : end]
            tile = back_ref[end - 16 : end, : c.half].astype(F32)
            tile = last_rows(c, tile, row_ref[0:1, :], row_ref[8:9, :])
            back_ref[end - 16 : end, : c.half] = tile.astype(BF)


def expert(c, order, place, half, rows, pack, own_w, oth_w, bias, ga):
    rows = rows.reshape(c.X * c.SP, c.D)
    args = [rows, pack, own_w, oth_w, bias, ga]
    count = c.CR[half]
    specs = [whole(rows, 1), whole(pack, 1)]
    specs += [cols_of((c.half, c.fblk))] * 2
    specs += [cols_of((1, c.fblk)), cols_of((count, c.fblk))]
    outs = [
        shape_of((count, c.F), BF),
        shape_of((count, c.F), BF),
        shape_of((8, c.F), F32),
    ]
    out_specs = [cols_of((count, c.fblk))] * 2 + [cols_of((8, c.fblk))]
    late = [shape_of((count, c.D), BF), shape_of((count, 128), F32)]
    late.append(shape_of((c.X * c.SP, c.D), BF))
    result = call(
        order,
        functools.partial(expert_body, c, half),
        place,
        args,
        specs,
        outs + late,
        out_specs + [whole(o, 1) for o in late],
        (c.F // c.fblk,),
        [
            pltpu.VMEM((count, c.D), F32),
            pltpu.VMEM((count, 128), F32),
            pltpu.VMEM((16, c.half), F32),
            pltpu.VMEM((c.X * c.SP, 128), BF),
        ],
        name="expert",
    )
    return (*result[:5], result[5].reshape(c.X, c.SP, c.D))


def produce_body(c, place, *refs):
    cols, acts, packs, own_ref, oth_ref, out_ref = refs[:2], refs[2:4], refs[4:6], *refs[6:9]
    accs = refs[9:]
    step = pl.program_id(0)

    @pl.when(step == 0)
    def _():
        for acc_ref in accs:
            acc_ref[...] = jnp.zeros_like(acc_ref)

    weights = jnp.concatenate([own_ref[...], oth_ref[...]], axis=1)
    for half in range(2):
        for at in row_chunks(c.CR[half], 320):
            accs[half][at, :] += dot_nn(acts[half][at, :], weights)

    @pl.when(step == pl.num_programs(0) - 1)
    def _():
        for half in range(2):
            values = (accs[half][...] * cols[half][:, 0:1]).astype(BF)
            values = dot_tn(packs[half][...], values).astype(BF)
            for j in range(c.X):
                rows = values[j * c.SP : (j + 1) * c.SP]
                out_ref[j, half * c.SP : (half + 1) * c.SP, :] = rows


def produce(c, order, place, cols, acts, packs, own_w, oth_w):
    out = shape_of((c.X, 2 * c.SP, c.D), BF)
    return call(
        order,
        functools.partial(produce_body, c),
        place,
        [*cols, *acts, *packs, own_w, oth_w],
        [whole(col) for col in cols]
        + [cols_of((rows, c.fblk)) for rows in c.CR]
        + [whole(pack) for pack in packs]
        + [rows_of((c.fblk, c.half))] * 2,
        [out],
        [whole(out, 1)],
        (c.F // c.fblk,),
        [pltpu.VMEM((rows, c.D), F32) for rows in c.CR],
        name="produce",
    )[0]


def grad_second_body(c, own, place, *refs):
    all_ref, cols, acts = refs[0], refs[1:3], refs[3:5]
    out_ref, row_ref = refs[-2:]

    @pl.when(pl.program_id(0) == 0)
    def _():
        for half, base in enumerate((0, c.CR[0])):
            rows_at = slice(base, base + c.CR[half])
            row_ref[rows_at, :] = (all_ref[rows_at, :].astype(F32) * cols[half][:, 0:1]).astype(BF)

    acc = dot_tn(acts[0][...], row_ref[: c.CR[0], :])
    acc = acc + dot_tn(acts[1][...], row_ref[c.CR[0] :, :])
    if own:
        acc = acc + refs[5][...].astype(F32)
    out_ref[...] = acc.astype(out_ref.dtype)


def grad_second(c, order, place, rows, cols, acts, add=None):
    own = add is not None
    args = [rows, *cols, *acts]
    total = sum(c.CR)
    specs = [pl.BlockSpec((total, c.half), lambda i, s: (0, 0 if own else 1))]
    specs += [whole(col) for col in cols] + [cols_of((count, c.fblk)) for count in c.CR]
    if own:
        args.append(add)
        specs.append(rows_of((c.fblk, c.half)))
    out = shape_of((c.F, c.half), F32 if own else BF)
    return call(
        order,
        functools.partial(grad_second_body, c, own),
        place,
        args,
        specs,
        [out],
        [rows_of((c.fblk, c.half))],
        (c.F // c.fblk,),
        [pltpu.VMEM((total, c.half), BF)],
        name="grad_second",
    )[0]


def grad_first_body(c, own, place, *refs):
    acc = dot_tn(refs[0][...], refs[2][...]) + dot_tn(refs[1][...], refs[3][...])
    if own:
        acc = acc + refs[4][...].astype(F32)
    refs[-1][...] = acc.astype(refs[-1].dtype)


def grad_first(c, order, place, rows, gps, add=None):
    own = add is not None
    args = [*rows, *gps]
    specs = [pl.BlockSpec((count, c.half), lambda i, s: (0, 0 if own else 1)) for count in c.CR]
    specs += [cols_of((count, c.fblk)) for count in c.CR]
    if own:
        args.append(add)
        specs.append(cols_of((c.half, c.fblk)))
    out = shape_of((c.half, c.F), F32 if own else BF)
    return call(
        order,
        functools.partial(grad_first_body, c, own),
        place,
        args,
        specs,
        [out],
        [cols_of((c.half, c.fblk))],
        (c.F // c.fblk,),
        name="grad_first",
    )[0]


def combine_body(c, with_dots, place, *refs):
    refs = list(refs)
    extras = [] if with_dots else [refs.pop(0), refs.pop(0)]
    halves = 2 if with_dots else 1
    rows, refs = refs[:halves], refs[halves:]
    tails = []
    if with_dots:
        tails, refs = refs[:2], refs[2:]
    mine_ref = refs.pop(0)
    groups = [(0, g) for g in groups_a(c)] + [(1, g) for g in groups_b(c)]
    outs, (hot_ref, row_ref) = refs[: len(groups)], refs[len(groups) :]
    pad = hot_ref.shape[1] // c.X

    @pl.when(pl.program_id(0) == 0)
    def _():
        row_ref[...] = jnp.zeros_like(row_ref)
        slots = lax.broadcasted_iota(I32, (c.R, pad), 1)
        for k in range(c.n):
            at = pl.multiple_of((place[1] ^ k) * c.R, 16)
            for j in range(c.X):
                hot = (mine_ref[pl.ds(at, c.R), j : j + 1] == slots).astype(BF)
                hot_ref[k * c.R : (k + 1) * c.R, j * pad : (j + 1) * pad] = hot
        if with_dots:
            wide = (c.SP, c.half)
            eye = lax.broadcasted_iota(I32, wide, 0) == lax.broadcasted_iota(I32, wide, 1)
            lane = lax.broadcasted_iota(I32, (1, 128), 1)
            for half in range(2):
                for j in range(c.X):
                    high, low = last_pair(c, tails[half][j], c.half)
                    high = jnp.sum(jnp.where(eye, high, 0.0), axis=1, keepdims=True)
                    low = jnp.sum(jnp.where(eye, low, 0.0), axis=1, keepdims=True)
                    e = expert_of(c, place, j)
                    cols = jnp.where(lane == e, high, jnp.where(lane == e + 64, low, 0.0))
                    at = j * pad + half * c.SP
                    row_ref[at : at + c.SP, :128] = cols.astype(BF)
            pulls = dot_nn(hot_ref[...], row_ref[:, :128]).astype(BF)
            expert = lax.broadcasted_iota(I32, (c.E, 128), 0)
            lane = lax.broadcasted_iota(I32, (c.E, 128), 1)
            pick = ((lane == expert) | (lane == expert + 64)).astype(BF)
            for (side, group), out_ref in zip(groups, outs):
                for at, k in enumerate(group):
                    if side == 0:
                        got = dot_nt(pick, pulls[k * c.R : (k + 1) * c.R])
                        out_ref[at, c.R :, :] = jnp.zeros((c.E, c.half), BF)
                        out_ref[at, c.R :, : c.R] = got.astype(BF)

    for half, rows_ref in enumerate(rows):
        size = rows_ref.shape[1]
        for j in range(c.X):
            at = j * pad + half * size
            row_ref[at : at + size, :] = rows_ref[j]
    result = dot_nn(hot_ref[...], row_ref[...]).astype(BF)
    for half in range(2):

        @pl.when(pl.program_id(0) == half)
        def _():
            for (side, group), out_ref in zip(groups, outs):
                if side == half:
                    for at, k in enumerate(group):
                        out_ref[at, : c.R, :] = result[k * c.R : (k + 1) * c.R]
                        if extras:
                            more = extras[0].shape[1] // 2
                            extra = [e[k, half * more : (half + 1) * more, :] for e in extras]
                            total = extra[0].astype(F32) + extra[1].astype(F32)
                            out_ref[at, c.R :, :] = total.astype(BF)


def combine(c, order, place, rows, mine, extra=None, cost=0):
    pad = up(2 * c.SP, 128)
    args = list(rows)
    specs = [pl.BlockSpec((c.X, r.shape[1], c.half), lambda i, s: (0, 0, i ^ s[2])) for r in rows]
    if extra is None:
        args += list(rows)
        specs += [pl.BlockSpec((c.X, 16, c.half), lambda i, s: (0, c.SP // 16 - 1, 0))] * 2
        outs = piece_outs(c, c.E)
    else:
        args = [*extra, *args]
        specs = [whole(e) for e in extra] + specs
        outs = piece_outs(c, extra[0].shape[1] // 2, extra[0].shape[1] // 2)
    args.append(mine)
    specs.append(whole(mine))
    result = call(
        order,
        functools.partial(combine_body, c, extra is None),
        place,
        args,
        specs,
        outs,
        [whole(o, 1) for o in outs],
        (2,),
        [pltpu.VMEM((c.n * c.R, c.X * pad), BF), pltpu.VMEM((c.X * pad, c.half), BF)],
        name="combine",
        cost=cost,
    )
    return list(result)


def back_two_body(c, place, *refs):
    refs = list(refs)
    groups = groups_of(c)
    heads, refs = refs[: c.n * len(groups)], refs[c.n * len(groups) :]
    count = (len(refs) - 13 - c.n) // 2
    a, b, refs = refs[:count], refs[count : 2 * count], refs[2 * count :]
    w_ref, after_ref, probs_ref, keep_ref = refs[:4]
    cot_ref, hid_ref, small_ref, table_ref, ga_ref, proj_own_ref, proj_oth_ref = refs[4:11]
    mixes, (gb_ref, sums_ref) = refs[11:-2], refs[-2:]
    sum_a = add_up(a)
    live = live_rows(c, place[1] * c.R, c.R)
    cot = jnp.where(live, cot_ref[...], BF(0))
    eshift = table_ref[: c.E, :]
    router = table_ref[c.E : 2 * c.E, :]
    kept = keep_ref[...] > 0
    pulls = jnp.where(kept, sum_a[c.R :, : c.R] + dot_nt(eshift, cot), 0.0)
    probs = probs_ref[...]
    glog = (probs * (pulls - jnp.sum(probs * pulls, axis=0, keepdims=True))).astype(BF)
    two = jnp.concatenate([sum_a[: c.R], add_up(b)], axis=1) + dot_tn(glog, router)
    normed, inv_std = norm_rows(after_ref[...])
    grad_after = cot.astype(F32) + norm_back(two, small_row(c, small_ref, 1), normed, inv_std)
    ga_ref[...] = grad_after
    low = grad_after.astype(BF)
    gb_ref[...] = low
    high, rest = split_low(probs * keep_ref[...])
    hid = jnp.where(live, hid_ref[...], BF(0))
    sums_ref[0:1, :] = jnp.sum(two * normed, axis=0, keepdims=True)
    sums_ref[1:2, :] = jnp.sum(two, axis=0, keepdims=True)
    sums_ref[2:3, :] = jnp.sum(low.astype(F32), axis=0, keepdims=True)
    sums_ref[3:8, :] = jnp.zeros((5, c.D), F32)
    sums_ref[8 : 8 + c.E, :] = dot_nn(high, cot) + dot_nn(rest, cot)
    sums_ref[8 + c.E : 8 + 2 * c.E, :] = dot_nn(glog, hid)
    for k in range(c.n):
        lane = place[1] ^ k
        mix = dot_nt(gb_ref[:, : c.half], w_ref[2 * lane])
        mix = mix + dot_nt(gb_ref[:, c.half :], w_ref[2 * lane + 1])
        mixes[k][...] = mix.astype(BF)
    height = sums_ref.shape[0]
    for cols, out_ref in ((own_cols(c, place), proj_own_ref), (other_cols(c, place), proj_oth_ref)):
        sums = sums_ref[:, cols].astype(BF)
        for k in range(c.n):
            for group, (at, lanes) in enumerate(groups):
                part = dot_tn(heads[k * len(groups) + group][...], gb_ref[:, cols])
                out_ref[k, at : at + lanes, :] = part.astype(BF)
            out_ref[k, c.W : c.W + height, :] = sums
            rest = out_ref.shape[1] - c.W - height
            out_ref[k, c.W + height :, :] = jnp.zeros((rest, c.half), BF)


def back_two(c, order, place, heads, sums, proj, lanes, cotangent, hidden, small, table):
    height = 8 + 2 * c.E
    rows = up(c.W + height, 32)
    args = [pair[0] for pair in flat(heads)]
    specs = [
        pl.BlockSpec((None, c.R, a.shape[2]), lambda i, s, at=at: (at, s[1], 0))
        for a, at in flat(heads)
    ]
    args += [*sums[0], *sums[1], proj, *lanes, cotangent, hidden, small, table]
    lane_rows = pl.BlockSpec((c.R, c.D), lambda i, s: (s[1], 0))
    specs += [first_block(a) for a in [*sums[0], *sums[1]]]
    specs += [whole(a) for a in [proj, *lanes]] + [lane_rows, lane_rows]
    specs += [whole(small), whole(table)]
    outs = [shape_of((c.R, c.D), F32)] + [shape_of((c.n, rows, c.half), BF)] * 2
    outs += [shape_of((c.R, c.W), BF) for _ in range(c.n)]
    result = call(
        order,
        functools.partial(back_two_body, c),
        place,
        args,
        specs,
        outs,
        [whole(o) for o in outs],
        (1,),
        [pltpu.VMEM((c.R, c.D), BF), pltpu.VMEM((height, c.D), F32)],
        name="back_two",
    )
    return (*result[:3], list(result[3:]))


def block_out_body(c, place, *refs):
    refs = list(refs)
    count = (len(refs) - 6) // 2
    a, b, refs = refs[:count], refs[count : 2 * count], refs[2 * count :]
    after_ref, probs_ref, keep_ref, table_ref, out_ref, proj_ref = refs
    high, low = split_low(probs_ref[...] * keep_ref[...])
    eshift = table_ref[: c.E, :]
    shift = dot_tn(high, eshift) + dot_tn(low, eshift)
    more = proj_ref.shape[0] // 2
    for h, pieces in enumerate((a, b)):
        cols = slice(h * c.half, (h + 1) * c.half)
        total = add_up([ref.at[: c.R, :] for ref in pieces])
        out_ref[h] = (after_ref[:, cols] + total + shift[:, cols]).astype(BF)
        proj_ref[h * more : (h + 1) * more, :] = same_sum(c, pieces, slice(c.R, c.R + more)).astype(BF)


def block_out(c, order, place, sums, after, probs, keep, table):
    args = [*sums[0], *sums[1], after, probs, keep, table]
    more = 2 * (sums[0][0].shape[1] - c.R)
    outs = [shape_of((2, c.R, c.half), BF), shape_of((more, c.half), BF)]
    return call(
        order,
        functools.partial(block_out_body, c),
        place,
        args,
        [first_block(a) for a in args[:-4]] + [whole(a) for a in args[-4:]],
        outs,
        [whole(o) for o in outs],
        (1,),
        name="block_out",
    )


def grad_one_body(c, place, dqkv_ref, normed_ref, own_ref, oth_ref, *outs):
    sums_ref = outs[-1]
    groups = [(0, g) for g in groups_a(c)] + [(1, g) for g in groups_b(c)]
    for side in range(2):
        cols = slice(side * c.half, (side + 1) * c.half)
        weights = [jnp.where(place[2] == side, own_ref[p], oth_ref[p]) for p in range(3)]
        gain = jnp.zeros((1, c.half), F32)
        shift = jnp.zeros((1, c.half), F32)
        for (where, group), out_ref in zip(groups, outs):
            if where != side:
                continue
            for row, k in enumerate(group):
                rows_at = pl.ds(pl.multiple_of((place[1] ^ k) * c.R, 16), c.R)
                acc = None
                for part in range(3):
                    rows = dqkv_ref[rows_at, part * c.W : (part + 1) * c.W]
                    term = dot_nt(rows, weights[part])
                    acc = term if acc is None else acc + term
                out_ref[row, : c.R, :] = acc.astype(BF)
                normed = normed_ref[rows_at, cols].astype(F32)
                gain = gain + jnp.sum(acc * normed, axis=0, keepdims=True)
                shift = shift + jnp.sum(acc, axis=0, keepdims=True)
        sums_ref[0:1, cols] = gain
        sums_ref[1:2, cols] = shift
        row = lax.broadcasted_iota(I32, (16, 1), 0)
        tile = jnp.where(row == 0, gain, jnp.where(row == 1, shift, 0.0)).astype(BF)
        for (where, group), out_ref in zip(groups, outs):
            if where == side:
                for at in range(len(group)):
                    out_ref[at, c.R :, :] = tile


def grad_one(c, order, place, dqkv, normed, own_w, oth_w):
    outs = piece_outs(c, 16, 16) + [shape_of((2, c.D), F32)]
    result = call(
        order,
        functools.partial(grad_one_body, c),
        place,
        [dqkv, normed, own_w, oth_w],
        [whole(dqkv), whole(normed), whole(own_w), whole(oth_w)],
        outs,
        [whole(o) for o in outs],
        (1,),
        name="grad_one",
    )
    return list(result[:-1]), result[-1]


def grad_qkv_body(c, place, hid_ref, dqkv_ref, own_ref, oth_ref):
    own_ref[0] = dot_tn(hid_ref[:, own_cols(c, place)], dqkv_ref[...]).astype(BF)
    oth_ref[0] = dot_tn(hid_ref[:, other_cols(c, place)], dqkv_ref[...]).astype(BF)


def grad_qkv(c, order, place, hidden, dqkv):
    specs = [whole(hidden, 1), cols_of((c.TP, c.W))]
    if c.W % 128:
        dqkv = dqkv.reshape(c.TP, 3, c.W).transpose(1, 0, 2)
        specs[1] = pl.BlockSpec((None, c.TP, c.W), lambda i, s: (i, 0, 0))
    return call(
        order,
        functools.partial(grad_qkv_body, c),
        place,
        [hidden, dqkv],
        specs,
        [shape_of((3, c.half, c.W), BF)] * 2,
        [rows_of((1, c.half, c.W))] * 2,
        (3,),
        name="grad_qkv",
    )


def back_one_body(c, place, *refs):
    refs = list(refs)
    count = (len(refs) - 4) // 2
    a, b, refs = refs[:count], refs[count : 2 * count], refs[2 * count :]
    tok_ref, after_ref, small_ref, out_ref = refs
    live = live_rows(c, place[1] * c.R, c.R)
    normed, inv_std = norm_rows(jnp.where(live, tok_ref[...].astype(F32), 0.0))
    one = jnp.concatenate([add_up(a)[: c.R], add_up(b)[: c.R]], axis=1)
    grad = after_ref[...] + norm_back(one, small_row(c, small_ref, 0), normed, inv_std)
    for h in range(2):
        out_ref[h] = grad[:, h * c.half : (h + 1) * c.half].astype(BF)


def back_one(c, order, place, sums, tokens, after, small):
    args = [*sums[0], *sums[1], tokens, after, small]
    lane_rows = pl.BlockSpec((c.R, c.D), lambda i, s: (s[1], 0))
    specs = [first_block(a) for a in args[:-3]] + [lane_rows, whole(after), whole(small)]
    out = shape_of((2, c.R, c.half), BF)
    return call(
        order,
        functools.partial(back_one_body, c),
        place,
        args,
        specs,
        [out],
        [whole(out)],
        (1,),
        name="back_one",
    )[0]


def assemble_body(c, place, *refs):
    pieces, out_ref = refs[:-1], refs[-1]
    for k in range(c.n):

        @pl.when((place[1] ^ k) == pl.program_id(0))
        def _():
            for h in range(2):
                values = pieces[2 * k + h][...].astype(out_ref.dtype)
                out_ref[:, h * c.half : (h + 1) * c.half] = values


def assemble(c, order, place, pieces, dtype):
    out = shape_of((c.T, c.D), dtype)
    return call(
        order,
        functools.partial(assemble_body, c),
        place,
        [pair[0] for pair in flat(pieces)],
        [
            pl.BlockSpec((None, c.R, c.half), lambda i, s, at=at: (at, 0, 0))
            for _, at in flat(pieces)
        ],
        [out],
        [rows_of((c.R, c.D))],
        (-(-c.T // c.R),),
        name="assemble",
    )[0]


def local(
    tokens,
    cotangent,
    w_qkv,
    qv_bias,
    w_proj,
    proj_bias,
    norm_gains,
    norm_shifts,
    w_router,
    expert_shift,
    w_first,
    w_second,
    first_bias,
    routes,
    priority,
):
    T, D = tokens.shape
    n = lax.axis_size("mp")
    E = w_router.shape[1]
    S = 16 * T // (5 * E)
    R = up(-(-T // n), 16)
    F = w_first.shape[2]
    W = w_proj.shape[0]
    win = up(IMG_LEN + 15, 16)
    Q = (S + 1) // 2
    cap = (9 * T + 4 * EXP_DEV - 1) // (4 * EXP_DEV)
    X = E // EXP_DEV
    full = min(cap // S, X)
    c = Sizes(
        T=T,
        D=D,
        half=D // 2,
        n=n,
        X=X,
        E=E,
        S=S,
        Q=Q,
        SP=up(Q + 2, 16),
        CR=(up(min(cap, X * Q), 16), up(full * (S - Q) + max(0, cap - full * S - Q), 16)),
        R=R,
        TP=n * R,
        W=W,
        images=T // IMG_LEN,
        quarters=n // EXP_DEV,
        F=F,
        cap=cap,
        win=win,
        fblk=min(1024, F),
    )
    order = Order()
    dp, mp, grid = lax.axis_index("dp"), lax.axis_index("mp"), lax.axis_index("grid")
    place = jnp.stack([dp, mp, grid, mp // c.quarters]).astype(I32)

    slot, blocks, rt, grad_out = route(c, order, place, routes, priority, cotangent)
    grad_in = trade(grad_out, "dp")

    def both_halves(rows):
        rows = jnp.pad(rows, ((0, up(rows.shape[0], 16) - rows.shape[0]), (0, 0)))
        other = swap_grid(rows)
        return jnp.where(
            grid == 0,
            jnp.concatenate([rows, other], axis=1),
            jnp.concatenate([other, rows], axis=1),
        )

    wide_bias = jnp.pad(qv_bias, ((0, 0), (0, c.half - W)))
    small = both_halves(
        jnp.concatenate([norm_gains, norm_shifts, proj_bias[None], wide_bias], axis=0)
    )
    qkv_own = w_qkv.transpose(1, 0, 2)
    qkv_oth = swap_grid(qkv_own)

    first_own = w_first[0]
    second_own = w_second[0]
    proj = lax.all_gather(w_proj, ("mp", "grid"))

    outs = [shape_of((c.TP, D), BF), shape_of((c.TP, 3 * W), BF), shape_of((c.TP, D), BF)]
    hidden_one, qkv, normed_one = call(
        order,
        functools.partial(qkv_body, c),
        place,
        [tokens, small, qkv_own, qkv_oth],
        [rows_of((c.R, D)), whole(small), whole(qkv_own), whole(qkv_oth)],
        outs,
        [rows_of((c.R, D)), rows_of((c.R, 3 * W)), rows_of((c.R, D))],
        (n,),
        [pltpu.VMEM((D, 3 * W), BF)],
        name="qkv",
    )
    bias_rows = F // 2 // c.half
    tied = held(jnp.concatenate([expert_shift, w_router.T]), qkv)
    table = both_halves(tied)
    bias = both_halves(held(first_bias.reshape(bias_rows, c.half), qkv))[:bias_rows]
    bias = bias.reshape(bias_rows, 2, c.half).transpose(1, 0, 2).reshape(1, F).astype(F32)
    order.tie(proj)
    second_oth = swap_grid(held(second_own, qkv))
    first_oth = swap_grid(held(first_own, qkv))
    groups = groups_of(c)
    out = shape_of((len(groups), c.TP, groups[0][1]), BF)
    mix = call(
        order,
        functools.partial(attend_body, c),
        place,
        [qkv],
        [whole(qkv)],
        [out],
        [whole(out)],
        (c.images,),
        name="attend",
    )[0]
    mixes, _ = gather_mp(c, mix)
    hidden_two, weight, after, probs = middle(
        c, order, place, mixes, proj, tokens, small, table, blocks
    )

    rows_a = trade(dispatch(c, order, place, slot, hidden_two, weight, 0), "dp")
    rows_b = dispatch(c, order, place, slot, hidden_two, weight, 1)
    ga_a, ga_b, grad_all, pack_a, pack_b = grad_active(
        c, order, place, grad_in, second_own, second_oth
    )
    rows_b = trade(held(rows_b, rows_a, grad_all), "dp")
    act_a, gp_a, gb_a, all_a, col_a, back_a = expert(
        c, order, place, 0, rows_a, pack_a, first_own, first_oth, bias, ga_a
    )
    back_a = trade(held(back_a, rows_b), "dp")
    act_b, gp_b, gb_b, all_b, col_b, back_b = expert(
        c, order, place, 1, rows_b, pack_b, first_own, first_oth, bias, ga_b
    )
    back_b = trade(held(back_b, back_a), "dp")
    cols, acts, gps, alls = [col_a, col_b], [act_a, act_b], [gp_a, gp_b], [all_a, all_b]
    second_part = swap_grid(grad_second(c, order, place, grad_all, cols, acts))
    order.tie(back_a)
    first_part = swap_grid(grad_first(c, order, place, alls, gps))
    mine, keep, keep_lane = keep_of(c, order, place, grad_in, blocks, rt)
    keep_mask = keep[:, :2, :].transpose(0, 2, 1).reshape(c.TP, 2)[:T].astype(I32)
    mine = mine.transpose(0, 2, 1).reshape(c.TP, 8)
    packs = [pack_a, pack_b]
    prod = produce(c, order, place, cols, acts, packs, second_own, second_oth)
    gb = (gb_a + gb_b)[0:1].reshape(2, F // 2)
    gb_own = lax.dynamic_index_in_dim(gb, grid, 0, True)
    gb_oth = lax.dynamic_index_in_dim(gb, 1 - grid, 0, True)
    grad_fbias = gb_own + swap_grid(gb_oth)

    pieces = combine(c, order, place, [back_a, back_b], mine)
    prod = trade(held(prod, back_b), "dp")
    two_sums = reduce_start(c, pieces)
    grad_second_out = grad_second(c, order, place, grad_all, cols, acts, second_part)
    two_sums = reduce_end(c, order, two_sums)
    grad_after, proj_a, proj_b, grad_mix = back_two(
        c,
        order,
        place,
        mixes,
        two_sums,
        proj,
        [after, probs, keep_lane],
        cotangent,
        hidden_two,
        small,
        table,
    )
    grad_mix = [grad_mix[0]] + [swap_mp(c, grad_mix[k], k) for k in range(1, n)]
    proj_parts = [proj_a, swap_grid(proj_b)]
    pieces = combine(c, order, place, [prod], mine, proj_parts, cost=10)
    out_sums = reduce_start(c, [held(p, *grad_mix) for p in pieces])

    outs = [shape_of((c.TP, 3 * W), BF), shape_of((8, 3 * W), F32)]
    dqkv, dqkv_sums = call(
        order,
        functools.partial(attend_back_body, c),
        place,
        [qkv, *grad_mix],
        [whole(qkv)] + [whole(p) for p in grad_mix],
        outs,
        [whole(o) for o in outs],
        (c.images,),
        [pltpu.VMEM((c.TP, W), BF)],
        name="attend_back",
    )
    one_pieces, one_parts = grad_one(c, order, place, dqkv, normed_one, qkv_own, qkv_oth)
    one_sums = reduce_start(c, one_pieces)
    out_sums = reduce_end(c, order, out_sums)
    qkv_a, qkv_b = grad_qkv(c, order, place, hidden_one, dqkv)
    qkv_b = swap_grid(qkv_b)
    qkv_low = (qkv_a.astype(F32) + qkv_b.astype(F32)).astype(BF)
    qkv_sum = sum_dp_start(c, qkv_low.reshape(-1, c.half))
    one_sums = reduce_end(c, order, one_sums)
    qkv_sum = sum_dp_turn(c, qkv_sum)
    order.tie(qkv_sum)
    grad_low = back_one(c, order, place, one_sums, tokens, grad_after, small)
    out_lane, proj_sum = block_out(c, order, place, out_sums, after, probs, keep_lane, table)

    qv_rows = jnp.concatenate([dqkv_sums[0:1, :W], dqkv_sums[0:1, 2 * W :]], axis=0)
    sums_one = held(first_sums(c, one_sums, one_parts), grad_low)
    sums_one = chip_sums(c, sums_one, qv_rows, grid).astype(BF)
    proj_end = proj_sum.shape[0]
    shared = jnp.concatenate([proj_sum, sums_one], axis=0)
    shared = jnp.pad(shared, ((0, up(shared.shape[0], 16 * c.X) - shared.shape[0]), (0, 0)))
    shared = sum_dp_start(c, shared)

    def last_expert_kernel(before):
        for value in before:
            order.tie(value)
        return grad_first(c, order, place, alls, gps, first_part), order.hold

    grad_low, out_lane, last, grad_first_out = gather_both(c, grad_low, out_lane, last_expert_kernel)
    grad_w_qkv = sum_dp_end(c, qkv_sum).reshape(3, c.half, W)
    shared = sum_dp_end(c, sum_dp_turn(c, held(shared, *last)))
    sums_one = shared[proj_end:]
    rest = shared[W : W + 8 + 2 * E]
    grad_tokens = assemble(c, order, place, grad_low, F32)
    block = assemble(c, order, place, out_lane, BF)
    return (
        block,
        grad_tokens,
        grad_w_qkv.transpose(1, 0, 2),
        sums_one[2:3, :W],
        shared[:W],
        rest[2],
        jnp.stack([sums_one[0], rest[0]]),
        jnp.stack([sums_one[1], rest[1]]),
        rest[8 + E : 8 + 2 * E].T,
        rest[8 : 8 + E],
        grad_first_out[None],
        grad_second_out[None],
        grad_fbias,
        keep_mask,
    )


def solution(mesh):
    return jax.shard_map(
        local,
        mesh=mesh,
        in_specs=(
            P(("dp", "grid"), None),
            P(("dp", "grid"), None),
            P("grid", None, "mp"),
            P("grid", "mp"),
            P("mp", "grid"),
            P("grid"),
            P(None, "grid"),
            P(None, "grid"),
            P("grid", None),
            P(None, "grid"),
            P(("dp", "mp"), "grid", None),
            P(("dp", "mp"), None, "grid"),
            P(("dp", "mp"), "grid"),
            P(("dp", "grid"), None),
            P(("dp", "grid"), None),
        ),
        out_specs=(
            P(("dp", "grid"), None),
            P(("dp", "grid"), None),
            P("grid", None, "mp"),
            P("grid", "mp"),
            P("mp", "grid"),
            P("grid"),
            P(None, "grid"),
            P(None, "grid"),
            P("grid", None),
            P(None, "grid"),
            P(("dp", "mp"), "grid", None),
            P(("dp", "mp"), None, "grid"),
            P(("dp", "mp"), "grid"),
            P(("dp", "grid"), None),
        ),
        check_vma=False,
    )
```

```python
import functools
from typing import NamedTuple

import jax
import jax.numpy as jnp
from jax import lax
from jax.experimental import pallas as pl
from jax.experimental.pallas import tpu as pltpu
from jax.sharding import PartitionSpec as P

HEAD = 64
IMG_LEN = 197
EXP_DEV = 4
BF = jnp.bfloat16
F32 = jnp.float32
I32 = jnp.int32
VMEM_BYTES = 56 * 1024 * 1024
LOW = -1e30


class Sizes(NamedTuple):
    T: int
    D: int
    half: int
    n: int
    X: int
    E: int
    S: int
    Q: int
    SP: int
    CR: tuple
    R: int
    TP: int
    W: int
    images: int
    quarters: int
    F: int
    cap: int
    win: int
    fblk: int


class Order:
    def __init__(self):
        self.after = []

    def tie(self, value):
        self.after.append(value)

    def hold(self, *values):
        return lax.optimization_barrier((*values, *self.after))[: len(values)]


def up(value, step):
    return -(-value // step) * step


def dot_nn(a, b):
    return jnp.dot(a, b, preferred_element_type=F32)


def dot_nt(a, b):
    return lax.dot_general(a, b, (((1,), (1,)), ((), ())), preferred_element_type=F32)


def dot_tn(a, b):
    return lax.dot_general(a, b, (((0,), (0,)), ((), ())), preferred_element_type=F32)


def split_low(values):
    high = values.astype(BF)
    return high, (values - high.astype(F32)).astype(BF)


def shape_of(dims, dtype):
    return jax.ShapeDtypeStruct(dims, dtype)


def whole(array, buffers=None):
    dims = tuple(array.shape)
    extra = {} if buffers is None else {"pipeline_mode": pl.Buffered(buffers)}
    return pl.BlockSpec(dims, lambda i, s: (0,) * len(dims), **extra)


def rows_of(dims):
    return pl.BlockSpec(dims, lambda i, s: (i,) + (0,) * (len(dims) - 1))


def cols_of(dims):
    return pl.BlockSpec(dims, lambda i, s: (0,) * (len(dims) - 1) + (i,))


def call(order, body, place, args, specs, outs, out_specs, grid, scratch=(), name=None, cost=0):
    extra = order.after
    count = len(args)

    def wrapped(place, *refs):
        body(place, *refs[:count], *refs[count + len(extra) :])

    result = pl.pallas_call(
        wrapped,
        grid_spec=pltpu.PrefetchScalarGridSpec(
            num_scalar_prefetch=1,
            grid=grid,
            in_specs=list(specs) + [pl.BlockSpec(memory_space=pl.ANY)] * len(extra),
            out_specs=list(out_specs),
            scratch_shapes=list(scratch),
        ),
        out_shape=list(outs),
        compiler_params=pltpu.CompilerParams(
            dimension_semantics=("arbitrary",) * len(grid), vmem_limit_bytes=VMEM_BYTES
        ),
        cost_estimate=pl.CostEstimate(
            flops=1000 + int(1.1e9 * cost), bytes_accessed=1000, transcendentals=0
        ),
        name=name,
    )(place, *args, *extra)
    order.after = [min(result, key=lambda o: o.size)]
    return result


def swap_mp(c, value, mask):
    return lax.ppermute(value, "mp", [(i, i ^ mask) for i in range(c.n)])


def swap_grid(value):
    return lax.ppermute(value, "grid", [(0, 1), (1, 0)])


def held(value, *others):
    return lax.optimization_barrier((value, *others))[0]


def trade(value, axis):
    return lax.all_to_all(value, axis, split_axis=0, concat_axis=0, tiled=True)


def groups_a(c):
    return [[0, 2], [1, 3]] if c.n == 4 else [[k] for k in range(c.n)]


def groups_b(c):
    return [[0, 1], [2, 3]] if c.n == 4 else [[k] for k in range(c.n)]


def reduce_start(c, arrays):
    a, b = arrays[: len(arrays) // 2], arrays[len(arrays) // 2 :]
    if c.n != 4:
        return [[x[0]] + [swap_mp(c, x[k], k) for k in range(1, c.n)] for x in (a, b)]
    return [[a[0], swap_mp(c, a[1], 1)], [b[0], swap_mp(c, b[1], 2)]]


def reduce_end(c, order, state):
    if c.n != 4:
        return state
    (a, ra), (b, rb) = state
    ra, rb = order.hold(ra, rb)
    ta = (a[1:].astype(F32) + ra[1:].astype(F32)).astype(BF)
    tb = (b[1:].astype(F32) + rb[1:].astype(F32)).astype(BF)
    order.tie(ta)
    order.tie(tb)
    return [[a, ra, swap_mp(c, ta, 2)], [b, rb, swap_mp(c, tb, 1)]]


def piece_outs(c, more_a=0, more_b=0):
    outs = [shape_of((len(g), c.R + more_a, c.half), BF) for g in groups_a(c)]
    return outs + [shape_of((len(g), c.R + more_b, c.half), BF) for g in groups_b(c)]


def first_block(array):
    dims = tuple(array.shape)
    return pl.BlockSpec((None,) + dims[1:], lambda i, s: (0, 0, 0))


def same_sum(c, refs, rows):
    parts = [ref[rows, :].astype(F32) for ref in refs]
    if c.n == 4:
        return (parts[0] + parts[1]).astype(BF).astype(F32) + parts[2]
    while len(parts) > 1:
        parts = [parts[i] + parts[i + 1] for i in range(0, len(parts), 2)]
    return parts[0]


def add_up(refs):
    total = refs[0][...].astype(F32)
    for ref in refs[1:]:
        total = total + ref[...].astype(F32)
    return total


def sum_dp_start(c, value):
    return trade(value.reshape((c.X, value.shape[0] // c.X) + value.shape[1:]), "dp")


def sum_dp_turn(c, parts):
    total = jnp.sum(parts.astype(F32), axis=0).astype(BF)
    return jnp.broadcast_to(total[None], (c.X,) + total.shape)


def sum_dp_end(c, spread):
    return trade(spread, "dp").reshape((-1,) + spread.shape[2:]).astype(F32)


def gather_mp(c, value, until=None):
    if c.n != 4 or value.shape[0] != 2:
        parts = [value] + [swap_mp(c, value, k) for k in range(1, c.n)]
        return [[(p, h) for h in range(value.shape[0])] for p in parts], parts[1:]
    one = swap_mp(c, value, 1)
    two = swap_mp(c, value, 2)
    ends = one[0:1], two[1:2]
    if until is not None:
        ends = held(ends[0], *until), held(ends[1], *until)
    far_a = swap_mp(c, ends[0], 2)
    far_b = swap_mp(c, ends[1], 1)
    near = [[(p, 0), (p, 1)] for p in (value, one, two)]
    return near + [[(far_a, 0), (far_b, 0)]], [one, two]


def gather_both(c, first, second, filler):
    if c.n != 4:
        filled, _ = filler([first])
        return gather_mp(c, first)[0], gather_mp(c, second)[0], (first,), filled
    one, two = swap_mp(c, first, 1), swap_mp(c, first, 2)
    near = jnp.concatenate([one[0:1], second]), jnp.concatenate([two[1:2], second])
    by_two, by_one = [swap_mp(c, x, mask) for x, mask in zip(near, (2, 1))]
    filled, hold = filler(near)
    by_two, by_one = hold(by_two, by_one)
    far_a, far_b = swap_mp(c, by_one[1:2], 2), swap_mp(c, by_two[2:3], 1)
    pieces = [[(p, 0), (p, 1)] for p in (first, one, two)] + [[(by_two, 0), (by_one, 0)]]
    others = [[(second, 0), (second, 1)], [(by_one, 1), (by_one, 2)], [(by_two, 1), (by_two, 2)]]
    return pieces, others + [[(far_a, 0), (far_b, 0)]], (by_one, by_two), filled


def flat(pieces):
    return [pair for piece in pieces for pair in piece]


def fold(c, value, axes):
    for axis, size in axes:
        mask = 1
        while mask < size:
            value = value + lax.ppermute(value, axis, [(i, i ^ mask) for i in range(size)])
            mask *= 2
    return value


def first_sums(c, sums, one_parts):
    if c.n != 4:
        return fold(c, one_parts, (("mp", c.n),))
    halves = []
    for a, b, far in sums:
        pair = (a[0, c.R : c.R + 2].astype(F32) + b[0, c.R : c.R + 2].astype(F32)).astype(BF)
        halves.append(pair.astype(F32) + far[0, c.R : c.R + 2].astype(F32))
    return jnp.concatenate(halves, axis=1)


def chip_sums(c, one, parts, grid):
    def half_of(side):
        cols = lax.dynamic_slice_in_dim(one, side * c.half, c.half, 1)
        row = lax.dynamic_index_in_dim(parts, side, 0, True)
        return jnp.concatenate([cols, jnp.pad(row, ((0, 0), (0, c.half - c.W)))], axis=0)

    return half_of(grid) + swap_grid(half_of(1 - grid))


def expert_of(c, place, j):
    return j * EXP_DEV + place[3]


def window_slot(c, slot):
    return jnp.where(slot < c.Q, slot, slot + (c.SP - c.Q))


def count_places(c, rank_ref, rt_ref, slot_ref, blocks_ref, rtb_ref):
    pad = jnp.full((2, c.TP - c.T), -1, I32)
    rank = jnp.concatenate([rank_ref[...], pad], axis=1)
    rt = jnp.concatenate([rt_ref[...], pad], axis=1)
    side = 64
    index = lax.broadcasted_iota(I32, (side, c.TP), 0)
    rows = [(index == (rank[k : k + 1] >> 6)).astype(BF) for k in range(2)]
    cols = [index == (rank[k : k + 1] & 63) for k in range(2)]
    table = jnp.zeros((side, side), F32)
    for k in range(2):
        named = (rt[k : k + 1] + 1).astype(F32)
        table = table + dot_nt(rows[k], jnp.where(cols[k], named, 0.0).astype(BF))
    up_to = lax.broadcasted_iota(I32, (side, side), 0) < lax.broadcasted_iota(I32, (side, side), 1)
    above = lax.broadcasted_iota(I32, (side, side), 0) > lax.broadcasted_iota(I32, (side, side), 1)
    lane = lax.broadcasted_iota(I32, (1, 128), 1)
    named = [(table == e + 1.0).astype(F32) for e in range(c.E)]
    along = dot_nn(jnp.concatenate(named, axis=0).astype(BF), up_to.astype(BF))
    numbers = jnp.zeros((side, 128), F32)
    for e in range(c.E):
        numbers = numbers + jnp.where(lane == e, jnp.sum(named[e], axis=1, keepdims=True), 0.0)
    down = dot_nn(above.astype(BF), numbers.astype(BF))
    place_of = jnp.zeros((side, side), F32)
    for e in range(c.E):
        here = along[e * side : (e + 1) * side] + down[:, e : e + 1]
        place_of = place_of + named[e] * here
    place_of = place_of.astype(I32)
    high = (place_of >> 4).astype(F32).astype(BF)
    low = (place_of & 15).astype(F32).astype(BF)
    places = []
    for k in range(2):
        values = dot_tn(high, rows[k]) * 16.0 + dot_tn(low, rows[k])
        places.append(jnp.sum(jnp.where(cols[k], values, 0.0), axis=0, keepdims=True).astype(I32))
    for e in range(c.E):
        second = jnp.where(rt[1:2, :] == e, places[1], -1)
        slot_ref[e : e + 1, :] = jnp.where(rt[0:1, :] == e, places[0], second)
    for r in range(c.n):
        blocks_ref[r] = slot_ref[:, r * c.R : (r + 1) * c.R]
        rtb_ref[r] = jnp.concatenate([rt[:, r * c.R : (r + 1) * c.R]] * 4, axis=0)
    numbers = jnp.sum(numbers, axis=0, keepdims=True)
    return jnp.concatenate([numbers, jnp.zeros((1, c.half - 128), F32)], axis=1).astype(I32)


def fill_hot(c, place, slot_ref, hot_ref, halves):
    for j in range(c.X):
        row = window_slot(c, slot_ref[pl.ds(expert_of(c, place, j), 1), :])
        for index, half in enumerate(halves):
            slots = lax.broadcasted_iota(I32, (c.SP, c.TP), 0) + half * c.SP
            hot_ref[index, j * c.SP : (j + 1) * c.SP, :] = (slots == row).astype(BF)


def route_body(c, place, *refs):
    rank_ref, rt_ref, src_ref, slot_ref, blocks_ref, rtb_ref, out_ref, hot_ref, sum_ref = refs

    @pl.when(pl.program_id(0) == 0)
    def _():
        numbers = count_places(c, rank_ref, rt_ref, slot_ref, blocks_ref, rtb_ref)
        sum_ref[0:1, :] = (numbers >> 4).astype(F32)
        sum_ref[1:2, :] = (numbers & 15).astype(F32)
        fill_hot(c, place, slot_ref, hot_ref, (0, 1))

    for half in range(2):
        acc = dot_nn(hot_ref[half, :, : c.T], src_ref[...])
        for j in range(c.X):
            at = (2 * j + half) * c.SP
            out_ref[at : at + c.SP, :] = acc[j * c.SP : (j + 1) * c.SP].astype(BF)
            if half == 0:

                @pl.when(pl.program_id(0) == 0)
                def _():
                    tile = acc[(j + 1) * c.SP - 16 : (j + 1) * c.SP]
                    tile = last_rows(c, tile, sum_ref[0:1, :], sum_ref[1:2, :])
                    out_ref[at + c.SP - 16 : at + c.SP, :] = tile.astype(BF)


def route(c, order, place, routes, priority, source):
    rank = priority.T
    rt = routes.T
    outs = [
        shape_of((c.E, c.TP), I32),
        shape_of((c.n, c.E, c.R), I32),
        shape_of((c.n, 8, c.R), I32),
        shape_of((2 * c.X * c.SP, c.D), BF),
    ]
    result = call(
        order,
        functools.partial(route_body, c),
        place,
        [rank, rt, source],
        [whole(rank), whole(rt)]
        + [pl.BlockSpec((c.T, c.half), lambda i, s: (0, i ^ s[2]))],
        outs,
        [whole(o) for o in outs[:3]] + [cols_of((2 * c.X * c.SP, c.half))],
        (2,),
        [pltpu.VMEM((2, c.X * c.SP, c.TP), BF), pltpu.VMEM((8, c.half), F32)],
        name="route",
    )
    return (*result[:3], result[3].reshape(c.X, 2 * c.SP, c.D))


def keep_body(c, place, tail_ref, slot_ref, rt_ref, mine_ref, keep_ref, lane_ref):
    earlier = jnp.zeros((1, 128), F32)
    for b in range(c.X):
        high, low = last_pair(c, tail_ref[b], 128)
        earlier = earlier + jnp.where(b < place[0], high * 16.0 + low, 0.0)
    wide = (c.E, 128)
    eye = lax.broadcasted_iota(I32, wide, 0) == lax.broadcasted_iota(I32, wide, 1)
    offset = jnp.sum(jnp.where(eye, earlier, 0.0), axis=1, keepdims=True).astype(I32)
    slot = slot_ref[0]
    kept = (slot >= 0) & (slot + offset < c.cap)
    slots = jnp.where(kept, window_slot(c, slot), -1)
    expert = lax.broadcasted_iota(I32, (c.E, 1), 0)
    for j in range(8):
        if j < c.X:
            here = jnp.where(expert == expert_of(c, place, j), slots, -1)
            mine_ref[0, j : j + 1, :] = jnp.max(here, axis=0, keepdims=True)
        else:
            mine_ref[0, j : j + 1, :] = jnp.full((1, c.R), -1, I32)
    rows = []
    for k in range(2):
        picked = jnp.where((rt_ref[0, k : k + 1, :] == expert) & kept, 1.0, 0.0)
        rows.append(jnp.sum(picked, axis=0, keepdims=True))
    keep_ref[0] = jnp.concatenate(rows * 4, axis=0)

    @pl.when(pl.program_id(0) == place[1])
    def _():
        lane_ref[...] = jnp.where(kept, 1.0, 0.0)


def keep_of(c, order, place, rows, blocks, rt):
    outs = [
        shape_of((c.n, 8, c.R), I32),
        shape_of((c.n, 8, c.R), F32),
        shape_of((c.E, c.R), F32),
    ]
    tail = pl.BlockSpec((c.X, 16, c.half), lambda i, s: (0, c.SP // 16 - 1, 0))
    return call(
        order,
        functools.partial(keep_body, c),
        place,
        [rows, blocks, rt],
        [tail, rows_of((1, c.E, c.R)), rows_of((1, 8, c.R))],
        outs,
        [rows_of((1, 8, c.R)), rows_of((1, 8, c.R)), whole(outs[2])],
        (c.n,),
        name="keep",
    )


def last_rows(c, tile, high, low):
    row = lax.broadcasted_iota(I32, (16, 1), 0)
    return jnp.where(row == 14, high, jnp.where(row == 15, low, tile))


def put_gates(c, place, hot_ref, weights, acc, out_ref):
    gates = dot_nn(hot_ref[0], weights)
    lane = lax.broadcasted_iota(I32, (1, 128), 1)
    wide = (c.SP, c.half)
    eye = lax.broadcasted_iota(I32, wide, 0) == lax.broadcasted_iota(I32, wide, 1)
    for j in range(c.X):
        e = expert_of(c, place, j)
        mine = gates[j * c.SP : (j + 1) * c.SP]
        rows = []
        for at in (e, e + 64):
            col = jnp.sum(jnp.where(lane == at, mine, 0.0), axis=1, keepdims=True)
            rows.append(jnp.sum(jnp.where(eye, col, 0.0), axis=0, keepdims=True))
        end = (j + 1) * c.SP
        tile = last_rows(c, acc[end - 16 : end], rows[0], rows[1])
        out_ref[end - 16 : end, :] = tile.astype(BF)


def dispatch_body(c, half, place, slot_ref, src_ref, weight_ref, out_ref, hot_ref):
    @pl.when(pl.program_id(0) == 0)
    def _():
        fill_hot(c, place, slot_ref, hot_ref, (half,))

    acc = dot_nn(hot_ref[0], src_ref[...])
    out_ref[...] = acc.astype(BF)

    @pl.when(pl.program_id(0) == 0)
    def _():
        put_gates(c, place, hot_ref, weight_ref[...], acc, out_ref)


def dispatch(c, order, place, slot, source, weight, half):
    return call(
        order,
        functools.partial(dispatch_body, c, half),
        place,
        [slot, source, weight],
        [whole(slot), pl.BlockSpec((c.TP, c.half), lambda i, s: (0, i ^ s[2])), whole(weight)],
        [shape_of((c.X * c.SP, c.D), BF)],
        [cols_of((c.X * c.SP, c.half))],
        (2,),
        [pltpu.VMEM((1, c.X * c.SP, c.TP), BF)],
        name="dispatch",
    )[0].reshape(c.X, c.SP, c.D)


def norm_rows(values):
    centred = values - jnp.mean(values, axis=-1, keepdims=True)
    inv_std = lax.rsqrt(jnp.mean(centred * centred, axis=-1, keepdims=True) + 1e-06)
    return centred * inv_std, inv_std


def norm_back(grad_norm, gain, normed, inv_std):
    scaled = grad_norm * gain
    return inv_std * (
        scaled
        - jnp.mean(scaled, axis=-1, keepdims=True)
        - normed * jnp.mean(scaled * normed, axis=-1, keepdims=True)
    )


def small_row(c, small_ref, index, count=1):
    return small_ref[index : index + count, :].astype(F32)


def own_cols(c, place):
    return pl.ds(pl.multiple_of(place[2] * c.half, c.half), c.half)


def other_cols(c, place):
    return pl.ds(pl.multiple_of((1 - place[2]) * c.half, c.half), c.half)


def live_rows(c, first, count):
    return (first + lax.broadcasted_iota(I32, (count, 1), 0)) < c.T


def qkv_body(c, place, *refs):
    tok_ref, small_ref, own_ref, oth_ref, hid_ref, qkv_ref, normed_ref, mix_ref, w_ref, all_ref = refs
    step = pl.program_id(0)

    @pl.when(step == 0)
    def _():
        mix_ref[...] = jnp.zeros_like(mix_ref)
        for part in range(3):
            lanes = slice(part * c.W, (part + 1) * c.W)
            w_ref[own_cols(c, place), lanes] = own_ref[part]
            w_ref[other_cols(c, place), lanes] = oth_ref[part]

    @pl.when(step < c.n)
    def _():
        live = live_rows(c, step * c.R, c.R)
        values = jnp.where(live, tok_ref[...].astype(F32), 0.0)
        normed, _ = norm_rows(values)
        hidden = normed * small_row(c, small_ref, 0) + small_row(c, small_ref, 2)
        normed_ref[...] = normed.astype(BF)
        hidden = jnp.where(live, hidden, 0.0).astype(BF)
        hid_ref[...] = hidden
        acc = dot_nn(hidden, w_ref[...])
        bias = small_row(c, small_ref, 5)
        zero = jnp.zeros((1, c.W), F32)
        shift = jnp.concatenate([bias[:, : c.W], zero, bias[:, c.half : c.half + c.W]], axis=1)
        result = (acc + shift).astype(BF)
        qkv_ref[...] = result
        all_ref[pl.ds(pl.multiple_of(step * c.R, 16), c.R), :] = result

    @pl.when(step >= c.n)
    def _():
        attend(c, step - c.n, all_ref, mix_ref)


def image_window(c, image):
    start = image * IMG_LEN
    low = pl.multiple_of(start // 16 * 16, 16)
    return low, start - low


def groups_of(c):
    lanes = min(128, c.W)
    return [(at, lanes) for at in range(0, c.W, lanes)]


def head_mask(lanes, head):
    lane = lax.broadcasted_iota(I32, (1, lanes), 1)
    return (lane >= head * HEAD) & (lane < (head + 1) * HEAD)


def stack_heads(c, values):
    heads = range(c.W // HEAD)
    return jnp.concatenate([jnp.where(head_mask(c.W, h), values, BF(0)) for h in heads], axis=0)


def pick_heads(c, values):
    total = None
    for h in range(c.W // HEAD):
        part = jnp.where(head_mask(c.W, h), values[h * c.win : (h + 1) * c.win], 0.0)
        total = part if total is None else total + part
    return total


def attend(c, image, qkv_ref, mix_ref):
    low, off = image_window(c, image)
    row = lax.broadcasted_iota(I32, (c.win, 1), 0)
    col = lax.broadcasted_iota(I32, (1, c.win), 1)
    in_row = (row >= off) & (row < off + IMG_LEN)
    in_col = (col >= off) & (col < off + IMG_LEN)
    q = stack_heads(c, qkv_ref[pl.ds(low, c.win), : c.W] * BF(HEAD**-0.5))
    k = qkv_ref[pl.ds(low, c.win), c.W : 2 * c.W]
    v = qkv_ref[pl.ds(low, c.win), 2 * c.W :]
    scores = jnp.where(in_col, dot_nt(q, k), LOW)
    exps = jnp.exp(scores - jnp.max(scores, axis=-1, keepdims=True))
    probs = exps * (1.0 / jnp.sum(exps, axis=-1, keepdims=True))
    total = pick_heads(c, dot_nn(probs.astype(BF), v)).astype(BF)
    for group, (at, lanes) in enumerate(groups_of(c)):
        old = mix_ref[group, pl.ds(low, c.win), :]
        mix_ref[group, pl.ds(low, c.win), :] = jnp.where(in_row, total[:, at : at + lanes], old)


def attend_back_body(c, place, qkv_ref, *refs):
    pieces, (out_ref, sums_ref, grad_ref) = refs[: c.n], refs[c.n :]

    @pl.when(pl.program_id(0) == 0)
    def _():
        out_ref[...] = jnp.zeros_like(out_ref)
        sums_ref[...] = jnp.zeros_like(sums_ref)
        for k in range(c.n):
            at = pl.multiple_of((place[1] ^ k) * c.R, 16)
            grad_ref[pl.ds(at, c.R), :] = pieces[k][...]

    low, off = image_window(c, pl.program_id(0))
    row = lax.broadcasted_iota(I32, (c.win, 1), 0)
    in_row = (row >= off) & (row < off + IMG_LEN)
    scale = HEAD**-0.5
    q = stack_heads(c, qkv_ref[pl.ds(low, c.win), : c.W] * BF(scale))
    k = qkv_ref[pl.ds(low, c.win), c.W : 2 * c.W]
    v = qkv_ref[pl.ds(low, c.win), 2 * c.W :]
    do = stack_heads(c, jnp.where(in_row, grad_ref[pl.ds(low, c.win), :], BF(0)))
    scores = jnp.where(in_row, dot_nt(k, q), LOW)
    exps = jnp.exp(scores - jnp.max(scores, axis=0, keepdims=True))
    soft = exps * (1.0 / jnp.sum(exps, axis=0, keepdims=True))
    dp = dot_nt(v, do)
    delta = jnp.sum(soft * dp, axis=0, keepdims=True)
    ds = (soft * (dp - delta)).astype(BF)
    dq = pick_heads(c, dot_tn(ds, k)) * scale
    dk = dot_nn(ds, q)
    dv = dot_nn(soft.astype(BF), do)
    for part, grad in enumerate((dq, dk, dv)):
        lanes = slice(part * c.W, (part + 1) * c.W)
        low_grad = jnp.where(in_row, grad, 0.0).astype(BF)
        old = out_ref[pl.ds(low, c.win), lanes]
        out_ref[pl.ds(low, c.win), lanes] = jnp.where(in_row, low_grad, old)
        sums_ref[0:1, lanes] += jnp.sum(low_grad.astype(F32), axis=0, keepdims=True)


def middle_rows(c, place, step, mixes, tok_ref, small_ref, table_ref, slot_ref, proj_ref):
    branch = dot_nn(jnp.concatenate([mix[...] for mix in mixes], axis=1), proj_ref[...])
    live = live_rows(c, step * c.R, c.R)
    tok = jnp.where(live, tok_ref[...].astype(F32), 0.0)
    after = tok + branch + small_row(c, small_ref, 4)
    normed, _ = norm_rows(after)
    hidden = (normed * small_row(c, small_ref, 1) + small_row(c, small_ref, 3)).astype(BF)
    router = table_ref[c.E : 2 * c.E, :]
    logits = dot_nt(router, hidden)
    exps = jnp.exp(logits - jnp.max(logits, axis=0, keepdims=True))
    probs = exps / jnp.sum(exps, axis=0, keepdims=True)
    weight = jnp.where(slot_ref[0] >= 0, probs, 0.0)
    high, rest = split_low(weight)
    lane = lax.broadcasted_iota(I32, (c.E, 128), 1)
    index = lax.broadcasted_iota(I32, (c.E, 128), 0)
    both = dot_tn(high, (lane == index).astype(BF)) + dot_tn(rest, (lane == index + 64).astype(BF))
    return after, hidden, probs, both.astype(BF)


def middle_body(c, place, *refs):
    refs = list(refs)
    count = c.n * len(groups_of(c))
    mixes, refs = refs[:count], refs[count:]
    w_ref, tok_ref, small_ref, table_ref, blocks_ref, slot_ref = refs[:6]
    hid_ref, weight_ref, after_ref, probs_ref, out_ref = refs[6:11]
    proj_ref, hids_ref, weights_ref, hot_ref = refs[11:]
    step = pl.program_id(0)

    @pl.when(step == 0)
    def _():
        for k in range(c.n):
            for h in range(2):
                cols = slice(h * c.half, (h + 1) * c.half)
                proj_ref[k * c.W : (k + 1) * c.W, cols] = w_ref[(place[1] ^ k) * 2 + h]

    @pl.when(step < c.n)
    def _():
        after, hidden, probs, weight = middle_rows(
            c, place, step, mixes, tok_ref, small_ref, table_ref, blocks_ref, proj_ref
        )
        rows = pl.ds(pl.multiple_of(step * c.R, 16), c.R)
        hid_ref[...] = hidden
        hids_ref[rows, :] = hidden
        weight_ref[...] = weight
        weights_ref[rows, :] = weight

        @pl.when(step == place[1])
        def _():
            after_ref[...] = after
            probs_ref[...] = probs

    @pl.when(step == c.n)
    def _():
        fill_hot(c, place, slot_ref, hot_ref, (0,))

    @pl.when(step >= c.n)
    def _():
        cols = pl.multiple_of(((step - c.n) ^ place[2]) * c.half, c.half)
        acc = dot_nn(hot_ref[0], hids_ref[:, pl.ds(cols, c.half)])
        out_ref[...] = acc.astype(BF)

        @pl.when(step == c.n)
        def _():
            put_gates(c, place, hot_ref, weights_ref[...], acc, out_ref)


def middle(c, order, place, mixes, proj, tokens, small, table, blocks, slot):
    def early(dims):
        return pl.BlockSpec(dims, lambda i, s: (jnp.minimum(i, c.n - 1),) + (0,) * (len(dims) - 1))

    args = [pair[0] for pair in flat(mixes)] + [proj, tokens, small, table, blocks, slot]
    specs = [
        pl.BlockSpec((None, c.R, a.shape[2]), lambda i, s, at=at: (at, jnp.minimum(i, c.n - 1), 0))
        for a, at in flat(mixes)
    ]
    specs += [whole(proj), early((c.R, c.D)), whole(small), whole(table)]
    specs += [early((1, c.E, c.R)), whole(slot)]
    outs = [
        shape_of((c.TP, c.D), BF),
        shape_of((c.TP, 128), BF),
        shape_of((c.R, c.D), F32),
        shape_of((c.E, c.R), F32),
        shape_of((c.X * c.SP, c.D), BF),
    ]
    late = pl.BlockSpec((c.X * c.SP, c.half), lambda i, s: (0, jnp.maximum(i - c.n, 0)))
    result = call(
        order,
        functools.partial(middle_body, c),
        place,
        args,
        specs,
        outs,
        [early((c.R, c.D)), early((c.R, 128)), whole(outs[2]), whole(outs[3]), late],
        (c.n + 2,),
        [
            pltpu.VMEM((c.D, c.D), BF),
            pltpu.VMEM((c.TP, c.D), BF),
            pltpu.VMEM((c.TP, 128), BF),
            pltpu.VMEM((1, c.X * c.SP, c.TP), BF),
        ],
        name="middle",
    )
    return (*result[:4], result[4].reshape(c.X, c.SP, c.D))


def fill_packs(c, place, tails, packs):
    lane = lax.broadcasted_iota(I32, (1, 128), 1)
    here = place[0] * EXP_DEV + place[3]
    state = [jnp.zeros((1, 1), F32)] * 3
    for j in range(c.X):
        high, low = last_pair(c, tails[j], 128)
        number = jnp.sum(jnp.where(lane == here, high * 16.0 + low, 0.0), axis=1, keepdims=True)
        kept = jnp.clip(c.cap - state[0], 0.0, number)
        first = jnp.minimum(kept, float(c.Q))
        sizes = first, kept - first
        for half in range(2):
            wide = (c.CR[half], c.SP)
            slot = lax.broadcasted_iota(I32, wide, 1)
            at = lax.broadcasted_iota(I32, wide, 0) - state[1 + half].astype(I32)
            hot = (at == slot) & (slot < sizes[half].astype(I32))
            packs[half][:, j * c.SP : (j + 1) * c.SP] = hot.astype(BF)
        state = [state[0] + number, state[1] + sizes[0], state[2] + sizes[1]]


def last_pair(c, tile, lanes):
    tile = tile[:, :lanes].astype(F32)
    return tile[14:15, :], tile[15:16, :]


def row_chunks(rows, size):
    return [slice(at, min(at + size, rows)) for at in range(0, rows, size)]


def grad_active_body(c, place, rows_ref, own_ref, oth_ref, *outs):
    gas, all_ref, packs = outs[:2], outs[2], outs[3:]

    @pl.when(pl.program_id(0) == 0)
    def _():
        tails = [rows_ref[j, c.SP - 16 : c.SP, :] for j in range(c.X)]
        fill_packs(c, place, tails, packs)
        for half, base in enumerate((0, c.CR[0])):
            rows = [rows_ref[j, half * c.SP : (half + 1) * c.SP, :] for j in range(c.X)]
            got = dot_nn(packs[half][...], jnp.concatenate(rows, axis=0))
            all_ref[base : base + c.CR[half], :] = got.astype(BF)

    weights = jnp.concatenate([own_ref[...], oth_ref[...]], axis=1)
    for half, base in enumerate((0, c.CR[0])):
        for at in row_chunks(c.CR[half], 320):
            values = all_ref[base + at.start : base + at.stop, :]
            gas[half][at, :] = dot_nt(values, weights).astype(BF)


def grad_active(c, order, place, rows, own_w, oth_w):
    outs = [shape_of((count, c.F), BF) for count in c.CR] + [shape_of((sum(c.CR), c.D), BF)]
    outs += [shape_of((count, c.X * c.SP), BF) for count in c.CR]
    return call(
        order,
        functools.partial(grad_active_body, c),
        place,
        [rows, own_w, oth_w],
        [whole(rows, 1)] + [rows_of((c.fblk, c.half))] * 2,
        outs,
        [cols_of((count, c.fblk)) for count in c.CR] + [whole(o) for o in outs[2:]],
        (c.F // c.fblk,),
        name="grad_active",
    )


def expert_body(c, half, place, *refs):
    rows_ref, pack_ref, own_ref, oth_ref, bias_ref, ga_ref = refs[:6]
    act_ref, gp_ref, gb_ref, all_ref, col_ref, back_ref = refs[6:12]
    acc_ref, dot_ref, row_ref, wide_ref = refs[12:]
    step = pl.program_id(0)

    @pl.when(step == 0)
    def _():
        acc_ref[...] = jnp.zeros_like(acc_ref)
        dot_ref[...] = jnp.zeros_like(dot_ref)
        all_ref[...] = dot_nn(pack_ref[...], rows_ref[...]).astype(BF)
        eye = lax.broadcasted_iota(I32, (c.SP, c.SP), 0) == lax.broadcasted_iota(I32, (c.SP, c.SP), 1)
        lane = lax.broadcasted_iota(I32, (1, 128), 1)
        for j in range(c.X):
            end = (j + 1) * c.SP
            high, low = last_pair(c, rows_ref[end - 16 : end, :], c.SP)
            high = jnp.sum(jnp.where(eye, high, 0.0), axis=1, keepdims=True)
            low = jnp.sum(jnp.where(eye, low, 0.0), axis=1, keepdims=True)
            both = jnp.where(lane == 0, high, jnp.where(lane == 1, low, 0.0))
            wide_ref[j * c.SP : end, :] = both.astype(BF)
        both = dot_nn(pack_ref[...], wide_ref[...])
        col_ref[...] = jnp.broadcast_to(both[:, 0:1] + both[:, 1:2], (c.CR[half], 128))

    bias = bias_ref[...]
    weights = jnp.concatenate([own_ref[...], oth_ref[...]], axis=0)
    summed = jnp.zeros((1, c.fblk), F32)
    lead = 0.7978845608028654
    cube = lead * 0.044715
    chunks = row_chunks(c.CR[half], 224)
    ahead = dot_nn(all_ref[chunks[0], :], weights)
    for i, rows_at in enumerate(chunks):
        pre = ahead + bias
        if i + 1 < len(chunks):
            ahead = dot_nn(all_ref[chunks[i + 1], :], weights)
        square = pre * pre
        turn = jnp.tanh(pre * (cube * square + lead))
        above = 1.0 + turn
        active = (0.5 * pre) * above
        slope = above * (1.0 + (1.0 - turn) * (pre * (3 * cube * square + lead)))
        ga = ga_ref[rows_at, :].astype(F32)
        product = active * ga
        part = product[:, 0:128]
        for lane in range(128, c.fblk, 128):
            part = part + product[:, lane : lane + 128]
        dot_ref[rows_at, :] += part
        grad = ga * slope * (0.5 * col_ref[rows_at, 0:1])
        act_ref[rows_at, :] = active.astype(BF)
        grad_low = grad.astype(BF)
        gp_ref[rows_at, :] = grad_low
        summed = summed + jnp.sum(grad, axis=0, keepdims=True)
        acc_ref[rows_at, :] += dot_nt(grad_low, weights)
    gb_ref[...] = jnp.broadcast_to(summed, (8, c.fblk))

    @pl.when(step == pl.num_programs(0) - 1)
    def _():
        ones = jnp.ones((8, 128), BF)
        row_ref[...] = jnp.zeros_like(row_ref)
        back_ref[...] = dot_tn(pack_ref[...], acc_ref[...].astype(BF)).astype(BF)
        a, rest = split_low(dot_ref[...])
        total = dot_nt(ones, a) + dot_nt(ones, rest)
        high, low = split_low(total)
        high = dot_nn(high, pack_ref[...])
        low = dot_nn(low, pack_ref[...])
        for j in range(c.X):
            end = (j + 1) * c.SP
            row_ref[0:8, : c.SP] = high[:, j * c.SP : end]
            row_ref[8:16, : c.SP] = low[:, j * c.SP : end]
            tile = back_ref[end - 16 : end, : c.half].astype(F32)
            tile = last_rows(c, tile, row_ref[0:1, :], row_ref[8:9, :])
            back_ref[end - 16 : end, : c.half] = tile.astype(BF)


def expert(c, order, place, half, rows, pack, own_w, oth_w, bias, ga):
    rows = rows.reshape(c.X * c.SP, c.D)
    args = [rows, pack, own_w, oth_w, bias, ga]
    count = c.CR[half]
    specs = [whole(rows, 1), whole(pack, 1)]
    specs += [cols_of((c.half, c.fblk))] * 2
    specs += [cols_of((1, c.fblk)), cols_of((count, c.fblk))]
    outs = [
        shape_of((count, c.F), BF),
        shape_of((count, c.F), BF),
        shape_of((8, c.F), F32),
    ]
    out_specs = [cols_of((count, c.fblk))] * 2 + [cols_of((8, c.fblk))]
    late = [shape_of((count, c.D), BF), shape_of((count, 128), F32)]
    late.append(shape_of((c.X * c.SP, c.D), BF))
    result = call(
        order,
        functools.partial(expert_body, c, half),
        place,
        args,
        specs,
        outs + late,
        out_specs + [whole(o, 1) for o in late],
        (c.F // c.fblk,),
        [
            pltpu.VMEM((count, c.D), F32),
            pltpu.VMEM((count, 128), F32),
            pltpu.VMEM((16, c.half), F32),
            pltpu.VMEM((c.X * c.SP, 128), BF),
        ],
        name="expert",
    )
    return (*result[:5], result[5].reshape(c.X, c.SP, c.D))


def produce_body(c, place, *refs):
    cols, acts, packs, own_ref, oth_ref, out_ref = refs[:2], refs[2:4], refs[4:6], *refs[6:9]
    accs = refs[9:]
    step = pl.program_id(0)

    @pl.when(step == 0)
    def _():
        for acc_ref in accs:
            acc_ref[...] = jnp.zeros_like(acc_ref)

    weights = jnp.concatenate([own_ref[...], oth_ref[...]], axis=1)
    for half in range(2):
        for at in row_chunks(c.CR[half], 320):
            accs[half][at, :] += dot_nn(acts[half][at, :], weights)

    @pl.when(step == pl.num_programs(0) - 1)
    def _():
        for half in range(2):
            values = (accs[half][...] * cols[half][:, 0:1]).astype(BF)
            values = dot_tn(packs[half][...], values).astype(BF)
            for j in range(c.X):
                rows = values[j * c.SP : (j + 1) * c.SP]
                out_ref[j, half * c.SP : (half + 1) * c.SP, :] = rows


def produce(c, order, place, cols, acts, packs, own_w, oth_w):
    out = shape_of((c.X, 2 * c.SP, c.D), BF)
    return call(
        order,
        functools.partial(produce_body, c),
        place,
        [*cols, *acts, *packs, own_w, oth_w],
        [whole(col) for col in cols]
        + [cols_of((rows, c.fblk)) for rows in c.CR]
        + [whole(pack) for pack in packs]
        + [rows_of((c.fblk, c.half))] * 2,
        [out],
        [whole(out, 1)],
        (c.F // c.fblk,),
        [pltpu.VMEM((rows, c.D), F32) for rows in c.CR],
        name="produce",
    )[0]


def grad_second_body(c, own, place, *refs):
    all_ref, cols, acts = refs[0], refs[1:3], refs[3:5]
    out_ref, row_ref = refs[-2:]

    @pl.when(pl.program_id(0) == 0)
    def _():
        for half, base in enumerate((0, c.CR[0])):
            rows_at = slice(base, base + c.CR[half])
            row_ref[rows_at, :] = (all_ref[rows_at, :].astype(F32) * cols[half][:, 0:1]).astype(BF)

    acc = dot_tn(acts[0][...], row_ref[: c.CR[0], :])
    acc = acc + dot_tn(acts[1][...], row_ref[c.CR[0] :, :])
    if own:
        acc = acc + refs[5][...].astype(F32)
    out_ref[...] = acc.astype(out_ref.dtype)


def grad_second(c, order, place, rows, cols, acts, add=None):
    own = add is not None
    args = [rows, *cols, *acts]
    total = sum(c.CR)
    specs = [pl.BlockSpec((total, c.half), lambda i, s: (0, 0 if own else 1))]
    specs += [whole(col) for col in cols] + [cols_of((count, c.fblk)) for count in c.CR]
    if own:
        args.append(add)
        specs.append(rows_of((c.fblk, c.half)))
    out = shape_of((c.F, c.half), F32 if own else BF)
    return call(
        order,
        functools.partial(grad_second_body, c, own),
        place,
        args,
        specs,
        [out],
        [rows_of((c.fblk, c.half))],
        (c.F // c.fblk,),
        [pltpu.VMEM((total, c.half), BF)],
        name="grad_second",
    )[0]


def grad_first_body(c, own, place, *refs):
    acc = dot_tn(refs[0][...], refs[2][...]) + dot_tn(refs[1][...], refs[3][...])
    if own:
        acc = acc + refs[4][...].astype(F32)
    refs[-1][...] = acc.astype(refs[-1].dtype)


def grad_first(c, order, place, rows, gps, add=None):
    own = add is not None
    args = [*rows, *gps]
    specs = [pl.BlockSpec((count, c.half), lambda i, s: (0, 0 if own else 1)) for count in c.CR]
    specs += [cols_of((count, c.fblk)) for count in c.CR]
    if own:
        args.append(add)
        specs.append(cols_of((c.half, c.fblk)))
    out = shape_of((c.half, c.F), F32 if own else BF)
    return call(
        order,
        functools.partial(grad_first_body, c, own),
        place,
        args,
        specs,
        [out],
        [cols_of((c.half, c.fblk))],
        (c.F // c.fblk,),
        name="grad_first",
    )[0]


def combine_body(c, with_dots, place, *refs):
    refs = list(refs)
    extras = [] if with_dots else [refs.pop(0), refs.pop(0)]
    halves = 2 if with_dots else 1
    rows, refs = refs[:halves], refs[halves:]
    tails = []
    if with_dots:
        tails, refs = refs[:2], refs[2:]
    mine_ref = refs.pop(0)
    groups = [(0, g) for g in groups_a(c)] + [(1, g) for g in groups_b(c)]
    outs, (hot_ref, row_ref) = refs[: len(groups)], refs[len(groups) :]
    pad = hot_ref.shape[1] // c.X

    @pl.when(pl.program_id(0) == 0)
    def _():
        row_ref[...] = jnp.zeros_like(row_ref)
        slots = lax.broadcasted_iota(I32, (c.R, pad), 1)
        for k in range(c.n):
            at = pl.multiple_of((place[1] ^ k) * c.R, 16)
            for j in range(c.X):
                hot = (mine_ref[pl.ds(at, c.R), j : j + 1] == slots).astype(BF)
                hot_ref[k * c.R : (k + 1) * c.R, j * pad : (j + 1) * pad] = hot
        if with_dots:
            wide = (c.SP, c.half)
            eye = lax.broadcasted_iota(I32, wide, 0) == lax.broadcasted_iota(I32, wide, 1)
            lane = lax.broadcasted_iota(I32, (1, 128), 1)
            for half in range(2):
                for j in range(c.X):
                    high, low = last_pair(c, tails[half][j], c.half)
                    high = jnp.sum(jnp.where(eye, high, 0.0), axis=1, keepdims=True)
                    low = jnp.sum(jnp.where(eye, low, 0.0), axis=1, keepdims=True)
                    e = expert_of(c, place, j)
                    cols = jnp.where(lane == e, high, jnp.where(lane == e + 64, low, 0.0))
                    at = j * pad + half * c.SP
                    row_ref[at : at + c.SP, :128] = cols.astype(BF)
            pulls = dot_nn(hot_ref[...], row_ref[:, :128]).astype(BF)
            expert = lax.broadcasted_iota(I32, (c.E, 128), 0)
            lane = lax.broadcasted_iota(I32, (c.E, 128), 1)
            pick = ((lane == expert) | (lane == expert + 64)).astype(BF)
            for (side, group), out_ref in zip(groups, outs):
                for at, k in enumerate(group):
                    if side == 0:
                        got = dot_nt(pick, pulls[k * c.R : (k + 1) * c.R])
                        out_ref[at, c.R :, :] = jnp.zeros((c.E, c.half), BF)
                        out_ref[at, c.R :, : c.R] = got.astype(BF)

    for half, rows_ref in enumerate(rows):
        size = rows_ref.shape[1]
        for j in range(c.X):
            at = j * pad + half * size
            row_ref[at : at + size, :] = rows_ref[j]
    result = dot_nn(hot_ref[...], row_ref[...]).astype(BF)
    for half in range(2):

        @pl.when(pl.program_id(0) == half)
        def _():
            for (side, group), out_ref in zip(groups, outs):
                if side == half:
                    for at, k in enumerate(group):
                        out_ref[at, : c.R, :] = result[k * c.R : (k + 1) * c.R]
                        if extras:
                            more = extras[0].shape[1] // 2
                            extra = [e[k, half * more : (half + 1) * more, :] for e in extras]
                            total = extra[0].astype(F32) + extra[1].astype(F32)
                            out_ref[at, c.R :, :] = total.astype(BF)


def combine(c, order, place, rows, mine, extra=None, cost=0):
    pad = up(2 * c.SP, 128)
    args = list(rows)
    specs = [pl.BlockSpec((c.X, r.shape[1], c.half), lambda i, s: (0, 0, i ^ s[2])) for r in rows]
    if extra is None:
        args += list(rows)
        specs += [pl.BlockSpec((c.X, 16, c.half), lambda i, s: (0, c.SP // 16 - 1, 0))] * 2
        outs = piece_outs(c, c.E)
    else:
        args = [*extra, *args]
        specs = [whole(e) for e in extra] + specs
        outs = piece_outs(c, extra[0].shape[1] // 2, extra[0].shape[1] // 2)
    args.append(mine)
    specs.append(whole(mine))
    result = call(
        order,
        functools.partial(combine_body, c, extra is None),
        place,
        args,
        specs,
        outs,
        [whole(o, 1) for o in outs],
        (2,),
        [pltpu.VMEM((c.n * c.R, c.X * pad), BF), pltpu.VMEM((c.X * pad, c.half), BF)],
        name="combine",
        cost=cost,
    )
    return list(result)


def back_two_body(c, place, *refs):
    refs = list(refs)
    groups = groups_of(c)
    heads, refs = refs[: c.n * len(groups)], refs[c.n * len(groups) :]
    count = (len(refs) - 13 - c.n) // 2
    a, b, refs = refs[:count], refs[count : 2 * count], refs[2 * count :]
    w_ref, after_ref, probs_ref, keep_ref = refs[:4]
    cot_ref, hid_ref, small_ref, table_ref, ga_ref, proj_own_ref, proj_oth_ref = refs[4:11]
    mixes, (gb_ref, sums_ref) = refs[11:-2], refs[-2:]
    sum_a = add_up(a)
    live = live_rows(c, place[1] * c.R, c.R)
    cot = jnp.where(live, cot_ref[...], BF(0))
    eshift = table_ref[: c.E, :]
    router = table_ref[c.E : 2 * c.E, :]
    kept = keep_ref[...] > 0
    pulls = jnp.where(kept, sum_a[c.R :, : c.R] + dot_nt(eshift, cot), 0.0)
    probs = probs_ref[...]
    glog = (probs * (pulls - jnp.sum(probs * pulls, axis=0, keepdims=True))).astype(BF)
    two = jnp.concatenate([sum_a[: c.R], add_up(b)], axis=1) + dot_tn(glog, router)
    normed, inv_std = norm_rows(after_ref[...])
    grad_after = cot.astype(F32) + norm_back(two, small_row(c, small_ref, 1), normed, inv_std)
    ga_ref[...] = grad_after
    low = grad_after.astype(BF)
    gb_ref[...] = low
    high, rest = split_low(probs * keep_ref[...])
    hid = jnp.where(live, hid_ref[...], BF(0))
    sums_ref[0:1, :] = jnp.sum(two * normed, axis=0, keepdims=True)
    sums_ref[1:2, :] = jnp.sum(two, axis=0, keepdims=True)
    sums_ref[2:3, :] = jnp.sum(low.astype(F32), axis=0, keepdims=True)
    sums_ref[3:8, :] = jnp.zeros((5, c.D), F32)
    sums_ref[8 : 8 + c.E, :] = dot_nn(high, cot) + dot_nn(rest, cot)
    sums_ref[8 + c.E : 8 + 2 * c.E, :] = dot_nn(glog, hid)
    for k in range(c.n):
        lane = place[1] ^ k
        mix = dot_nt(gb_ref[:, : c.half], w_ref[2 * lane])
        mix = mix + dot_nt(gb_ref[:, c.half :], w_ref[2 * lane + 1])
        mixes[k][...] = mix.astype(BF)
    height = sums_ref.shape[0]
    for cols, out_ref in ((own_cols(c, place), proj_own_ref), (other_cols(c, place), proj_oth_ref)):
        sums = sums_ref[:, cols].astype(BF)
        for k in range(c.n):
            for group, (at, lanes) in enumerate(groups):
                part = dot_tn(heads[k * len(groups) + group][...], gb_ref[:, cols])
                out_ref[k, at : at + lanes, :] = part.astype(BF)
            out_ref[k, c.W : c.W + height, :] = sums
            rest = out_ref.shape[1] - c.W - height
            out_ref[k, c.W + height :, :] = jnp.zeros((rest, c.half), BF)


def back_two(c, order, place, heads, sums, proj, lanes, cotangent, hidden, small, table):
    height = 8 + 2 * c.E
    rows = up(c.W + height, 32)
    args = [pair[0] for pair in flat(heads)]
    specs = [
        pl.BlockSpec((None, c.R, a.shape[2]), lambda i, s, at=at: (at, s[1], 0))
        for a, at in flat(heads)
    ]
    args += [*sums[0], *sums[1], proj, *lanes, cotangent, hidden, small, table]
    lane_rows = pl.BlockSpec((c.R, c.D), lambda i, s: (s[1], 0))
    specs += [first_block(a) for a in [*sums[0], *sums[1]]]
    specs += [whole(a) for a in [proj, *lanes]] + [lane_rows, lane_rows]
    specs += [whole(small), whole(table)]
    outs = [shape_of((c.R, c.D), F32)] + [shape_of((c.n, rows, c.half), BF)] * 2
    outs += [shape_of((c.R, c.W), BF) for _ in range(c.n)]
    result = call(
        order,
        functools.partial(back_two_body, c),
        place,
        args,
        specs,
        outs,
        [whole(o) for o in outs],
        (1,),
        [pltpu.VMEM((c.R, c.D), BF), pltpu.VMEM((height, c.D), F32)],
        name="back_two",
    )
    return (*result[:3], list(result[3:]))


def block_out_body(c, place, *refs):
    refs = list(refs)
    count = (len(refs) - 6) // 2
    a, b, refs = refs[:count], refs[count : 2 * count], refs[2 * count :]
    after_ref, probs_ref, keep_ref, table_ref, out_ref, proj_ref = refs
    high, low = split_low(probs_ref[...] * keep_ref[...])
    eshift = table_ref[: c.E, :]
    shift = dot_tn(high, eshift) + dot_tn(low, eshift)
    more = proj_ref.shape[0] // 2
    for h, pieces in enumerate((a, b)):
        cols = slice(h * c.half, (h + 1) * c.half)
        total = add_up([ref.at[: c.R, :] for ref in pieces])
        out_ref[h] = (after_ref[:, cols] + total + shift[:, cols]).astype(BF)
        proj_ref[h * more : (h + 1) * more, :] = same_sum(c, pieces, slice(c.R, c.R + more)).astype(BF)


def block_out(c, order, place, sums, after, probs, keep, table):
    args = [*sums[0], *sums[1], after, probs, keep, table]
    more = 2 * (sums[0][0].shape[1] - c.R)
    outs = [shape_of((2, c.R, c.half), BF), shape_of((more, c.half), BF)]
    return call(
        order,
        functools.partial(block_out_body, c),
        place,
        args,
        [first_block(a) for a in args[:-4]] + [whole(a) for a in args[-4:]],
        outs,
        [whole(o) for o in outs],
        (1,),
        name="block_out",
    )


def grad_one_body(c, place, dqkv_ref, normed_ref, own_ref, oth_ref, *outs):
    sums_ref = outs[-1]
    groups = [(0, g) for g in groups_a(c)] + [(1, g) for g in groups_b(c)]
    for side in range(2):
        cols = slice(side * c.half, (side + 1) * c.half)
        weights = [jnp.where(place[2] == side, own_ref[p], oth_ref[p]) for p in range(3)]
        gain = jnp.zeros((1, c.half), F32)
        shift = jnp.zeros((1, c.half), F32)
        for (where, group), out_ref in zip(groups, outs):
            if where != side:
                continue
            for row, k in enumerate(group):
                rows_at = pl.ds(pl.multiple_of((place[1] ^ k) * c.R, 16), c.R)
                acc = None
                for part in range(3):
                    rows = dqkv_ref[rows_at, part * c.W : (part + 1) * c.W]
                    term = dot_nt(rows, weights[part])
                    acc = term if acc is None else acc + term
                out_ref[row, : c.R, :] = acc.astype(BF)
                normed = normed_ref[rows_at, cols].astype(F32)
                gain = gain + jnp.sum(acc * normed, axis=0, keepdims=True)
                shift = shift + jnp.sum(acc, axis=0, keepdims=True)
        sums_ref[0:1, cols] = gain
        sums_ref[1:2, cols] = shift
        row = lax.broadcasted_iota(I32, (16, 1), 0)
        tile = jnp.where(row == 0, gain, jnp.where(row == 1, shift, 0.0)).astype(BF)
        for (where, group), out_ref in zip(groups, outs):
            if where == side:
                for at in range(len(group)):
                    out_ref[at, c.R :, :] = tile


def grad_one(c, order, place, dqkv, normed, own_w, oth_w):
    outs = piece_outs(c, 16, 16) + [shape_of((2, c.D), F32)]
    result = call(
        order,
        functools.partial(grad_one_body, c),
        place,
        [dqkv, normed, own_w, oth_w],
        [whole(dqkv), whole(normed), whole(own_w), whole(oth_w)],
        outs,
        [whole(o) for o in outs],
        (1,),
        name="grad_one",
    )
    return list(result[:-1]), result[-1]


def grad_qkv_body(c, place, hid_ref, dqkv_ref, own_ref, oth_ref):
    own_ref[0] = dot_tn(hid_ref[:, own_cols(c, place)], dqkv_ref[...]).astype(BF)
    oth_ref[0] = dot_tn(hid_ref[:, other_cols(c, place)], dqkv_ref[...]).astype(BF)


def grad_qkv(c, order, place, hidden, dqkv):
    specs = [whole(hidden, 1), cols_of((c.TP, c.W))]
    if c.W % 128:
        dqkv = dqkv.reshape(c.TP, 3, c.W).transpose(1, 0, 2)
        specs[1] = pl.BlockSpec((None, c.TP, c.W), lambda i, s: (i, 0, 0))
    return call(
        order,
        functools.partial(grad_qkv_body, c),
        place,
        [hidden, dqkv],
        specs,
        [shape_of((3, c.half, c.W), BF)] * 2,
        [rows_of((1, c.half, c.W))] * 2,
        (3,),
        name="grad_qkv",
    )


def back_one_body(c, place, *refs):
    refs = list(refs)
    count = (len(refs) - 4) // 2
    a, b, refs = refs[:count], refs[count : 2 * count], refs[2 * count :]
    tok_ref, after_ref, small_ref, out_ref = refs
    live = live_rows(c, place[1] * c.R, c.R)
    normed, inv_std = norm_rows(jnp.where(live, tok_ref[...].astype(F32), 0.0))
    one = jnp.concatenate([add_up(a)[: c.R], add_up(b)[: c.R]], axis=1)
    grad = after_ref[...] + norm_back(one, small_row(c, small_ref, 0), normed, inv_std)
    for h in range(2):
        out_ref[h] = grad[:, h * c.half : (h + 1) * c.half].astype(BF)


def back_one(c, order, place, sums, tokens, after, small):
    args = [*sums[0], *sums[1], tokens, after, small]
    lane_rows = pl.BlockSpec((c.R, c.D), lambda i, s: (s[1], 0))
    specs = [first_block(a) for a in args[:-3]] + [lane_rows, whole(after), whole(small)]
    out = shape_of((2, c.R, c.half), BF)
    return call(
        order,
        functools.partial(back_one_body, c),
        place,
        args,
        specs,
        [out],
        [whole(out)],
        (1,),
        name="back_one",
    )[0]


def assemble_body(c, place, *refs):
    pieces, out_ref = refs[:-1], refs[-1]
    for k in range(c.n):

        @pl.when((place[1] ^ k) == pl.program_id(0))
        def _():
            for h in range(2):
                values = pieces[2 * k + h][...].astype(out_ref.dtype)
                out_ref[:, h * c.half : (h + 1) * c.half] = values


def assemble(c, order, place, pieces, dtype):
    out = shape_of((c.T, c.D), dtype)
    return call(
        order,
        functools.partial(assemble_body, c),
        place,
        [pair[0] for pair in flat(pieces)],
        [
            pl.BlockSpec((None, c.R, c.half), lambda i, s, at=at: (at, 0, 0))
            for _, at in flat(pieces)
        ],
        [out],
        [rows_of((c.R, c.D))],
        (-(-c.T // c.R),),
        name="assemble",
    )[0]


def local(
    tokens,
    cotangent,
    w_qkv,
    qv_bias,
    w_proj,
    proj_bias,
    norm_gains,
    norm_shifts,
    w_router,
    expert_shift,
    w_first,
    w_second,
    first_bias,
    routes,
    priority,
):
    T, D = tokens.shape
    n = lax.axis_size("mp")
    E = w_router.shape[1]
    S = 16 * T // (5 * E)
    R = up(-(-T // n), 16)
    F = w_first.shape[2]
    W = w_proj.shape[0]
    win = up(IMG_LEN + 15, 16)
    Q = (S + 1) // 2
    cap = (9 * T + 4 * EXP_DEV - 1) // (4 * EXP_DEV)
    X = E // EXP_DEV
    full = min(cap // S, X)
    c = Sizes(
        T=T,
        D=D,
        half=D // 2,
        n=n,
        X=X,
        E=E,
        S=S,
        Q=Q,
        SP=up(Q + 2, 16),
        CR=(up(min(cap, X * Q), 16), up(full * (S - Q) + max(0, cap - full * S - Q), 16)),
        R=R,
        TP=n * R,
        W=W,
        images=T // IMG_LEN,
        quarters=n // EXP_DEV,
        F=F,
        cap=cap,
        win=win,
        fblk=min(1024, F),
    )
    order = Order()
    dp, mp, grid = lax.axis_index("dp"), lax.axis_index("mp"), lax.axis_index("grid")
    place = jnp.stack([dp, mp, grid, mp // c.quarters]).astype(I32)

    slot, blocks, rt, grad_out = route(c, order, place, routes, priority, cotangent)
    grad_in = trade(grad_out, "dp")

    def both_halves(rows):
        rows = jnp.pad(rows, ((0, up(rows.shape[0], 16) - rows.shape[0]), (0, 0)))
        other = swap_grid(rows)
        return jnp.where(
            grid == 0,
            jnp.concatenate([rows, other], axis=1),
            jnp.concatenate([other, rows], axis=1),
        )

    wide_bias = jnp.pad(qv_bias, ((0, 0), (0, c.half - W)))
    small = both_halves(
        jnp.concatenate([norm_gains, norm_shifts, proj_bias[None], wide_bias], axis=0)
    )
    qkv_own = w_qkv.transpose(1, 0, 2)
    qkv_oth = swap_grid(qkv_own)

    first_own = w_first[0]
    second_own = w_second[0]
    proj = lax.all_gather(w_proj, ("mp", "grid"))

    groups = groups_of(c)
    outs = [shape_of((c.TP, D), BF), shape_of((c.TP, 3 * W), BF), shape_of((c.TP, D), BF)]
    outs.append(shape_of((len(groups), c.TP, groups[0][1]), BF))

    def first_steps(width):
        return pl.BlockSpec((c.R, width), lambda i, s: (jnp.minimum(i, n - 1), 0))

    hidden_one, qkv, normed_one, mix = call(
        order,
        functools.partial(qkv_body, c),
        place,
        [tokens, small, qkv_own, qkv_oth],
        [first_steps(D), whole(small), whole(qkv_own), whole(qkv_oth)],
        outs,
        [first_steps(D), first_steps(3 * W), first_steps(D), whole(outs[3])],
        (n + c.images,),
        [pltpu.VMEM((D, 3 * W), BF), pltpu.VMEM((c.TP, 3 * W), BF)],
        name="qkv",
    )
    bias_rows = F // 2 // c.half
    tied = held(jnp.concatenate([expert_shift, w_router.T]), qkv)
    table = both_halves(tied)
    bias = both_halves(held(first_bias.reshape(bias_rows, c.half), qkv))[:bias_rows]
    bias = bias.reshape(bias_rows, 2, c.half).transpose(1, 0, 2).reshape(1, F).astype(F32)
    second_oth = swap_grid(held(second_own, qkv))
    first_oth = swap_grid(held(first_own, qkv))
    mixes, _ = gather_mp(c, held(mix, proj))
    hidden_two, weight, after, probs, rows_a = middle(
        c, order, place, mixes, proj, tokens, small, table, blocks, slot
    )

    rows_a = trade(rows_a, "dp")
    rows_b = dispatch(c, order, place, slot, hidden_two, weight, 1)
    ga_a, ga_b, grad_all, pack_a, pack_b = grad_active(
        c, order, place, grad_in, second_own, second_oth
    )
    rows_b = trade(held(rows_b, rows_a, grad_all), "dp")
    act_a, gp_a, gb_a, all_a, col_a, back_a = expert(
        c, order, place, 0, rows_a, pack_a, first_own, first_oth, bias, ga_a
    )
    back_a = trade(held(back_a, rows_b), "dp")
    act_b, gp_b, gb_b, all_b, col_b, back_b = expert(
        c, order, place, 1, rows_b, pack_b, first_own, first_oth, bias, ga_b
    )
    back_b = trade(held(back_b, back_a), "dp")
    cols, acts, gps, alls = [col_a, col_b], [act_a, act_b], [gp_a, gp_b], [all_a, all_b]
    second_part = swap_grid(grad_second(c, order, place, grad_all, cols, acts))
    order.tie(back_a)
    first_part = swap_grid(grad_first(c, order, place, alls, gps))
    mine, keep, keep_lane = keep_of(c, order, place, grad_in, blocks, rt)
    keep_mask = keep[:, :2, :].transpose(0, 2, 1).reshape(c.TP, 2)[:T].astype(I32)
    mine = mine.transpose(0, 2, 1).reshape(c.TP, 8)
    packs = [pack_a, pack_b]
    prod = produce(c, order, place, cols, acts, packs, second_own, second_oth)
    gb = (gb_a + gb_b)[0:1].reshape(2, F // 2)
    gb_own = lax.dynamic_index_in_dim(gb, grid, 0, True)
    gb_oth = lax.dynamic_index_in_dim(gb, 1 - grid, 0, True)
    grad_fbias = gb_own + swap_grid(gb_oth)

    pieces = combine(c, order, place, [back_a, back_b], mine)
    prod = trade(held(prod, back_b), "dp")
    two_sums = reduce_start(c, pieces)
    grad_second_out = grad_second(c, order, place, grad_all, cols, acts, second_part)
    two_sums = reduce_end(c, order, two_sums)
    grad_after, proj_a, proj_b, grad_mix = back_two(
        c,
        order,
        place,
        mixes,
        two_sums,
        proj,
        [after, probs, keep_lane],
        cotangent,
        hidden_two,
        small,
        table,
    )
    grad_mix = [grad_mix[0]] + [swap_mp(c, grad_mix[k], k) for k in range(1, n)]
    proj_parts = [proj_a, swap_grid(proj_b)]
    pieces = combine(c, order, place, [prod], mine, proj_parts, cost=10)
    out_sums = reduce_start(c, [held(p, *grad_mix) for p in pieces])

    outs = [shape_of((c.TP, 3 * W), BF), shape_of((8, 3 * W), F32)]
    dqkv, dqkv_sums = call(
        order,
        functools.partial(attend_back_body, c),
        place,
        [qkv, *grad_mix],
        [whole(qkv)] + [whole(p) for p in grad_mix],
        outs,
        [whole(o) for o in outs],
        (c.images,),
        [pltpu.VMEM((c.TP, W), BF)],
        name="attend_back",
    )
    one_pieces, one_parts = grad_one(c, order, place, dqkv, normed_one, qkv_own, qkv_oth)
    one_sums = reduce_start(c, one_pieces)
    out_sums = reduce_end(c, order, out_sums)
    qkv_a, qkv_b = grad_qkv(c, order, place, hidden_one, dqkv)
    qkv_b = swap_grid(qkv_b)
    qkv_low = (qkv_a.astype(F32) + qkv_b.astype(F32)).astype(BF)
    qkv_sum = sum_dp_start(c, qkv_low.reshape(-1, c.half))
    one_sums = reduce_end(c, order, one_sums)
    qkv_sum = sum_dp_turn(c, qkv_sum)
    order.tie(qkv_sum)
    grad_low = back_one(c, order, place, one_sums, tokens, grad_after, small)
    out_lane, proj_sum = block_out(c, order, place, out_sums, after, probs, keep_lane, table)

    qv_rows = jnp.concatenate([dqkv_sums[0:1, :W], dqkv_sums[0:1, 2 * W :]], axis=0)
    sums_one = held(first_sums(c, one_sums, one_parts), grad_low)
    sums_one = chip_sums(c, sums_one, qv_rows, grid).astype(BF)
    proj_end = proj_sum.shape[0]
    shared = jnp.concatenate([proj_sum, sums_one], axis=0)
    shared = jnp.pad(shared, ((0, up(shared.shape[0], 16 * c.X) - shared.shape[0]), (0, 0)))
    shared = sum_dp_start(c, shared)

    def last_expert_kernel(before):
        for value in before:
            order.tie(value)
        return grad_first(c, order, place, alls, gps, first_part), order.hold

    grad_low, out_lane, last, grad_first_out = gather_both(c, grad_low, out_lane, last_expert_kernel)
    grad_w_qkv = sum_dp_end(c, qkv_sum).reshape(3, c.half, W)
    shared = sum_dp_end(c, sum_dp_turn(c, held(shared, *last)))
    sums_one = shared[proj_end:]
    rest = shared[W : W + 8 + 2 * E]
    grad_tokens = assemble(c, order, place, grad_low, F32)
    block = assemble(c, order, place, out_lane, BF)
    return (
        block,
        grad_tokens,
        grad_w_qkv.transpose(1, 0, 2),
        sums_one[2:3, :W],
        shared[:W],
        rest[2],
        jnp.stack([sums_one[0], rest[0]]),
        jnp.stack([sums_one[1], rest[1]]),
        rest[8 + E : 8 + 2 * E].T,
        rest[8 : 8 + E],
        grad_first_out[None],
        grad_second_out[None],
        grad_fbias,
        keep_mask,
    )


def solution(mesh):
    return jax.shard_map(
        local,
        mesh=mesh,
        in_specs=(
            P(("dp", "grid"), None),
            P(("dp", "grid"), None),
            P("grid", None, "mp"),
            P("grid", "mp"),
            P("mp", "grid"),
            P("grid"),
            P(None, "grid"),
            P(None, "grid"),
            P("grid", None),
            P(None, "grid"),
            P(("dp", "mp"), "grid", None),
            P(("dp", "mp"), None, "grid"),
            P(("dp", "mp"), "grid"),
            P(("dp", "grid"), None),
            P(("dp", "grid"), None),
        ),
        out_specs=(
            P(("dp", "grid"), None),
            P(("dp", "grid"), None),
            P("grid", None, "mp"),
            P("grid", "mp"),
            P("mp", "grid"),
            P("grid"),
            P(None, "grid"),
            P(None, "grid"),
            P("grid", None),
            P(None, "grid"),
            P(("dp", "mp"), "grid", None),
            P(("dp", "mp"), None, "grid"),
            P(("dp", "mp"), "grid"),
            P(("dp", "grid"), None),
        ),
        check_vma=False,
    )
```

```python
import functools
from typing import NamedTuple

import jax
import jax.numpy as jnp
from jax import lax
from jax.experimental import pallas as pl
from jax.experimental.pallas import tpu as pltpu
from jax.sharding import PartitionSpec as P

HEAD = 64
IMG_LEN = 197
EXP_DEV = 4
BF = jnp.bfloat16
F32 = jnp.float32
I32 = jnp.int32
VMEM_BYTES = 56 * 1024 * 1024
LOW = -1e30


class Sizes(NamedTuple):
    T: int
    D: int
    half: int
    n: int
    X: int
    E: int
    S: int
    Q: int
    SP: int
    CR: tuple
    R: int
    TP: int
    W: int
    images: int
    quarters: int
    F: int
    cap: int
    win: int
    fblk: int


class Order:
    def __init__(self):
        self.after = []

    def tie(self, value):
        self.after.append(value)

    def hold(self, *values):
        return lax.optimization_barrier((*values, *self.after))[: len(values)]


def up(value, step):
    return -(-value // step) * step


def dot_nn(a, b):
    return jnp.dot(a, b, preferred_element_type=F32)


def dot_nt(a, b):
    return lax.dot_general(a, b, (((1,), (1,)), ((), ())), preferred_element_type=F32)


def dot_tn(a, b):
    return lax.dot_general(a, b, (((0,), (0,)), ((), ())), preferred_element_type=F32)


def split_low(values):
    high = values.astype(BF)
    return high, (values - high.astype(F32)).astype(BF)


def shape_of(dims, dtype):
    return jax.ShapeDtypeStruct(dims, dtype)


def whole(array, buffers=None):
    dims = tuple(array.shape)
    extra = {} if buffers is None else {"pipeline_mode": pl.Buffered(buffers)}
    return pl.BlockSpec(dims, lambda i, s: (0,) * len(dims), **extra)


def rows_of(dims):
    return pl.BlockSpec(dims, lambda i, s: (i,) + (0,) * (len(dims) - 1))


def cols_of(dims):
    return pl.BlockSpec(dims, lambda i, s: (0,) * (len(dims) - 1) + (i,))


def call(order, body, place, args, specs, outs, out_specs, grid, scratch=(), name=None, cost=0):
    extra = order.after
    count = len(args)

    def wrapped(place, *refs):
        body(place, *refs[:count], *refs[count + len(extra) :])

    result = pl.pallas_call(
        wrapped,
        grid_spec=pltpu.PrefetchScalarGridSpec(
            num_scalar_prefetch=1,
            grid=grid,
            in_specs=list(specs) + [pl.BlockSpec(memory_space=pl.ANY)] * len(extra),
            out_specs=list(out_specs),
            scratch_shapes=list(scratch),
        ),
        out_shape=list(outs),
        compiler_params=pltpu.CompilerParams(
            dimension_semantics=("arbitrary",) * len(grid), vmem_limit_bytes=VMEM_BYTES
        ),
        cost_estimate=pl.CostEstimate(
            flops=1000 + int(1.1e9 * cost), bytes_accessed=1000, transcendentals=0
        ),
        name=name,
    )(place, *args, *extra)
    order.after = [min(result, key=lambda o: o.size)]
    return result


def swap_mp(c, value, mask):
    return lax.ppermute(value, "mp", [(i, i ^ mask) for i in range(c.n)])


def swap_grid(value):
    return lax.ppermute(value, "grid", [(0, 1), (1, 0)])


def held(value, *others):
    return lax.optimization_barrier((value, *others))[0]


def trade(value, axis):
    return lax.all_to_all(value, axis, split_axis=0, concat_axis=0, tiled=True)


def groups_a(c):
    return [[0, 2], [1, 3]] if c.n == 4 else [[k] for k in range(c.n)]


def groups_b(c):
    return [[0, 1], [2, 3]] if c.n == 4 else [[k] for k in range(c.n)]


def reduce_start(c, arrays):
    a, b = arrays[: len(arrays) // 2], arrays[len(arrays) // 2 :]
    if c.n != 4:
        return [[x[0]] + [swap_mp(c, x[k], k) for k in range(1, c.n)] for x in (a, b)]
    return [[a[0], swap_mp(c, a[1], 1)], [b[0], swap_mp(c, b[1], 2)]]


def reduce_end(c, order, state):
    if c.n != 4:
        return state
    (a, ra), (b, rb) = state
    ra, rb = order.hold(ra, rb)
    ta = (a[1:].astype(F32) + ra[1:].astype(F32)).astype(BF)
    tb = (b[1:].astype(F32) + rb[1:].astype(F32)).astype(BF)
    order.tie(ta)
    order.tie(tb)
    return [[a, ra, swap_mp(c, ta, 2)], [b, rb, swap_mp(c, tb, 1)]]


def piece_outs(c, more_a=0, more_b=0):
    outs = [shape_of((len(g), c.R + more_a, c.half), BF) for g in groups_a(c)]
    return outs + [shape_of((len(g), c.R + more_b, c.half), BF) for g in groups_b(c)]


def first_block(array):
    dims = tuple(array.shape)
    return pl.BlockSpec((None,) + dims[1:], lambda i, s: (0, 0, 0))


def same_sum(c, refs, rows):
    parts = [ref[rows, :].astype(F32) for ref in refs]
    if c.n == 4:
        return (parts[0] + parts[1]).astype(BF).astype(F32) + parts[2]
    while len(parts) > 1:
        parts = [parts[i] + parts[i + 1] for i in range(0, len(parts), 2)]
    return parts[0]


def add_up(refs):
    total = refs[0][...].astype(F32)
    for ref in refs[1:]:
        total = total + ref[...].astype(F32)
    return total


def sum_dp_start(c, value):
    return trade(value.reshape((c.X, value.shape[0] // c.X) + value.shape[1:]), "dp")


def sum_dp_turn(c, parts):
    total = jnp.sum(parts.astype(F32), axis=0).astype(BF)
    return jnp.broadcast_to(total[None], (c.X,) + total.shape)


def sum_dp_end(c, spread):
    return trade(spread, "dp").reshape((-1,) + spread.shape[2:]).astype(F32)


def gather_mp(c, value, until=None):
    if c.n != 4 or value.shape[0] != 2:
        parts = [value] + [swap_mp(c, value, k) for k in range(1, c.n)]
        return [[(p, h) for h in range(value.shape[0])] for p in parts], parts[1:]
    one = swap_mp(c, value, 1)
    two = swap_mp(c, value, 2)
    ends = one[0:1], two[1:2]
    if until is not None:
        ends = held(ends[0], *until), held(ends[1], *until)
    far_a = swap_mp(c, ends[0], 2)
    far_b = swap_mp(c, ends[1], 1)
    near = [[(p, 0), (p, 1)] for p in (value, one, two)]
    return near + [[(far_a, 0), (far_b, 0)]], [one, two]


def gather_both(c, first, second, filler):
    if c.n != 4:
        filled, _ = filler([first])
        return gather_mp(c, first)[0], gather_mp(c, second)[0], (first,), filled
    one, two = swap_mp(c, first, 1), swap_mp(c, first, 2)
    near = jnp.concatenate([one[0:1], second]), jnp.concatenate([two[1:2], second])
    by_two, by_one = [swap_mp(c, x, mask) for x, mask in zip(near, (2, 1))]
    filled, hold = filler(near)
    by_two, by_one = hold(by_two, by_one)
    far_a, far_b = swap_mp(c, by_one[1:2], 2), swap_mp(c, by_two[2:3], 1)
    pieces = [[(p, 0), (p, 1)] for p in (first, one, two)] + [[(by_two, 0), (by_one, 0)]]
    others = [[(second, 0), (second, 1)], [(by_one, 1), (by_one, 2)], [(by_two, 1), (by_two, 2)]]
    return pieces, others + [[(far_a, 0), (far_b, 0)]], (by_one, by_two), filled


def flat(pieces):
    return [pair for piece in pieces for pair in piece]


def fold(c, value, axes):
    for axis, size in axes:
        mask = 1
        while mask < size:
            value = value + lax.ppermute(value, axis, [(i, i ^ mask) for i in range(size)])
            mask *= 2
    return value


def first_sums(c, sums, one_parts):
    if c.n != 4:
        return fold(c, one_parts, (("mp", c.n),))
    halves = []
    for a, b, far in sums:
        pair = (a[0, c.R : c.R + 2].astype(F32) + b[0, c.R : c.R + 2].astype(F32)).astype(BF)
        halves.append(pair.astype(F32) + far[0, c.R : c.R + 2].astype(F32))
    return jnp.concatenate(halves, axis=1)


def chip_sums(c, one, parts, grid):
    def half_of(side):
        cols = lax.dynamic_slice_in_dim(one, side * c.half, c.half, 1)
        row = lax.dynamic_index_in_dim(parts, side, 0, True)
        return jnp.concatenate([cols, jnp.pad(row, ((0, 0), (0, c.half - c.W)))], axis=0)

    return half_of(grid) + swap_grid(half_of(1 - grid))


def expert_of(c, place, j):
    return j * EXP_DEV + place[3]


def window_slot(c, slot):
    return jnp.where(slot < c.Q, slot, slot + (c.SP - c.Q))


def count_places(c, rank_ref, rt_ref, slot_ref, blocks_ref, rtb_ref):
    pad = jnp.full((2, c.TP - c.T), -1, I32)
    rank = jnp.concatenate([rank_ref[...], pad], axis=1)
    rt = jnp.concatenate([rt_ref[...], pad], axis=1)
    side = 64
    index = lax.broadcasted_iota(I32, (side, c.TP), 0)
    rows = [(index == (rank[k : k + 1] >> 6)).astype(BF) for k in range(2)]
    cols = [index == (rank[k : k + 1] & 63) for k in range(2)]
    table = jnp.zeros((side, side), F32)
    for k in range(2):
        named = (rt[k : k + 1] + 1).astype(F32)
        table = table + dot_nt(rows[k], jnp.where(cols[k], named, 0.0).astype(BF))
    up_to = lax.broadcasted_iota(I32, (side, side), 0) < lax.broadcasted_iota(I32, (side, side), 1)
    above = lax.broadcasted_iota(I32, (side, side), 0) > lax.broadcasted_iota(I32, (side, side), 1)
    lane = lax.broadcasted_iota(I32, (1, 128), 1)
    named = [(table == e + 1.0).astype(F32) for e in range(c.E)]
    along = dot_nn(jnp.concatenate(named, axis=0).astype(BF), up_to.astype(BF))
    numbers = jnp.zeros((side, 128), F32)
    for e in range(c.E):
        numbers = numbers + jnp.where(lane == e, jnp.sum(named[e], axis=1, keepdims=True), 0.0)
    down = dot_nn(above.astype(BF), numbers.astype(BF))
    place_of = jnp.zeros((side, side), F32)
    for e in range(c.E):
        here = along[e * side : (e + 1) * side] + down[:, e : e + 1]
        place_of = place_of + named[e] * here
    place_of = place_of.astype(I32)
    high = (place_of >> 4).astype(F32).astype(BF)
    low = (place_of & 15).astype(F32).astype(BF)
    places = []
    for k in range(2):
        values = dot_tn(high, rows[k]) * 16.0 + dot_tn(low, rows[k])
        places.append(jnp.sum(jnp.where(cols[k], values, 0.0), axis=0, keepdims=True).astype(I32))
    for e in range(c.E):
        second = jnp.where(rt[1:2, :] == e, places[1], -1)
        slot_ref[e : e + 1, :] = jnp.where(rt[0:1, :] == e, places[0], second)
    for r in range(c.n):
        blocks_ref[r] = slot_ref[:, r * c.R : (r + 1) * c.R]
        rtb_ref[r] = jnp.concatenate([rt[:, r * c.R : (r + 1) * c.R]] * 4, axis=0)
    numbers = jnp.sum(numbers, axis=0, keepdims=True)
    return jnp.concatenate([numbers, jnp.zeros((1, c.half - 128), F32)], axis=1).astype(I32)


def fill_hot(c, place, slot_ref, hot_ref, halves):
    for j in range(c.X):
        row = window_slot(c, slot_ref[pl.ds(expert_of(c, place, j), 1), :])
        for index, half in enumerate(halves):
            slots = lax.broadcasted_iota(I32, (c.SP, c.TP), 0) + half * c.SP
            hot_ref[index, j * c.SP : (j + 1) * c.SP, :] = (slots == row).astype(BF)


def route_body(c, place, *refs):
    rank_ref, rt_ref, src_ref, slot_ref, blocks_ref, rtb_ref, out_ref, hot_ref, sum_ref = refs

    @pl.when(pl.program_id(0) == 0)
    def _():
        numbers = count_places(c, rank_ref, rt_ref, slot_ref, blocks_ref, rtb_ref)
        sum_ref[0:1, :] = (numbers >> 4).astype(F32)
        sum_ref[1:2, :] = (numbers & 15).astype(F32)
        fill_hot(c, place, slot_ref, hot_ref, (0, 1))

    for half in range(2):
        acc = dot_nn(hot_ref[half, :, : c.T], src_ref[...])
        for j in range(c.X):
            at = (2 * j + half) * c.SP
            out_ref[at : at + c.SP, :] = acc[j * c.SP : (j + 1) * c.SP].astype(BF)
            if half == 0:

                @pl.when(pl.program_id(0) == 0)
                def _():
                    tile = acc[(j + 1) * c.SP - 16 : (j + 1) * c.SP]
                    tile = last_rows(c, tile, sum_ref[0:1, :], sum_ref[1:2, :])
                    out_ref[at + c.SP - 16 : at + c.SP, :] = tile.astype(BF)


def route(c, order, place, routes, priority, source):
    rank = priority.T
    rt = routes.T
    outs = [
        shape_of((c.E, c.TP), I32),
        shape_of((c.n, c.E, c.R), I32),
        shape_of((c.n, 8, c.R), I32),
        shape_of((2 * c.X * c.SP, c.D), BF),
    ]
    result = call(
        order,
        functools.partial(route_body, c),
        place,
        [rank, rt, source],
        [whole(rank), whole(rt)]
        + [pl.BlockSpec((c.T, c.half), lambda i, s: (0, i ^ s[2]))],
        outs,
        [whole(o) for o in outs[:3]] + [cols_of((2 * c.X * c.SP, c.half))],
        (2,),
        [pltpu.VMEM((2, c.X * c.SP, c.TP), BF), pltpu.VMEM((8, c.half), F32)],
        name="route",
    )
    return (*result[:3], result[3].reshape(c.X, 2 * c.SP, c.D))


def keep_body(c, place, tail_ref, slot_ref, rt_ref, mine_ref, keep_ref, lane_ref):
    earlier = jnp.zeros((1, 128), F32)
    for b in range(c.X):
        high, low = last_pair(c, tail_ref[b], 128)
        earlier = earlier + jnp.where(b < place[0], high * 16.0 + low, 0.0)
    wide = (c.E, 128)
    eye = lax.broadcasted_iota(I32, wide, 0) == lax.broadcasted_iota(I32, wide, 1)
    offset = jnp.sum(jnp.where(eye, earlier, 0.0), axis=1, keepdims=True).astype(I32)
    slot = slot_ref[0]
    kept = (slot >= 0) & (slot + offset < c.cap)
    slots = jnp.where(kept, window_slot(c, slot), -1)
    expert = lax.broadcasted_iota(I32, (c.E, 1), 0)
    for j in range(8):
        if j < c.X:
            here = jnp.where(expert == expert_of(c, place, j), slots, -1)
            mine_ref[0, j : j + 1, :] = jnp.max(here, axis=0, keepdims=True)
        else:
            mine_ref[0, j : j + 1, :] = jnp.full((1, c.R), -1, I32)
    rows = []
    for k in range(2):
        picked = jnp.where((rt_ref[0, k : k + 1, :] == expert) & kept, 1.0, 0.0)
        rows.append(jnp.sum(picked, axis=0, keepdims=True))
    keep_ref[0] = jnp.concatenate(rows * 4, axis=0)

    @pl.when(pl.program_id(0) == place[1])
    def _():
        lane_ref[...] = jnp.where(kept, 1.0, 0.0)


def keep_of(c, order, place, rows, blocks, rt):
    outs = [
        shape_of((c.n, 8, c.R), I32),
        shape_of((c.n, 8, c.R), F32),
        shape_of((c.E, c.R), F32),
    ]
    tail = pl.BlockSpec((c.X, 16, c.half), lambda i, s: (0, c.SP // 16 - 1, 0))
    return call(
        order,
        functools.partial(keep_body, c),
        place,
        [rows, blocks, rt],
        [tail, rows_of((1, c.E, c.R)), rows_of((1, 8, c.R))],
        outs,
        [rows_of((1, 8, c.R)), rows_of((1, 8, c.R)), whole(outs[2])],
        (c.n,),
        name="keep",
    )


def last_rows(c, tile, high, low):
    row = lax.broadcasted_iota(I32, (16, 1), 0)
    return jnp.where(row == 14, high, jnp.where(row == 15, low, tile))


def put_gates(c, place, hot_ref, weights, acc, out_ref):
    gates = dot_nn(hot_ref[0], weights)
    lane = lax.broadcasted_iota(I32, (1, 128), 1)
    wide = (c.SP, c.half)
    eye = lax.broadcasted_iota(I32, wide, 0) == lax.broadcasted_iota(I32, wide, 1)
    for j in range(c.X):
        e = expert_of(c, place, j)
        mine = gates[j * c.SP : (j + 1) * c.SP]
        rows = []
        for at in (e, e + 64):
            col = jnp.sum(jnp.where(lane == at, mine, 0.0), axis=1, keepdims=True)
            rows.append(jnp.sum(jnp.where(eye, col, 0.0), axis=0, keepdims=True))
        end = (j + 1) * c.SP
        tile = last_rows(c, acc[end - 16 : end], rows[0], rows[1])
        out_ref[end - 16 : end, :] = tile.astype(BF)


def dispatch_body(c, half, place, slot_ref, src_ref, weight_ref, out_ref, hot_ref):
    @pl.when(pl.program_id(0) == 0)
    def _():
        fill_hot(c, place, slot_ref, hot_ref, (half,))

    acc = dot_nn(hot_ref[0], src_ref[...])
    out_ref[...] = acc.astype(BF)

    @pl.when(pl.program_id(0) == 0)
    def _():
        put_gates(c, place, hot_ref, weight_ref[...], acc, out_ref)


def dispatch(c, order, place, slot, source, weight, half):
    return call(
        order,
        functools.partial(dispatch_body, c, half),
        place,
        [slot, source, weight],
        [whole(slot), pl.BlockSpec((c.TP, c.half), lambda i, s: (0, i ^ s[2])), whole(weight)],
        [shape_of((c.X * c.SP, c.D), BF)],
        [cols_of((c.X * c.SP, c.half))],
        (2,),
        [pltpu.VMEM((1, c.X * c.SP, c.TP), BF)],
        name="dispatch",
    )[0].reshape(c.X, c.SP, c.D)


def norm_rows(values):
    centred = values - jnp.mean(values, axis=-1, keepdims=True)
    inv_std = lax.rsqrt(jnp.mean(centred * centred, axis=-1, keepdims=True) + 1e-06)
    return centred * inv_std, inv_std


def norm_back(grad_norm, gain, normed, inv_std):
    scaled = grad_norm * gain
    return inv_std * (
        scaled
        - jnp.mean(scaled, axis=-1, keepdims=True)
        - normed * jnp.mean(scaled * normed, axis=-1, keepdims=True)
    )


def small_row(c, small_ref, index, count=1):
    return small_ref[index : index + count, :].astype(F32)


def own_cols(c, place):
    return pl.ds(pl.multiple_of(place[2] * c.half, c.half), c.half)


def other_cols(c, place):
    return pl.ds(pl.multiple_of((1 - place[2]) * c.half, c.half), c.half)


def last_block(c):
    return (c.T - 1) // c.R


def own_rows(c):
    return pl.BlockSpec((c.R, c.D), lambda i, s: (jnp.minimum(s[1], last_block(c)), 0))


def live_rows(c, first, count):
    return (first + lax.broadcasted_iota(I32, (count, 1), 0)) < c.T


def qkv_body(c, place, *refs):
    tok_ref, small_ref, own_ref, oth_ref, hid_ref, qkv_ref, normed_ref, mix_ref, w_ref, all_ref = refs
    step = pl.program_id(0)

    @pl.when(step == 0)
    def _():
        mix_ref[...] = jnp.zeros_like(mix_ref)
        for part in range(3):
            lanes = slice(part * c.W, (part + 1) * c.W)
            w_ref[own_cols(c, place), lanes] = own_ref[part]
            w_ref[other_cols(c, place), lanes] = oth_ref[part]

    @pl.when(step < c.n)
    def _():
        live = live_rows(c, step * c.R, c.R)
        values = jnp.where(live, tok_ref[...].astype(F32), 0.0)
        normed, _ = norm_rows(values)
        hidden = normed * small_row(c, small_ref, 0) + small_row(c, small_ref, 2)
        normed_ref[...] = normed.astype(BF)
        hidden = jnp.where(live, hidden, 0.0).astype(BF)
        hid_ref[...] = hidden
        acc = dot_nn(hidden, w_ref[...])
        bias = small_row(c, small_ref, 5)
        zero = jnp.zeros((1, c.W), F32)
        shift = jnp.concatenate([bias[:, : c.W], zero, bias[:, c.half : c.half + c.W]], axis=1)
        result = (acc + shift).astype(BF)
        qkv_ref[...] = result
        all_ref[pl.ds(pl.multiple_of(step * c.R, 16), c.R), :] = result

    @pl.when(step >= c.n)
    def _():
        attend(c, step - c.n, all_ref, mix_ref)


def image_window(c, image):
    start = image * IMG_LEN
    low = pl.multiple_of(start // 16 * 16, 16)
    return low, start - low


def groups_of(c):
    lanes = min(128, c.W)
    return [(at, lanes) for at in range(0, c.W, lanes)]


def head_mask(lanes, head):
    lane = lax.broadcasted_iota(I32, (1, lanes), 1)
    return (lane >= head * HEAD) & (lane < (head + 1) * HEAD)


def stack_heads(c, values):
    heads = range(c.W // HEAD)
    return jnp.concatenate([jnp.where(head_mask(c.W, h), values, BF(0)) for h in heads], axis=0)


def pick_heads(c, values):
    total = None
    for h in range(c.W // HEAD):
        part = jnp.where(head_mask(c.W, h), values[h * c.win : (h + 1) * c.win], 0.0)
        total = part if total is None else total + part
    return total


def attend(c, image, qkv_ref, mix_ref):
    low, off = image_window(c, image)
    row = lax.broadcasted_iota(I32, (c.win, 1), 0)
    col = lax.broadcasted_iota(I32, (1, c.win), 1)
    in_row = (row >= off) & (row < off + IMG_LEN)
    in_col = (col >= off) & (col < off + IMG_LEN)
    q = stack_heads(c, qkv_ref[pl.ds(low, c.win), : c.W] * BF(HEAD**-0.5))
    k = qkv_ref[pl.ds(low, c.win), c.W : 2 * c.W]
    v = qkv_ref[pl.ds(low, c.win), 2 * c.W :]
    scores = jnp.where(in_col, dot_nt(q, k), LOW)
    exps = jnp.exp(scores - jnp.max(scores, axis=-1, keepdims=True))
    probs = exps * (1.0 / jnp.sum(exps, axis=-1, keepdims=True))
    total = pick_heads(c, dot_nn(probs.astype(BF), v)).astype(BF)
    for group, (at, lanes) in enumerate(groups_of(c)):
        old = mix_ref[group, pl.ds(low, c.win), :]
        mix_ref[group, pl.ds(low, c.win), :] = jnp.where(in_row, total[:, at : at + lanes], old)


def attend_back_body(c, place, qkv_ref, *refs):
    pieces, (out_ref, sums_ref, grad_ref) = refs[: c.n], refs[c.n :]

    @pl.when(pl.program_id(0) == 0)
    def _():
        out_ref[...] = jnp.zeros_like(out_ref)
        sums_ref[...] = jnp.zeros_like(sums_ref)
        for k in range(c.n):
            at = pl.multiple_of((place[1] ^ k) * c.R, 16)
            grad_ref[pl.ds(at, c.R), :] = pieces[k][...]

    low, off = image_window(c, pl.program_id(0))
    row = lax.broadcasted_iota(I32, (c.win, 1), 0)
    in_row = (row >= off) & (row < off + IMG_LEN)
    scale = HEAD**-0.5
    q = stack_heads(c, qkv_ref[pl.ds(low, c.win), : c.W] * BF(scale))
    k = qkv_ref[pl.ds(low, c.win), c.W : 2 * c.W]
    v = qkv_ref[pl.ds(low, c.win), 2 * c.W :]
    do = stack_heads(c, jnp.where(in_row, grad_ref[pl.ds(low, c.win), :], BF(0)))
    scores = jnp.where(in_row, dot_nt(k, q), LOW)
    exps = jnp.exp(scores - jnp.max(scores, axis=0, keepdims=True))
    soft = exps * (1.0 / jnp.sum(exps, axis=0, keepdims=True))
    dp = dot_nt(v, do)
    delta = jnp.sum(soft * dp, axis=0, keepdims=True)
    ds = (soft * (dp - delta)).astype(BF)
    dq = pick_heads(c, dot_tn(ds, k)) * scale
    dk = dot_nn(ds, q)
    dv = dot_nn(soft.astype(BF), do)
    for part, grad in enumerate((dq, dk, dv)):
        lanes = slice(part * c.W, (part + 1) * c.W)
        low_grad = jnp.where(in_row, grad, 0.0).astype(BF)
        old = out_ref[pl.ds(low, c.win), lanes]
        out_ref[pl.ds(low, c.win), lanes] = jnp.where(in_row, low_grad, old)
        sums_ref[0:1, lanes] += jnp.sum(low_grad.astype(F32), axis=0, keepdims=True)


def middle_rows(c, place, step, mixes, tok_ref, small_ref, table_ref, slot_ref, proj_ref):
    branch = dot_nn(jnp.concatenate([mix[...] for mix in mixes], axis=1), proj_ref[...])
    live = live_rows(c, step * c.R, c.R)
    tok = jnp.where(live, tok_ref[...].astype(F32), 0.0)
    after = tok + branch + small_row(c, small_ref, 4)
    normed, _ = norm_rows(after)
    hidden = (normed * small_row(c, small_ref, 1) + small_row(c, small_ref, 3)).astype(BF)
    router = table_ref[c.E : 2 * c.E, :]
    logits = dot_nt(router, hidden)
    exps = jnp.exp(logits - jnp.max(logits, axis=0, keepdims=True))
    probs = exps / jnp.sum(exps, axis=0, keepdims=True)
    weight = jnp.where(slot_ref[0] >= 0, probs, 0.0)
    high, rest = split_low(weight)
    lane = lax.broadcasted_iota(I32, (c.E, 128), 1)
    index = lax.broadcasted_iota(I32, (c.E, 128), 0)
    both = dot_tn(high, (lane == index).astype(BF)) + dot_tn(rest, (lane == index + 64).astype(BF))
    return after, hidden, probs, both.astype(BF)


def middle_body(c, place, *refs):
    refs = list(refs)
    count = c.n * len(groups_of(c))
    mixes, refs = refs[:count], refs[count:]
    w_ref, tok_ref, small_ref, table_ref, blocks_ref, slot_ref = refs[:6]
    hid_ref, weight_ref, after_ref, probs_ref, out_ref = refs[6:11]
    proj_ref, hids_ref, weights_ref, hot_ref = refs[11:]
    step = pl.program_id(0)

    @pl.when(step == 0)
    def _():
        for k in range(c.n):
            for h in range(2):
                cols = slice(h * c.half, (h + 1) * c.half)
                proj_ref[k * c.W : (k + 1) * c.W, cols] = w_ref[(place[1] ^ k) * 2 + h]

    @pl.when(step < c.n)
    def _():
        after, hidden, probs, weight = middle_rows(
            c, place, step, mixes, tok_ref, small_ref, table_ref, blocks_ref, proj_ref
        )
        rows = pl.ds(pl.multiple_of(step * c.R, 16), c.R)
        hid_ref[...] = hidden
        hids_ref[rows, :] = hidden
        weight_ref[...] = weight
        weights_ref[rows, :] = weight

        @pl.when(step == place[1])
        def _():
            after_ref[...] = after
            probs_ref[...] = probs

    @pl.when(step == c.n)
    def _():
        fill_hot(c, place, slot_ref, hot_ref, (0,))

    @pl.when(step >= c.n)
    def _():
        cols = pl.multiple_of(((step - c.n) ^ place[2]) * c.half, c.half)
        acc = dot_nn(hot_ref[0], hids_ref[:, pl.ds(cols, c.half)])
        out_ref[...] = acc.astype(BF)

        @pl.when(step == c.n)
        def _():
            put_gates(c, place, hot_ref, weights_ref[...], acc, out_ref)


def middle(c, order, place, mixes, proj, tokens, small, table, blocks, slot):
    def early(dims):
        return pl.BlockSpec(dims, lambda i, s: (jnp.minimum(i, c.n - 1),) + (0,) * (len(dims) - 1))

    args = [pair[0] for pair in flat(mixes)] + [proj, tokens, small, table, blocks, slot]
    specs = [
        pl.BlockSpec((None, c.R, a.shape[2]), lambda i, s, at=at: (at, jnp.minimum(i, c.n - 1), 0))
        for a, at in flat(mixes)
    ]
    tok_rows = pl.BlockSpec((c.R, c.D), lambda i, s: (jnp.minimum(i, last_block(c)), 0))
    specs += [whole(proj), tok_rows, whole(small), whole(table)]
    specs += [early((1, c.E, c.R)), whole(slot)]
    outs = [
        shape_of((c.TP, c.D), BF),
        shape_of((c.TP, 128), BF),
        shape_of((c.R, c.D), F32),
        shape_of((c.E, c.R), F32),
        shape_of((c.X * c.SP, c.D), BF),
    ]
    late = pl.BlockSpec((c.X * c.SP, c.half), lambda i, s: (0, jnp.maximum(i - c.n, 0)))
    result = call(
        order,
        functools.partial(middle_body, c),
        place,
        args,
        specs,
        outs,
        [early((c.R, c.D)), early((c.R, 128)), whole(outs[2]), whole(outs[3]), late],
        (c.n + 2,),
        [
            pltpu.VMEM((c.D, c.D), BF),
            pltpu.VMEM((c.TP, c.D), BF),
            pltpu.VMEM((c.TP, 128), BF),
            pltpu.VMEM((1, c.X * c.SP, c.TP), BF),
        ],
        name="middle",
    )
    return (*result[:4], result[4].reshape(c.X, c.SP, c.D))


def fill_packs(c, place, tails, packs):
    lane = lax.broadcasted_iota(I32, (1, 128), 1)
    here = place[0] * EXP_DEV + place[3]
    state = [jnp.zeros((1, 1), F32)] * 3
    for j in range(c.X):
        high, low = last_pair(c, tails[j], 128)
        number = jnp.sum(jnp.where(lane == here, high * 16.0 + low, 0.0), axis=1, keepdims=True)
        kept = jnp.clip(c.cap - state[0], 0.0, number)
        first = jnp.minimum(kept, float(c.Q))
        sizes = first, kept - first
        for half in range(2):
            wide = (c.CR[half], c.SP)
            slot = lax.broadcasted_iota(I32, wide, 1)
            at = lax.broadcasted_iota(I32, wide, 0) - state[1 + half].astype(I32)
            hot = (at == slot) & (slot < sizes[half].astype(I32))
            packs[half][:, j * c.SP : (j + 1) * c.SP] = hot.astype(BF)
        state = [state[0] + number, state[1] + sizes[0], state[2] + sizes[1]]


def last_pair(c, tile, lanes):
    tile = tile[:, :lanes].astype(F32)
    return tile[14:15, :], tile[15:16, :]


def row_chunks(rows, size):
    return [slice(at, min(at + size, rows)) for at in range(0, rows, size)]


def grad_active_body(c, place, rows_ref, own_ref, oth_ref, *outs):
    gas, all_ref, packs = outs[:2], outs[2], outs[3:]

    @pl.when(pl.program_id(0) == 0)
    def _():
        tails = [rows_ref[j, c.SP - 16 : c.SP, :] for j in range(c.X)]
        fill_packs(c, place, tails, packs)
        for half, base in enumerate((0, c.CR[0])):
            rows = [rows_ref[j, half * c.SP : (half + 1) * c.SP, :] for j in range(c.X)]
            got = dot_nn(packs[half][...], jnp.concatenate(rows, axis=0))
            all_ref[base : base + c.CR[half], :] = got.astype(BF)

    weights = jnp.concatenate([own_ref[...], oth_ref[...]], axis=1)
    for half, base in enumerate((0, c.CR[0])):
        for at in row_chunks(c.CR[half], 320):
            values = all_ref[base + at.start : base + at.stop, :]
            gas[half][at, :] = dot_nt(values, weights).astype(BF)


def grad_active(c, order, place, rows, own_w, oth_w):
    outs = [shape_of((count, c.F), BF) for count in c.CR] + [shape_of((sum(c.CR), c.D), BF)]
    outs += [shape_of((count, c.X * c.SP), BF) for count in c.CR]
    return call(
        order,
        functools.partial(grad_active_body, c),
        place,
        [rows, own_w, oth_w],
        [whole(rows, 1)] + [rows_of((c.fblk, c.half))] * 2,
        outs,
        [cols_of((count, c.fblk)) for count in c.CR] + [whole(o) for o in outs[2:]],
        (c.F // c.fblk,),
        name="grad_active",
    )


def expert_body(c, half, place, *refs):
    rows_ref, pack_ref, own_ref, oth_ref, bias_ref, ga_ref = refs[:6]
    act_ref, gp_ref, gb_ref, all_ref, col_ref, back_ref = refs[6:12]
    acc_ref, dot_ref, row_ref, wide_ref = refs[12:]
    step = pl.program_id(0)

    @pl.when(step == 0)
    def _():
        acc_ref[...] = jnp.zeros_like(acc_ref)
        dot_ref[...] = jnp.zeros_like(dot_ref)
        all_ref[...] = dot_nn(pack_ref[...], rows_ref[...]).astype(BF)
        eye = lax.broadcasted_iota(I32, (c.SP, c.SP), 0) == lax.broadcasted_iota(I32, (c.SP, c.SP), 1)
        lane = lax.broadcasted_iota(I32, (1, 128), 1)
        for j in range(c.X):
            end = (j + 1) * c.SP
            high, low = last_pair(c, rows_ref[end - 16 : end, :], c.SP)
            high = jnp.sum(jnp.where(eye, high, 0.0), axis=1, keepdims=True)
            low = jnp.sum(jnp.where(eye, low, 0.0), axis=1, keepdims=True)
            both = jnp.where(lane == 0, high, jnp.where(lane == 1, low, 0.0))
            wide_ref[j * c.SP : end, :] = both.astype(BF)
        both = dot_nn(pack_ref[...], wide_ref[...])
        col_ref[...] = jnp.broadcast_to(both[:, 0:1] + both[:, 1:2], (c.CR[half], 128))

    bias = bias_ref[...]
    weights = jnp.concatenate([own_ref[...], oth_ref[...]], axis=0)
    summed = jnp.zeros((1, c.fblk), F32)
    lead = 0.7978845608028654
    cube = lead * 0.044715
    chunks = row_chunks(c.CR[half], 224)
    ahead = dot_nn(all_ref[chunks[0], :], weights)
    for i, rows_at in enumerate(chunks):
        pre = ahead + bias
        if i + 1 < len(chunks):
            ahead = dot_nn(all_ref[chunks[i + 1], :], weights)
        square = pre * pre
        turn = jnp.tanh(pre * (cube * square + lead))
        above = 1.0 + turn
        active = (0.5 * pre) * above
        slope = above * (1.0 + (1.0 - turn) * (pre * (3 * cube * square + lead)))
        ga = ga_ref[rows_at, :].astype(F32)
        product = active * ga
        part = product[:, 0:128]
        for lane in range(128, c.fblk, 128):
            part = part + product[:, lane : lane + 128]
        dot_ref[rows_at, :] += part
        grad = ga * slope * (0.5 * col_ref[rows_at, 0:1])
        act_ref[rows_at, :] = active.astype(BF)
        grad_low = grad.astype(BF)
        gp_ref[rows_at, :] = grad_low
        summed = summed + jnp.sum(grad, axis=0, keepdims=True)
        acc_ref[rows_at, :] += dot_nt(grad_low, weights)
    gb_ref[...] = jnp.broadcast_to(summed, (8, c.fblk))

    @pl.when(step == pl.num_programs(0) - 1)
    def _():
        ones = jnp.ones((8, 128), BF)
        row_ref[...] = jnp.zeros_like(row_ref)
        back_ref[...] = dot_tn(pack_ref[...], acc_ref[...].astype(BF)).astype(BF)
        a, rest = split_low(dot_ref[...])
        total = dot_nt(ones, a) + dot_nt(ones, rest)
        high, low = split_low(total)
        high = dot_nn(high, pack_ref[...])
        low = dot_nn(low, pack_ref[...])
        for j in range(c.X):
            end = (j + 1) * c.SP
            row_ref[0:8, : c.SP] = high[:, j * c.SP : end]
            row_ref[8:16, : c.SP] = low[:, j * c.SP : end]
            tile = back_ref[end - 16 : end, : c.half].astype(F32)
            tile = last_rows(c, tile, row_ref[0:1, :], row_ref[8:9, :])
            back_ref[end - 16 : end, : c.half] = tile.astype(BF)


def expert(c, order, place, half, rows, pack, own_w, oth_w, bias, ga):
    rows = rows.reshape(c.X * c.SP, c.D)
    args = [rows, pack, own_w, oth_w, bias, ga]
    count = c.CR[half]
    specs = [whole(rows, 1), whole(pack, 1)]
    specs += [cols_of((c.half, c.fblk))] * 2
    specs += [cols_of((1, c.fblk)), cols_of((count, c.fblk))]
    outs = [
        shape_of((count, c.F), BF),
        shape_of((count, c.F), BF),
        shape_of((8, c.F), F32),
    ]
    out_specs = [cols_of((count, c.fblk))] * 2 + [cols_of((8, c.fblk))]
    late = [shape_of((count, c.D), BF), shape_of((count, 128), F32)]
    late.append(shape_of((c.X * c.SP, c.D), BF))
    result = call(
        order,
        functools.partial(expert_body, c, half),
        place,
        args,
        specs,
        outs + late,
        out_specs + [whole(o, 1) for o in late],
        (c.F // c.fblk,),
        [
            pltpu.VMEM((count, c.D), F32),
            pltpu.VMEM((count, 128), F32),
            pltpu.VMEM((16, c.half), F32),
            pltpu.VMEM((c.X * c.SP, 128), BF),
        ],
        name="expert",
    )
    return (*result[:5], result[5].reshape(c.X, c.SP, c.D))


def produce_body(c, place, *refs):
    cols, acts, packs, own_ref, oth_ref, out_ref = refs[:2], refs[2:4], refs[4:6], *refs[6:9]
    accs = refs[9:]
    step = pl.program_id(0)

    @pl.when(step == 0)
    def _():
        for acc_ref in accs:
            acc_ref[...] = jnp.zeros_like(acc_ref)

    weights = jnp.concatenate([own_ref[...], oth_ref[...]], axis=1)
    for half in range(2):
        for at in row_chunks(c.CR[half], 320):
            accs[half][at, :] += dot_nn(acts[half][at, :], weights)

    @pl.when(step == pl.num_programs(0) - 1)
    def _():
        for half in range(2):
            values = (accs[half][...] * cols[half][:, 0:1]).astype(BF)
            values = dot_tn(packs[half][...], values).astype(BF)
            for j in range(c.X):
                rows = values[j * c.SP : (j + 1) * c.SP]
                out_ref[j, half * c.SP : (half + 1) * c.SP, :] = rows


def produce(c, order, place, cols, acts, packs, own_w, oth_w):
    out = shape_of((c.X, 2 * c.SP, c.D), BF)
    return call(
        order,
        functools.partial(produce_body, c),
        place,
        [*cols, *acts, *packs, own_w, oth_w],
        [whole(col) for col in cols]
        + [cols_of((rows, c.fblk)) for rows in c.CR]
        + [whole(pack) for pack in packs]
        + [rows_of((c.fblk, c.half))] * 2,
        [out],
        [whole(out, 1)],
        (c.F // c.fblk,),
        [pltpu.VMEM((rows, c.D), F32) for rows in c.CR],
        name="produce",
    )[0]


def grad_second_body(c, own, place, *refs):
    all_ref, cols, acts = refs[0], refs[1:3], refs[3:5]
    out_ref, row_ref = refs[-2:]

    @pl.when(pl.program_id(0) == 0)
    def _():
        for half, base in enumerate((0, c.CR[0])):
            rows_at = slice(base, base + c.CR[half])
            row_ref[rows_at, :] = (all_ref[rows_at, :].astype(F32) * cols[half][:, 0:1]).astype(BF)

    acc = dot_tn(acts[0][...], row_ref[: c.CR[0], :])
    acc = acc + dot_tn(acts[1][...], row_ref[c.CR[0] :, :])
    if own:
        acc = acc + refs[5][...].astype(F32)
    out_ref[...] = acc.astype(out_ref.dtype)


def grad_second(c, order, place, rows, cols, acts, add=None):
    own = add is not None
    args = [rows, *cols, *acts]
    total = sum(c.CR)
    specs = [pl.BlockSpec((total, c.half), lambda i, s: (0, 0 if own else 1))]
    specs += [whole(col) for col in cols] + [cols_of((count, c.fblk)) for count in c.CR]
    if own:
        args.append(add)
        specs.append(rows_of((c.fblk, c.half)))
    out = shape_of((c.F, c.half), F32 if own else BF)
    return call(
        order,
        functools.partial(grad_second_body, c, own),
        place,
        args,
        specs,
        [out],
        [rows_of((c.fblk, c.half))],
        (c.F // c.fblk,),
        [pltpu.VMEM((total, c.half), BF)],
        name="grad_second",
    )[0]


def grad_first_body(c, own, place, *refs):
    acc = dot_tn(refs[0][...], refs[2][...]) + dot_tn(refs[1][...], refs[3][...])
    if own:
        acc = acc + refs[4][...].astype(F32)
    refs[-1][...] = acc.astype(refs[-1].dtype)


def grad_first(c, order, place, rows, gps, add=None):
    own = add is not None
    args = [*rows, *gps]
    specs = [pl.BlockSpec((count, c.half), lambda i, s: (0, 0 if own else 1)) for count in c.CR]
    specs += [cols_of((count, c.fblk)) for count in c.CR]
    if own:
        args.append(add)
        specs.append(cols_of((c.half, c.fblk)))
    out = shape_of((c.half, c.F), F32 if own else BF)
    return call(
        order,
        functools.partial(grad_first_body, c, own),
        place,
        args,
        specs,
        [out],
        [cols_of((c.half, c.fblk))],
        (c.F // c.fblk,),
        name="grad_first",
    )[0]


def combine_body(c, with_dots, place, *refs):
    refs = list(refs)
    extras = [] if with_dots else [refs.pop(0), refs.pop(0)]
    halves = 2 if with_dots else 1
    rows, refs = refs[:halves], refs[halves:]
    tails = []
    if with_dots:
        tails, refs = refs[:2], refs[2:]
    mine_ref = refs.pop(0)
    groups = [(0, g) for g in groups_a(c)] + [(1, g) for g in groups_b(c)]
    outs, (hot_ref, row_ref) = refs[: len(groups)], refs[len(groups) :]
    pad = hot_ref.shape[1] // c.X

    @pl.when(pl.program_id(0) == 0)
    def _():
        row_ref[...] = jnp.zeros_like(row_ref)
        slots = lax.broadcasted_iota(I32, (c.R, pad), 1)
        for k in range(c.n):
            at = pl.multiple_of((place[1] ^ k) * c.R, 16)
            for j in range(c.X):
                hot = (mine_ref[pl.ds(at, c.R), j : j + 1] == slots).astype(BF)
                hot_ref[k * c.R : (k + 1) * c.R, j * pad : (j + 1) * pad] = hot
        if with_dots:
            wide = (c.SP, c.half)
            eye = lax.broadcasted_iota(I32, wide, 0) == lax.broadcasted_iota(I32, wide, 1)
            lane = lax.broadcasted_iota(I32, (1, 128), 1)
            for half in range(2):
                for j in range(c.X):
                    high, low = last_pair(c, tails[half][j], c.half)
                    high = jnp.sum(jnp.where(eye, high, 0.0), axis=1, keepdims=True)
                    low = jnp.sum(jnp.where(eye, low, 0.0), axis=1, keepdims=True)
                    e = expert_of(c, place, j)
                    cols = jnp.where(lane == e, high, jnp.where(lane == e + 64, low, 0.0))
                    at = j * pad + half * c.SP
                    row_ref[at : at + c.SP, :128] = cols.astype(BF)
            pulls = dot_nn(hot_ref[...], row_ref[:, :128]).astype(BF)
            expert = lax.broadcasted_iota(I32, (c.E, 128), 0)
            lane = lax.broadcasted_iota(I32, (c.E, 128), 1)
            pick = ((lane == expert) | (lane == expert + 64)).astype(BF)
            for (side, group), out_ref in zip(groups, outs):
                for at, k in enumerate(group):
                    if side == 0:
                        got = dot_nt(pick, pulls[k * c.R : (k + 1) * c.R])
                        out_ref[at, c.R :, :] = jnp.zeros((c.E, c.half), BF)
                        out_ref[at, c.R :, : c.R] = got.astype(BF)

    for half, rows_ref in enumerate(rows):
        size = rows_ref.shape[1]
        for j in range(c.X):
            at = j * pad + half * size
            row_ref[at : at + size, :] = rows_ref[j]
    result = dot_nn(hot_ref[...], row_ref[...]).astype(BF)
    for half in range(2):

        @pl.when(pl.program_id(0) == half)
        def _():
            for (side, group), out_ref in zip(groups, outs):
                if side == half:
                    for at, k in enumerate(group):
                        out_ref[at, : c.R, :] = result[k * c.R : (k + 1) * c.R]
                        if extras:
                            more = extras[0].shape[1] // 2
                            extra = [e[k, half * more : (half + 1) * more, :] for e in extras]
                            total = extra[0].astype(F32) + extra[1].astype(F32)
                            out_ref[at, c.R :, :] = total.astype(BF)


def combine(c, order, place, rows, mine, extra=None, cost=0):
    pad = up(2 * c.SP, 128)
    args = list(rows)
    specs = [pl.BlockSpec((c.X, r.shape[1], c.half), lambda i, s: (0, 0, i ^ s[2])) for r in rows]
    if extra is None:
        args += list(rows)
        specs += [pl.BlockSpec((c.X, 16, c.half), lambda i, s: (0, c.SP // 16 - 1, 0))] * 2
        outs = piece_outs(c, c.E)
    else:
        args = [*extra, *args]
        specs = [whole(e) for e in extra] + specs
        outs = piece_outs(c, extra[0].shape[1] // 2, extra[0].shape[1] // 2)
    args.append(mine)
    specs.append(whole(mine))
    result = call(
        order,
        functools.partial(combine_body, c, extra is None),
        place,
        args,
        specs,
        outs,
        [whole(o, 1) for o in outs],
        (2,),
        [pltpu.VMEM((c.n * c.R, c.X * pad), BF), pltpu.VMEM((c.X * pad, c.half), BF)],
        name="combine",
        cost=cost,
    )
    return list(result)


def back_two_body(c, place, *refs):
    refs = list(refs)
    groups = groups_of(c)
    heads, refs = refs[: c.n * len(groups)], refs[c.n * len(groups) :]
    count = (len(refs) - 13 - c.n) // 2
    a, b, refs = refs[:count], refs[count : 2 * count], refs[2 * count :]
    w_ref, after_ref, probs_ref, keep_ref = refs[:4]
    cot_ref, hid_ref, small_ref, table_ref, ga_ref, proj_own_ref, proj_oth_ref = refs[4:11]
    mixes, (gb_ref, sums_ref) = refs[11:-2], refs[-2:]
    sum_a = add_up(a)
    live = live_rows(c, place[1] * c.R, c.R)
    cot = jnp.where(live, cot_ref[...], BF(0))
    eshift = table_ref[: c.E, :]
    router = table_ref[c.E : 2 * c.E, :]
    kept = keep_ref[...] > 0
    pulls = jnp.where(kept, sum_a[c.R :, : c.R] + dot_nt(eshift, cot), 0.0)
    probs = probs_ref[...]
    glog = (probs * (pulls - jnp.sum(probs * pulls, axis=0, keepdims=True))).astype(BF)
    two = jnp.concatenate([sum_a[: c.R], add_up(b)], axis=1) + dot_tn(glog, router)
    normed, inv_std = norm_rows(after_ref[...])
    grad_after = cot.astype(F32) + norm_back(two, small_row(c, small_ref, 1), normed, inv_std)
    ga_ref[...] = grad_after
    low = grad_after.astype(BF)
    gb_ref[...] = low
    high, rest = split_low(probs * keep_ref[...])
    hid = jnp.where(live, hid_ref[...], BF(0))
    sums_ref[0:1, :] = jnp.sum(two * normed, axis=0, keepdims=True)
    sums_ref[1:2, :] = jnp.sum(two, axis=0, keepdims=True)
    sums_ref[2:3, :] = jnp.sum(low.astype(F32), axis=0, keepdims=True)
    sums_ref[3:8, :] = jnp.zeros((5, c.D), F32)
    sums_ref[8 : 8 + c.E, :] = dot_nn(high, cot) + dot_nn(rest, cot)
    sums_ref[8 + c.E : 8 + 2 * c.E, :] = dot_nn(glog, hid)
    for k in range(c.n):
        lane = place[1] ^ k
        mix = dot_nt(gb_ref[:, : c.half], w_ref[2 * lane])
        mix = mix + dot_nt(gb_ref[:, c.half :], w_ref[2 * lane + 1])
        mixes[k][...] = mix.astype(BF)
    height = sums_ref.shape[0]
    for cols, out_ref in ((own_cols(c, place), proj_own_ref), (other_cols(c, place), proj_oth_ref)):
        sums = sums_ref[:, cols].astype(BF)
        part = dot_tn(jnp.concatenate([head[...] for head in heads], axis=1), gb_ref[:, cols])
        for k in range(c.n):
            out_ref[k, : c.W, :] = part[k * c.W : (k + 1) * c.W].astype(BF)
            out_ref[k, c.W : c.W + height, :] = sums
            rest = out_ref.shape[1] - c.W - height
            out_ref[k, c.W + height :, :] = jnp.zeros((rest, c.half), BF)


def back_two(c, order, place, heads, sums, proj, lanes, cotangent, hidden, small, table):
    height = 8 + 2 * c.E
    rows = up(c.W + height, 32)
    args = [pair[0] for pair in flat(heads)]
    specs = [
        pl.BlockSpec((None, c.R, a.shape[2]), lambda i, s, at=at: (at, s[1], 0))
        for a, at in flat(heads)
    ]
    args += [*sums[0], *sums[1], proj, *lanes, cotangent, hidden, small, table]
    hid_rows = pl.BlockSpec((c.R, c.D), lambda i, s: (s[1], 0))
    specs += [first_block(a) for a in [*sums[0], *sums[1]]]
    specs += [whole(a) for a in [proj, *lanes]] + [own_rows(c), hid_rows]
    specs += [whole(small), whole(table)]
    outs = [shape_of((c.R, c.D), F32)] + [shape_of((c.n, rows, c.half), BF)] * 2
    outs += [shape_of((c.R, c.W), BF) for _ in range(c.n)]
    result = call(
        order,
        functools.partial(back_two_body, c),
        place,
        args,
        specs,
        outs,
        [whole(o) for o in outs],
        (1,),
        [pltpu.VMEM((c.R, c.D), BF), pltpu.VMEM((height, c.D), F32)],
        name="back_two",
    )
    return (*result[:3], list(result[3:]))


def block_out_body(c, place, *refs):
    refs = list(refs)
    count = (len(refs) - 6) // 2
    a, b, refs = refs[:count], refs[count : 2 * count], refs[2 * count :]
    after_ref, probs_ref, keep_ref, table_ref, out_ref, proj_ref = refs
    high, low = split_low(probs_ref[...] * keep_ref[...])
    eshift = table_ref[: c.E, :]
    shift = dot_tn(high, eshift) + dot_tn(low, eshift)
    more = proj_ref.shape[0] // 2
    for h, pieces in enumerate((a, b)):
        cols = slice(h * c.half, (h + 1) * c.half)
        total = add_up([ref.at[: c.R, :] for ref in pieces])
        out_ref[h] = (after_ref[:, cols] + total + shift[:, cols]).astype(BF)
        proj_ref[h * more : (h + 1) * more, :] = same_sum(c, pieces, slice(c.R, c.R + more)).astype(BF)


def block_out(c, order, place, sums, after, probs, keep, table):
    args = [*sums[0], *sums[1], after, probs, keep, table]
    more = 2 * (sums[0][0].shape[1] - c.R)
    outs = [shape_of((2, c.R, c.half), BF), shape_of((more, c.half), BF)]
    return call(
        order,
        functools.partial(block_out_body, c),
        place,
        args,
        [first_block(a) for a in args[:-4]] + [whole(a) for a in args[-4:]],
        outs,
        [whole(o) for o in outs],
        (1,),
        name="block_out",
    )


def grad_one_body(c, place, dqkv_ref, normed_ref, own_ref, oth_ref, *outs):
    sums_ref = outs[-1]
    groups = [(0, g) for g in groups_a(c)] + [(1, g) for g in groups_b(c)]
    for side in range(2):
        cols = slice(side * c.half, (side + 1) * c.half)
        weights = [jnp.where(place[2] == side, own_ref[p], oth_ref[p]) for p in range(3)]
        weights = jnp.concatenate(weights, axis=1)
        gain = jnp.zeros((1, c.half), F32)
        shift = jnp.zeros((1, c.half), F32)
        for (where, group), out_ref in zip(groups, outs):
            if where != side:
                continue
            for row, k in enumerate(group):
                rows_at = pl.ds(pl.multiple_of((place[1] ^ k) * c.R, 16), c.R)
                acc = dot_nt(dqkv_ref[rows_at, :], weights)
                out_ref[row, : c.R, :] = acc.astype(BF)
                normed = normed_ref[rows_at, cols].astype(F32)
                gain = gain + jnp.sum(acc * normed, axis=0, keepdims=True)
                shift = shift + jnp.sum(acc, axis=0, keepdims=True)
        sums_ref[0:1, cols] = gain
        sums_ref[1:2, cols] = shift
        row = lax.broadcasted_iota(I32, (16, 1), 0)
        tile = jnp.where(row == 0, gain, jnp.where(row == 1, shift, 0.0)).astype(BF)
        for (where, group), out_ref in zip(groups, outs):
            if where == side:
                for at in range(len(group)):
                    out_ref[at, c.R :, :] = tile


def grad_one(c, order, place, dqkv, normed, own_w, oth_w):
    outs = piece_outs(c, 16, 16) + [shape_of((2, c.D), F32)]
    result = call(
        order,
        functools.partial(grad_one_body, c),
        place,
        [dqkv, normed, own_w, oth_w],
        [whole(dqkv), whole(normed), whole(own_w), whole(oth_w)],
        outs,
        [whole(o) for o in outs],
        (1,),
        name="grad_one",
    )
    return list(result[:-1]), result[-1]


def grad_qkv_body(c, place, hid_ref, dqkv_ref, own_ref, oth_ref):
    own_ref[0] = dot_tn(hid_ref[:, own_cols(c, place)], dqkv_ref[...]).astype(BF)
    oth_ref[0] = dot_tn(hid_ref[:, other_cols(c, place)], dqkv_ref[...]).astype(BF)


def grad_qkv(c, order, place, hidden, dqkv):
    specs = [whole(hidden, 1), cols_of((c.TP, c.W))]
    if c.W % 128:
        dqkv = dqkv.reshape(c.TP, 3, c.W).transpose(1, 0, 2)
        specs[1] = pl.BlockSpec((None, c.TP, c.W), lambda i, s: (i, 0, 0))
    return call(
        order,
        functools.partial(grad_qkv_body, c),
        place,
        [hidden, dqkv],
        specs,
        [shape_of((3, c.half, c.W), BF)] * 2,
        [rows_of((1, c.half, c.W))] * 2,
        (3,),
        name="grad_qkv",
    )


def back_one_body(c, place, *refs):
    refs = list(refs)
    count = (len(refs) - 4) // 2
    a, b, refs = refs[:count], refs[count : 2 * count], refs[2 * count :]
    tok_ref, after_ref, small_ref, out_ref = refs
    live = live_rows(c, place[1] * c.R, c.R)
    normed, inv_std = norm_rows(jnp.where(live, tok_ref[...].astype(F32), 0.0))
    one = jnp.concatenate([add_up(a)[: c.R], add_up(b)[: c.R]], axis=1)
    grad = after_ref[...] + norm_back(one, small_row(c, small_ref, 0), normed, inv_std)
    for h in range(2):
        out_ref[h] = grad[:, h * c.half : (h + 1) * c.half].astype(BF)


def back_one(c, order, place, sums, tokens, after, small):
    args = [*sums[0], *sums[1], tokens, after, small]
    specs = [first_block(a) for a in args[:-3]] + [own_rows(c), whole(after), whole(small)]
    out = shape_of((2, c.R, c.half), BF)
    return call(
        order,
        functools.partial(back_one_body, c),
        place,
        args,
        specs,
        [out],
        [whole(out)],
        (1,),
        name="back_one",
    )[0]


def assemble_body(c, place, *refs):
    pieces, out_ref = refs[:-1], refs[-1]
    for k in range(c.n):

        @pl.when((place[1] ^ k) == pl.program_id(0))
        def _():
            for h in range(2):
                values = pieces[2 * k + h][...].astype(out_ref.dtype)
                out_ref[:, h * c.half : (h + 1) * c.half] = values


def assemble(c, order, place, pieces, dtype):
    out = shape_of((c.T, c.D), dtype)
    return call(
        order,
        functools.partial(assemble_body, c),
        place,
        [pair[0] for pair in flat(pieces)],
        [
            pl.BlockSpec((None, c.R, c.half), lambda i, s, at=at: (at, 0, 0))
            for _, at in flat(pieces)
        ],
        [out],
        [rows_of((c.R, c.D))],
        (-(-c.T // c.R),),
        name="assemble",
    )[0]


def local(
    tokens,
    cotangent,
    w_qkv,
    qv_bias,
    w_proj,
    proj_bias,
    norm_gains,
    norm_shifts,
    w_router,
    expert_shift,
    w_first,
    w_second,
    first_bias,
    routes,
    priority,
):
    T, D = tokens.shape
    n = lax.axis_size("mp")
    E = w_router.shape[1]
    S = 16 * T // (5 * E)
    R = up(-(-T // n), 16)
    F = w_first.shape[2]
    W = w_proj.shape[0]
    win = up(IMG_LEN + 15, 16)
    Q = (S + 1) // 2
    cap = (9 * T + 4 * EXP_DEV - 1) // (4 * EXP_DEV)
    X = E // EXP_DEV
    full = min(cap // S, X)
    c = Sizes(
        T=T,
        D=D,
        half=D // 2,
        n=n,
        X=X,
        E=E,
        S=S,
        Q=Q,
        SP=up(Q + 2, 16),
        CR=(up(min(cap, X * Q), 16), up(full * (S - Q) + max(0, cap - full * S - Q), 16)),
        R=R,
        TP=n * R,
        W=W,
        images=T // IMG_LEN,
        quarters=n // EXP_DEV,
        F=F,
        cap=cap,
        win=win,
        fblk=min(1024, F),
    )
    order = Order()
    dp, mp, grid = lax.axis_index("dp"), lax.axis_index("mp"), lax.axis_index("grid")
    place = jnp.stack([dp, mp, grid, mp // c.quarters]).astype(I32)

    slot, blocks, rt, grad_out = route(c, order, place, routes, priority, cotangent)
    grad_in = trade(grad_out, "dp")

    def both_halves(rows):
        rows = jnp.pad(rows, ((0, up(rows.shape[0], 16) - rows.shape[0]), (0, 0)))
        other = swap_grid(rows)
        return jnp.where(
            grid == 0,
            jnp.concatenate([rows, other], axis=1),
            jnp.concatenate([other, rows], axis=1),
        )

    wide_bias = jnp.pad(qv_bias, ((0, 0), (0, c.half - W)))
    small = both_halves(
        jnp.concatenate([norm_gains, norm_shifts, proj_bias[None], wide_bias], axis=0)
    )
    qkv_own = w_qkv.transpose(1, 0, 2)
    qkv_oth = swap_grid(qkv_own)

    first_own = w_first[0]
    second_own = w_second[0]
    proj = lax.all_gather(w_proj, ("mp", "grid"))

    groups = groups_of(c)
    outs = [shape_of((c.TP, D), BF), shape_of((c.TP, 3 * W), BF), shape_of((c.TP, D), BF)]
    outs.append(shape_of((len(groups), c.TP, groups[0][1]), BF))

    def first_steps(width):
        return pl.BlockSpec((c.R, width), lambda i, s: (jnp.minimum(i, n - 1), 0))

    hidden_one, qkv, normed_one, mix = call(
        order,
        functools.partial(qkv_body, c),
        place,
        [tokens, small, qkv_own, qkv_oth],
        [
            pl.BlockSpec((R, D), lambda i, s: (jnp.minimum(i, last_block(c)), 0)),
            whole(small),
            whole(qkv_own),
            whole(qkv_oth),
        ],
        outs,
        [first_steps(D), first_steps(3 * W), first_steps(D), whole(outs[3])],
        (n + c.images,),
        [pltpu.VMEM((D, 3 * W), BF), pltpu.VMEM((c.TP, 3 * W), BF)],
        name="qkv",
    )
    bias_rows = F // 2 // c.half
    tied = held(jnp.concatenate([expert_shift, w_router.T]), qkv)
    table = both_halves(tied)
    bias = both_halves(held(first_bias.reshape(bias_rows, c.half), qkv))[:bias_rows]
    bias = bias.reshape(bias_rows, 2, c.half).transpose(1, 0, 2).reshape(1, F).astype(F32)
    second_oth = swap_grid(held(second_own, qkv))
    first_oth = swap_grid(held(first_own, qkv))
    mixes, _ = gather_mp(c, held(mix, proj))
    hidden_two, weight, after, probs, rows_a = middle(
        c, order, place, mixes, proj, tokens, small, table, blocks, slot
    )

    rows_a = trade(rows_a, "dp")
    rows_b = dispatch(c, order, place, slot, hidden_two, weight, 1)
    ga_a, ga_b, grad_all, pack_a, pack_b = grad_active(
        c, order, place, grad_in, second_own, second_oth
    )
    rows_b = trade(held(rows_b, rows_a, grad_all), "dp")
    act_a, gp_a, gb_a, all_a, col_a, back_a = expert(
        c, order, place, 0, rows_a, pack_a, first_own, first_oth, bias, ga_a
    )
    back_a = trade(held(back_a, rows_b), "dp")
    act_b, gp_b, gb_b, all_b, col_b, back_b = expert(
        c, order, place, 1, rows_b, pack_b, first_own, first_oth, bias, ga_b
    )
    back_b = trade(held(back_b, back_a), "dp")
    cols, acts, gps, alls = [col_a, col_b], [act_a, act_b], [gp_a, gp_b], [all_a, all_b]
    second_part = swap_grid(grad_second(c, order, place, grad_all, cols, acts))
    order.tie(back_a)
    first_part = swap_grid(grad_first(c, order, place, alls, gps))
    mine, keep, keep_lane = keep_of(c, order, place, grad_in, blocks, rt)
    keep_mask = keep[:, :2, :].transpose(0, 2, 1).reshape(c.TP, 2)[:T].astype(I32)
    mine = mine.transpose(0, 2, 1).reshape(c.TP, 8)
    order.tie(mine)
    packs = [pack_a, pack_b]
    prod = produce(c, order, place, cols, acts, packs, second_own, second_oth)
    gb = (gb_a + gb_b)[0:1].reshape(2, F // 2)
    gb_own = lax.dynamic_index_in_dim(gb, grid, 0, True)
    gb_oth = lax.dynamic_index_in_dim(gb, 1 - grid, 0, True)
    grad_fbias = gb_own + swap_grid(gb_oth)

    pieces = combine(c, order, place, [back_a, back_b], mine)
    prod = trade(held(prod, back_b), "dp")
    two_sums = reduce_start(c, pieces)
    grad_second_out = grad_second(c, order, place, grad_all, cols, acts, second_part)
    two_sums = reduce_end(c, order, two_sums)
    grad_after, proj_a, proj_b, grad_mix = back_two(
        c,
        order,
        place,
        mixes,
        two_sums,
        proj,
        [after, probs, keep_lane],
        cotangent,
        hidden_two,
        small,
        table,
    )
    grad_mix = [grad_mix[0]] + [swap_mp(c, grad_mix[k], k) for k in range(1, n)]
    proj_parts = [proj_a, swap_grid(proj_b)]
    pieces = combine(c, order, place, [prod], mine, proj_parts, cost=10)
    out_sums = reduce_start(c, [held(p, *grad_mix) for p in pieces])

    outs = [shape_of((c.TP, 3 * W), BF), shape_of((8, 3 * W), F32)]
    dqkv, dqkv_sums = call(
        order,
        functools.partial(attend_back_body, c),
        place,
        [qkv, *grad_mix],
        [whole(qkv)] + [whole(p) for p in grad_mix],
        outs,
        [whole(o) for o in outs],
        (c.images,),
        [pltpu.VMEM((c.TP, W), BF)],
        name="attend_back",
    )
    one_pieces, one_parts = grad_one(c, order, place, dqkv, normed_one, qkv_own, qkv_oth)
    one_sums = reduce_start(c, one_pieces)
    out_sums = reduce_end(c, order, out_sums)
    qkv_a, qkv_b = grad_qkv(c, order, place, hidden_one, dqkv)
    qkv_b = swap_grid(qkv_b)
    qkv_low = (qkv_a.astype(F32) + qkv_b.astype(F32)).astype(BF)
    qkv_sum = sum_dp_start(c, qkv_low.reshape(-1, c.half))
    one_sums = reduce_end(c, order, one_sums)
    grad_low = back_one(c, order, place, one_sums, tokens, grad_after, small)
    qkv_sum = sum_dp_turn(c, qkv_sum)
    order.tie(qkv_sum)
    out_lane, proj_sum = block_out(c, order, place, out_sums, after, probs, keep_lane, table)

    qv_rows = jnp.concatenate([dqkv_sums[0:1, :W], dqkv_sums[0:1, 2 * W :]], axis=0)
    sums_one = held(first_sums(c, one_sums, one_parts), grad_low)
    sums_one = chip_sums(c, sums_one, qv_rows, grid).astype(BF)
    proj_end = proj_sum.shape[0]
    shared = jnp.concatenate([proj_sum, sums_one], axis=0)
    shared = jnp.pad(shared, ((0, up(shared.shape[0], 16 * c.X) - shared.shape[0]), (0, 0)))
    shared = sum_dp_start(c, shared)

    def last_expert_kernel(before):
        for value in before:
            order.tie(value)
        return grad_first(c, order, place, alls, gps, first_part), order.hold

    grad_low, out_lane, last, grad_first_out = gather_both(c, grad_low, out_lane, last_expert_kernel)
    grad_w_qkv = sum_dp_end(c, qkv_sum).reshape(3, c.half, W)
    shared = sum_dp_end(c, sum_dp_turn(c, held(shared, *last)))
    sums_one = shared[proj_end:]
    rest = shared[W : W + 8 + 2 * E]
    grad_tokens = assemble(c, order, place, grad_low, F32)
    block = assemble(c, order, place, out_lane, BF)
    return (
        block,
        grad_tokens,
        grad_w_qkv.transpose(1, 0, 2),
        sums_one[2:3, :W],
        shared[:W],
        rest[2],
        jnp.stack([sums_one[0], rest[0]]),
        jnp.stack([sums_one[1], rest[1]]),
        rest[8 + E : 8 + 2 * E].T,
        rest[8 : 8 + E],
        grad_first_out[None],
        grad_second_out[None],
        grad_fbias,
        keep_mask,
    )


def solution(mesh):
    return jax.shard_map(
        local,
        mesh=mesh,
        in_specs=(
            P(("dp", "grid"), None),
            P(("dp", "grid"), None),
            P("grid", None, "mp"),
            P("grid", "mp"),
            P("mp", "grid"),
            P("grid"),
            P(None, "grid"),
            P(None, "grid"),
            P("grid", None),
            P(None, "grid"),
            P(("dp", "mp"), "grid", None),
            P(("dp", "mp"), None, "grid"),
            P(("dp", "mp"), "grid"),
            P(("dp", "grid"), None),
            P(("dp", "grid"), None),
        ),
        out_specs=(
            P(("dp", "grid"), None),
            P(("dp", "grid"), None),
            P("grid", None, "mp"),
            P("grid", "mp"),
            P("mp", "grid"),
            P("grid"),
            P(None, "grid"),
            P(None, "grid"),
            P("grid", None),
            P(None, "grid"),
            P(("dp", "mp"), "grid", None),
            P(("dp", "mp"), None, "grid"),
            P(("dp", "mp"), "grid"),
            P(("dp", "grid"), None),
        ),
        check_vma=False,
    )
```

```python
import functools
from typing import NamedTuple

import jax
import jax.numpy as jnp
from jax import lax
from jax.experimental import pallas as pl
from jax.experimental.pallas import tpu as pltpu
from jax.sharding import PartitionSpec as P

HEAD = 64
IMG_LEN = 197
EXP_DEV = 4
BF = jnp.bfloat16
F32 = jnp.float32
I32 = jnp.int32
VMEM_BYTES = 56 * 1024 * 1024
LOW = -1e30


class Sizes(NamedTuple):
    T: int
    D: int
    half: int
    n: int
    X: int
    E: int
    S: int
    Q: int
    SP: int
    CR: tuple
    R: int
    TP: int
    W: int
    images: int
    quarters: int
    F: int
    cap: int
    win: int
    fblk: int


class Order:
    def __init__(self):
        self.after = []

    def tie(self, value):
        self.after.append(value)

    def hold(self, *values):
        return lax.optimization_barrier((*values, *self.after))[: len(values)]


def up(value, step):
    return -(-value // step) * step


def dot_nn(a, b):
    return jnp.dot(a, b, preferred_element_type=F32)


def dot_nt(a, b):
    return lax.dot_general(a, b, (((1,), (1,)), ((), ())), preferred_element_type=F32)


def dot_tn(a, b):
    return lax.dot_general(a, b, (((0,), (0,)), ((), ())), preferred_element_type=F32)


def split_low(values):
    high = values.astype(BF)
    return high, (values - high.astype(F32)).astype(BF)


def shape_of(dims, dtype):
    return jax.ShapeDtypeStruct(dims, dtype)


def whole(array, buffers=None):
    dims = tuple(array.shape)
    extra = {} if buffers is None else {"pipeline_mode": pl.Buffered(buffers)}
    return pl.BlockSpec(dims, lambda i, s: (0,) * len(dims), **extra)


def rows_of(dims):
    return pl.BlockSpec(dims, lambda i, s: (i,) + (0,) * (len(dims) - 1))


def cols_of(dims):
    return pl.BlockSpec(dims, lambda i, s: (0,) * (len(dims) - 1) + (i,))


def call(order, body, place, args, specs, outs, out_specs, grid, scratch=(), name=None, cost=0):
    extra = order.after
    count = len(args)

    def wrapped(place, *refs):
        body(place, *refs[:count], *refs[count + len(extra) :])

    result = pl.pallas_call(
        wrapped,
        grid_spec=pltpu.PrefetchScalarGridSpec(
            num_scalar_prefetch=1,
            grid=grid,
            in_specs=list(specs) + [pl.BlockSpec(memory_space=pl.ANY)] * len(extra),
            out_specs=list(out_specs),
            scratch_shapes=list(scratch),
        ),
        out_shape=list(outs),
        compiler_params=pltpu.CompilerParams(
            dimension_semantics=("arbitrary",) * len(grid), vmem_limit_bytes=VMEM_BYTES
        ),
        cost_estimate=pl.CostEstimate(
            flops=1000 + int(1.1e9 * cost), bytes_accessed=1000, transcendentals=0
        ),
        name=name,
    )(place, *args, *extra)
    order.after = [min(result, key=lambda o: o.size)]
    return result


def swap_mp(c, value, mask):
    return lax.ppermute(value, "mp", [(i, i ^ mask) for i in range(c.n)])


def swap_grid(value):
    return lax.ppermute(value, "grid", [(0, 1), (1, 0)])


def held(value, *others):
    return lax.optimization_barrier((value, *others))[0]


def trade(value, axis):
    return lax.all_to_all(value, axis, split_axis=0, concat_axis=0, tiled=True)


def groups_a(c):
    return [[0, 2], [1, 3]] if c.n == 4 else [[k] for k in range(c.n)]


def groups_b(c):
    return [[0, 1], [2, 3]] if c.n == 4 else [[k] for k in range(c.n)]


def reduce_start(c, arrays):
    a, b = arrays[: len(arrays) // 2], arrays[len(arrays) // 2 :]
    if c.n != 4:
        return [[x[0]] + [swap_mp(c, x[k], k) for k in range(1, c.n)] for x in (a, b)]
    return [[a[0], swap_mp(c, a[1], 1)], [b[0], swap_mp(c, b[1], 2)]]


def reduce_end(c, order, state):
    if c.n != 4:
        return state
    (a, ra), (b, rb) = state
    ra, rb = order.hold(ra, rb)
    ta = (a[1:].astype(F32) + ra[1:].astype(F32)).astype(BF)
    tb = (b[1:].astype(F32) + rb[1:].astype(F32)).astype(BF)
    order.tie(ta)
    order.tie(tb)
    return [[a, ra, swap_mp(c, ta, 2)], [b, rb, swap_mp(c, tb, 1)]]


def piece_outs(c, more_a=0, more_b=0):
    outs = [shape_of((len(g), c.R + more_a, c.half), BF) for g in groups_a(c)]
    return outs + [shape_of((len(g), c.R + more_b, c.half), BF) for g in groups_b(c)]


def first_block(array):
    dims = tuple(array.shape)
    return pl.BlockSpec((None,) + dims[1:], lambda i, s: (0, 0, 0))


def same_sum(c, refs, rows):
    parts = [ref[rows, :].astype(F32) for ref in refs]
    if c.n == 4:
        return (parts[0] + parts[1]).astype(BF).astype(F32) + parts[2]
    while len(parts) > 1:
        parts = [parts[i] + parts[i + 1] for i in range(0, len(parts), 2)]
    return parts[0]


def add_up(refs):
    total = refs[0][...].astype(F32)
    for ref in refs[1:]:
        total = total + ref[...].astype(F32)
    return total


def sum_dp_start(c, value):
    return trade(value.reshape((c.X, value.shape[0] // c.X) + value.shape[1:]), "dp")


def sum_dp_turn(c, parts):
    total = jnp.sum(parts.astype(F32), axis=0).astype(BF)
    return jnp.broadcast_to(total[None], (c.X,) + total.shape)


def sum_dp_end(c, spread):
    return trade(spread, "dp").reshape((-1,) + spread.shape[2:]).astype(F32)


def gather_mp(c, value, until=None):
    if c.n != 4 or value.shape[0] != 2:
        parts = [value] + [swap_mp(c, value, k) for k in range(1, c.n)]
        return [[(p, h) for h in range(value.shape[0])] for p in parts], parts[1:]
    one = swap_mp(c, value, 1)
    two = swap_mp(c, value, 2)
    ends = one[0:1], two[1:2]
    if until is not None:
        ends = held(ends[0], *until), held(ends[1], *until)
    far_a = swap_mp(c, ends[0], 2)
    far_b = swap_mp(c, ends[1], 1)
    near = [[(p, 0), (p, 1)] for p in (value, one, two)]
    return near + [[(far_a, 0), (far_b, 0)]], [one, two]


def gather_both(c, first, second, filler):
    if c.n != 4:
        filled, _ = filler([first])
        return gather_mp(c, first)[0], gather_mp(c, second)[0], (first,), filled
    one, two = swap_mp(c, first, 1), swap_mp(c, first, 2)
    near = jnp.concatenate([one[0:1], second]), jnp.concatenate([two[1:2], second])
    by_two, by_one = [swap_mp(c, x, mask) for x, mask in zip(near, (2, 1))]
    filled, hold = filler(near)
    by_two, by_one = hold(by_two, by_one)
    far_a, far_b = swap_mp(c, by_one[1:2], 2), swap_mp(c, by_two[2:3], 1)
    pieces = [[(p, 0), (p, 1)] for p in (first, one, two)] + [[(by_two, 0), (by_one, 0)]]
    others = [[(second, 0), (second, 1)], [(by_one, 1), (by_one, 2)], [(by_two, 1), (by_two, 2)]]
    return pieces, others + [[(far_a, 0), (far_b, 0)]], (by_one, by_two), filled


def flat(pieces):
    return [pair for piece in pieces for pair in piece]


def fold(c, value, axes):
    for axis, size in axes:
        mask = 1
        while mask < size:
            value = value + lax.ppermute(value, axis, [(i, i ^ mask) for i in range(size)])
            mask *= 2
    return value


def first_sums(c, sums, one_parts):
    if c.n != 4:
        return fold(c, one_parts, (("mp", c.n),))
    halves = []
    for a, b, far in sums:
        pair = (a[0, c.R : c.R + 2].astype(F32) + b[0, c.R : c.R + 2].astype(F32)).astype(BF)
        halves.append(pair.astype(F32) + far[0, c.R : c.R + 2].astype(F32))
    return jnp.concatenate(halves, axis=1)


def chip_sums(c, one, parts, grid):
    def half_of(side):
        cols = lax.dynamic_slice_in_dim(one, side * c.half, c.half, 1)
        row = lax.dynamic_index_in_dim(parts, side, 0, True)
        return jnp.concatenate([cols, jnp.pad(row, ((0, 0), (0, c.half - c.W)))], axis=0)

    return half_of(grid) + swap_grid(half_of(1 - grid))


def expert_of(c, place, j):
    return j * EXP_DEV + place[3]


def window_slot(c, slot):
    return jnp.where(slot < c.Q, slot, slot + (c.SP - c.Q))


def count_places(c, rank_ref, rt_ref, slot_ref, blocks_ref, rtb_ref):
    pad = jnp.full((2, c.TP - c.T), -1, I32)
    rank = jnp.concatenate([rank_ref[...], pad], axis=1)
    rt = jnp.concatenate([rt_ref[...], pad], axis=1)
    side = 64
    index = lax.broadcasted_iota(I32, (side, c.TP), 0)
    rows = [(index == (rank[k : k + 1] >> 6)).astype(BF) for k in range(2)]
    cols = [index == (rank[k : k + 1] & 63) for k in range(2)]
    table = jnp.zeros((side, side), F32)
    for k in range(2):
        named = (rt[k : k + 1] + 1).astype(F32)
        table = table + dot_nt(rows[k], jnp.where(cols[k], named, 0.0).astype(BF))
    up_to = lax.broadcasted_iota(I32, (side, side), 0) < lax.broadcasted_iota(I32, (side, side), 1)
    above = lax.broadcasted_iota(I32, (side, side), 0) > lax.broadcasted_iota(I32, (side, side), 1)
    lane = lax.broadcasted_iota(I32, (1, 128), 1)
    named = [(table == e + 1.0).astype(F32) for e in range(c.E)]
    along = dot_nn(jnp.concatenate(named, axis=0).astype(BF), up_to.astype(BF))
    numbers = jnp.zeros((side, 128), F32)
    for e in range(c.E):
        numbers = numbers + jnp.where(lane == e, jnp.sum(named[e], axis=1, keepdims=True), 0.0)
    down = dot_nn(above.astype(BF), numbers.astype(BF))
    place_of = jnp.zeros((side, side), F32)
    for e in range(c.E):
        here = along[e * side : (e + 1) * side] + down[:, e : e + 1]
        place_of = place_of + named[e] * here
    place_of = place_of.astype(I32)
    high = (place_of >> 4).astype(F32).astype(BF)
    low = (place_of & 15).astype(F32).astype(BF)
    places = []
    for k in range(2):
        values = dot_tn(high, rows[k]) * 16.0 + dot_tn(low, rows[k])
        places.append(jnp.sum(jnp.where(cols[k], values, 0.0), axis=0, keepdims=True).astype(I32))
    for e in range(c.E):
        second = jnp.where(rt[1:2, :] == e, places[1], -1)
        slot_ref[e : e + 1, :] = jnp.where(rt[0:1, :] == e, places[0], second)
    for r in range(c.n):
        blocks_ref[r] = slot_ref[:, r * c.R : (r + 1) * c.R]
        rtb_ref[r] = jnp.concatenate([rt[:, r * c.R : (r + 1) * c.R]] * 4, axis=0)
    numbers = jnp.sum(numbers, axis=0, keepdims=True)
    return jnp.concatenate([numbers, jnp.zeros((1, c.half - 128), F32)], axis=1).astype(I32)


def fill_hot(c, place, slot_ref, hot_ref, halves):
    for j in range(c.X):
        row = window_slot(c, slot_ref[pl.ds(expert_of(c, place, j), 1), :])
        for index, half in enumerate(halves):
            slots = lax.broadcasted_iota(I32, (c.SP, c.TP), 0) + half * c.SP
            hot_ref[index, j * c.SP : (j + 1) * c.SP, :] = (slots == row).astype(BF)


def route_body(c, place, *refs):
    rank_ref, rt_ref, src_ref, slot_ref, blocks_ref, rtb_ref, out_ref, hot_ref, sum_ref = refs

    @pl.when(pl.program_id(0) == 0)
    def _():
        numbers = count_places(c, rank_ref, rt_ref, slot_ref, blocks_ref, rtb_ref)
        sum_ref[0:1, :] = (numbers >> 4).astype(F32)
        sum_ref[1:2, :] = (numbers & 15).astype(F32)
        fill_hot(c, place, slot_ref, hot_ref, (0, 1))

    for half in range(2):
        acc = dot_nn(hot_ref[half, :, : c.T], src_ref[...])
        for j in range(c.X):
            at = (2 * j + half) * c.SP
            out_ref[at : at + c.SP, :] = acc[j * c.SP : (j + 1) * c.SP].astype(BF)
            if half == 0:

                @pl.when(pl.program_id(0) == 0)
                def _():
                    tile = acc[(j + 1) * c.SP - 16 : (j + 1) * c.SP]
                    tile = last_rows(c, tile, sum_ref[0:1, :], sum_ref[1:2, :])
                    out_ref[at + c.SP - 16 : at + c.SP, :] = tile.astype(BF)


def route(c, order, place, routes, priority, source):
    rank = priority.T
    rt = routes.T
    outs = [
        shape_of((c.E, c.TP), I32),
        shape_of((c.n, c.E, c.R), I32),
        shape_of((c.n, 8, c.R), I32),
        shape_of((2 * c.X * c.SP, c.D), BF),
    ]
    result = call(
        order,
        functools.partial(route_body, c),
        place,
        [rank, rt, source],
        [whole(rank), whole(rt)]
        + [pl.BlockSpec((c.T, c.half), lambda i, s: (0, i ^ s[2]))],
        outs,
        [whole(o) for o in outs[:3]] + [cols_of((2 * c.X * c.SP, c.half))],
        (2,),
        [pltpu.VMEM((2, c.X * c.SP, c.TP), BF), pltpu.VMEM((8, c.half), F32)],
        name="route",
    )
    return (*result[:3], result[3].reshape(c.X, 2 * c.SP, c.D))


def keep_body(c, place, tail_ref, slot_ref, rt_ref, mine_ref, keep_ref, lane_ref):
    earlier = jnp.zeros((1, 128), F32)
    for b in range(c.X):
        high, low = last_pair(c, tail_ref[b], 128)
        earlier = earlier + jnp.where(b < place[0], high * 16.0 + low, 0.0)
    wide = (c.E, 128)
    eye = lax.broadcasted_iota(I32, wide, 0) == lax.broadcasted_iota(I32, wide, 1)
    offset = jnp.sum(jnp.where(eye, earlier, 0.0), axis=1, keepdims=True).astype(I32)
    slot = slot_ref[0]
    kept = (slot >= 0) & (slot + offset < c.cap)
    slots = jnp.where(kept, window_slot(c, slot), -1)
    expert = lax.broadcasted_iota(I32, (c.E, 1), 0)
    for j in range(8):
        if j < c.X:
            here = jnp.where(expert == expert_of(c, place, j), slots, -1)
            mine_ref[0, j : j + 1, :] = jnp.max(here, axis=0, keepdims=True)
        else:
            mine_ref[0, j : j + 1, :] = jnp.full((1, c.R), -1, I32)
    rows = []
    for k in range(2):
        picked = jnp.where((rt_ref[0, k : k + 1, :] == expert) & kept, 1.0, 0.0)
        rows.append(jnp.sum(picked, axis=0, keepdims=True))
    keep_ref[0] = jnp.concatenate(rows * 4, axis=0)

    @pl.when(pl.program_id(0) == place[1])
    def _():
        lane_ref[...] = jnp.where(kept, 1.0, 0.0)


def keep_of(c, order, place, rows, blocks, rt):
    outs = [
        shape_of((c.n, 8, c.R), I32),
        shape_of((c.n, 8, c.R), F32),
        shape_of((c.E, c.R), F32),
    ]
    tail = pl.BlockSpec((c.X, 16, c.half), lambda i, s: (0, c.SP // 16 - 1, 0))
    return call(
        order,
        functools.partial(keep_body, c),
        place,
        [rows, blocks, rt],
        [tail, rows_of((1, c.E, c.R)), rows_of((1, 8, c.R))],
        outs,
        [rows_of((1, 8, c.R)), rows_of((1, 8, c.R)), whole(outs[2])],
        (c.n,),
        name="keep",
    )


def last_rows(c, tile, high, low):
    row = lax.broadcasted_iota(I32, (16, 1), 0)
    return jnp.where(row == 14, high, jnp.where(row == 15, low, tile))


def put_gates(c, place, hot_ref, weights, acc, out_ref):
    gates = dot_nn(hot_ref[0], weights)
    lane = lax.broadcasted_iota(I32, (1, 128), 1)
    wide = (c.SP, c.half)
    eye = lax.broadcasted_iota(I32, wide, 0) == lax.broadcasted_iota(I32, wide, 1)
    for j in range(c.X):
        e = expert_of(c, place, j)
        mine = gates[j * c.SP : (j + 1) * c.SP]
        rows = []
        for at in (e, e + 64):
            col = jnp.sum(jnp.where(lane == at, mine, 0.0), axis=1, keepdims=True)
            rows.append(jnp.sum(jnp.where(eye, col, 0.0), axis=0, keepdims=True))
        end = (j + 1) * c.SP
        tile = last_rows(c, acc[end - 16 : end], rows[0], rows[1])
        out_ref[end - 16 : end, :] = tile.astype(BF)


def dispatch_body(c, half, place, slot_ref, src_ref, weight_ref, out_ref, hot_ref):
    @pl.when(pl.program_id(0) == 0)
    def _():
        fill_hot(c, place, slot_ref, hot_ref, (half,))

    acc = dot_nn(hot_ref[0], src_ref[...])
    out_ref[...] = acc.astype(BF)

    @pl.when(pl.program_id(0) == 0)
    def _():
        put_gates(c, place, hot_ref, weight_ref[...], acc, out_ref)


def dispatch(c, order, place, slot, source, weight, half):
    return call(
        order,
        functools.partial(dispatch_body, c, half),
        place,
        [slot, source, weight],
        [whole(slot), pl.BlockSpec((c.TP, c.half), lambda i, s: (0, i ^ s[2])), whole(weight)],
        [shape_of((c.X * c.SP, c.D), BF)],
        [cols_of((c.X * c.SP, c.half))],
        (2,),
        [pltpu.VMEM((1, c.X * c.SP, c.TP), BF)],
        name="dispatch",
    )[0].reshape(c.X, c.SP, c.D)


def norm_rows(values):
    centred = values - jnp.mean(values, axis=-1, keepdims=True)
    inv_std = lax.rsqrt(jnp.mean(centred * centred, axis=-1, keepdims=True) + 1e-06)
    return centred * inv_std, inv_std


def norm_back(grad_norm, gain, normed, inv_std):
    scaled = grad_norm * gain
    return inv_std * (
        scaled
        - jnp.mean(scaled, axis=-1, keepdims=True)
        - normed * jnp.mean(scaled * normed, axis=-1, keepdims=True)
    )


def small_row(c, small_ref, index, count=1):
    return small_ref[index : index + count, :].astype(F32)


def own_cols(c, place):
    return pl.ds(pl.multiple_of(place[2] * c.half, c.half), c.half)


def other_cols(c, place):
    return pl.ds(pl.multiple_of((1 - place[2]) * c.half, c.half), c.half)


def last_block(c):
    return (c.T - 1) // c.R


def own_rows(c):
    return pl.BlockSpec((c.R, c.D), lambda i, s: (jnp.minimum(s[1], last_block(c)), 0))


def live_rows(c, first, count):
    return (first + lax.broadcasted_iota(I32, (count, 1), 0)) < c.T


def qkv_body(c, place, *refs):
    tok_ref, small_ref, own_ref, oth_ref, hid_ref, qkv_ref, normed_ref, mix_ref, w_ref, all_ref = refs
    step = pl.program_id(0)

    @pl.when(step == 0)
    def _():
        mix_ref[...] = jnp.zeros_like(mix_ref)
        for part in range(3):
            lanes = slice(part * c.W, (part + 1) * c.W)
            w_ref[own_cols(c, place), lanes] = own_ref[part]
            w_ref[other_cols(c, place), lanes] = oth_ref[part]

    @pl.when(step < c.n)
    def _():
        live = live_rows(c, step * c.R, c.R)
        values = jnp.where(live, tok_ref[...].astype(F32), 0.0)
        normed, _ = norm_rows(values)
        hidden = normed * small_row(c, small_ref, 0) + small_row(c, small_ref, 2)
        normed_ref[...] = normed.astype(BF)
        hidden = jnp.where(live, hidden, 0.0).astype(BF)
        hid_ref[...] = hidden
        acc = dot_nn(hidden, w_ref[...])
        bias = small_row(c, small_ref, 5)
        zero = jnp.zeros((1, c.W), F32)
        shift = jnp.concatenate([bias[:, : c.W], zero, bias[:, c.half : c.half + c.W]], axis=1)
        result = (acc + shift).astype(BF)
        qkv_ref[...] = result
        all_ref[pl.ds(pl.multiple_of(step * c.R, 16), c.R), :] = result

    @pl.when(step >= c.n)
    def _():
        attend(c, step - c.n, all_ref, mix_ref)


def image_window(c, image):
    start = image * IMG_LEN
    low = pl.multiple_of(start // 16 * 16, 16)
    return low, start - low


def groups_of(c):
    lanes = min(128, c.W)
    return [(at, lanes) for at in range(0, c.W, lanes)]


def head_mask(lanes, head):
    lane = lax.broadcasted_iota(I32, (1, lanes), 1)
    return (lane >= head * HEAD) & (lane < (head + 1) * HEAD)


def stack_heads(c, values):
    heads = range(c.W // HEAD)
    return jnp.concatenate([jnp.where(head_mask(c.W, h), values, BF(0)) for h in heads], axis=0)


def pick_heads(c, values):
    total = None
    for h in range(c.W // HEAD):
        part = jnp.where(head_mask(c.W, h), values[h * c.win : (h + 1) * c.win], 0.0)
        total = part if total is None else total + part
    return total


def attend(c, image, qkv_ref, mix_ref):
    low, off = image_window(c, image)
    row = lax.broadcasted_iota(I32, (c.win, 1), 0)
    col = lax.broadcasted_iota(I32, (1, c.win), 1)
    in_row = (row >= off) & (row < off + IMG_LEN)
    in_col = (col >= off) & (col < off + IMG_LEN)
    q = stack_heads(c, qkv_ref[pl.ds(low, c.win), : c.W] * BF(HEAD**-0.5))
    k = qkv_ref[pl.ds(low, c.win), c.W : 2 * c.W]
    v = qkv_ref[pl.ds(low, c.win), 2 * c.W :]
    scores = jnp.where(in_col, dot_nt(q, k), LOW)
    exps = jnp.exp(scores - jnp.max(scores, axis=-1, keepdims=True))
    probs = exps * (1.0 / jnp.sum(exps, axis=-1, keepdims=True))
    total = pick_heads(c, dot_nn(probs.astype(BF), v)).astype(BF)
    for group, (at, lanes) in enumerate(groups_of(c)):
        old = mix_ref[group, pl.ds(low, c.win), :]
        mix_ref[group, pl.ds(low, c.win), :] = jnp.where(in_row, total[:, at : at + lanes], old)


def attend_back_body(c, place, qkv_ref, *refs):
    pieces, (out_ref, sums_ref, grad_ref) = refs[: c.n], refs[c.n :]

    @pl.when(pl.program_id(0) == 0)
    def _():
        out_ref[...] = jnp.zeros_like(out_ref)
        sums_ref[...] = jnp.zeros_like(sums_ref)
        for k in range(c.n):
            at = pl.multiple_of((place[1] ^ k) * c.R, 16)
            grad_ref[pl.ds(at, c.R), :] = pieces[k][...]

    low, off = image_window(c, pl.program_id(0))
    row = lax.broadcasted_iota(I32, (c.win, 1), 0)
    in_row = (row >= off) & (row < off + IMG_LEN)
    scale = HEAD**-0.5
    q = stack_heads(c, qkv_ref[pl.ds(low, c.win), : c.W] * BF(scale))
    k = qkv_ref[pl.ds(low, c.win), c.W : 2 * c.W]
    v = qkv_ref[pl.ds(low, c.win), 2 * c.W :]
    do = stack_heads(c, jnp.where(in_row, grad_ref[pl.ds(low, c.win), :], BF(0)))
    scores = jnp.where(in_row, dot_nt(k, q), LOW)
    exps = jnp.exp(scores - jnp.max(scores, axis=0, keepdims=True))
    soft = exps * (1.0 / jnp.sum(exps, axis=0, keepdims=True))
    dp = dot_nt(v, do)
    delta = jnp.sum(soft * dp, axis=0, keepdims=True)
    ds = (soft * (dp - delta)).astype(BF)
    dq = pick_heads(c, dot_tn(ds, k)) * scale
    dk = dot_nn(ds, q)
    dv = dot_nn(soft.astype(BF), do)
    for part, grad in enumerate((dq, dk, dv)):
        lanes = slice(part * c.W, (part + 1) * c.W)
        low_grad = jnp.where(in_row, grad, 0.0).astype(BF)
        old = out_ref[pl.ds(low, c.win), lanes]
        out_ref[pl.ds(low, c.win), lanes] = jnp.where(in_row, low_grad, old)
        sums_ref[0:1, lanes] += jnp.sum(low_grad.astype(F32), axis=0, keepdims=True)


def middle_rows(c, place, step, mixes, tok_ref, small_ref, table_ref, slot_ref, proj_ref):
    branch = dot_nn(jnp.concatenate([mix[...] for mix in mixes], axis=1), proj_ref[...])
    live = live_rows(c, step * c.R, c.R)
    tok = jnp.where(live, tok_ref[...].astype(F32), 0.0)
    after = tok + branch + small_row(c, small_ref, 4)
    normed, _ = norm_rows(after)
    hidden = (normed * small_row(c, small_ref, 1) + small_row(c, small_ref, 3)).astype(BF)
    router = table_ref[c.E : 2 * c.E, :]
    logits = dot_nt(router, hidden)
    exps = jnp.exp(logits - jnp.max(logits, axis=0, keepdims=True))
    probs = exps / jnp.sum(exps, axis=0, keepdims=True)
    weight = jnp.where(slot_ref[0] >= 0, probs, 0.0)
    high, rest = split_low(weight)
    lane = lax.broadcasted_iota(I32, (c.E, 128), 1)
    index = lax.broadcasted_iota(I32, (c.E, 128), 0)
    both = dot_tn(high, (lane == index).astype(BF)) + dot_tn(rest, (lane == index + 64).astype(BF))
    return after, hidden, probs, both.astype(BF)


def middle_body(c, place, *refs):
    refs = list(refs)
    count = c.n * len(groups_of(c))
    mixes, refs = refs[:count], refs[count:]
    w_ref, tok_ref, small_ref, table_ref, blocks_ref, slot_ref = refs[:6]
    hid_ref, weight_ref, after_ref, probs_ref, out_ref = refs[6:11]
    proj_ref, hids_ref, weights_ref, hot_ref = refs[11:]
    step = pl.program_id(0)

    @pl.when(step == 0)
    def _():
        for k in range(c.n):
            for h in range(2):
                cols = slice(h * c.half, (h + 1) * c.half)
                proj_ref[k * c.W : (k + 1) * c.W, cols] = w_ref[(place[1] ^ k) * 2 + h]

    @pl.when(step < c.n)
    def _():
        after, hidden, probs, weight = middle_rows(
            c, place, step, mixes, tok_ref, small_ref, table_ref, blocks_ref, proj_ref
        )
        rows = pl.ds(pl.multiple_of(step * c.R, 16), c.R)
        hid_ref[...] = hidden
        hids_ref[rows, :] = hidden
        weight_ref[...] = weight
        weights_ref[rows, :] = weight

        @pl.when(step == place[1])
        def _():
            after_ref[...] = after
            probs_ref[...] = probs

    @pl.when(step == c.n)
    def _():
        fill_hot(c, place, slot_ref, hot_ref, (0,))

    @pl.when(step >= c.n)
    def _():
        cols = pl.multiple_of(((step - c.n) ^ place[2]) * c.half, c.half)
        acc = dot_nn(hot_ref[0], hids_ref[:, pl.ds(cols, c.half)])
        out_ref[...] = acc.astype(BF)

        @pl.when(step == c.n)
        def _():
            put_gates(c, place, hot_ref, weights_ref[...], acc, out_ref)


def middle(c, order, place, mixes, proj, tokens, small, table, blocks, slot):
    def early(dims):
        return pl.BlockSpec(dims, lambda i, s: (jnp.minimum(i, c.n - 1),) + (0,) * (len(dims) - 1))

    args = [pair[0] for pair in flat(mixes)] + [proj, tokens, small, table, blocks, slot]
    specs = [
        pl.BlockSpec((None, c.R, a.shape[2]), lambda i, s, at=at: (at, jnp.minimum(i, c.n - 1), 0))
        for a, at in flat(mixes)
    ]
    tok_rows = pl.BlockSpec((c.R, c.D), lambda i, s: (jnp.minimum(i, last_block(c)), 0))
    specs += [whole(proj), tok_rows, whole(small), whole(table)]
    specs += [early((1, c.E, c.R)), whole(slot)]
    outs = [
        shape_of((c.TP, c.D), BF),
        shape_of((c.TP, 128), BF),
        shape_of((c.R, c.D), F32),
        shape_of((c.E, c.R), F32),
        shape_of((c.X * c.SP, c.D), BF),
    ]
    late = pl.BlockSpec((c.X * c.SP, c.half), lambda i, s: (0, jnp.maximum(i - c.n, 0)))
    result = call(
        order,
        functools.partial(middle_body, c),
        place,
        args,
        specs,
        outs,
        [early((c.R, c.D)), early((c.R, 128)), whole(outs[2]), whole(outs[3]), late],
        (c.n + 2,),
        [
            pltpu.VMEM((c.D, c.D), BF),
            pltpu.VMEM((c.TP, c.D), BF),
            pltpu.VMEM((c.TP, 128), BF),
            pltpu.VMEM((1, c.X * c.SP, c.TP), BF),
        ],
        name="middle",
    )
    return (*result[:4], result[4].reshape(c.X, c.SP, c.D))


def fill_packs(c, place, tails, packs):
    lane = lax.broadcasted_iota(I32, (1, 128), 1)
    here = place[0] * EXP_DEV + place[3]
    state = [jnp.zeros((1, 1), F32)] * 3
    for j in range(c.X):
        high, low = last_pair(c, tails[j], 128)
        number = jnp.sum(jnp.where(lane == here, high * 16.0 + low, 0.0), axis=1, keepdims=True)
        kept = jnp.clip(c.cap - state[0], 0.0, number)
        first = jnp.minimum(kept, float(c.Q))
        sizes = first, kept - first
        for half in range(2):
            wide = (c.CR[half], c.SP)
            slot = lax.broadcasted_iota(I32, wide, 1)
            at = lax.broadcasted_iota(I32, wide, 0) - state[1 + half].astype(I32)
            hot = (at == slot) & (slot < sizes[half].astype(I32))
            packs[half][:, j * c.SP : (j + 1) * c.SP] = hot.astype(BF)
        state = [state[0] + number, state[1] + sizes[0], state[2] + sizes[1]]


def last_pair(c, tile, lanes):
    tile = tile[:, :lanes].astype(F32)
    return tile[14:15, :], tile[15:16, :]


def row_chunks(rows, size):
    return [slice(at, min(at + size, rows)) for at in range(0, rows, size)]


def grad_active_body(c, place, rows_ref, own_ref, oth_ref, *outs):
    gas, all_ref, packs = outs[:2], outs[2], outs[3:]

    @pl.when(pl.program_id(0) == 0)
    def _():
        tails = [rows_ref[j, c.SP - 16 : c.SP, :] for j in range(c.X)]
        fill_packs(c, place, tails, packs)
        for half, base in enumerate((0, c.CR[0])):
            rows = [rows_ref[j, half * c.SP : (half + 1) * c.SP, :] for j in range(c.X)]
            got = dot_nn(packs[half][...], jnp.concatenate(rows, axis=0))
            all_ref[base : base + c.CR[half], :] = got.astype(BF)

    weights = jnp.concatenate([own_ref[...], oth_ref[...]], axis=1)
    for half, base in enumerate((0, c.CR[0])):
        for at in row_chunks(c.CR[half], 320):
            values = all_ref[base + at.start : base + at.stop, :]
            gas[half][at, :] = dot_nt(values, weights).astype(BF)


def grad_active(c, order, place, rows, own_w, oth_w):
    outs = [shape_of((count, c.F), BF) for count in c.CR] + [shape_of((sum(c.CR), c.D), BF)]
    outs += [shape_of((count, c.X * c.SP), BF) for count in c.CR]
    return call(
        order,
        functools.partial(grad_active_body, c),
        place,
        [rows, own_w, oth_w],
        [whole(rows, 1)] + [rows_of((c.fblk, c.half))] * 2,
        outs,
        [cols_of((count, c.fblk)) for count in c.CR] + [whole(o) for o in outs[2:]],
        (c.F // c.fblk,),
        name="grad_active",
    )


def expert_body(c, half, place, *refs):
    rows_ref, pack_ref, own_ref, oth_ref, bias_ref, ga_ref = refs[:6]
    act_ref, gp_ref, gb_ref, all_ref, col_ref, back_ref = refs[6:12]
    acc_ref, dot_ref, row_ref, wide_ref = refs[12:]
    step = pl.program_id(0)

    @pl.when(step == 0)
    def _():
        acc_ref[...] = jnp.zeros_like(acc_ref)
        dot_ref[...] = jnp.zeros_like(dot_ref)
        all_ref[...] = dot_nn(pack_ref[...], rows_ref[...]).astype(BF)
        eye = lax.broadcasted_iota(I32, (c.SP, c.SP), 0) == lax.broadcasted_iota(I32, (c.SP, c.SP), 1)
        lane = lax.broadcasted_iota(I32, (1, 128), 1)
        for j in range(c.X):
            end = (j + 1) * c.SP
            high, low = last_pair(c, rows_ref[end - 16 : end, :], c.SP)
            high = jnp.sum(jnp.where(eye, high, 0.0), axis=1, keepdims=True)
            low = jnp.sum(jnp.where(eye, low, 0.0), axis=1, keepdims=True)
            both = jnp.where(lane == 0, high, jnp.where(lane == 1, low, 0.0))
            wide_ref[j * c.SP : end, :] = both.astype(BF)
        both = dot_nn(pack_ref[...], wide_ref[...])
        col_ref[...] = jnp.broadcast_to(both[:, 0:1] + both[:, 1:2], (c.CR[half], 128))

    bias = bias_ref[...]
    weights = jnp.concatenate([own_ref[...], oth_ref[...]], axis=0)
    summed = jnp.zeros((1, c.fblk), F32)
    lead = 0.7978845608028654
    cube = lead * 0.044715
    chunks = row_chunks(c.CR[half], 224)
    ahead = dot_nn(all_ref[chunks[0], :], weights)
    for i, rows_at in enumerate(chunks):
        pre = ahead + bias
        if i + 1 < len(chunks):
            ahead = dot_nn(all_ref[chunks[i + 1], :], weights)
        square = pre * pre
        turn = jnp.tanh(pre * (cube * square + lead))
        above = 1.0 + turn
        active = (0.5 * pre) * above
        slope = above * (1.0 + (1.0 - turn) * (pre * (3 * cube * square + lead)))
        ga = ga_ref[rows_at, :].astype(F32)
        product = active * ga
        part = product[:, 0:128]
        for lane in range(128, c.fblk, 128):
            part = part + product[:, lane : lane + 128]
        dot_ref[rows_at, :] += part
        grad = ga * slope * (0.5 * col_ref[rows_at, 0:1])
        act_ref[rows_at, :] = active.astype(BF)
        grad_low = grad.astype(BF)
        gp_ref[rows_at, :] = grad_low
        summed = summed + jnp.sum(grad, axis=0, keepdims=True)
        acc_ref[rows_at, :] += dot_nt(grad_low, weights)
    gb_ref[...] = jnp.broadcast_to(summed, (8, c.fblk))

    @pl.when(step == pl.num_programs(0) - 1)
    def _():
        ones = jnp.ones((8, 128), BF)
        row_ref[...] = jnp.zeros_like(row_ref)
        back_ref[...] = dot_tn(pack_ref[...], acc_ref[...].astype(BF)).astype(BF)
        a, rest = split_low(dot_ref[...])
        total = dot_nt(ones, a) + dot_nt(ones, rest)
        high, low = split_low(total)
        high = dot_nn(high, pack_ref[...])
        low = dot_nn(low, pack_ref[...])
        for j in range(c.X):
            end = (j + 1) * c.SP
            row_ref[0:8, : c.SP] = high[:, j * c.SP : end]
            row_ref[8:16, : c.SP] = low[:, j * c.SP : end]
            tile = back_ref[end - 16 : end, : c.half].astype(F32)
            tile = last_rows(c, tile, row_ref[0:1, :], row_ref[8:9, :])
            back_ref[end - 16 : end, : c.half] = tile.astype(BF)


def expert(c, order, place, half, rows, pack, own_w, oth_w, bias, ga):
    rows = rows.reshape(c.X * c.SP, c.D)
    args = [rows, pack, own_w, oth_w, bias, ga]
    count = c.CR[half]
    specs = [whole(rows, 1), whole(pack, 1)]
    specs += [cols_of((c.half, c.fblk))] * 2
    specs += [cols_of((1, c.fblk)), cols_of((count, c.fblk))]
    outs = [
        shape_of((count, c.F), BF),
        shape_of((count, c.F), BF),
        shape_of((8, c.F), F32),
    ]
    out_specs = [cols_of((count, c.fblk))] * 2 + [cols_of((8, c.fblk))]
    late = [shape_of((count, c.D), BF), shape_of((count, 128), F32)]
    late.append(shape_of((c.X * c.SP, c.D), BF))
    result = call(
        order,
        functools.partial(expert_body, c, half),
        place,
        args,
        specs,
        outs + late,
        out_specs + [whole(o, 1) for o in late],
        (c.F // c.fblk,),
        [
            pltpu.VMEM((count, c.D), F32),
            pltpu.VMEM((count, 128), F32),
            pltpu.VMEM((16, c.half), F32),
            pltpu.VMEM((c.X * c.SP, 128), BF),
        ],
        name="expert",
    )
    return (*result[:5], result[5].reshape(c.X, c.SP, c.D))


def produce_body(c, place, *refs):
    cols, acts, packs, own_ref, oth_ref, out_ref = refs[:2], refs[2:4], refs[4:6], *refs[6:9]
    accs = refs[9:]
    step = pl.program_id(0)

    @pl.when(step == 0)
    def _():
        for acc_ref in accs:
            acc_ref[...] = jnp.zeros_like(acc_ref)

    weights = jnp.concatenate([own_ref[...], oth_ref[...]], axis=1)
    for half in range(2):
        for at in row_chunks(c.CR[half], 320):
            accs[half][at, :] += dot_nn(acts[half][at, :], weights)

    @pl.when(step == pl.num_programs(0) - 1)
    def _():
        for half in range(2):
            values = (accs[half][...] * cols[half][:, 0:1]).astype(BF)
            values = dot_tn(packs[half][...], values).astype(BF)
            for j in range(c.X):
                rows = values[j * c.SP : (j + 1) * c.SP]
                out_ref[j, half * c.SP : (half + 1) * c.SP, :] = rows


def produce(c, order, place, cols, acts, packs, own_w, oth_w):
    out = shape_of((c.X, 2 * c.SP, c.D), BF)
    return call(
        order,
        functools.partial(produce_body, c),
        place,
        [*cols, *acts, *packs, own_w, oth_w],
        [whole(col) for col in cols]
        + [cols_of((rows, c.fblk)) for rows in c.CR]
        + [whole(pack) for pack in packs]
        + [rows_of((c.fblk, c.half))] * 2,
        [out],
        [whole(out, 1)],
        (c.F // c.fblk,),
        [pltpu.VMEM((rows, c.D), F32) for rows in c.CR],
        name="produce",
    )[0]


def grad_second_body(c, own, place, *refs):
    all_ref, cols, acts = refs[0], refs[1:3], refs[3:5]
    out_ref, row_ref = refs[-2:]

    @pl.when(pl.program_id(0) == 0)
    def _():
        for half, base in enumerate((0, c.CR[0])):
            rows_at = slice(base, base + c.CR[half])
            row_ref[rows_at, :] = (all_ref[rows_at, :].astype(F32) * cols[half][:, 0:1]).astype(BF)

    acc = dot_tn(acts[0][...], row_ref[: c.CR[0], :])
    acc = acc + dot_tn(acts[1][...], row_ref[c.CR[0] :, :])
    if own:
        acc = acc + refs[5][...].astype(F32)
    out_ref[...] = acc.astype(out_ref.dtype)


def grad_second(c, order, place, rows, cols, acts, add=None):
    own = add is not None
    args = [rows, *cols, *acts]
    total = sum(c.CR)
    specs = [pl.BlockSpec((total, c.half), lambda i, s: (0, 0 if own else 1))]
    specs += [whole(col) for col in cols] + [cols_of((count, c.fblk)) for count in c.CR]
    if own:
        args.append(add)
        specs.append(rows_of((c.fblk, c.half)))
    out = shape_of((c.F, c.half), F32 if own else BF)
    return call(
        order,
        functools.partial(grad_second_body, c, own),
        place,
        args,
        specs,
        [out],
        [rows_of((c.fblk, c.half))],
        (c.F // c.fblk,),
        [pltpu.VMEM((total, c.half), BF)],
        name="grad_second",
    )[0]


def grad_first_body(c, own, place, *refs):
    acc = dot_tn(refs[0][...], refs[2][...]) + dot_tn(refs[1][...], refs[3][...])
    if own:
        acc = acc + refs[4][...].astype(F32)
    refs[-1][...] = acc.astype(refs[-1].dtype)


def grad_first(c, order, place, rows, gps, add=None):
    own = add is not None
    args = [*rows, *gps]
    specs = [pl.BlockSpec((count, c.half), lambda i, s: (0, 0 if own else 1)) for count in c.CR]
    specs += [cols_of((count, c.fblk)) for count in c.CR]
    if own:
        args.append(add)
        specs.append(cols_of((c.half, c.fblk)))
    out = shape_of((c.half, c.F), F32 if own else BF)
    return call(
        order,
        functools.partial(grad_first_body, c, own),
        place,
        args,
        specs,
        [out],
        [cols_of((c.half, c.fblk))],
        (c.F // c.fblk,),
        name="grad_first",
    )[0]


def combine_body(c, with_dots, place, *refs):
    refs = list(refs)
    extras = [] if with_dots else [refs.pop(0), refs.pop(0)]
    halves = 2 if with_dots else 1
    rows, refs = refs[:halves], refs[halves:]
    tails = []
    if with_dots:
        tails, refs = refs[:2], refs[2:]
    mine_ref = refs.pop(0)
    groups = [(0, g) for g in groups_a(c)] + [(1, g) for g in groups_b(c)]
    outs, (hot_ref, row_ref) = refs[: len(groups)], refs[len(groups) :]
    pad = hot_ref.shape[1] // c.X

    @pl.when(pl.program_id(0) == 0)
    def _():
        row_ref[...] = jnp.zeros_like(row_ref)
        slots = lax.broadcasted_iota(I32, (c.R, pad), 1)
        for k in range(c.n):
            at = pl.multiple_of((place[1] ^ k) * c.R, 16)
            for j in range(c.X):
                hot = (mine_ref[pl.ds(at, c.R), j : j + 1] == slots).astype(BF)
                hot_ref[k * c.R : (k + 1) * c.R, j * pad : (j + 1) * pad] = hot
        if with_dots:
            wide = (c.SP, c.half)
            eye = lax.broadcasted_iota(I32, wide, 0) == lax.broadcasted_iota(I32, wide, 1)
            lane = lax.broadcasted_iota(I32, (1, 128), 1)
            for half in range(2):
                for j in range(c.X):
                    high, low = last_pair(c, tails[half][j], c.half)
                    high = jnp.sum(jnp.where(eye, high, 0.0), axis=1, keepdims=True)
                    low = jnp.sum(jnp.where(eye, low, 0.0), axis=1, keepdims=True)
                    e = expert_of(c, place, j)
                    cols = jnp.where(lane == e, high, jnp.where(lane == e + 64, low, 0.0))
                    at = j * pad + half * c.SP
                    row_ref[at : at + c.SP, :128] = cols.astype(BF)
            pulls = dot_nn(hot_ref[...], row_ref[:, :128]).astype(BF)
            expert = lax.broadcasted_iota(I32, (c.E, 128), 0)
            lane = lax.broadcasted_iota(I32, (c.E, 128), 1)
            pick = ((lane == expert) | (lane == expert + 64)).astype(BF)
            for (side, group), out_ref in zip(groups, outs):
                for at, k in enumerate(group):
                    if side == 0:
                        got = dot_nt(pick, pulls[k * c.R : (k + 1) * c.R])
                        out_ref[at, c.R :, :] = jnp.zeros((c.E, c.half), BF)
                        out_ref[at, c.R :, : c.R] = got.astype(BF)

    for half, rows_ref in enumerate(rows):
        size = rows_ref.shape[1]
        for j in range(c.X):
            at = j * pad + half * size
            row_ref[at : at + size, :] = rows_ref[j]
    result = dot_nn(hot_ref[...], row_ref[...]).astype(BF)
    for half in range(2):

        @pl.when(pl.program_id(0) == half)
        def _():
            for (side, group), out_ref in zip(groups, outs):
                if side == half:
                    for at, k in enumerate(group):
                        out_ref[at, : c.R, :] = result[k * c.R : (k + 1) * c.R]
                        if extras:
                            more = extras[0].shape[1] // 2
                            extra = [e[k, half * more : (half + 1) * more, :] for e in extras]
                            total = extra[0].astype(F32) + extra[1].astype(F32)
                            out_ref[at, c.R :, :] = total.astype(BF)


def combine(c, order, place, rows, mine, extra=None, cost=0):
    pad = up(2 * c.SP, 128)
    args = list(rows)
    specs = [pl.BlockSpec((c.X, r.shape[1], c.half), lambda i, s: (0, 0, i ^ s[2])) for r in rows]
    if extra is None:
        args += list(rows)
        specs += [pl.BlockSpec((c.X, 16, c.half), lambda i, s: (0, c.SP // 16 - 1, 0))] * 2
        outs = piece_outs(c, c.E)
    else:
        args = [*extra, *args]
        specs = [whole(e) for e in extra] + specs
        outs = piece_outs(c, extra[0].shape[1] // 2, extra[0].shape[1] // 2)
    args.append(mine)
    specs.append(whole(mine))
    result = call(
        order,
        functools.partial(combine_body, c, extra is None),
        place,
        args,
        specs,
        outs,
        [whole(o, 1) for o in outs],
        (2,),
        [pltpu.VMEM((c.n * c.R, c.X * pad), BF), pltpu.VMEM((c.X * pad, c.half), BF)],
        name="combine",
        cost=cost,
    )
    return list(result)


def back_two_body(c, place, *refs):
    refs = list(refs)
    groups = groups_of(c)
    heads, refs = refs[: c.n * len(groups)], refs[c.n * len(groups) :]
    count = (len(refs) - 13 - c.n) // 2
    a, b, refs = refs[:count], refs[count : 2 * count], refs[2 * count :]
    w_ref, after_ref, probs_ref, keep_ref = refs[:4]
    cot_ref, hid_ref, small_ref, table_ref, ga_ref, proj_own_ref, proj_oth_ref = refs[4:11]
    mixes, (gb_ref, sums_ref) = refs[11:-2], refs[-2:]
    sum_a = add_up(a)
    live = live_rows(c, place[1] * c.R, c.R)
    cot = jnp.where(live, cot_ref[...], BF(0))
    eshift = table_ref[: c.E, :]
    router = table_ref[c.E : 2 * c.E, :]
    kept = keep_ref[...] > 0
    pulls = jnp.where(kept, sum_a[c.R :, : c.R] + dot_nt(eshift, cot), 0.0)
    probs = probs_ref[...]
    glog = (probs * (pulls - jnp.sum(probs * pulls, axis=0, keepdims=True))).astype(BF)
    two = jnp.concatenate([sum_a[: c.R], add_up(b)], axis=1) + dot_tn(glog, router)
    normed, inv_std = norm_rows(after_ref[...])
    grad_after = cot.astype(F32) + norm_back(two, small_row(c, small_ref, 1), normed, inv_std)
    ga_ref[...] = grad_after
    low = grad_after.astype(BF)
    gb_ref[...] = low
    high, rest = split_low(probs * keep_ref[...])
    hid = jnp.where(live, hid_ref[...], BF(0))
    sums_ref[0:1, :] = jnp.sum(two * normed, axis=0, keepdims=True)
    sums_ref[1:2, :] = jnp.sum(two, axis=0, keepdims=True)
    sums_ref[2:3, :] = jnp.sum(low.astype(F32), axis=0, keepdims=True)
    sums_ref[3:8, :] = jnp.zeros((5, c.D), F32)
    sums_ref[8 : 8 + c.E, :] = dot_nn(high, cot) + dot_nn(rest, cot)
    sums_ref[8 + c.E : 8 + 2 * c.E, :] = dot_nn(glog, hid)
    for k in range(c.n):
        lane = place[1] ^ k
        mix = dot_nt(gb_ref[:, : c.half], w_ref[2 * lane])
        mix = mix + dot_nt(gb_ref[:, c.half :], w_ref[2 * lane + 1])
        mixes[k][...] = mix.astype(BF)
    height = sums_ref.shape[0]
    for cols, out_ref in ((own_cols(c, place), proj_own_ref), (other_cols(c, place), proj_oth_ref)):
        sums = sums_ref[:, cols].astype(BF)
        part = dot_tn(jnp.concatenate([head[...] for head in heads], axis=1), gb_ref[:, cols])
        for k in range(c.n):
            out_ref[k, : c.W, :] = part[k * c.W : (k + 1) * c.W].astype(BF)
            out_ref[k, c.W : c.W + height, :] = sums
            rest = out_ref.shape[1] - c.W - height
            out_ref[k, c.W + height :, :] = jnp.zeros((rest, c.half), BF)


def back_two(c, order, place, heads, sums, proj, lanes, cotangent, hidden, small, table):
    height = 8 + 2 * c.E
    rows = up(c.W + height, 32)
    args = [pair[0] for pair in flat(heads)]
    specs = [
        pl.BlockSpec((None, c.R, a.shape[2]), lambda i, s, at=at: (at, s[1], 0))
        for a, at in flat(heads)
    ]
    args += [*sums[0], *sums[1], proj, *lanes, cotangent, hidden, small, table]
    hid_rows = pl.BlockSpec((c.R, c.D), lambda i, s: (s[1], 0))
    specs += [first_block(a) for a in [*sums[0], *sums[1]]]
    specs += [whole(a) for a in [proj, *lanes]] + [own_rows(c), hid_rows]
    specs += [whole(small), whole(table)]
    outs = [shape_of((c.R, c.D), F32)] + [shape_of((c.n, rows, c.half), BF)] * 2
    outs += [shape_of((c.R, c.W), BF) for _ in range(c.n)]
    result = call(
        order,
        functools.partial(back_two_body, c),
        place,
        args,
        specs,
        outs,
        [whole(o) for o in outs],
        (1,),
        [pltpu.VMEM((c.R, c.D), BF), pltpu.VMEM((height, c.D), F32)],
        name="back_two",
    )
    return (*result[:3], list(result[3:]))


def block_out_body(c, place, *refs):
    refs = list(refs)
    count = (len(refs) - 6) // 2
    a, b, refs = refs[:count], refs[count : 2 * count], refs[2 * count :]
    after_ref, probs_ref, keep_ref, table_ref, out_ref, proj_ref = refs
    high, low = split_low(probs_ref[...] * keep_ref[...])
    eshift = table_ref[: c.E, :]
    shift = dot_tn(high, eshift) + dot_tn(low, eshift)
    more = proj_ref.shape[0] // 2
    for h, pieces in enumerate((a, b)):
        cols = slice(h * c.half, (h + 1) * c.half)
        total = add_up([ref.at[: c.R, :] for ref in pieces])
        out_ref[h] = (after_ref[:, cols] + total + shift[:, cols]).astype(BF)
        proj_ref[h * more : (h + 1) * more, :] = same_sum(c, pieces, slice(c.R, c.R + more)).astype(BF)


def block_out(c, order, place, sums, after, probs, keep, table):
    args = [*sums[0], *sums[1], after, probs, keep, table]
    more = 2 * (sums[0][0].shape[1] - c.R)
    outs = [shape_of((2, c.R, c.half), BF), shape_of((more, c.half), BF)]
    return call(
        order,
        functools.partial(block_out_body, c),
        place,
        args,
        [first_block(a) for a in args[:-4]] + [whole(a) for a in args[-4:]],
        outs,
        [whole(o) for o in outs],
        (1,),
        name="block_out",
    )


def grad_one_body(c, place, dqkv_ref, normed_ref, own_ref, oth_ref, *outs):
    sums_ref = outs[-1]
    groups = [(0, g) for g in groups_a(c)] + [(1, g) for g in groups_b(c)]
    for side in range(2):
        cols = slice(side * c.half, (side + 1) * c.half)
        weights = [jnp.where(place[2] == side, own_ref[p], oth_ref[p]) for p in range(3)]
        weights = jnp.concatenate(weights, axis=1)
        gain = jnp.zeros((1, c.half), F32)
        shift = jnp.zeros((1, c.half), F32)
        for (where, group), out_ref in zip(groups, outs):
            if where != side:
                continue
            for row, k in enumerate(group):
                rows_at = pl.ds(pl.multiple_of((place[1] ^ k) * c.R, 16), c.R)
                acc = dot_nt(dqkv_ref[rows_at, :], weights)
                out_ref[row, : c.R, :] = acc.astype(BF)
                normed = normed_ref[rows_at, cols].astype(F32)
                gain = gain + jnp.sum(acc * normed, axis=0, keepdims=True)
                shift = shift + jnp.sum(acc, axis=0, keepdims=True)
        sums_ref[0:1, cols] = gain
        sums_ref[1:2, cols] = shift
        row = lax.broadcasted_iota(I32, (16, 1), 0)
        tile = jnp.where(row == 0, gain, jnp.where(row == 1, shift, 0.0)).astype(BF)
        for (where, group), out_ref in zip(groups, outs):
            if where == side:
                for at in range(len(group)):
                    out_ref[at, c.R :, :] = tile


def grad_one(c, order, place, dqkv, normed, own_w, oth_w):
    outs = piece_outs(c, 16, 16) + [shape_of((2, c.D), F32)]
    result = call(
        order,
        functools.partial(grad_one_body, c),
        place,
        [dqkv, normed, own_w, oth_w],
        [whole(dqkv), whole(normed), whole(own_w), whole(oth_w)],
        outs,
        [whole(o) for o in outs],
        (1,),
        name="grad_one",
    )
    return list(result[:-1]), result[-1]


def grad_qkv_body(c, place, hid_ref, dqkv_ref, own_ref, oth_ref):
    own_ref[0] = dot_tn(hid_ref[:, own_cols(c, place)], dqkv_ref[...]).astype(BF)
    oth_ref[0] = dot_tn(hid_ref[:, other_cols(c, place)], dqkv_ref[...]).astype(BF)


def grad_qkv(c, order, place, hidden, dqkv):
    specs = [whole(hidden, 1), cols_of((c.TP, c.W))]
    if c.W % 128:
        dqkv = dqkv.reshape(c.TP, 3, c.W).transpose(1, 0, 2)
        specs[1] = pl.BlockSpec((None, c.TP, c.W), lambda i, s: (i, 0, 0))
    return call(
        order,
        functools.partial(grad_qkv_body, c),
        place,
        [hidden, dqkv],
        specs,
        [shape_of((3, c.half, c.W), BF)] * 2,
        [rows_of((1, c.half, c.W))] * 2,
        (3,),
        name="grad_qkv",
    )


def back_one_body(c, place, *refs):
    refs = list(refs)
    count = (len(refs) - 4) // 2
    a, b, refs = refs[:count], refs[count : 2 * count], refs[2 * count :]
    tok_ref, after_ref, small_ref, out_ref = refs
    live = live_rows(c, place[1] * c.R, c.R)
    normed, inv_std = norm_rows(jnp.where(live, tok_ref[...].astype(F32), 0.0))
    one = jnp.concatenate([add_up(a)[: c.R], add_up(b)[: c.R]], axis=1)
    grad = after_ref[...] + norm_back(one, small_row(c, small_ref, 0), normed, inv_std)
    for h in range(2):
        out_ref[h] = grad[:, h * c.half : (h + 1) * c.half].astype(BF)


def back_one(c, order, place, sums, tokens, after, small):
    args = [*sums[0], *sums[1], tokens, after, small]
    specs = [first_block(a) for a in args[:-3]] + [own_rows(c), whole(after), whole(small)]
    out = shape_of((2, c.R, c.half), BF)
    return call(
        order,
        functools.partial(back_one_body, c),
        place,
        args,
        specs,
        [out],
        [whole(out)],
        (1,),
        name="back_one",
    )[0]


def assemble_body(c, place, *refs):
    pieces, out_ref = refs[:-1], refs[-1]
    for k in range(c.n):

        @pl.when((place[1] ^ k) == pl.program_id(0))
        def _():
            for h in range(2):
                values = pieces[2 * k + h][...].astype(out_ref.dtype)
                out_ref[:, h * c.half : (h + 1) * c.half] = values


def assemble(c, order, place, pieces, dtype):
    out = shape_of((c.T, c.D), dtype)
    return call(
        order,
        functools.partial(assemble_body, c),
        place,
        [pair[0] for pair in flat(pieces)],
        [
            pl.BlockSpec((None, c.R, c.half), lambda i, s, at=at: (at, 0, 0))
            for _, at in flat(pieces)
        ],
        [out],
        [rows_of((c.R, c.D))],
        (-(-c.T // c.R),),
        name="assemble",
    )[0]


def local(
    tokens,
    cotangent,
    w_qkv,
    qv_bias,
    w_proj,
    proj_bias,
    norm_gains,
    norm_shifts,
    w_router,
    expert_shift,
    w_first,
    w_second,
    first_bias,
    routes,
    priority,
):
    T, D = tokens.shape
    n = lax.axis_size("mp")
    E = w_router.shape[1]
    S = 16 * T // (5 * E)
    R = up(-(-T // n), 16)
    F = w_first.shape[2]
    W = w_proj.shape[0]
    win = up(IMG_LEN + 15, 16)
    Q = (S + 1) // 2
    cap = (9 * T + 4 * EXP_DEV - 1) // (4 * EXP_DEV)
    X = E // EXP_DEV
    full = min(cap // S, X)
    c = Sizes(
        T=T,
        D=D,
        half=D // 2,
        n=n,
        X=X,
        E=E,
        S=S,
        Q=Q,
        SP=up(Q + 2, 16),
        CR=(up(min(cap, X * Q), 16), up(full * (S - Q) + max(0, cap - full * S - Q), 16)),
        R=R,
        TP=n * R,
        W=W,
        images=T // IMG_LEN,
        quarters=n // EXP_DEV,
        F=F,
        cap=cap,
        win=win,
        fblk=min(1024, F),
    )
    order = Order()
    dp, mp, grid = lax.axis_index("dp"), lax.axis_index("mp"), lax.axis_index("grid")
    place = jnp.stack([dp, mp, grid, mp // c.quarters]).astype(I32)

    slot, blocks, rt, grad_out = route(c, order, place, routes, priority, cotangent)
    grad_in = trade(grad_out, "dp")

    def both_halves(rows):
        rows = jnp.pad(rows, ((0, up(rows.shape[0], 16) - rows.shape[0]), (0, 0)))
        other = swap_grid(rows)
        return jnp.where(
            grid == 0,
            jnp.concatenate([rows, other], axis=1),
            jnp.concatenate([other, rows], axis=1),
        )

    wide_bias = jnp.pad(qv_bias, ((0, 0), (0, c.half - W)))
    small = both_halves(
        jnp.concatenate([norm_gains, norm_shifts, proj_bias[None], wide_bias], axis=0)
    )
    qkv_own = w_qkv.transpose(1, 0, 2)
    qkv_oth = swap_grid(qkv_own)

    first_own = w_first[0]
    second_own = w_second[0]
    proj = lax.all_gather(w_proj, ("mp", "grid"))

    groups = groups_of(c)
    outs = [shape_of((c.TP, D), BF), shape_of((c.TP, 3 * W), BF), shape_of((c.TP, D), BF)]
    outs.append(shape_of((len(groups), c.TP, groups[0][1]), BF))

    def first_steps(width):
        return pl.BlockSpec((c.R, width), lambda i, s: (jnp.minimum(i, n - 1), 0))

    hidden_one, qkv, normed_one, mix = call(
        order,
        functools.partial(qkv_body, c),
        place,
        [tokens, small, qkv_own, qkv_oth],
        [
            pl.BlockSpec((R, D), lambda i, s: (jnp.minimum(i, last_block(c)), 0)),
            whole(small),
            whole(qkv_own),
            whole(qkv_oth),
        ],
        outs,
        [first_steps(D), first_steps(3 * W), first_steps(D), whole(outs[3])],
        (n + c.images,),
        [pltpu.VMEM((D, 3 * W), BF), pltpu.VMEM((c.TP, 3 * W), BF)],
        name="qkv",
    )
    bias_rows = F // 2 // c.half
    tied = held(jnp.concatenate([expert_shift, w_router.T]), qkv)
    table = both_halves(tied)
    bias = both_halves(held(first_bias.reshape(bias_rows, c.half), qkv))[:bias_rows]
    bias = bias.reshape(bias_rows, 2, c.half).transpose(1, 0, 2).reshape(1, F).astype(F32)
    second_oth = swap_grid(held(second_own, qkv))
    first_oth = swap_grid(held(first_own, qkv))
    mixes, _ = gather_mp(c, held(mix, proj))
    hidden_two, weight, after, probs, rows_a = middle(
        c, order, place, mixes, proj, tokens, small, table, blocks, slot
    )

    rows_a = trade(rows_a, "dp")
    rows_b = dispatch(c, order, place, slot, hidden_two, weight, 1)
    ga_a, ga_b, grad_all, pack_a, pack_b = grad_active(
        c, order, place, grad_in, second_own, second_oth
    )
    mine, keep, keep_lane = keep_of(c, order, place, grad_in, blocks, rt)
    keep_mask = keep[:, :2, :].transpose(0, 2, 1).reshape(c.TP, 2)[:T].astype(I32)
    mine = mine.transpose(0, 2, 1).reshape(c.TP, 8)
    rows_b = trade(held(rows_b, rows_a, grad_all, keep_lane), "dp")
    act_a, gp_a, gb_a, all_a, col_a, back_a = expert(
        c, order, place, 0, rows_a, pack_a, first_own, first_oth, bias, ga_a
    )
    back_a = trade(held(back_a, rows_b), "dp")
    act_b, gp_b, gb_b, all_b, col_b, back_b = expert(
        c, order, place, 1, rows_b, pack_b, first_own, first_oth, bias, ga_b
    )
    back_b = trade(held(back_b, back_a), "dp")
    cols, acts, gps, alls = [col_a, col_b], [act_a, act_b], [gp_a, gp_b], [all_a, all_b]
    second_part = swap_grid(grad_second(c, order, place, grad_all, cols, acts))
    order.tie(back_a)
    first_part = swap_grid(grad_first(c, order, place, alls, gps))
    packs = [pack_a, pack_b]
    order.tie(mine)
    prod = produce(c, order, place, cols, acts, packs, second_own, second_oth)
    gb = (gb_a + gb_b)[0:1].reshape(2, F // 2)
    gb_own = lax.dynamic_index_in_dim(gb, grid, 0, True)
    gb_oth = lax.dynamic_index_in_dim(gb, 1 - grid, 0, True)
    grad_fbias = gb_own + swap_grid(gb_oth)

    pieces = combine(c, order, place, [back_a, back_b], mine)
    prod = trade(held(prod, back_b), "dp")
    two_sums = reduce_start(c, pieces)
    grad_second_out = grad_second(c, order, place, grad_all, cols, acts, second_part)
    two_sums = reduce_end(c, order, two_sums)
    grad_after, proj_a, proj_b, grad_mix = back_two(
        c,
        order,
        place,
        mixes,
        two_sums,
        proj,
        [after, probs, keep_lane],
        cotangent,
        hidden_two,
        small,
        table,
    )
    grad_mix = [grad_mix[0]] + [swap_mp(c, grad_mix[k], k) for k in range(1, n)]
    proj_parts = [proj_a, swap_grid(proj_b)]
    pieces = combine(c, order, place, [prod], mine, proj_parts, cost=10)
    out_sums = reduce_start(c, [held(p, *grad_mix) for p in pieces])

    outs = [shape_of((c.TP, 3 * W), BF), shape_of((8, 3 * W), F32)]
    dqkv, dqkv_sums = call(
        order,
        functools.partial(attend_back_body, c),
        place,
        [qkv, *grad_mix],
        [whole(qkv)] + [whole(p) for p in grad_mix],
        outs,
        [whole(o) for o in outs],
        (c.images,),
        [pltpu.VMEM((c.TP, W), BF)],
        name="attend_back",
    )
    one_pieces, one_parts = grad_one(c, order, place, dqkv, normed_one, qkv_own, qkv_oth)
    one_sums = reduce_start(c, one_pieces)
    out_sums = reduce_end(c, order, out_sums)
    qkv_a, qkv_b = grad_qkv(c, order, place, hidden_one, dqkv)
    qkv_b = swap_grid(qkv_b)
    qkv_low = (qkv_a.astype(F32) + qkv_b.astype(F32)).astype(BF)
    qkv_sum = sum_dp_start(c, qkv_low.reshape(-1, c.half))
    one_sums = reduce_end(c, order, one_sums)
    grad_low = back_one(c, order, place, one_sums, tokens, grad_after, small)
    qkv_sum = sum_dp_turn(c, qkv_sum)
    order.tie(qkv_sum)
    out_lane, proj_sum = block_out(c, order, place, out_sums, after, probs, keep_lane, table)

    qv_rows = jnp.concatenate([dqkv_sums[0:1, :W], dqkv_sums[0:1, 2 * W :]], axis=0)
    sums_one = held(first_sums(c, one_sums, one_parts), grad_low)
    sums_one = chip_sums(c, sums_one, qv_rows, grid).astype(BF)
    proj_end = proj_sum.shape[0]
    shared = jnp.concatenate([proj_sum, sums_one], axis=0)
    shared = jnp.pad(shared, ((0, up(shared.shape[0], 16 * c.X) - shared.shape[0]), (0, 0)))
    shared = sum_dp_start(c, shared)

    def last_expert_kernel(before):
        for value in before:
            order.tie(value)
        return grad_first(c, order, place, alls, gps, first_part), order.hold

    grad_low, out_lane, last, grad_first_out = gather_both(c, grad_low, out_lane, last_expert_kernel)
    grad_w_qkv = sum_dp_end(c, qkv_sum).reshape(3, c.half, W)
    shared = sum_dp_end(c, sum_dp_turn(c, held(shared, *last)))
    sums_one = shared[proj_end:]
    rest = shared[W : W + 8 + 2 * E]
    grad_tokens = assemble(c, order, place, grad_low, F32)
    block = assemble(c, order, place, out_lane, BF)
    return (
        block,
        grad_tokens,
        grad_w_qkv.transpose(1, 0, 2),
        sums_one[2:3, :W],
        shared[:W],
        rest[2],
        jnp.stack([sums_one[0], rest[0]]),
        jnp.stack([sums_one[1], rest[1]]),
        rest[8 + E : 8 + 2 * E].T,
        rest[8 : 8 + E],
        grad_first_out[None],
        grad_second_out[None],
        grad_fbias,
        keep_mask,
    )


def solution(mesh):
    return jax.shard_map(
        local,
        mesh=mesh,
        in_specs=(
            P(("dp", "grid"), None),
            P(("dp", "grid"), None),
            P("grid", None, "mp"),
            P("grid", "mp"),
            P("mp", "grid"),
            P("grid"),
            P(None, "grid"),
            P(None, "grid"),
            P("grid", None),
            P(None, "grid"),
            P(("dp", "mp"), "grid", None),
            P(("dp", "mp"), None, "grid"),
            P(("dp", "mp"), "grid"),
            P(("dp", "grid"), None),
            P(("dp", "grid"), None),
        ),
        out_specs=(
            P(("dp", "grid"), None),
            P(("dp", "grid"), None),
            P("grid", None, "mp"),
            P("grid", "mp"),
            P("mp", "grid"),
            P("grid"),
            P(None, "grid"),
            P(None, "grid"),
            P("grid", None),
            P(None, "grid"),
            P(("dp", "mp"), "grid", None),
            P(("dp", "mp"), None, "grid"),
            P(("dp", "mp"), "grid"),
            P(("dp", "grid"), None),
        ),
        check_vma=False,
    )
```

```python
import functools
from typing import NamedTuple

import jax
import jax.numpy as jnp
from jax import lax
from jax.experimental import pallas as pl
from jax.experimental.pallas import tpu as pltpu
from jax.sharding import PartitionSpec as P

HEAD = 64
IMG_LEN = 197
EXP_DEV = 4
BF = jnp.bfloat16
F32 = jnp.float32
I32 = jnp.int32
VMEM_BYTES = 56 * 1024 * 1024
LOW = -1e30


class Sizes(NamedTuple):
    T: int
    D: int
    half: int
    n: int
    X: int
    E: int
    S: int
    Q: int
    SP: int
    CR: tuple
    R: int
    TP: int
    W: int
    images: int
    quarters: int
    F: int
    cap: int
    win: int
    fblk: int


class Order:
    def __init__(self):
        self.after = []

    def tie(self, value):
        self.after.append(value)

    def hold(self, *values):
        return lax.optimization_barrier((*values, *self.after))[: len(values)]


def up(value, step):
    return -(-value // step) * step


def dot_nn(a, b):
    return jnp.dot(a, b, preferred_element_type=F32)


def dot_nt(a, b):
    return lax.dot_general(a, b, (((1,), (1,)), ((), ())), preferred_element_type=F32)


def dot_tn(a, b):
    return lax.dot_general(a, b, (((0,), (0,)), ((), ())), preferred_element_type=F32)


def split_low(values):
    high = values.astype(BF)
    return high, (values - high.astype(F32)).astype(BF)


def shape_of(dims, dtype):
    return jax.ShapeDtypeStruct(dims, dtype)


def whole(array, buffers=None):
    dims = tuple(array.shape)
    extra = {} if buffers is None else {"pipeline_mode": pl.Buffered(buffers)}
    return pl.BlockSpec(dims, lambda i, s: (0,) * len(dims), **extra)


def rows_of(dims):
    return pl.BlockSpec(dims, lambda i, s: (i,) + (0,) * (len(dims) - 1))


def cols_of(dims):
    return pl.BlockSpec(dims, lambda i, s: (0,) * (len(dims) - 1) + (i,))


def call(order, body, place, args, specs, outs, out_specs, grid, scratch=(), name=None, cost=0):
    extra = order.after
    count = len(args)

    def wrapped(place, *refs):
        body(place, *refs[:count], *refs[count + len(extra) :])

    result = pl.pallas_call(
        wrapped,
        grid_spec=pltpu.PrefetchScalarGridSpec(
            num_scalar_prefetch=1,
            grid=grid,
            in_specs=list(specs) + [pl.BlockSpec(memory_space=pl.ANY)] * len(extra),
            out_specs=list(out_specs),
            scratch_shapes=list(scratch),
        ),
        out_shape=list(outs),
        compiler_params=pltpu.CompilerParams(
            dimension_semantics=("arbitrary",) * len(grid), vmem_limit_bytes=VMEM_BYTES
        ),
        cost_estimate=pl.CostEstimate(
            flops=1000 + int(1.1e9 * cost), bytes_accessed=1000, transcendentals=0
        ),
        name=name,
    )(place, *args, *extra)
    order.after = [min(result, key=lambda o: o.size)]
    return result


def swap_mp(c, value, mask):
    return lax.ppermute(value, "mp", [(i, i ^ mask) for i in range(c.n)])


def swap_grid(value):
    return lax.ppermute(value, "grid", [(0, 1), (1, 0)])


def held(value, *others):
    return lax.optimization_barrier((value, *others))[0]


def trade(value, axis):
    return lax.all_to_all(value, axis, split_axis=0, concat_axis=0, tiled=True)


def groups_a(c):
    return [[0, 2], [1, 3]] if c.n == 4 else [[k] for k in range(c.n)]


def groups_b(c):
    return [[0, 1], [2, 3]] if c.n == 4 else [[k] for k in range(c.n)]


def reduce_start(c, arrays):
    a, b = arrays[: len(arrays) // 2], arrays[len(arrays) // 2 :]
    if c.n != 4:
        return [[x[0]] + [swap_mp(c, x[k], k) for k in range(1, c.n)] for x in (a, b)]
    return [[a[0], swap_mp(c, a[1], 1)], [b[0], swap_mp(c, b[1], 2)]]


def reduce_end(c, order, state):
    if c.n != 4:
        return state
    (a, ra), (b, rb) = state
    ra, rb = order.hold(ra, rb)
    ta = (a[1:].astype(F32) + ra[1:].astype(F32)).astype(BF)
    tb = (b[1:].astype(F32) + rb[1:].astype(F32)).astype(BF)
    order.tie(ta)
    order.tie(tb)
    return [[a, ra, swap_mp(c, ta, 2)], [b, rb, swap_mp(c, tb, 1)]]


def piece_outs(c, more_a=0, more_b=0):
    outs = [shape_of((len(g), c.R + more_a, c.half), BF) for g in groups_a(c)]
    return outs + [shape_of((len(g), c.R + more_b, c.half), BF) for g in groups_b(c)]


def first_block(array):
    dims = tuple(array.shape)
    return pl.BlockSpec((None,) + dims[1:], lambda i, s: (0, 0, 0))


def same_sum(c, refs, rows):
    parts = [ref[rows, :].astype(F32) for ref in refs]
    if c.n == 4:
        return (parts[0] + parts[1]).astype(BF).astype(F32) + parts[2]
    while len(parts) > 1:
        parts = [parts[i] + parts[i + 1] for i in range(0, len(parts), 2)]
    return parts[0]


def add_up(refs):
    total = refs[0][...].astype(F32)
    for ref in refs[1:]:
        total = total + ref[...].astype(F32)
    return total


def sum_dp_start(c, value):
    return trade(value.reshape((c.X, value.shape[0] // c.X) + value.shape[1:]), "dp")


def sum_dp_turn(c, parts):
    total = jnp.sum(parts.astype(F32), axis=0).astype(BF)
    return jnp.broadcast_to(total[None], (c.X,) + total.shape)


def sum_dp_end(c, spread):
    return trade(spread, "dp").reshape((-1,) + spread.shape[2:]).astype(F32)


def gather_mp(c, value, until=None):
    if c.n != 4 or value.shape[0] != 2:
        parts = [value] + [swap_mp(c, value, k) for k in range(1, c.n)]
        return [[(p, h) for h in range(value.shape[0])] for p in parts], parts[1:]
    one = swap_mp(c, value, 1)
    two = swap_mp(c, value, 2)
    ends = one[0:1], two[1:2]
    if until is not None:
        ends = held(ends[0], *until), held(ends[1], *until)
    far_a = swap_mp(c, ends[0], 2)
    far_b = swap_mp(c, ends[1], 1)
    near = [[(p, 0), (p, 1)] for p in (value, one, two)]
    return near + [[(far_a, 0), (far_b, 0)]], [one, two]


def gather_both(c, first, second, filler):
    if c.n != 4:
        filled, _ = filler([first])
        return gather_mp(c, first)[0], gather_mp(c, second)[0], (first,), filled
    one, two = swap_mp(c, first, 1), swap_mp(c, first, 2)
    near = jnp.concatenate([one[0:1], second]), jnp.concatenate([two[1:2], second])
    by_two, by_one = [swap_mp(c, x, mask) for x, mask in zip(near, (2, 1))]
    filled, hold = filler(near)
    by_two, by_one = hold(by_two, by_one)
    far_a, far_b = swap_mp(c, by_one[1:2], 2), swap_mp(c, by_two[2:3], 1)
    pieces = [[(p, 0), (p, 1)] for p in (first, one, two)] + [[(by_two, 0), (by_one, 0)]]
    others = [[(second, 0), (second, 1)], [(by_one, 1), (by_one, 2)], [(by_two, 1), (by_two, 2)]]
    return pieces, others + [[(far_a, 0), (far_b, 0)]], (by_one, by_two), filled


def flat(pieces):
    return [pair for piece in pieces for pair in piece]


def fold(c, value, axes):
    for axis, size in axes:
        mask = 1
        while mask < size:
            value = value + lax.ppermute(value, axis, [(i, i ^ mask) for i in range(size)])
            mask *= 2
    return value


def first_sums(c, sums, one_parts):
    if c.n != 4:
        return fold(c, one_parts, (("mp", c.n),))
    halves = []
    for a, b, far in sums:
        pair = (a[0, c.R : c.R + 2].astype(F32) + b[0, c.R : c.R + 2].astype(F32)).astype(BF)
        halves.append(pair.astype(F32) + far[0, c.R : c.R + 2].astype(F32))
    return jnp.concatenate(halves, axis=1)


def chip_sums(c, one, parts, grid):
    def half_of(side):
        cols = lax.dynamic_slice_in_dim(one, side * c.half, c.half, 1)
        row = lax.dynamic_index_in_dim(parts, side, 0, True)
        return jnp.concatenate([cols, jnp.pad(row, ((0, 0), (0, c.half - c.W)))], axis=0)

    return half_of(grid) + swap_grid(half_of(1 - grid))


def expert_of(c, place, j):
    return j * EXP_DEV + place[3]


def window_slot(c, slot):
    return jnp.where(slot < c.Q, slot, slot + (c.SP - c.Q))


def count_places(c, rank_ref, rt_ref, slot_ref, blocks_ref, rtb_ref):
    pad = jnp.full((2, c.TP - c.T), -1, I32)
    rank = jnp.concatenate([rank_ref[...], pad], axis=1)
    rt = jnp.concatenate([rt_ref[...], pad], axis=1)
    side = 64
    index = lax.broadcasted_iota(I32, (side, c.TP), 0)
    rows = [(index == (rank[k : k + 1] >> 6)).astype(BF) for k in range(2)]
    cols = [index == (rank[k : k + 1] & 63) for k in range(2)]
    table = jnp.zeros((side, side), F32)
    for k in range(2):
        named = (rt[k : k + 1] + 1).astype(F32)
        table = table + dot_nt(rows[k], jnp.where(cols[k], named, 0.0).astype(BF))
    up_to = lax.broadcasted_iota(I32, (side, side), 0) < lax.broadcasted_iota(I32, (side, side), 1)
    above = lax.broadcasted_iota(I32, (side, side), 0) > lax.broadcasted_iota(I32, (side, side), 1)
    lane = lax.broadcasted_iota(I32, (1, 128), 1)
    named = [(table == e + 1.0).astype(F32) for e in range(c.E)]
    along = dot_nn(jnp.concatenate(named, axis=0).astype(BF), up_to.astype(BF))
    numbers = jnp.zeros((side, 128), F32)
    for e in range(c.E):
        numbers = numbers + jnp.where(lane == e, jnp.sum(named[e], axis=1, keepdims=True), 0.0)
    down = dot_nn(above.astype(BF), numbers.astype(BF))
    place_of = jnp.zeros((side, side), F32)
    for e in range(c.E):
        here = along[e * side : (e + 1) * side] + down[:, e : e + 1]
        place_of = place_of + named[e] * here
    place_of = place_of.astype(I32)
    high = (place_of >> 4).astype(F32).astype(BF)
    low = (place_of & 15).astype(F32).astype(BF)
    places = []
    for k in range(2):
        values = dot_tn(high, rows[k]) * 16.0 + dot_tn(low, rows[k])
        places.append(jnp.sum(jnp.where(cols[k], values, 0.0), axis=0, keepdims=True).astype(I32))
    for e in range(c.E):
        second = jnp.where(rt[1:2, :] == e, places[1], -1)
        slot_ref[e : e + 1, :] = jnp.where(rt[0:1, :] == e, places[0], second)
    for r in range(c.n):
        blocks_ref[r] = slot_ref[:, r * c.R : (r + 1) * c.R]
        rtb_ref[r] = jnp.concatenate([rt[:, r * c.R : (r + 1) * c.R]] * 4, axis=0)
    numbers = jnp.sum(numbers, axis=0, keepdims=True)
    return jnp.concatenate([numbers, jnp.zeros((1, c.half - 128), F32)], axis=1).astype(I32)


def fill_hot(c, place, slot_ref, hot_ref, halves):
    for j in range(c.X):
        row = window_slot(c, slot_ref[pl.ds(expert_of(c, place, j), 1), :])
        for index, half in enumerate(halves):
            slots = lax.broadcasted_iota(I32, (c.SP, c.TP), 0) + half * c.SP
            hot_ref[index, j * c.SP : (j + 1) * c.SP, :] = (slots == row).astype(BF)


def route_body(c, place, *refs):
    rank_ref, rt_ref, src_ref, slot_ref, blocks_ref, rtb_ref, out_ref, hot_ref, sum_ref = refs

    @pl.when(pl.program_id(0) == 0)
    def _():
        numbers = count_places(c, rank_ref, rt_ref, slot_ref, blocks_ref, rtb_ref)
        sum_ref[0:1, :] = (numbers >> 4).astype(F32)
        sum_ref[1:2, :] = (numbers & 15).astype(F32)
        fill_hot(c, place, slot_ref, hot_ref, (0, 1))

    for half in range(2):
        acc = dot_nn(hot_ref[half, :, : c.T], src_ref[...])
        for j in range(c.X):
            at = (2 * j + half) * c.SP
            out_ref[at : at + c.SP, :] = acc[j * c.SP : (j + 1) * c.SP].astype(BF)
            if half == 0:

                @pl.when(pl.program_id(0) == 0)
                def _():
                    tile = acc[(j + 1) * c.SP - 16 : (j + 1) * c.SP]
                    tile = last_rows(c, tile, sum_ref[0:1, :], sum_ref[1:2, :])
                    out_ref[at + c.SP - 16 : at + c.SP, :] = tile.astype(BF)


def route(c, order, place, routes, priority, source):
    rank = priority.T
    rt = routes.T
    outs = [
        shape_of((c.E, c.TP), I32),
        shape_of((c.n, c.E, c.R), I32),
        shape_of((c.n, 8, c.R), I32),
        shape_of((2 * c.X * c.SP, c.D), BF),
    ]
    result = call(
        order,
        functools.partial(route_body, c),
        place,
        [rank, rt, source],
        [whole(rank), whole(rt)]
        + [pl.BlockSpec((c.T, c.half), lambda i, s: (0, i ^ s[2]))],
        outs,
        [whole(o) for o in outs[:3]] + [cols_of((2 * c.X * c.SP, c.half))],
        (2,),
        [pltpu.VMEM((2, c.X * c.SP, c.TP), BF), pltpu.VMEM((8, c.half), F32)],
        name="route",
    )
    return (*result[:3], result[3].reshape(c.X, 2 * c.SP, c.D))


def keep_body(c, place, tail_ref, slot_ref, rt_ref, mine_ref, keep_ref, lane_ref):
    earlier = jnp.zeros((1, 128), F32)
    for b in range(c.X):
        high, low = last_pair(c, tail_ref[b], 128)
        earlier = earlier + jnp.where(b < place[0], high * 16.0 + low, 0.0)
    wide = (c.E, 128)
    eye = lax.broadcasted_iota(I32, wide, 0) == lax.broadcasted_iota(I32, wide, 1)
    offset = jnp.sum(jnp.where(eye, earlier, 0.0), axis=1, keepdims=True).astype(I32)
    slot = slot_ref[0]
    kept = (slot >= 0) & (slot + offset < c.cap)
    slots = jnp.where(kept, window_slot(c, slot), -1)
    expert = lax.broadcasted_iota(I32, (c.E, 1), 0)
    for j in range(8):
        if j < c.X:
            here = jnp.where(expert == expert_of(c, place, j), slots, -1)
            mine_ref[0, j : j + 1, :] = jnp.max(here, axis=0, keepdims=True)
        else:
            mine_ref[0, j : j + 1, :] = jnp.full((1, c.R), -1, I32)
    rows = []
    for k in range(2):
        picked = jnp.where((rt_ref[0, k : k + 1, :] == expert) & kept, 1.0, 0.0)
        rows.append(jnp.sum(picked, axis=0, keepdims=True))
    keep_ref[0] = jnp.concatenate(rows * 4, axis=0)

    @pl.when(pl.program_id(0) == place[1])
    def _():
        lane_ref[...] = jnp.where(kept, 1.0, 0.0)


def keep_of(c, order, place, rows, blocks, rt):
    outs = [
        shape_of((c.n, 8, c.R), I32),
        shape_of((c.n, 8, c.R), F32),
        shape_of((c.E, c.R), F32),
    ]
    tail = pl.BlockSpec((c.X, 16, c.half), lambda i, s: (0, c.SP // 16 - 1, 0))
    return call(
        order,
        functools.partial(keep_body, c),
        place,
        [rows, blocks, rt],
        [tail, rows_of((1, c.E, c.R)), rows_of((1, 8, c.R))],
        outs,
        [rows_of((1, 8, c.R)), rows_of((1, 8, c.R)), whole(outs[2])],
        (c.n,),
        name="keep",
    )


def last_rows(c, tile, high, low):
    row = lax.broadcasted_iota(I32, (16, 1), 0)
    return jnp.where(row == 14, high, jnp.where(row == 15, low, tile))


def put_gates(c, place, hot_ref, weights, acc, out_ref):
    gates = dot_nn(hot_ref[0], weights)
    lane = lax.broadcasted_iota(I32, (1, 128), 1)
    wide = (c.SP, c.half)
    eye = lax.broadcasted_iota(I32, wide, 0) == lax.broadcasted_iota(I32, wide, 1)
    for j in range(c.X):
        e = expert_of(c, place, j)
        mine = gates[j * c.SP : (j + 1) * c.SP]
        rows = []
        for at in (e, e + 64):
            col = jnp.sum(jnp.where(lane == at, mine, 0.0), axis=1, keepdims=True)
            rows.append(jnp.sum(jnp.where(eye, col, 0.0), axis=0, keepdims=True))
        end = (j + 1) * c.SP
        tile = last_rows(c, acc[end - 16 : end], rows[0], rows[1])
        out_ref[end - 16 : end, :] = tile.astype(BF)


def dispatch_body(c, half, place, slot_ref, src_ref, weight_ref, out_ref, hot_ref):
    @pl.when(pl.program_id(0) == 0)
    def _():
        fill_hot(c, place, slot_ref, hot_ref, (half,))

    acc = dot_nn(hot_ref[0], src_ref[...])
    out_ref[...] = acc.astype(BF)

    @pl.when(pl.program_id(0) == 0)
    def _():
        put_gates(c, place, hot_ref, weight_ref[...], acc, out_ref)


def dispatch(c, order, place, slot, source, weight, half):
    return call(
        order,
        functools.partial(dispatch_body, c, half),
        place,
        [slot, source, weight],
        [whole(slot), pl.BlockSpec((c.TP, c.half), lambda i, s: (0, i ^ s[2])), whole(weight)],
        [shape_of((c.X * c.SP, c.D), BF)],
        [cols_of((c.X * c.SP, c.half))],
        (2,),
        [pltpu.VMEM((1, c.X * c.SP, c.TP), BF)],
        name="dispatch",
    )[0].reshape(c.X, c.SP, c.D)


def norm_rows(values):
    centred = values - jnp.mean(values, axis=-1, keepdims=True)
    inv_std = lax.rsqrt(jnp.mean(centred * centred, axis=-1, keepdims=True) + 1e-06)
    return centred * inv_std, inv_std


def norm_back(grad_norm, gain, normed, inv_std):
    scaled = grad_norm * gain
    return inv_std * (
        scaled
        - jnp.mean(scaled, axis=-1, keepdims=True)
        - normed * jnp.mean(scaled * normed, axis=-1, keepdims=True)
    )


def small_row(c, small_ref, index, count=1):
    return small_ref[index : index + count, :].astype(F32)


def own_cols(c, place):
    return pl.ds(pl.multiple_of(place[2] * c.half, c.half), c.half)


def other_cols(c, place):
    return pl.ds(pl.multiple_of((1 - place[2]) * c.half, c.half), c.half)


def last_block(c):
    return (c.T - 1) // c.R


def own_rows(c):
    return pl.BlockSpec((c.R, c.D), lambda i, s: (jnp.minimum(s[1], last_block(c)), 0))


def live_rows(c, first, count):
    return (first + lax.broadcasted_iota(I32, (count, 1), 0)) < c.T


def qkv_body(c, place, *refs):
    tok_ref, small_ref, own_ref, oth_ref, hid_ref, qkv_ref, normed_ref, mix_ref, w_ref, all_ref = refs
    step = pl.program_id(0)

    @pl.when(step == 0)
    def _():
        mix_ref[...] = jnp.zeros_like(mix_ref)
        for part in range(3):
            lanes = slice(part * c.W, (part + 1) * c.W)
            w_ref[own_cols(c, place), lanes] = own_ref[part]
            w_ref[other_cols(c, place), lanes] = oth_ref[part]

    @pl.when(step < c.n)
    def _():
        live = live_rows(c, step * c.R, c.R)
        values = jnp.where(live, tok_ref[...].astype(F32), 0.0)
        normed, _ = norm_rows(values)
        hidden = normed * small_row(c, small_ref, 0) + small_row(c, small_ref, 2)
        normed_ref[...] = normed.astype(BF)
        hidden = jnp.where(live, hidden, 0.0).astype(BF)
        hid_ref[...] = hidden
        acc = dot_nn(hidden, w_ref[...])
        bias = small_row(c, small_ref, 5)
        zero = jnp.zeros((1, c.W), F32)
        shift = jnp.concatenate([bias[:, : c.W], zero, bias[:, c.half : c.half + c.W]], axis=1)
        result = (acc + shift).astype(BF)
        qkv_ref[...] = result
        all_ref[pl.ds(pl.multiple_of(step * c.R, 16), c.R), :] = result

    @pl.when(step >= c.n)
    def _():
        attend(c, step - c.n, all_ref, mix_ref)


def image_window(c, image):
    start = image * IMG_LEN
    low = pl.multiple_of(start // 16 * 16, 16)
    return low, start - low


def groups_of(c):
    lanes = min(128, c.W)
    return [(at, lanes) for at in range(0, c.W, lanes)]


def head_mask(lanes, head):
    lane = lax.broadcasted_iota(I32, (1, lanes), 1)
    return (lane >= head * HEAD) & (lane < (head + 1) * HEAD)


def stack_heads(c, values):
    heads = range(c.W // HEAD)
    return jnp.concatenate([jnp.where(head_mask(c.W, h), values, BF(0)) for h in heads], axis=0)


def pick_heads(c, values):
    total = None
    for h in range(c.W // HEAD):
        part = jnp.where(head_mask(c.W, h), values[h * c.win : (h + 1) * c.win], 0.0)
        total = part if total is None else total + part
    return total


def attend(c, image, qkv_ref, mix_ref):
    low, off = image_window(c, image)
    row = lax.broadcasted_iota(I32, (c.win, 1), 0)
    col = lax.broadcasted_iota(I32, (1, c.win), 1)
    in_row = (row >= off) & (row < off + IMG_LEN)
    in_col = (col >= off) & (col < off + IMG_LEN)
    q = stack_heads(c, qkv_ref[pl.ds(low, c.win), : c.W] * BF(HEAD**-0.5))
    k = qkv_ref[pl.ds(low, c.win), c.W : 2 * c.W]
    v = qkv_ref[pl.ds(low, c.win), 2 * c.W :]
    scores = jnp.where(in_col, dot_nt(q, k), LOW)
    exps = jnp.exp(scores - jnp.max(scores, axis=-1, keepdims=True))
    probs = exps * (1.0 / jnp.sum(exps, axis=-1, keepdims=True))
    total = pick_heads(c, dot_nn(probs.astype(BF), v)).astype(BF)
    for group, (at, lanes) in enumerate(groups_of(c)):
        old = mix_ref[group, pl.ds(low, c.win), :]
        mix_ref[group, pl.ds(low, c.win), :] = jnp.where(in_row, total[:, at : at + lanes], old)


def attend_back_body(c, place, qkv_ref, *refs):
    pieces, (out_ref, sums_ref, grad_ref) = refs[: c.n], refs[c.n :]

    @pl.when(pl.program_id(0) == 0)
    def _():
        out_ref[...] = jnp.zeros_like(out_ref)
        sums_ref[...] = jnp.zeros_like(sums_ref)
        for k in range(c.n):
            at = pl.multiple_of((place[1] ^ k) * c.R, 16)
            grad_ref[pl.ds(at, c.R), :] = pieces[k][...]

    low, off = image_window(c, pl.program_id(0))
    row = lax.broadcasted_iota(I32, (c.win, 1), 0)
    in_row = (row >= off) & (row < off + IMG_LEN)
    scale = HEAD**-0.5
    q = stack_heads(c, qkv_ref[pl.ds(low, c.win), : c.W] * BF(scale))
    k = qkv_ref[pl.ds(low, c.win), c.W : 2 * c.W]
    v = qkv_ref[pl.ds(low, c.win), 2 * c.W :]
    do = stack_heads(c, jnp.where(in_row, grad_ref[pl.ds(low, c.win), :], BF(0)))
    scores = jnp.where(in_row, dot_nt(k, q), LOW)
    exps = jnp.exp(scores - jnp.max(scores, axis=0, keepdims=True))
    soft = exps * (1.0 / jnp.sum(exps, axis=0, keepdims=True))
    dp = dot_nt(v, do)
    delta = jnp.sum(soft * dp, axis=0, keepdims=True)
    ds = (soft * (dp - delta)).astype(BF)
    dq = pick_heads(c, dot_tn(ds, k)) * scale
    dk = dot_nn(ds, q)
    dv = dot_nn(soft.astype(BF), do)
    for part, grad in enumerate((dq, dk, dv)):
        lanes = slice(part * c.W, (part + 1) * c.W)
        low_grad = jnp.where(in_row, grad, 0.0).astype(BF)
        old = out_ref[pl.ds(low, c.win), lanes]
        out_ref[pl.ds(low, c.win), lanes] = jnp.where(in_row, low_grad, old)
        sums_ref[0:1, lanes] += jnp.sum(low_grad.astype(F32), axis=0, keepdims=True)


def middle_rows(c, place, step, mixes, tok_ref, small_ref, table_ref, slot_ref, proj_ref):
    branch = dot_nn(jnp.concatenate([mix[...] for mix in mixes], axis=1), proj_ref[...])
    live = live_rows(c, step * c.R, c.R)
    tok = jnp.where(live, tok_ref[...].astype(F32), 0.0)
    after = tok + branch + small_row(c, small_ref, 4)
    normed, _ = norm_rows(after)
    hidden = (normed * small_row(c, small_ref, 1) + small_row(c, small_ref, 3)).astype(BF)
    router = table_ref[c.E : 2 * c.E, :]
    logits = dot_nt(router, hidden)
    exps = jnp.exp(logits - jnp.max(logits, axis=0, keepdims=True))
    probs = exps / jnp.sum(exps, axis=0, keepdims=True)
    weight = jnp.where(slot_ref[0] >= 0, probs, 0.0)
    high, rest = split_low(weight)
    lane = lax.broadcasted_iota(I32, (c.E, 128), 1)
    index = lax.broadcasted_iota(I32, (c.E, 128), 0)
    both = dot_tn(high, (lane == index).astype(BF)) + dot_tn(rest, (lane == index + 64).astype(BF))
    return after, hidden, probs, both.astype(BF)


def middle_body(c, place, *refs):
    refs = list(refs)
    count = c.n * len(groups_of(c))
    mixes, refs = refs[:count], refs[count:]
    w_ref, tok_ref, small_ref, table_ref, blocks_ref, slot_ref = refs[:6]
    hid_ref, weight_ref, after_ref, probs_ref, out_ref = refs[6:11]
    proj_ref, hids_ref, weights_ref, hot_ref = refs[11:]
    step = pl.program_id(0)

    @pl.when(step == 0)
    def _():
        for k in range(c.n):
            for h in range(2):
                cols = slice(h * c.half, (h + 1) * c.half)
                proj_ref[k * c.W : (k + 1) * c.W, cols] = w_ref[(place[1] ^ k) * 2 + h]

    @pl.when(step < c.n)
    def _():
        after, hidden, probs, weight = middle_rows(
            c, place, step, mixes, tok_ref, small_ref, table_ref, blocks_ref, proj_ref
        )
        rows = pl.ds(pl.multiple_of(step * c.R, 16), c.R)
        hid_ref[...] = hidden
        hids_ref[rows, :] = hidden
        weight_ref[...] = weight
        weights_ref[rows, :] = weight

        @pl.when(step == place[1])
        def _():
            after_ref[...] = after
            probs_ref[...] = probs

    @pl.when(step == c.n)
    def _():
        fill_hot(c, place, slot_ref, hot_ref, (0,))

    @pl.when(step >= c.n)
    def _():
        cols = pl.multiple_of(((step - c.n) ^ place[2]) * c.half, c.half)
        acc = dot_nn(hot_ref[0], hids_ref[:, pl.ds(cols, c.half)])
        out_ref[...] = acc.astype(BF)

        @pl.when(step == c.n)
        def _():
            put_gates(c, place, hot_ref, weights_ref[...], acc, out_ref)


def middle(c, order, place, mixes, proj, tokens, small, table, blocks, slot):
    def early(dims):
        return pl.BlockSpec(dims, lambda i, s: (jnp.minimum(i, c.n - 1),) + (0,) * (len(dims) - 1))

    args = [pair[0] for pair in flat(mixes)] + [proj, tokens, small, table, blocks, slot]
    specs = [
        pl.BlockSpec((None, c.R, a.shape[2]), lambda i, s, at=at: (at, jnp.minimum(i, c.n - 1), 0))
        for a, at in flat(mixes)
    ]
    tok_rows = pl.BlockSpec((c.R, c.D), lambda i, s: (jnp.minimum(i, last_block(c)), 0))
    specs += [whole(proj), tok_rows, whole(small), whole(table)]
    specs += [early((1, c.E, c.R)), whole(slot)]
    outs = [
        shape_of((c.TP, c.D), BF),
        shape_of((c.TP, 128), BF),
        shape_of((c.R, c.D), F32),
        shape_of((c.E, c.R), F32),
        shape_of((c.X * c.SP, c.D), BF),
    ]
    late = pl.BlockSpec((c.X * c.SP, c.half), lambda i, s: (0, jnp.maximum(i - c.n, 0)))
    result = call(
        order,
        functools.partial(middle_body, c),
        place,
        args,
        specs,
        outs,
        [early((c.R, c.D)), early((c.R, 128)), whole(outs[2]), whole(outs[3]), late],
        (c.n + 2,),
        [
            pltpu.VMEM((c.D, c.D), BF),
            pltpu.VMEM((c.TP, c.D), BF),
            pltpu.VMEM((c.TP, 128), BF),
            pltpu.VMEM((1, c.X * c.SP, c.TP), BF),
        ],
        name="middle",
    )
    return (*result[:4], result[4].reshape(c.X, c.SP, c.D))


def fill_packs(c, place, tails, packs):
    lane = lax.broadcasted_iota(I32, (1, 128), 1)
    here = place[0] * EXP_DEV + place[3]
    state = [jnp.zeros((1, 1), F32)] * 3
    for j in range(c.X):
        high, low = last_pair(c, tails[j], 128)
        number = jnp.sum(jnp.where(lane == here, high * 16.0 + low, 0.0), axis=1, keepdims=True)
        kept = jnp.clip(c.cap - state[0], 0.0, number)
        first = jnp.minimum(kept, float(c.Q))
        sizes = first, kept - first
        for half in range(2):
            wide = (c.CR[half], c.SP)
            slot = lax.broadcasted_iota(I32, wide, 1)
            at = lax.broadcasted_iota(I32, wide, 0) - state[1 + half].astype(I32)
            hot = (at == slot) & (slot < sizes[half].astype(I32))
            packs[half][:, j * c.SP : (j + 1) * c.SP] = hot.astype(BF)
        state = [state[0] + number, state[1] + sizes[0], state[2] + sizes[1]]


def last_pair(c, tile, lanes):
    tile = tile[:, :lanes].astype(F32)
    return tile[14:15, :], tile[15:16, :]


def row_chunks(rows, size):
    return [slice(at, min(at + size, rows)) for at in range(0, rows, size)]


def grad_active_body(c, place, rows_ref, own_ref, oth_ref, *outs):
    gas, all_ref, packs = outs[:2], outs[2], outs[3:]

    @pl.when(pl.program_id(0) == 0)
    def _():
        tails = [rows_ref[j, c.SP - 16 : c.SP, :] for j in range(c.X)]
        fill_packs(c, place, tails, packs)
        for half, base in enumerate((0, c.CR[0])):
            rows = [rows_ref[j, half * c.SP : (half + 1) * c.SP, :] for j in range(c.X)]
            got = dot_nn(packs[half][...], jnp.concatenate(rows, axis=0))
            all_ref[base : base + c.CR[half], :] = got.astype(BF)

    weights = jnp.concatenate([own_ref[...], oth_ref[...]], axis=1)
    for half, base in enumerate((0, c.CR[0])):
        for at in row_chunks(c.CR[half], 320):
            values = all_ref[base + at.start : base + at.stop, :]
            gas[half][at, :] = dot_nt(values, weights).astype(BF)


def grad_active(c, order, place, rows, own_w, oth_w):
    outs = [shape_of((count, c.F), BF) for count in c.CR] + [shape_of((sum(c.CR), c.D), BF)]
    outs += [shape_of((count, c.X * c.SP), BF) for count in c.CR]
    return call(
        order,
        functools.partial(grad_active_body, c),
        place,
        [rows, own_w, oth_w],
        [whole(rows, 1)] + [rows_of((c.fblk, c.half))] * 2,
        outs,
        [cols_of((count, c.fblk)) for count in c.CR] + [whole(o) for o in outs[2:]],
        (c.F // c.fblk,),
        name="grad_active",
    )


def expert_body(c, half, place, *refs):
    rows_ref, pack_ref, own_ref, oth_ref, bias_ref, ga_ref = refs[:6]
    act_ref, gp_ref, gb_ref, all_ref, col_ref, back_ref = refs[6:12]
    acc_ref, dot_ref, row_ref, wide_ref = refs[12:]
    step = pl.program_id(0)

    @pl.when(step == 0)
    def _():
        acc_ref[...] = jnp.zeros_like(acc_ref)
        dot_ref[...] = jnp.zeros_like(dot_ref)
        all_ref[...] = dot_nn(pack_ref[...], rows_ref[...]).astype(BF)
        eye = lax.broadcasted_iota(I32, (c.SP, c.SP), 0) == lax.broadcasted_iota(I32, (c.SP, c.SP), 1)
        lane = lax.broadcasted_iota(I32, (1, 128), 1)
        for j in range(c.X):
            end = (j + 1) * c.SP
            high, low = last_pair(c, rows_ref[end - 16 : end, :], c.SP)
            high = jnp.sum(jnp.where(eye, high, 0.0), axis=1, keepdims=True)
            low = jnp.sum(jnp.where(eye, low, 0.0), axis=1, keepdims=True)
            both = jnp.where(lane == 0, high, jnp.where(lane == 1, low, 0.0))
            wide_ref[j * c.SP : end, :] = both.astype(BF)
        both = dot_nn(pack_ref[...], wide_ref[...])
        col_ref[...] = jnp.broadcast_to(both[:, 0:1] + both[:, 1:2], (c.CR[half], 128))

    bias = bias_ref[...]
    weights = jnp.concatenate([own_ref[...], oth_ref[...]], axis=0)
    summed = jnp.zeros((1, c.fblk), F32)
    lead = 0.7978845608028654
    cube = lead * 0.044715
    chunks = row_chunks(c.CR[half], 224)
    ahead = dot_nn(all_ref[chunks[0], :], weights)
    for i, rows_at in enumerate(chunks):
        pre = ahead + bias
        if i + 1 < len(chunks):
            ahead = dot_nn(all_ref[chunks[i + 1], :], weights)
        square = pre * pre
        turn = jnp.tanh(pre * (cube * square + lead))
        above = 1.0 + turn
        active = (0.5 * pre) * above
        slope = above * (1.0 + (1.0 - turn) * (pre * (3 * cube * square + lead)))
        ga = ga_ref[rows_at, :].astype(F32)
        product = active * ga
        part = product[:, 0:128]
        for lane in range(128, c.fblk, 128):
            part = part + product[:, lane : lane + 128]
        dot_ref[rows_at, :] += part
        grad = ga * slope * (0.5 * col_ref[rows_at, 0:1])
        act_ref[rows_at, :] = active.astype(BF)
        grad_low = grad.astype(BF)
        gp_ref[rows_at, :] = grad_low
        summed = summed + jnp.sum(grad, axis=0, keepdims=True)
        acc_ref[rows_at, :] += dot_nt(grad_low, weights)
    gb_ref[...] = jnp.broadcast_to(summed, (8, c.fblk))

    @pl.when(step == pl.num_programs(0) - 1)
    def _():
        ones = jnp.ones((8, 128), BF)
        row_ref[...] = jnp.zeros_like(row_ref)
        back_ref[...] = dot_tn(pack_ref[...], acc_ref[...].astype(BF)).astype(BF)
        a, rest = split_low(dot_ref[...])
        total = dot_nt(ones, a) + dot_nt(ones, rest)
        high, low = split_low(total)
        high = dot_nn(high, pack_ref[...])
        low = dot_nn(low, pack_ref[...])
        for j in range(c.X):
            end = (j + 1) * c.SP
            row_ref[0:8, : c.SP] = high[:, j * c.SP : end]
            row_ref[8:16, : c.SP] = low[:, j * c.SP : end]
            tile = back_ref[end - 16 : end, : c.half].astype(F32)
            tile = last_rows(c, tile, row_ref[0:1, :], row_ref[8:9, :])
            back_ref[end - 16 : end, : c.half] = tile.astype(BF)


def expert(c, order, place, half, rows, pack, own_w, oth_w, bias, ga):
    rows = rows.reshape(c.X * c.SP, c.D)
    args = [rows, pack, own_w, oth_w, bias, ga]
    count = c.CR[half]
    specs = [whole(rows, 1), whole(pack, 1)]
    specs += [cols_of((c.half, c.fblk))] * 2
    specs += [cols_of((1, c.fblk)), cols_of((count, c.fblk))]
    outs = [
        shape_of((count, c.F), BF),
        shape_of((count, c.F), BF),
        shape_of((8, c.F), F32),
    ]
    out_specs = [cols_of((count, c.fblk))] * 2 + [cols_of((8, c.fblk))]
    late = [shape_of((count, c.D), BF), shape_of((count, 128), F32)]
    late.append(shape_of((c.X * c.SP, c.D), BF))
    result = call(
        order,
        functools.partial(expert_body, c, half),
        place,
        args,
        specs,
        outs + late,
        out_specs + [whole(o, 1) for o in late],
        (c.F // c.fblk,),
        [
            pltpu.VMEM((count, c.D), F32),
            pltpu.VMEM((count, 128), F32),
            pltpu.VMEM((16, c.half), F32),
            pltpu.VMEM((c.X * c.SP, 128), BF),
        ],
        name="expert",
    )
    return (*result[:5], result[5].reshape(c.X, c.SP, c.D))


def produce_body(c, place, *refs):
    cols, acts, packs, own_ref, oth_ref, out_ref = refs[:2], refs[2:4], refs[4:6], *refs[6:9]
    accs = refs[9:]
    step = pl.program_id(0)

    @pl.when(step == 0)
    def _():
        for acc_ref in accs:
            acc_ref[...] = jnp.zeros_like(acc_ref)

    weights = jnp.concatenate([own_ref[...], oth_ref[...]], axis=1)
    for half in range(2):
        for at in row_chunks(c.CR[half], 320):
            accs[half][at, :] += dot_nn(acts[half][at, :], weights)

    @pl.when(step == pl.num_programs(0) - 1)
    def _():
        for half in range(2):
            values = (accs[half][...] * cols[half][:, 0:1]).astype(BF)
            values = dot_tn(packs[half][...], values).astype(BF)
            for j in range(c.X):
                rows = values[j * c.SP : (j + 1) * c.SP]
                out_ref[j, half * c.SP : (half + 1) * c.SP, :] = rows


def produce(c, order, place, cols, acts, packs, own_w, oth_w):
    out = shape_of((c.X, 2 * c.SP, c.D), BF)
    return call(
        order,
        functools.partial(produce_body, c),
        place,
        [*cols, *acts, *packs, own_w, oth_w],
        [whole(col) for col in cols]
        + [cols_of((rows, c.fblk)) for rows in c.CR]
        + [whole(pack) for pack in packs]
        + [rows_of((c.fblk, c.half))] * 2,
        [out],
        [whole(out, 1)],
        (c.F // c.fblk,),
        [pltpu.VMEM((rows, c.D), F32) for rows in c.CR],
        name="produce",
    )[0]


def grad_second_body(c, own, place, *refs):
    all_ref, cols, acts = refs[0], refs[1:3], refs[3:5]
    out_ref, row_ref = refs[-2:]

    @pl.when(pl.program_id(0) == 0)
    def _():
        for half, base in enumerate((0, c.CR[0])):
            rows_at = slice(base, base + c.CR[half])
            row_ref[rows_at, :] = (all_ref[rows_at, :].astype(F32) * cols[half][:, 0:1]).astype(BF)

    acc = dot_tn(acts[0][...], row_ref[: c.CR[0], :])
    acc = acc + dot_tn(acts[1][...], row_ref[c.CR[0] :, :])
    if own:
        acc = acc + refs[5][...].astype(F32)
    out_ref[...] = acc.astype(out_ref.dtype)


def grad_second(c, order, place, rows, cols, acts, add=None):
    own = add is not None
    args = [rows, *cols, *acts]
    total = sum(c.CR)
    specs = [pl.BlockSpec((total, c.half), lambda i, s: (0, 0 if own else 1))]
    specs += [whole(col) for col in cols] + [cols_of((count, c.fblk)) for count in c.CR]
    if own:
        args.append(add)
        specs.append(rows_of((c.fblk, c.half)))
    out = shape_of((c.F, c.half), F32 if own else BF)
    return call(
        order,
        functools.partial(grad_second_body, c, own),
        place,
        args,
        specs,
        [out],
        [rows_of((c.fblk, c.half))],
        (c.F // c.fblk,),
        [pltpu.VMEM((total, c.half), BF)],
        name="grad_second",
    )[0]


def grad_first_body(c, own, place, *refs):
    acc = dot_tn(refs[0][...], refs[2][...]) + dot_tn(refs[1][...], refs[3][...])
    if own:
        acc = acc + refs[4][...].astype(F32)
    refs[-1][...] = acc.astype(refs[-1].dtype)


def grad_first(c, order, place, rows, gps, add=None):
    own = add is not None
    args = [*rows, *gps]
    specs = [pl.BlockSpec((count, c.half), lambda i, s: (0, 0 if own else 1)) for count in c.CR]
    specs += [cols_of((count, c.fblk)) for count in c.CR]
    if own:
        args.append(add)
        specs.append(cols_of((c.half, c.fblk)))
    out = shape_of((c.half, c.F), F32 if own else BF)
    return call(
        order,
        functools.partial(grad_first_body, c, own),
        place,
        args,
        specs,
        [out],
        [cols_of((c.half, c.fblk))],
        (c.F // c.fblk,),
        name="grad_first",
    )[0]


def combine_body(c, with_dots, place, *refs):
    refs = list(refs)
    extras = [] if with_dots else [refs.pop(0), refs.pop(0)]
    halves = 2 if with_dots else 1
    rows, refs = refs[:halves], refs[halves:]
    tails = []
    if with_dots:
        tails, refs = refs[:2], refs[2:]
    mine_ref = refs.pop(0)
    groups = [(0, g) for g in groups_a(c)] + [(1, g) for g in groups_b(c)]
    outs, (hot_ref, row_ref) = refs[: len(groups)], refs[len(groups) :]
    pad = hot_ref.shape[1] // c.X

    @pl.when(pl.program_id(0) == 0)
    def _():
        row_ref[...] = jnp.zeros_like(row_ref)
        slots = lax.broadcasted_iota(I32, (c.R, pad), 1)
        for k in range(c.n):
            at = pl.multiple_of((place[1] ^ k) * c.R, 16)
            for j in range(c.X):
                hot = (mine_ref[pl.ds(at, c.R), j : j + 1] == slots).astype(BF)
                hot_ref[k * c.R : (k + 1) * c.R, j * pad : (j + 1) * pad] = hot
        if with_dots:
            wide = (c.SP, c.half)
            eye = lax.broadcasted_iota(I32, wide, 0) == lax.broadcasted_iota(I32, wide, 1)
            lane = lax.broadcasted_iota(I32, (1, 128), 1)
            for half in range(2):
                for j in range(c.X):
                    high, low = last_pair(c, tails[half][j], c.half)
                    high = jnp.sum(jnp.where(eye, high, 0.0), axis=1, keepdims=True)
                    low = jnp.sum(jnp.where(eye, low, 0.0), axis=1, keepdims=True)
                    e = expert_of(c, place, j)
                    cols = jnp.where(lane == e, high, jnp.where(lane == e + 64, low, 0.0))
                    at = j * pad + half * c.SP
                    row_ref[at : at + c.SP, :128] = cols.astype(BF)
            pulls = dot_nn(hot_ref[...], row_ref[:, :128]).astype(BF)
            expert = lax.broadcasted_iota(I32, (c.E, 128), 0)
            lane = lax.broadcasted_iota(I32, (c.E, 128), 1)
            pick = ((lane == expert) | (lane == expert + 64)).astype(BF)
            for (side, group), out_ref in zip(groups, outs):
                for at, k in enumerate(group):
                    if side == 0:
                        got = dot_nt(pick, pulls[k * c.R : (k + 1) * c.R])
                        out_ref[at, c.R :, :] = jnp.zeros((c.E, c.half), BF)
                        out_ref[at, c.R :, : c.R] = got.astype(BF)

    for half, rows_ref in enumerate(rows):
        size = rows_ref.shape[1]
        for j in range(c.X):
            at = j * pad + half * size
            row_ref[at : at + size, :] = rows_ref[j]
    result = dot_nn(hot_ref[...], row_ref[...]).astype(BF)
    for half in range(2):

        @pl.when(pl.program_id(0) == half)
        def _():
            for (side, group), out_ref in zip(groups, outs):
                if side == half:
                    for at, k in enumerate(group):
                        out_ref[at, : c.R, :] = result[k * c.R : (k + 1) * c.R]
                        if extras:
                            more = extras[0].shape[1] // 2
                            extra = [e[k, half * more : (half + 1) * more, :] for e in extras]
                            total = extra[0].astype(F32) + extra[1].astype(F32)
                            out_ref[at, c.R :, :] = total.astype(BF)


def combine(c, order, place, rows, mine, extra=None, cost=0):
    pad = up(2 * c.SP, 128)
    args = list(rows)
    specs = [pl.BlockSpec((c.X, r.shape[1], c.half), lambda i, s: (0, 0, i ^ s[2])) for r in rows]
    if extra is None:
        args += list(rows)
        specs += [pl.BlockSpec((c.X, 16, c.half), lambda i, s: (0, c.SP // 16 - 1, 0))] * 2
        outs = piece_outs(c, c.E)
    else:
        args = [*extra, *args]
        specs = [whole(e) for e in extra] + specs
        outs = piece_outs(c, extra[0].shape[1] // 2, extra[0].shape[1] // 2)
    args.append(mine)
    specs.append(whole(mine))
    result = call(
        order,
        functools.partial(combine_body, c, extra is None),
        place,
        args,
        specs,
        outs,
        [whole(o, 1) for o in outs],
        (2,),
        [pltpu.VMEM((c.n * c.R, c.X * pad), BF), pltpu.VMEM((c.X * pad, c.half), BF)],
        name="combine",
        cost=cost,
    )
    return list(result)


def back_two_body(c, place, *refs):
    refs = list(refs)
    groups = groups_of(c)
    heads, refs = refs[: c.n * len(groups)], refs[c.n * len(groups) :]
    count = (len(refs) - 13 - c.n) // 2
    a, b, refs = refs[:count], refs[count : 2 * count], refs[2 * count :]
    w_ref, after_ref, probs_ref, keep_ref = refs[:4]
    cot_ref, hid_ref, small_ref, table_ref, ga_ref, proj_own_ref, proj_oth_ref = refs[4:11]
    mixes, (gb_ref, sums_ref) = refs[11:-2], refs[-2:]
    sum_a = add_up(a)
    live = live_rows(c, place[1] * c.R, c.R)
    cot = jnp.where(live, cot_ref[...], BF(0))
    eshift = table_ref[: c.E, :]
    router = table_ref[c.E : 2 * c.E, :]
    kept = keep_ref[...] > 0
    pulls = jnp.where(kept, sum_a[c.R :, : c.R] + dot_nt(eshift, cot), 0.0)
    probs = probs_ref[...]
    glog = (probs * (pulls - jnp.sum(probs * pulls, axis=0, keepdims=True))).astype(BF)
    two = jnp.concatenate([sum_a[: c.R], add_up(b)], axis=1) + dot_tn(glog, router)
    normed, inv_std = norm_rows(after_ref[...])
    grad_after = cot.astype(F32) + norm_back(two, small_row(c, small_ref, 1), normed, inv_std)
    ga_ref[...] = grad_after
    low = grad_after.astype(BF)
    gb_ref[...] = low
    high, rest = split_low(probs * keep_ref[...])
    hid = jnp.where(live, hid_ref[...], BF(0))
    sums_ref[0:1, :] = jnp.sum(two * normed, axis=0, keepdims=True)
    sums_ref[1:2, :] = jnp.sum(two, axis=0, keepdims=True)
    sums_ref[2:3, :] = jnp.sum(low.astype(F32), axis=0, keepdims=True)
    sums_ref[3:8, :] = jnp.zeros((5, c.D), F32)
    sums_ref[8 : 8 + c.E, :] = dot_nn(high, cot) + dot_nn(rest, cot)
    sums_ref[8 + c.E : 8 + 2 * c.E, :] = dot_nn(glog, hid)
    for k in range(c.n):
        lane = place[1] ^ k
        mix = dot_nt(gb_ref[:, : c.half], w_ref[2 * lane])
        mix = mix + dot_nt(gb_ref[:, c.half :], w_ref[2 * lane + 1])
        mixes[k][...] = mix.astype(BF)
    height = sums_ref.shape[0]
    for cols, out_ref in ((own_cols(c, place), proj_own_ref), (other_cols(c, place), proj_oth_ref)):
        sums = sums_ref[:, cols].astype(BF)
        part = dot_tn(jnp.concatenate([head[...] for head in heads], axis=1), gb_ref[:, cols])
        for k in range(c.n):
            out_ref[k, : c.W, :] = part[k * c.W : (k + 1) * c.W].astype(BF)
            out_ref[k, c.W : c.W + height, :] = sums
            rest = out_ref.shape[1] - c.W - height
            out_ref[k, c.W + height :, :] = jnp.zeros((rest, c.half), BF)


def back_two(c, order, place, heads, sums, proj, lanes, cotangent, hidden, small, table):
    height = 8 + 2 * c.E
    rows = up(c.W + height, 32)
    args = [pair[0] for pair in flat(heads)]
    specs = [
        pl.BlockSpec((None, c.R, a.shape[2]), lambda i, s, at=at: (at, s[1], 0))
        for a, at in flat(heads)
    ]
    args += [*sums[0], *sums[1], proj, *lanes, cotangent, hidden, small, table]
    hid_rows = pl.BlockSpec((c.R, c.D), lambda i, s: (s[1], 0))
    specs += [first_block(a) for a in [*sums[0], *sums[1]]]
    specs += [whole(a) for a in [proj, *lanes]] + [own_rows(c), hid_rows]
    specs += [whole(small), whole(table)]
    outs = [shape_of((c.R, c.D), F32)] + [shape_of((c.n, rows, c.half), BF)] * 2
    outs += [shape_of((c.R, c.W), BF) for _ in range(c.n)]
    result = call(
        order,
        functools.partial(back_two_body, c),
        place,
        args,
        specs,
        outs,
        [whole(o) for o in outs],
        (1,),
        [pltpu.VMEM((c.R, c.D), BF), pltpu.VMEM((height, c.D), F32)],
        name="back_two",
    )
    return (*result[:3], list(result[3:]))


def block_out_body(c, place, *refs):
    refs = list(refs)
    count = (len(refs) - 6) // 2
    a, b, refs = refs[:count], refs[count : 2 * count], refs[2 * count :]
    after_ref, probs_ref, keep_ref, table_ref, out_ref, proj_ref = refs
    high, low = split_low(probs_ref[...] * keep_ref[...])
    eshift = table_ref[: c.E, :]
    shift = dot_tn(high, eshift) + dot_tn(low, eshift)
    more = proj_ref.shape[0] // 2
    for h, pieces in enumerate((a, b)):
        cols = slice(h * c.half, (h + 1) * c.half)
        total = add_up([ref.at[: c.R, :] for ref in pieces])
        out_ref[h] = (after_ref[:, cols] + total + shift[:, cols]).astype(BF)
        proj_ref[h * more : (h + 1) * more, :] = same_sum(c, pieces, slice(c.R, c.R + more)).astype(BF)


def block_out(c, order, place, sums, after, probs, keep, table):
    args = [*sums[0], *sums[1], after, probs, keep, table]
    more = 2 * (sums[0][0].shape[1] - c.R)
    outs = [shape_of((2, c.R, c.half), BF), shape_of((more, c.half), BF)]
    return call(
        order,
        functools.partial(block_out_body, c),
        place,
        args,
        [first_block(a) for a in args[:-4]] + [whole(a) for a in args[-4:]],
        outs,
        [whole(o) for o in outs],
        (1,),
        name="block_out",
    )


def grad_one_body(c, place, dqkv_ref, normed_ref, own_ref, oth_ref, *outs):
    sums_ref = outs[-1]
    groups = [(0, g) for g in groups_a(c)] + [(1, g) for g in groups_b(c)]
    for side in range(2):
        cols = slice(side * c.half, (side + 1) * c.half)
        weights = [jnp.where(place[2] == side, own_ref[p], oth_ref[p]) for p in range(3)]
        weights = jnp.concatenate(weights, axis=1)
        gain = jnp.zeros((1, c.half), F32)
        shift = jnp.zeros((1, c.half), F32)
        for (where, group), out_ref in zip(groups, outs):
            if where != side:
                continue
            for row, k in enumerate(group):
                rows_at = pl.ds(pl.multiple_of((place[1] ^ k) * c.R, 16), c.R)
                acc = dot_nt(dqkv_ref[rows_at, :], weights)
                out_ref[row, : c.R, :] = acc.astype(BF)
                normed = normed_ref[rows_at, cols].astype(F32)
                gain = gain + jnp.sum(acc * normed, axis=0, keepdims=True)
                shift = shift + jnp.sum(acc, axis=0, keepdims=True)
        sums_ref[0:1, cols] = gain
        sums_ref[1:2, cols] = shift
        row = lax.broadcasted_iota(I32, (16, 1), 0)
        tile = jnp.where(row == 0, gain, jnp.where(row == 1, shift, 0.0)).astype(BF)
        for (where, group), out_ref in zip(groups, outs):
            if where == side:
                for at in range(len(group)):
                    out_ref[at, c.R :, :] = tile


def grad_one(c, order, place, dqkv, normed, own_w, oth_w):
    outs = piece_outs(c, 16, 16) + [shape_of((2, c.D), F32)]
    result = call(
        order,
        functools.partial(grad_one_body, c),
        place,
        [dqkv, normed, own_w, oth_w],
        [whole(dqkv), whole(normed), whole(own_w), whole(oth_w)],
        outs,
        [whole(o) for o in outs],
        (1,),
        name="grad_one",
    )
    return list(result[:-1]), result[-1]


def grad_qkv_body(c, place, hid_ref, dqkv_ref, own_ref, oth_ref):
    own_ref[0] = dot_tn(hid_ref[:, own_cols(c, place)], dqkv_ref[...]).astype(BF)
    oth_ref[0] = dot_tn(hid_ref[:, other_cols(c, place)], dqkv_ref[...]).astype(BF)


def grad_qkv(c, order, place, hidden, dqkv):
    specs = [whole(hidden, 1), cols_of((c.TP, c.W))]
    if c.W % 128:
        dqkv = dqkv.reshape(c.TP, 3, c.W).transpose(1, 0, 2)
        specs[1] = pl.BlockSpec((None, c.TP, c.W), lambda i, s: (i, 0, 0))
    return call(
        order,
        functools.partial(grad_qkv_body, c),
        place,
        [hidden, dqkv],
        specs,
        [shape_of((3, c.half, c.W), BF)] * 2,
        [rows_of((1, c.half, c.W))] * 2,
        (3,),
        name="grad_qkv",
    )


def back_one_body(c, place, *refs):
    refs = list(refs)
    count = (len(refs) - 4) // 2
    a, b, refs = refs[:count], refs[count : 2 * count], refs[2 * count :]
    tok_ref, after_ref, small_ref, out_ref = refs
    live = live_rows(c, place[1] * c.R, c.R)
    normed, inv_std = norm_rows(jnp.where(live, tok_ref[...].astype(F32), 0.0))
    one = jnp.concatenate([add_up(a)[: c.R], add_up(b)[: c.R]], axis=1)
    grad = after_ref[...] + norm_back(one, small_row(c, small_ref, 0), normed, inv_std)
    for h in range(2):
        out_ref[h] = grad[:, h * c.half : (h + 1) * c.half].astype(BF)


def back_one(c, order, place, sums, tokens, after, small):
    args = [*sums[0], *sums[1], tokens, after, small]
    specs = [first_block(a) for a in args[:-3]] + [own_rows(c), whole(after), whole(small)]
    out = shape_of((2, c.R, c.half), BF)
    return call(
        order,
        functools.partial(back_one_body, c),
        place,
        args,
        specs,
        [out],
        [whole(out)],
        (1,),
        name="back_one",
    )[0]


def assemble_body(c, place, *refs):
    pieces, out_ref = refs[:-1], refs[-1]
    for k in range(c.n):

        @pl.when((place[1] ^ k) == pl.program_id(0))
        def _():
            for h in range(2):
                values = pieces[2 * k + h][...].astype(out_ref.dtype)
                out_ref[:, h * c.half : (h + 1) * c.half] = values


def assemble(c, order, place, pieces, dtype):
    out = shape_of((c.T, c.D), dtype)
    return call(
        order,
        functools.partial(assemble_body, c),
        place,
        [pair[0] for pair in flat(pieces)],
        [
            pl.BlockSpec((None, c.R, c.half), lambda i, s, at=at: (at, 0, 0))
            for _, at in flat(pieces)
        ],
        [out],
        [rows_of((c.R, c.D))],
        (-(-c.T // c.R),),
        name="assemble",
    )[0]


def local(
    tokens,
    cotangent,
    w_qkv,
    qv_bias,
    w_proj,
    proj_bias,
    norm_gains,
    norm_shifts,
    w_router,
    expert_shift,
    w_first,
    w_second,
    first_bias,
    routes,
    priority,
):
    T, D = tokens.shape
    n = lax.axis_size("mp")
    E = w_router.shape[1]
    S = 16 * T // (5 * E)
    R = up(-(-T // n), 16)
    F = w_first.shape[2]
    W = w_proj.shape[0]
    win = up(IMG_LEN + 15, 16)
    Q = (S + 1) // 2
    cap = (9 * T + 4 * EXP_DEV - 1) // (4 * EXP_DEV)
    X = E // EXP_DEV
    full = min(cap // S, X)
    c = Sizes(
        T=T,
        D=D,
        half=D // 2,
        n=n,
        X=X,
        E=E,
        S=S,
        Q=Q,
        SP=up(Q + 2, 16),
        CR=(up(min(cap, X * Q), 16), up(full * (S - Q) + max(0, cap - full * S - Q), 16)),
        R=R,
        TP=n * R,
        W=W,
        images=T // IMG_LEN,
        quarters=n // EXP_DEV,
        F=F,
        cap=cap,
        win=win,
        fblk=min(1024, F),
    )
    order = Order()
    dp, mp, grid = lax.axis_index("dp"), lax.axis_index("mp"), lax.axis_index("grid")
    place = jnp.stack([dp, mp, grid, mp // c.quarters]).astype(I32)

    slot, blocks, rt, grad_out = route(c, order, place, routes, priority, cotangent)
    grad_in = trade(grad_out, "dp")

    def both_halves(rows):
        rows = jnp.pad(rows, ((0, up(rows.shape[0], 16) - rows.shape[0]), (0, 0)))
        other = swap_grid(rows)
        return jnp.where(
            grid == 0,
            jnp.concatenate([rows, other], axis=1),
            jnp.concatenate([other, rows], axis=1),
        )

    wide_bias = jnp.pad(qv_bias, ((0, 0), (0, c.half - W)))
    small = both_halves(
        jnp.concatenate([norm_gains, norm_shifts, proj_bias[None], wide_bias], axis=0)
    )
    qkv_own = w_qkv.transpose(1, 0, 2)
    qkv_oth = swap_grid(qkv_own)

    first_own = w_first[0]
    second_own = w_second[0]
    proj = lax.all_gather(w_proj, ("mp", "grid"))

    groups = groups_of(c)
    outs = [shape_of((c.TP, D), BF), shape_of((c.TP, 3 * W), BF), shape_of((c.TP, D), BF)]
    outs.append(shape_of((len(groups), c.TP, groups[0][1]), BF))

    def first_steps(width):
        return pl.BlockSpec((c.R, width), lambda i, s: (jnp.minimum(i, n - 1), 0))

    hidden_one, qkv, normed_one, mix = call(
        order,
        functools.partial(qkv_body, c),
        place,
        [tokens, small, qkv_own, qkv_oth],
        [
            pl.BlockSpec((R, D), lambda i, s: (jnp.minimum(i, last_block(c)), 0)),
            whole(small),
            whole(qkv_own),
            whole(qkv_oth),
        ],
        outs,
        [first_steps(D), first_steps(3 * W), first_steps(D), whole(outs[3])],
        (n + c.images,),
        [pltpu.VMEM((D, 3 * W), BF), pltpu.VMEM((c.TP, 3 * W), BF)],
        name="qkv",
    )
    bias_rows = F // 2 // c.half
    tied = held(jnp.concatenate([expert_shift, w_router.T]), qkv)
    table = both_halves(tied)
    bias = both_halves(held(first_bias.reshape(bias_rows, c.half), qkv))[:bias_rows]
    bias = bias.reshape(bias_rows, 2, c.half).transpose(1, 0, 2).reshape(1, F).astype(F32)
    second_oth = swap_grid(held(second_own, qkv))
    first_oth = swap_grid(held(first_own, qkv))
    mixes, _ = gather_mp(c, held(mix, proj))
    hidden_two, weight, after, probs, rows_a = middle(
        c, order, place, mixes, proj, tokens, small, table, blocks, slot
    )

    rows_a = trade(rows_a, "dp")
    rows_b = dispatch(c, order, place, slot, hidden_two, weight, 1)
    ga_a, ga_b, grad_all, pack_a, pack_b = grad_active(
        c, order, place, grad_in, second_own, second_oth
    )
    mine, keep, keep_lane = keep_of(c, order, place, grad_in, blocks, rt)
    keep_mask = keep[:, :2, :].transpose(0, 2, 1).reshape(c.TP, 2)[:T].astype(I32)
    mine = mine.transpose(0, 2, 1).reshape(c.TP, 8)
    rows_b = trade(held(rows_b, rows_a, grad_all, keep_lane), "dp")
    act_a, gp_a, gb_a, all_a, col_a, back_a = expert(
        c, order, place, 0, rows_a, pack_a, first_own, first_oth, bias, ga_a
    )
    back_a = trade(held(back_a, rows_b), "dp")
    act_b, gp_b, gb_b, all_b, col_b, back_b = expert(
        c, order, place, 1, rows_b, pack_b, first_own, first_oth, bias, ga_b
    )
    back_b = trade(held(back_b, back_a), "dp")
    cols, acts, gps, alls = [col_a, col_b], [act_a, act_b], [gp_a, gp_b], [all_a, all_b]
    second_part = swap_grid(grad_second(c, order, place, grad_all, cols, acts))
    order.tie(back_a)
    first_part = swap_grid(grad_first(c, order, place, alls, gps))
    packs = [pack_a, pack_b]
    order.tie(mine)
    prod = produce(c, order, place, cols, acts, packs, second_own, second_oth)
    gb = (gb_a + gb_b)[0:1].reshape(2, F // 2)
    gb_own = lax.dynamic_index_in_dim(gb, grid, 0, True)
    gb_oth = lax.dynamic_index_in_dim(gb, 1 - grid, 0, True)
    grad_fbias = gb_own + swap_grid(gb_oth)

    pieces = combine(c, order, place, [back_a, back_b], mine)
    prod = trade(held(prod, back_b), "dp")
    two_sums = reduce_start(c, pieces)
    grad_second_out = grad_second(c, order, place, grad_all, cols, acts, second_part)
    two_sums = reduce_end(c, order, two_sums)
    grad_after, proj_a, proj_b, grad_mix = back_two(
        c,
        order,
        place,
        mixes,
        two_sums,
        proj,
        [after, probs, keep_lane],
        cotangent,
        hidden_two,
        small,
        table,
    )
    grad_mix = [grad_mix[0]] + [swap_mp(c, grad_mix[k], k) for k in range(1, n)]
    proj_parts = [proj_a, swap_grid(proj_b)]
    pieces = combine(c, order, place, [prod], mine, proj_parts, cost=10)
    out_sums = reduce_start(c, [held(p, *grad_mix) for p in pieces])

    outs = [shape_of((c.TP, 3 * W), BF), shape_of((8, 3 * W), F32)]
    dqkv, dqkv_sums = call(
        order,
        functools.partial(attend_back_body, c),
        place,
        [qkv, *grad_mix],
        [whole(qkv)] + [whole(p) for p in grad_mix],
        outs,
        [whole(o) for o in outs],
        (c.images,),
        [pltpu.VMEM((c.TP, W), BF)],
        name="attend_back",
    )
    one_pieces, one_parts = grad_one(c, order, place, dqkv, normed_one, qkv_own, qkv_oth)
    one_sums = reduce_start(c, one_pieces)
    out_sums = reduce_end(c, order, out_sums)
    qkv_a, qkv_b = grad_qkv(c, order, place, hidden_one, dqkv)
    qkv_b = swap_grid(qkv_b)
    qkv_low = (qkv_a.astype(F32) + qkv_b.astype(F32)).astype(BF)
    qkv_sum = sum_dp_start(c, qkv_low.reshape(-1, c.half))
    one_sums = reduce_end(c, order, one_sums)
    grad_low = back_one(c, order, place, one_sums, tokens, grad_after, small)
    qkv_sum = sum_dp_turn(c, qkv_sum)
    order.tie(qkv_sum)
    out_lane, proj_sum = block_out(c, order, place, out_sums, after, probs, keep_lane, table)

    qv_rows = jnp.concatenate([dqkv_sums[0:1, :W], dqkv_sums[0:1, 2 * W :]], axis=0)
    sums_one = held(first_sums(c, one_sums, one_parts), grad_low)
    sums_one = chip_sums(c, sums_one, qv_rows, grid).astype(BF)
    proj_end = proj_sum.shape[0]
    shared = jnp.concatenate([proj_sum, sums_one], axis=0)
    shared = jnp.pad(shared, ((0, up(shared.shape[0], 16 * c.X) - shared.shape[0]), (0, 0)))
    shared = sum_dp_start(c, shared)

    def last_expert_kernel(before):
        for value in before:
            order.tie(value)
        return grad_first(c, order, place, alls, gps, first_part), order.hold

    grad_low, out_lane, last, grad_first_out = gather_both(c, grad_low, out_lane, last_expert_kernel)
    grad_w_qkv = sum_dp_end(c, qkv_sum).reshape(3, c.half, W)
    grad_tokens = assemble(c, order, place, grad_low, F32)
    shared = sum_dp_end(c, sum_dp_turn(c, held(shared, grad_tokens, *last)))
    sums_one = shared[proj_end:]
    rest = shared[W : W + 8 + 2 * E]
    block = assemble(c, order, place, out_lane, BF)
    return (
        block,
        grad_tokens,
        grad_w_qkv.transpose(1, 0, 2),
        sums_one[2:3, :W],
        shared[:W],
        rest[2],
        jnp.stack([sums_one[0], rest[0]]),
        jnp.stack([sums_one[1], rest[1]]),
        rest[8 + E : 8 + 2 * E].T,
        rest[8 : 8 + E],
        grad_first_out[None],
        grad_second_out[None],
        grad_fbias,
        keep_mask,
    )


def solution(mesh):
    return jax.shard_map(
        local,
        mesh=mesh,
        in_specs=(
            P(("dp", "grid"), None),
            P(("dp", "grid"), None),
            P("grid", None, "mp"),
            P("grid", "mp"),
            P("mp", "grid"),
            P("grid"),
            P(None, "grid"),
            P(None, "grid"),
            P("grid", None),
            P(None, "grid"),
            P(("dp", "mp"), "grid", None),
            P(("dp", "mp"), None, "grid"),
            P(("dp", "mp"), "grid"),
            P(("dp", "grid"), None),
            P(("dp", "grid"), None),
        ),
        out_specs=(
            P(("dp", "grid"), None),
            P(("dp", "grid"), None),
            P("grid", None, "mp"),
            P("grid", "mp"),
            P("mp", "grid"),
            P("grid"),
            P(None, "grid"),
            P(None, "grid"),
            P("grid", None),
            P(None, "grid"),
            P(("dp", "mp"), "grid", None),
            P(("dp", "mp"), None, "grid"),
            P(("dp", "mp"), "grid"),
            P(("dp", "grid"), None),
        ),
        check_vma=False,
    )
```
